32 devices in a mesh: dp: 2 (over y), row: 4 (over z), col: 4 (over x, core).
Axes of the slice: x: 2, y: 2, z: 4, core: 2. Of those that a mesh axis runs over, the one named last changes fastest.
Arguments:
- tokens_in: bfloat16 [4096, 1536], P(('dp', 'row'), 'col'), may hold values from -6 to 6
- seq_lengths: int32 [2, 4], P('dp'), may hold values from 1 to 1792, 2048 in all within a row
- attention_gain: bfloat16 [1536], P('col'), may hold values from 0.5 to 1.5
- query_weight: bfloat16 [1536, 1536], P('col', 'row'), may hold values from -0.15625 to 0.15625
- query_bias: bfloat16 [1536], P('row'), may hold values from -3 to 3
- keyvalue_weight: bfloat16 [1536, 512], P('col', 'row'), may hold values from -0.15625 to 0.15625
- keyvalue_bias: bfloat16 [512], P('row'), may hold values from -3 to 3
- output_weight: bfloat16 [1536, 1536], P('row', 'col'), may hold values from -0.625 to 0.625
- feedforward_gain: bfloat16 [1536], P('col'), may hold values from 0.5 to 1.5
- gate_weight: bfloat16 [1536, 8960], P('col', 'row'), may hold values from -0.15625 to 0.15625
- up_weight: bfloat16 [1536, 8960], P('col', 'row'), may hold values from -0.15625 to 0.15625
- down_weight: bfloat16 [8960, 1536], P('row', 'col'), may hold values from -0.0625 to 0.0625
- cotangent: bfloat16 [4096, 1536], P(('dp', 'row'), 'col'), may hold values from -6 to 6
Outputs:
- layer_out: bfloat16 [4096, 1536], P(('dp', 'row'), 'col')
- input_grad: bfloat16 [4096, 1536], P(('dp', 'row'), 'col')
- attention_gain_grad: float32 [1536], P('col')
- query_weight_grad: float32 [1536, 1536], P(('col', 'dp'), 'row')
- query_bias_grad: float32 [1536], P(('row', 'dp'))
- keyvalue_weight_grad: float32 [1536, 512], P(('col', 'dp'), 'row')
- keyvalue_bias_grad: float32 [512], P(('row', 'dp'))
- output_weight_grad: float32 [1536, 1536], P(('row', 'dp'), 'col')
- feedforward_gain_grad: float32 [1536], P('col')
- gate_weight_grad: float32 [1536, 8960], P(('col', 'dp'), 'row')
- up_weight_grad: float32 [1536, 8960], P(('col', 'dp'), 'row')
- down_weight_grad: float32 [8960, 1536], P(('row', 'dp'), 'col')
The draws below stay inside these ranges and needn't reach their ends.
Inputs may be any that keep to these rules, and one draw needn't show every extreme that they name: `seq_lengths`: each row holds the lengths of the 4 sequences of one group in order; a row sums to 2048 and its largest entry is 1792.
All inputs are finite; a program needn't handle non-finite values.
Results may differ from the reference program's by a relative error of at most 0.013.
Values may be sent and summed in bfloat16 or wider, within the bound.
A program may use at most 256 MiB of HBM per device.

```python
import math
from functools import partial
import jax
import jax.numpy as jnp
import numpy as np
from jax import lax

D = 1536
HEADS = 12
KV_HEADS = 2
HEAD = 128
FF = 8960
GROUP_TOK = 2048
SEQS = 4
Q_WIDTH = 1536
KV_WIDTH = 512
LONGEST = 1792
GROUPS = 2
TOKENS = 4096
N_DP = 2


def block_scale(stream_key, extent, shards, low, top_value):
    def one(dim, parts):
        steps = jax.random.uniform(jax.random.fold_in(jax.random.fold_in(stream_key, 6), dim), (parts,), jnp.float32, low / len(shards), top_value / len(shards))
        return jnp.repeat(jnp.exp(steps), extent[dim] // parts).reshape((-1,) + (1,) * (len(extent) - dim - 1))

    factor_of = one(*shards[0])
    for cut in shards[1:]:
        factor_of = factor_of * one(*cut)
    return factor_of


def profile(amount, total, bound, lean):
    weights = [(1 << 20) // math.isqrt(grade ** lean) + 1 for grade in range(2, amount + 1)]
    surplus, holding = total - bound - (amount - 1), [1] * (amount - 1)
    while surplus > 0:
        movable = [i for i in range(amount - 1) if holding[i] < bound]
        pool, left = sum([weights[i] for i in movable]), surplus
        for i in movable:
            more = min(bound - holding[i], max(1, left * weights[i] // pool), surplus)
            holding[i] = holding[i] + more
            surplus = surplus - more
    return np.array([bound] + holding)


def ragged_sizes(rng, count, total, limit, slope):
    if count == 2:
        one = jax.random.randint(rng, (), max(1, total - limit), min(limit, total - 1) + 1)
        return jnp.stack([one, total - one])
    sizes = jnp.asarray(profile(count, total, limit, slope), jnp.int32)
    couples = (count - 1) // 2
    giver, sink = sizes[1:1 + 2 * couples:2], sizes[2:2 + 2 * couples:2]
    slack = jnp.minimum(giver - 1, limit - sink)
    moved = jax.random.randint(jax.random.fold_in(rng, 1), (couples,), 0, 1 << 20) % (slack + 1)
    sizes = sizes.at[1:1 + 2 * couples:2].set(giver - moved).at[2:2 + 2 * couples:2].set(sink + moved)
    return sizes[jax.random.permutation(jax.random.fold_in(rng, 2), count)]


def scatter_about(rng, extent, spread, limit, cuts=(), held_as=jnp.bfloat16):
    entries = spread * jax.random.normal(rng, extent, jnp.float32)
    if cuts:
        entries = entries * block_scale(rng, extent, cuts, -0.22, 0.18)
    return jnp.clip(entries, -limit, limit).astype(held_as)


def setup_inputs(seed: int = 0) -> dict:
    arg_keys = jax.random.split(jax.random.key(seed), 14)
    tokens_in = scatter_about(arg_keys[0], (TOKENS, D), 1.0, 6.0, ((0, 8), (1, 4)))
    seq_lengths = jax.vmap(lambda own: ragged_sizes(own, SEQS, GROUP_TOK, LONGEST, 2))(jax.random.split(arg_keys[1], GROUPS)).reshape((GROUPS, SEQS)).astype(jnp.int32)
    attention_gain = jnp.clip(1.0 + 0.1 * jax.random.normal(arg_keys[2], (D,), jnp.float32), 0.5, 1.5).astype(jnp.bfloat16)
    query_weight = scatter_about(arg_keys[3], (D, Q_WIDTH), D ** -0.5, 0.15625, ((0, 4), (1, 4)))
    query_bias = scatter_about(arg_keys[4], (Q_WIDTH,), 0.5, 3.0, ((0, 4),))
    keyvalue_weight = scatter_about(arg_keys[5], (D, KV_WIDTH), D ** -0.5, 0.15625, ((0, 4), (1, 4)))
    keyvalue_bias = scatter_about(arg_keys[6], (KV_WIDTH,), 0.5, 3.0, ((0, 4),))
    output_weight = scatter_about(arg_keys[7], (Q_WIDTH, D), (Q_WIDTH // 16) ** -0.5, 0.625, ((0, 4), (1, 4)))
    feedforward_gain = jnp.clip(1.0 + 0.1 * jax.random.normal(arg_keys[8], (D,), jnp.float32), 0.5, 1.5).astype(jnp.bfloat16)
    gate_weight = scatter_about(arg_keys[9], (D, FF), D ** -0.5, 0.15625, ((0, 4), (1, 4)))
    up_weight = scatter_about(arg_keys[10], (D, FF), D ** -0.5, 0.15625, ((0, 4), (1, 4)))
    down_weight = scatter_about(arg_keys[11], (FF, D), FF ** -0.5, 0.0625, ((0, 4), (1, 4)))
    cotangent = scatter_about(arg_keys[12], (TOKENS, D), 1.0, 6.0, ((0, 8), (1, 4)))
    return dict(tokens_in=tokens_in, seq_lengths=seq_lengths, attention_gain=attention_gain, query_weight=query_weight, query_bias=query_bias, keyvalue_weight=keyvalue_weight, keyvalue_bias=keyvalue_bias, output_weight=output_weight, feedforward_gain=feedforward_gain, gate_weight=gate_weight, up_weight=up_weight, down_weight=down_weight, cotangent=cotangent)


@jax.custom_vjp
def low(v):
    return lax.optimization_barrier(v.astype(jnp.bfloat16)).astype(jnp.float32)

@jax.custom_vjp
def low_back(v):
    return v

def low_keep(v):
    return (low(v), None)

def low_pass(kept, grad):
    return (grad,)

def back_keep(v):
    return (v, None)

def back_low(kept, grad):
    return (low(grad),)
low.defvjp(low_keep, low_pass)
low_back.defvjp(back_keep, back_low)
epsilon = 1e-06
rope_base = 1000000.0
masked_score = -1e+30

def dense(left, right):
    return jnp.dot(left, right, precision=lax.Precision.HIGHEST)

def rms_norm(values, gain):
    return values * lax.rsqrt(lax.optimization_barrier(jnp.mean(values * values, axis=-1, keepdims=True)) + epsilon) * gain

def segment_table(lengths_row):
    seq_ends = jnp.cumsum(lengths_row).astype(jnp.int32)
    seq_starts = (seq_ends - lengths_row).astype(jnp.int32)
    places = jnp.arange(GROUP_TOK, dtype=jnp.int32)
    segment = lax.optimization_barrier(jnp.sum((places[:, None] >= seq_ends[None, :]).astype(jnp.int32), axis=1)).astype(jnp.int32)
    owners = segment[:, None] == jnp.arange(SEQS, dtype=jnp.int32)[None, :]
    seq_first = lax.optimization_barrier(jnp.sum(jnp.where(owners, seq_starts[None, :], 0), axis=1)).astype(jnp.int32)
    return (segment, places - seq_first)

def rotation(positions):
    half_size = HEAD // 2
    inverse_rates = rope_base ** (-jnp.arange(half_size, dtype=jnp.float32) * (2.0 / HEAD))
    angles = positions.astype(jnp.float32)[:, None] * inverse_rates[None, :]
    return (jnp.cos(angles), jnp.sin(angles))

def rotate(values, cosine, sine):
    half_size = HEAD // 2
    shaped = values.reshape(values.shape[0], -1, HEAD)
    first_half = shaped[..., :half_size]
    second_half = shaped[..., half_size:]
    cos_rows = cosine[:, None, :]
    sin_rows = sine[:, None, :]
    turned = jnp.concatenate([first_half * cos_rows - second_half * sin_rows, second_half * cos_rows + first_half * sin_rows], axis=-1)
    return turned.reshape(values.shape)

def attend(queries, key_rows, value_rows, segment):
    block_rows = min(512, GROUP_TOK)
    per_group = HEADS // KV_HEADS
    score_scale = HEAD ** (-0.5)
    places = jnp.arange(GROUP_TOK, dtype=jnp.int32)
    key_heads = key_rows.reshape(GROUP_TOK, KV_HEADS, HEAD)
    value_heads = value_rows.reshape(GROUP_TOK, KV_HEADS, HEAD)
    query_blocks = queries.reshape(GROUP_TOK // block_rows, block_rows, KV_HEADS, per_group, HEAD)
    offsets = jnp.arange(GROUP_TOK // block_rows, dtype=jnp.int32) * block_rows

    def one_block(block_item):
        query_block, offset = block_item
        scores = jnp.einsum('qkpd,skd->kpqs', query_block, key_heads, precision=lax.Precision.HIGHEST) * score_scale
        scores = low_back(scores)
        rows_here = offset + jnp.arange(block_rows, dtype=jnp.int32)
        segment_rows = lax.dynamic_slice_in_dim(segment, offset, block_rows)
        allowed = (segment_rows[:, None] == segment[None, :]) & (places[None, :] <= rows_here[:, None])
        scores = jnp.where(allowed, scores, masked_score)
        weights = low(jax.nn.softmax(scores, axis=-1))
        outcome = jnp.einsum('kpqs,skd->qkpd', weights, value_heads, precision=lax.Precision.HIGHEST)
        return outcome.reshape(block_rows, HEADS * HEAD)
    result = lax.map(jax.checkpoint(one_block), (query_blocks, offsets))
    return result.reshape(GROUP_TOK, HEADS * HEAD)

def group_layer(parameters, group_item):
    attention_gain, query_weight, query_bias, keyvalue_weight, keyvalue_bias, output_weight, feedforward_gain, gate_weight, up_weight, down_weight = parameters
    rows_in, lengths_row = group_item
    segment, positions = segment_table(lengths_row)
    cosine, sine = rotation(positions)
    normed = low(rms_norm(rows_in, attention_gain))
    query_pre = low_back(dense(normed, query_weight) + query_bias)
    pair_pre = low_back(dense(normed, keyvalue_weight) + keyvalue_bias).reshape(GROUP_TOK, KV_HEADS, 2, HEAD)
    queries = low(rotate(query_pre, cosine, sine))
    key_rows = low(rotate(pair_pre[:, :, 0, :].reshape(GROUP_TOK, KV_HEADS * HEAD), cosine, sine))
    value_rows = low(pair_pre[:, :, 1, :].reshape(GROUP_TOK, KV_HEADS * HEAD))
    attended = low_back(low(attend(queries, key_rows, value_rows, segment)))
    middle = rows_in + low_back(dense(attended, output_weight))
    normed_mlp = low(rms_norm(middle, feedforward_gain))
    gate_act = low_back(dense(normed_mlp, gate_weight))
    up_act = low_back(dense(normed_mlp, up_weight))
    hidden = low(jax.nn.silu(gate_act) * up_act)
    return middle + low_back(dense(hidden, down_weight))

def reference(tokens_in, seq_lengths, attention_gain, query_weight, query_bias, keyvalue_weight, keyvalue_bias, output_weight, feedforward_gain, gate_weight, up_weight, down_weight, cotangent):
    floats = (attention_gain, query_weight, query_bias, keyvalue_weight, keyvalue_bias, output_weight, feedforward_gain, gate_weight, up_weight, down_weight)
    parameters = tuple((argument.astype(jnp.float32) for argument in floats))
    start_rows = tokens_in.astype(jnp.float32)

    def forward(rows_all, *weights):
        layer = jax.checkpoint(partial(group_layer, weights))
        grouped = rows_all.reshape(N_DP, GROUP_TOK, D)
        return lax.map(layer, (grouped, seq_lengths)).reshape(N_DP * GROUP_TOK, D)
    layer_out, pullback = jax.vjp(forward, start_rows, *parameters)
    gradients = pullback(cotangent.astype(jnp.float32))
    return (layer_out.astype(jnp.bfloat16), gradients[0].astype(jnp.bfloat16), gradients[1], gradients[2], gradients[3], gradients[4], gradients[5], gradients[6], gradients[7], gradients[8], gradients[9], gradients[10])
```

```python
import jax
import jax.numpy as jnp
from jax import lax
from jax.sharding import PartitionSpec as P

HEAD = 128
epsilon = 1e-06
rope_base = 1000000.0
masked_score = -1e30
BF = jnp.bfloat16
F32 = jnp.float32


def dot(a, b, ca=1, cb=0):
    return lax.dot_general(a, b, (((ca,), (cb,)), ((), ())), preferred_element_type=F32)


def partner(value, axis, mask):
    pairs = [(s, s ^ mask) for s in range(lax.axis_size(axis))]
    return lax.ppermute(value, axis, pairs)


def gather(value, axis, dim=0):
    return lax.all_gather(value, axis, axis=dim, tiled=True)


def scatter_sum(value, axis, dim=0):
    return lax.psum_scatter(value.astype(BF), axis, scatter_dimension=dim, tiled=True)


def features_to_tokens(block):
    cols = lax.axis_size("col")
    sub = block.shape[0] // cols
    out = lax.all_to_all(block.reshape(cols, sub, -1), "col", 0, 0, tiled=True)
    return jnp.moveaxis(out, 0, 1).reshape(sub, -1)


def tokens_to_features(block):
    cols = lax.axis_size("col")
    sub = block.shape[0]
    parts = jnp.moveaxis(block.reshape(sub, cols, -1), 1, 0)
    out = lax.all_to_all(parts, "col", 0, 0, tiled=True)
    return out.reshape(cols * sub, -1)


def rotation(positions):
    half = HEAD // 2
    rates = rope_base ** (-jnp.arange(half, dtype=F32) * (2.0 / HEAD))
    angles = positions.astype(F32)[:, None] * rates[None, :]
    return jnp.cos(angles), jnp.sin(angles)


def rotate(values, cosine, sine):
    half = HEAD // 2
    shaped = values.reshape(values.shape[0], -1, HEAD)
    a, b = shaped[..., :half], shaped[..., half:]
    c, s = cosine[:, None, :], sine[:, None, :]
    turned = jnp.concatenate([a * c - b * s, b * c + a * s], axis=-1)
    return turned.reshape(values.shape)


def norm_back(grad, normal, inverse, gain):
    e = grad * gain
    mean = jnp.mean(e * normal, axis=-1, keepdims=True)
    return inverse * (e - normal * mean), jnp.sum(grad * normal, axis=0)


def on_device(
    tokens_in, seq_lengths, attention_gain, query_weight, query_bias, keyvalue_weight,
    keyvalue_bias, output_weight, feedforward_gain, gate_weight, up_weight, down_weight,
    cotangent,
):
    rows, cols = lax.axis_size("row"), lax.axis_size("col")
    col = lax.axis_index("col")
    row_tokens = tokens_in.shape[0]
    group = row_tokens * rows
    sub = row_tokens // cols
    wq_width = query_weight.shape[1]
    heads = wq_width // HEAD
    is_key = lax.axis_index("row") % 2 == 0
    places = jnp.arange(group, dtype=jnp.int32)
    lengths = seq_lengths[0]
    ends = jnp.cumsum(lengths)
    segment = jnp.sum((places[:, None] >= ends[None, :]).astype(jnp.int32), axis=1)
    owners = segment[:, None] == jnp.arange(lengths.shape[0], dtype=jnp.int32)[None, :]
    first = jnp.sum(jnp.where(owners, (ends - lengths)[None, :], 0), axis=1)
    positions = places - first
    own = lambda v: lax.dynamic_slice_in_dim(v.reshape(rows, cols, sub), col, 1, 1).reshape(-1)
    my_places, my_segment, my_positions = own(places), own(segment), own(positions)
    cosine, sine = rotation(my_positions)
    mate = partner(keyvalue_weight, "row", 1)
    mate_bias = partner(keyvalue_bias, "row", 1)
    key_w = jnp.where(is_key, keyvalue_weight, mate)
    value_w = jnp.where(is_key, mate, keyvalue_weight)
    kv_bias = jnp.where(
        is_key,
        jnp.concatenate([keyvalue_bias, mate_bias]),
        jnp.concatenate([mate_bias, keyvalue_bias]),
    )
    w_joint = gather(jnp.concatenate([query_weight, key_w, value_w], axis=1), "col")
    gain_attn = gather(attention_gain, "col").astype(F32)
    gain_mlp = gather(feedforward_gain, "col").astype(F32)
    w_out = gather(output_weight, "col", 1)
    w_gate = gather(gate_weight, "col")
    w_up = gather(up_weight, "col")
    w_down = gather(down_weight, "col", 1)
    inputs = features_to_tokens(tokens_in).astype(F32)
    inverse_attn = lax.rsqrt(jnp.mean(inputs * inputs, axis=-1, keepdims=True) + epsilon)
    normal_attn = inputs * inverse_attn
    normed = gather((normal_attn * gain_attn).astype(BF), "row")
    joint = dot(normed, w_joint) + jnp.concatenate([query_bias, kv_bias]).astype(F32)
    turned = rotate(joint[:, : wq_width + HEAD], cosine, sine).astype(BF)
    queries = turned[:, :wq_width]
    slots = jnp.concatenate([turned[:, wq_width:], joint[:, wq_width + HEAD :].astype(BF)], axis=1)
    slots_all = gather(slots, "col")
    order = lambda v: jnp.moveaxis(v.reshape(cols, rows, sub, -1), 0, 1).reshape(group, -1)
    slots_all = order(slots_all)
    keys, values = slots_all[:, :HEAD], slots_all[:, HEAD:]
    q_heads = queries.reshape(rows, sub, heads, HEAD)
    scale = HEAD ** (-0.5)

    def block_probs(r):
        limit = (r + 1) * row_tokens
        scores = jnp.einsum(
            "qhd,sd->hqs", q_heads[r], keys[:limit], preferred_element_type=F32
        ) * scale
        mine = slice(r * sub, (r + 1) * sub)
        allowed = (my_segment[mine][:, None] == segment[None, :limit]) & (
            places[None, :limit] <= my_places[mine][:, None]
        )
        scores = jnp.where(allowed[None], scores, masked_score)
        e = jnp.exp(scores - jnp.max(scores, axis=-1, keepdims=True))
        return e / jnp.sum(e, axis=-1, keepdims=True)

    attended = []
    for r in range(rows):
        p = block_probs(r)
        limit = (r + 1) * row_tokens
        attended.append(
            jnp.einsum("hqs,sd->qhd", p.astype(BF), values[:limit], preferred_element_type=F32)
            .astype(BF).reshape(sub, wq_width)
        )
    attended = jnp.concatenate(attended, axis=0)
    middle = inputs + scatter_sum(dot(attended, w_out), "row").astype(F32)
    inverse_mlp = lax.rsqrt(jnp.mean(middle * middle, axis=-1, keepdims=True) + epsilon)
    normal_mlp = middle * inverse_mlp
    normed_mlp = gather((normal_mlp * gain_mlp).astype(BF), "row")
    gate_act = dot(normed_mlp, w_gate)
    up_act = dot(normed_mlp, w_up)
    s = jax.nn.sigmoid(gate_act)
    hidden = (gate_act * s * up_act).astype(BF)
    branch = scatter_sum(dot(hidden, w_down), "row").astype(F32)
    layer_out = tokens_to_features((middle + branch).astype(BF))
    grad_out = features_to_tokens(cotangent)
    grad_out_all = gather(grad_out, "row")
    grad_hidden = dot(grad_out_all, w_down, 1, 1)
    grad_gate = (grad_hidden * up_act * s * (1.0 + gate_act * (1.0 - s))).astype(BF)
    grad_up = (grad_hidden * (gate_act * s)).astype(BF)
    grad_normed_mlp = scatter_sum(
        dot(grad_gate, w_gate, 1, 1) + dot(grad_up, w_up, 1, 1), "row"
    ).astype(F32)
    gw_down = dot(hidden, grad_out_all, 0, 0)
    gw_gate = dot(normed_mlp, grad_gate, 0, 0)
    gw_up = dot(normed_mlp, grad_up, 0, 0)
    back, gain_mlp_part = norm_back(grad_normed_mlp, normal_mlp, inverse_mlp, gain_mlp)
    grad_middle = grad_out.astype(F32) + back
    grad_middle_all = gather(grad_middle.astype(BF), "row")
    grad_heads = dot(grad_middle_all, w_out, 1, 1).astype(BF).reshape(rows, sub, heads, HEAD)
    gw_out = dot(attended, grad_middle_all, 0, 0)
    dq, dk, dv = [], 0.0, 0.0
    for r in range(rows):
        limit = (r + 1) * row_tokens
        p = block_probs(r)
        pad = ((0, group - limit), (0, 0))
        dv = dv + jnp.pad(jnp.einsum(
            "hqs,qhd->sd", p.astype(BF), grad_heads[r], preferred_element_type=F32), pad)
        g = jnp.einsum("qhd,sd->hqs", grad_heads[r], values[:limit], preferred_element_type=F32)
        ds = (p * (g - jnp.sum(p * g, axis=-1, keepdims=True))).astype(BF)
        dq.append(jnp.einsum("hqs,sd->qhd", ds, keys[:limit], preferred_element_type=F32)
                  .reshape(sub, wq_width) * scale)
        dk = dk + jnp.pad(jnp.einsum(
            "hqs,qhd->sd", ds, q_heads[r], preferred_element_type=F32) * scale, pad)
    dq = jnp.concatenate(dq, axis=0)
    dslots = jnp.concatenate([dk, dv], axis=1)
    dslots = jnp.moveaxis(dslots.reshape(rows, cols, sub, -1), 1, 0).reshape(group, -1)
    dslots = scatter_sum(dslots, "col").astype(F32)
    dturned = jnp.concatenate([dq, dslots[:, :HEAD]], axis=1)
    grad_joint = jnp.concatenate(
        [rotate(dturned, cosine, -sine), dslots[:, HEAD:]], axis=1
    ).astype(BF)
    grad_normed = scatter_sum(dot(grad_joint, w_joint, 1, 1), "row").astype(F32)
    gw_joint = dot(normed, grad_joint, 0, 0)
    g_bias = jnp.sum(grad_joint.astype(F32), axis=0)
    back, gain_attn_part = norm_back(grad_normed, normal_attn, inverse_attn, gain_attn)
    input_grad = tokens_to_features((grad_middle + back).astype(BF))
    both = lambda v, dim: scatter_sum(scatter_sum(v, "col", dim), "dp").astype(F32)

    def slot_share(v, axis):
        k, w = v[..., wq_width : wq_width + HEAD], v[..., wq_width + HEAD :]
        got = partner(jnp.where(is_key, w, k).astype(BF), "row", 1)
        return jnp.where(is_key, k, w) + got.astype(F32)

    gw_joint = scatter_sum(gw_joint, "col").astype(F32)
    gw_query = scatter_sum(gw_joint[:, :wq_width], "dp").astype(F32)
    gw_keyvalue = scatter_sum(slot_share(gw_joint, 1), "dp").astype(F32)
    g_bias = lax.psum(g_bias, "col")
    g_qb = lax.psum_scatter(g_bias[:wq_width], "dp", scatter_dimension=0, tiled=True)
    g_kvb = slot_share(g_bias, 0)
    g_kvb = lax.psum_scatter(g_kvb, "dp", scatter_dimension=0, tiled=True)
    gains = lax.psum((gain_attn_part, gain_mlp_part), ("dp", "row", "col"))
    mine = lambda v: lax.dynamic_slice_in_dim(v, col * (v.shape[0] // cols), v.shape[0] // cols)
    return (
        layer_out, input_grad, mine(gains[0]), gw_query, g_qb, gw_keyvalue, g_kvb,
        both(gw_out, 1), mine(gains[1]), both(gw_gate, 0), both(gw_up, 0), both(gw_down, 1),
    )


def solution(mesh):
    return jax.shard_map(
        on_device,
        mesh=mesh,
        in_specs=(
            P(("dp", "row"), "col"), P("dp", None), P("col"), P("col", "row"), P("row"),
            P("col", "row"), P("row"), P("row", "col"), P("col"), P("col", "row"),
            P("col", "row"), P("row", "col"), P(("dp", "row"), "col"),
        ),
        out_specs=(
            P(("dp", "row"), "col"), P(("dp", "row"), "col"), P("col"),
            P(("col", "dp"), "row"), P(("row", "dp")), P(("col", "dp"), "row"),
            P(("row", "dp")), P(("row", "dp"), "col"), P("col"), P(("col", "dp"), "row"),
            P(("col", "dp"), "row"), P(("row", "dp"), "col"),
        ),
        check_vma=False,
    )
```

```python
import functools

import jax
import jax.numpy as jnp
from jax import lax
from jax.experimental import pallas as pl
from jax.experimental.pallas import tpu as pltpu
from jax.sharding import PartitionSpec as P

HEAD = 128
epsilon = 1e-06
rope_base = 1000000.0
masked_score = -1e30
BF = jnp.bfloat16
F32 = jnp.float32
MESH = pl.DeviceIdType.MESH
ANY = pl.BlockSpec(memory_space=pl.ANY)
VMEM = pl.BlockSpec(memory_space=pltpu.VMEM)
VMEM_LIMIT = 60 * 2**20


def dot(a, b, ca=1, cb=0):
    return lax.dot_general(a, b, (((ca,), (cb,)), ((), ())), preferred_element_type=F32)


class Net:
    def __init__(self, sizes, send, recv, local):
        self.dp, self.R, self.C = sizes
        self.d = lax.axis_index("dp")
        self.r = lax.axis_index("row")
        self.c = lax.axis_index("col")
        half = self.dp // 2
        self.h = self.d // half
        self.send, self.recv, self.local = send, recv, local
        self.n = 0
        self.n_local = 0
        self.other_h = 1 - self.h
        self.mate = (lax.rem(self.d + half, self.dp), self.r, self.c)
        self.sibling = self.at_col(self.c + 1 - 2 * lax.rem(self.c, 2))
        self.across_c = lax.rem(self.c + 2, 4)
        self.across = self.at_col(self.across_c)

    def at_col(self, c):
        return (self.d, self.r, c)

    def at_row(self, r):
        return (self.d, r, self.c)

    def copy(self, src, dst, dev):
        i = self.n
        self.n += 1
        return pltpu.make_async_remote_copy(
            src_ref=src, dst_ref=dst, send_sem=self.send.at[i], recv_sem=self.recv.at[i],
            device_id=dev, device_id_type=MESH,
        )

    def like(self, copy_index, src, dst, dev):
        return pltpu.make_async_remote_copy(
            src_ref=src, dst_ref=dst, send_sem=self.send.at[copy_index],
            recv_sem=self.recv.at[copy_index], device_id=dev, device_id_type=MESH,
        )

    def here(self, src, dst):
        i = self.n_local
        self.n_local += 1
        return pltpu.make_async_copy(src, dst, self.local.at[i])

    def barrier(self):
        sem = pltpu.get_barrier_semaphore()
        for k in range(1, self.C):
            pl.semaphore_signal(
                sem, inc=1, device_id=self.at_col(lax.rem(self.c + k, self.C)), device_id_type=MESH
            )
        pl.semaphore_signal(sem, inc=1, device_id=self.mate, device_id_type=MESH)

        @pl.when(self.r > 0)
        def _():
            pl.semaphore_signal(sem, inc=1, device_id=self.at_row(self.r - 1), device_id_type=MESH)

        @pl.when(self.r < self.R - 1)
        def _():
            pl.semaphore_signal(sem, inc=1, device_id=self.at_row(self.r + 1), device_id_type=MESH)

        count = self.C + (self.r > 0).astype(jnp.int32) + (self.r < self.R - 1).astype(jnp.int32)
        pl.semaphore_wait(sem, count)


class LineGather:
    def __init__(self, net, buf):
        self.net, self.buf = net, buf
        r, R = net.r, net.R
        self.up_i, self.dn_i = [], []
        for s in range(R - 1):
            self.up_i.append(net.n)
            self.dn_i.append(net.n + 1)
            net.n += 2

    def _up(self, s, shard):
        net = self.net
        b = self.buf.at[jnp.clip(shard, 0, net.R - 1)]
        return net.like(self.up_i[s], b, b, net.at_row(jnp.minimum(net.r + 1, net.R - 1)))

    def _dn(self, s, shard):
        net = self.net
        b = self.buf.at[jnp.clip(shard, 0, net.R - 1)]
        return net.like(self.dn_i[s], b, b, net.at_row(jnp.maximum(net.r - 1, 0)))

    def step(self, s):
        net = self.net
        r, R = net.r, net.R
        if s > 0:

            @pl.when(r - s >= 0)
            def _():
                self._up(s - 1, r - s).wait_recv()

        if s < R - 1:

            @pl.when((r - s >= 0) & (r < R - 1))
            def _():
                self._up(s, r - s).start()

        if s > 0:

            @pl.when(r + s < R)
            def _():
                self._dn(s - 1, r + s).wait_recv()

        if s < R - 1:

            @pl.when((r + s < R) & (r > 0))
            def _():
                self._dn(s, r + s).start()

    def finish(self):
        net = self.net
        r, R = net.r, net.R
        for s in range(R - 1):

            @pl.when((r - s >= 0) & (r < R - 1))
            def _():
                self._up(s, r - s).wait_send()

            @pl.when((r + s < R) & (r > 0))
            def _():
                self._dn(s, r + s).wait_send()


class LineSum:
    def __init__(self, net, part, from_below, from_above):
        self.net, self.part, self.bu, self.bd = net, part, from_below, from_above
        self.base = net.n
        net.n += 2 * net.R

    def _dn(self, j):
        net = self.net
        j = jnp.clip(j, 0, net.R - 1)
        return net.like(
            self.base + j, self.part.at[j], self.bd.at[j], net.at_row(jnp.maximum(net.r - 1, 0))
        )

    def _up(self, j):
        net = self.net
        j = jnp.clip(j, 0, net.R - 1)
        return net.like(
            self.base + net.R + j, self.part.at[j], self.bu.at[j],
            net.at_row(jnp.minimum(net.r + 1, net.R - 1)),
        )

    def _add(self, j, buf):
        self.part[j] = (self.part[j].astype(F32) + buf[j].astype(F32)).astype(BF)

    def step(self, t):
        net = self.net
        r, R = net.r, net.R
        j = t - (R - 1 - r)
        k = R - 1 - (t - r)

        @pl.when((j >= 0) & (r < R - 1))
        def _():
            self._dn(j).wait_recv()

        @pl.when((j >= 0) & (j < r))
        def _():
            @pl.when(r < R - 1)
            def _():
                self._add(j, self.bd)

            self._dn(j).start()

        @pl.when((k <= R - 1) & (r > 0))
        def _():
            self._up(k).wait_recv()

        @pl.when((k <= R - 1) & (k > r))
        def _():
            @pl.when(r > 0)
            def _():
                self._add(k, self.bu)

            self._up(k).start()

    def finish(self):
        net = self.net
        r, R = net.r, net.R
        for j in range(R):

            @pl.when(j < r)
            def _():
                self._dn(j).wait_send()

            @pl.when(j > r)
            def _():
                self._up(j).wait_send()

    def total_into(self, out):
        net = self.net
        r, R = net.r, net.R
        out[...] += self.part[r].astype(F32)

        @pl.when(r < R - 1)
        def _():
            out[...] += self.bd[r].astype(F32)

        @pl.when(r > 0)
        def _():
            out[...] += self.bu[r].astype(F32)


class WeightGather:
    def __init__(self, net, src, full, by_rows, piece=0, pieces=1):
        self.net, self.full, self.by_rows = net, full, by_rows
        if by_rows:
            self.n, self.w = full.shape[0] // net.C, full.shape[1]
        else:
            self.n, self.w = full.shape[0] // pieces, full.shape[1] // net.C
        self.first = piece * self.n
        if src is not None:
            src = src.at[pl.ds(self.first, self.n)]
        c, p, h, o = net.c, net.across_c, net.h, net.other_h
        half = self.n // 2
        self.here = None
        if src is not None:
            self.here = net.here(src, self.view(c, 0, 2))
            own_half = src.at[pl.ds(pl.multiple_of(h * half, 16), half)]
            own = src
        else:
            own_half, own = self.view(c, h, 1), self.view(c, 0, 2)
        self.x = net.copy(own_half, self.view(c, h, 1), net.across)
        self.sib = net.copy(own, self.view(c, 0, 2), net.sibling)
        self.y = net.copy(self.view(p, h, 1), self.view(p, h, 1), net.mate)
        self.sib_h = net.copy(self.view(p, h, 1), self.view(p, h, 1), net.sibling)
        self.sib_o = net.copy(self.view(p, o, 1), self.view(p, o, 1), net.sibling)

    def view(self, b, h, halves):
        half = self.n // 2
        if self.by_rows:
            return self.full.at[pl.ds(pl.multiple_of(b * self.n + h * half, 16), halves * half)]
        return self.full.at[
            pl.ds(pl.multiple_of(self.first + h * half, 16), halves * half),
            pl.ds(pl.multiple_of(b * self.w, 128), self.w),
        ]

    def start(self):
        if self.here is not None:
            self.here.start()
        self.x.start()
        self.sib.start()

    def pass_x(self):
        self.x.wait_recv()
        self.y.start()
        self.sib_h.start()

    def pass_y(self):
        self.y.wait_recv()
        self.sib_o.start()

    def arrive(self):
        if self.here is not None:
            self.here.wait()
        self.sib.wait_recv()
        self.sib_h.wait_recv()
        self.sib_o.wait_recv()

    def finish(self):
        for cp in (self.x, self.sib, self.y, self.sib_h, self.sib_o):
            cp.wait_send()


def turn(values, cos2, sin2):
    heads = []
    for i in range(values.shape[1] // HEAD):
        v = values[:, i * HEAD : (i + 1) * HEAD]
        heads.append(v * cos2 + pltpu.roll(v, HEAD // 2, 1) * sin2)
    return jnp.concatenate(heads, axis=1) if len(heads) > 1 else heads[0]


def attention_kernel(
    sizes,
    tok, cot, wq, wkv, wo, wg, wu, small, qb, kvb, cos2, sin2, qpos,
    o_mid, o_nmlp, o_gains, o_normed, o_q, o_kv, o_att, o_cot, o_wj, o_wo, o_wg, o_wu,
    xin, cin, gains, kvb2, nall, call, wj, wov, kv, qs, att, part, rbu, rbd, send, recv, local,
):
    net = Net(sizes, send, recv, local)
    R, C, r, c = net.R, net.C, net.r, net.c
    sub, width = nall.shape[1], nall.shape[2]
    block = tok.shape[1]
    row_tok = sub * C
    n_tok = sub * R
    qw = wq.shape[1]
    slot = lax.rem(r, 2)
    partner = net.at_row(r + 1 - 2 * slot)
    net.barrier()

    def spread(src, dst):
        mine = pl.multiple_of(c * sub, sub)
        local_copy = net.here(src.at[pl.ds(mine, sub)], dst.at[c])
        copies = []
        for k in range(1, C):
            to = lax.rem(c + k, C)
            frm = lax.rem(c + C - k, C)
            i = net.n
            net.n += 1
            rows = pl.ds(pl.multiple_of(to * sub, sub), sub)
            copies.append(
                (net.like(i, src.at[rows], dst.at[c], net.at_col(to)),
                 net.like(i, src.at[rows], dst.at[frm], net.at_col(to)))
            )
        return local_copy, copies

    def begin(pair):
        pair[0].start()
        for out, _ in pair[1]:
            out.start()

    def arrived(pair):
        pair[0].wait()
        for _, inc in pair[1]:
            inc.wait_recv()

    tok_in, cot_in = spread(tok, xin), spread(cot, cin)
    begin(tok_in)
    gain_own = net.here(small, gains.at[c])
    gain_own.start()
    gain_copies = []
    for k in range(1, C):
        to, frm = lax.rem(c + k, C), lax.rem(c + C - k, C)
        i = net.n
        net.n += 1
        out = net.like(i, small, gains.at[c], net.at_col(to))
        gain_copies.append((out, net.like(i, small, gains.at[frm], net.at_col(to))))
        out.start()
    own_rows = pl.ds(pl.multiple_of(c * block, block), block)
    col_own = pl.ds(pl.multiple_of(qw + slot * HEAD, HEAD), HEAD)
    col_mate = pl.ds(pl.multiple_of(qw + (1 - slot) * HEAD, HEAD), HEAD)
    kv_x = net.copy(wkv, wj.at[own_rows, col_own], partner)
    kv_in = net.like(net.n - 1, wkv, wj.at[own_rows, col_mate], partner)
    kv_x.start()
    kvb_x = net.copy(kvb, kvb2.at[slot], partner)
    kvb_in = net.like(net.n - 1, kvb, kvb2.at[1 - slot], partner)
    kvb_x.start()
    kvb_own = net.here(kvb, kvb2.at[slot])
    kvb_own.start()
    wq_own = net.here(wq, wj.at[own_rows, pl.ds(0, qw)])
    wq_own.start()
    wkv_own = net.here(wkv, wj.at[own_rows, col_own])
    wkv_own.start()
    g_joint = WeightGather(net, None, wj, True)
    g_out = WeightGather(net, wo, wov, False)
    bulk = [WeightGather(net, w, o, False, i, 2) for w, o in ((wg, o_wg), (wu, o_wu)) for i in (0, 1)]

    arrived(tok_in)
    gain_own.wait()
    for _, inc in gain_copies:
        inc.wait_recv()
    for k in range(C):
        o_gains[:, k * block : (k + 1) * block] = gains[k, :, :block]
        o_gains[:, width + k * block : width + (k + 1) * block] = gains[k, :, block:]
    x = jnp.concatenate([xin[k].astype(F32) for k in range(C)], axis=1)
    o_mid[...] = x
    inv = lax.rsqrt(jnp.mean(x * x, axis=-1, keepdims=True) + epsilon)
    nall[r] = (x * inv * o_gains[0:1, :width]).astype(BF)
    g_n = LineGather(net, nall)
    g_n.step(0)
    wq_own.wait()
    wkv_own.wait()
    kv_in.wait_recv()
    g_joint.start()
    g_out.start()
    begin(cot_in)
    g_joint.pass_x()
    g_out.pass_x()
    bulk[0].start()
    g_joint.pass_y()
    g_n.step(1)
    g_out.pass_y()
    bulk[1].start()
    arrived(cot_in)
    for k in range(C):
        call[r, :, k * block : (k + 1) * block] = cin[k]
    g_n.step(2)
    bulk[0].pass_x()
    g_joint.arrive()
    kvb_own.wait()
    kvb_in.wait_recv()
    g_n.step(3)
    g_cot = LineGather(net, call)
    g_cot.step(0)
    bias = jnp.concatenate([qb[0:1, :], kvb2[0, 0:1, :], kvb2[1, 0:1, :]], axis=1)
    joint = dot(nall[...].reshape(n_tok, width), wj[...]) + bias
    key = turn(joint[:, qw : qw + HEAD], cos2[...], sin2[...]).astype(BF)
    kv[:, c, :, :HEAD] = key.reshape(R, sub, HEAD)
    kv[:, c, :, HEAD:] = joint[:, qw + HEAD :].astype(BF).reshape(R, sub, HEAD)
    kv_copies = []
    for k in range(1, C):
        to, frm = lax.rem(c + k, C), lax.rem(c + C - k, C)
        i = net.n
        net.n += 1
        out = net.like(i, kv.at[:, c], kv.at[:, c], net.at_col(to))
        kv_copies.append((out, net.like(i, kv.at[:, frm], kv.at[:, frm], net.at_col(to))))
        out.start()
    qs[...] = turn(joint[:, :qw], cos2[...], sin2[...]).astype(BF)
    out_normed = net.here(nall, o_normed)
    out_normed.start()
    out_wj = net.here(wj, o_wj)
    out_wj.start()
    for _, inc in kv_copies:
        inc.wait_recv()
    bulk[1].pass_x()
    bulk[2].start()
    bulk[3].start()
    bulk[0].pass_y()
    g_cot.step(1)
    out_kv = net.here(kv, o_kv)
    out_kv.start()
    scale = HEAD ** (-0.5)
    for rr in range(R):
        limit = (rr + 1) * row_tok
        keys = kv[: rr + 1, :, :, :HEAD].reshape(limit, HEAD)
        values = kv[: rr + 1, :, :, HEAD:].reshape(limit, HEAD)
        mine = slice(rr * sub, (rr + 1) * sub)
        place = lax.broadcasted_iota(jnp.int32, (sub, limit), 1)
        allowed = (place >= qpos[mine, 0:1]) & (place <= qpos[mine, 1:2])
        for h in range(qw // HEAD):
            cols = slice(h * HEAD, (h + 1) * HEAD)
            s = jnp.where(allowed, dot(qs[mine, cols], keys, 1, 1) * scale, masked_score)
            e = jnp.exp(s - jnp.max(s, axis=-1, keepdims=True))
            p = e * (1.0 / jnp.sum(e, axis=-1, keepdims=True))
            att[mine, cols] = dot(p.astype(BF), values).astype(BF)
    g_out.arrive()
    part[...] = dot(att[...], wov[...]).astype(BF).reshape(R, sub, width)
    rs = LineSum(net, part, rbu, rbd)
    rs.step(0)
    out_q = net.here(qs, o_q)
    out_q.start()
    out_att = net.here(att, o_att)
    out_att.start()
    out_wo = net.here(wov, o_wo)
    out_wo.start()
    g_cot.step(2)
    bulk[1].pass_y()
    bulk[2].pass_x()
    rs.step(1)
    g_cot.step(3)
    out_cot = net.here(call, o_cot)
    out_cot.start()
    bulk[3].pass_x()
    rs.step(2)
    bulk[2].pass_y()
    rs.step(3)
    rs.total_into(o_mid)
    mid = o_mid[...]
    inv = lax.rsqrt(jnp.mean(mid * mid, axis=-1, keepdims=True) + epsilon)
    o_nmlp[...] = (mid * inv * o_gains[0:1, width:]).astype(BF)
    bulk[3].pass_y()
    for g in bulk:
        g.arrive()
    for g in [g_joint, g_out, g_n, g_cot, rs] + bulk:
        g.finish()
    for out, _ in tok_in[1] + cot_in[1] + gain_copies + kv_copies:
        out.wait_send()
    kv_x.wait_send()
    kvb_x.wait_send()
    for cp in (out_normed, out_wj, out_kv, out_q, out_att, out_wo, out_cot):
        cp.wait()


def attention_forward(sizes, tok, cot, wq, wkv, wo, wg, wu, small, qb, kvb, cos2, sin2, qpos):
    dp, R, C = sizes
    sub = tok.shape[0] // C
    block = tok.shape[1]
    width = block * C
    qw, jw = wq.shape[1], wq.shape[1] + 2 * HEAD
    n = sub * R
    ff = wg.shape[0]
    shape = jax.ShapeDtypeStruct
    outs = [
        (shape((sub, width), F32), VMEM), (shape((sub, width), BF), VMEM),
        (shape((8, 2 * width), F32), VMEM), (shape((R, sub, width), BF), ANY),
        (shape((n, qw), BF), ANY), (shape((R, C, sub, 2 * HEAD), BF), ANY),
        (shape((n, qw), BF), ANY), (shape((R, sub, width), BF), ANY),
        (shape((width, jw), BF), ANY), (shape((qw, width), BF), ANY),
        (shape((ff, width), BF), ANY), (shape((ff, width), BF), ANY),
    ]
    return pl.pallas_call(
        functools.partial(attention_kernel, sizes),
        out_shape=[o for o, _ in outs],
        in_specs=[ANY] * 7 + [VMEM] * 6,
        out_specs=[s for _, s in outs],
        scratch_shapes=[
            pltpu.VMEM((C, sub, block), BF), pltpu.VMEM((C, sub, block), BF),
            pltpu.VMEM((C, 8, 2 * block), F32), pltpu.VMEM((2, 8, HEAD), F32),
            pltpu.VMEM((R, sub, width), BF), pltpu.VMEM((R, sub, width), BF),
            pltpu.VMEM((width, jw), BF), pltpu.VMEM((qw, width), BF),
            pltpu.VMEM((R, C, sub, 2 * HEAD), BF), pltpu.VMEM((n, qw), BF),
            pltpu.VMEM((n, qw), BF), pltpu.VMEM((R, sub, width), BF),
            pltpu.VMEM((R, sub, width), BF), pltpu.VMEM((R, sub, width), BF),
            pltpu.SemaphoreType.DMA((64,)), pltpu.SemaphoreType.DMA((64,)),
            pltpu.SemaphoreType.DMA((24,)),
        ],
        compiler_params=pltpu.CompilerParams(
            collective_id=1, has_side_effects=True, vmem_limit_bytes=VMEM_LIMIT
        ),
        name="attention_forward",
    )(tok, cot, wq, wkv, wo, wg, wu, small, qb, kvb, cos2, sin2, qpos)


def feedforward_kernel(
    sizes,
    nmlp, mid, gains, cot, wg, wu, wd,
    o_gmid, o_gain, o_down, o_sum,
    w_gate, w_up, w_down, xall, call, gh, hid, gg, gu, gh_r, hid_r, gg_r, gu_r, acc, part, rbu, rbd, rx,
    send, recv, local,
):
    net = Net(sizes, send, recv, local)
    R, C, r, c = net.R, net.C, net.r, net.c
    sub, width = nmlp.shape
    n_tok = sub * R
    ff = w_gate.shape[0]
    tile = hid.shape[2]
    tiles = hid.shape[0]
    rest = hid_r.shape[1]
    g_down = WeightGather(net, wd, w_down, False)
    in_cot = net.here(cot, call)
    in_gate = net.here(wg, w_gate)
    in_up = net.here(wu, w_up)
    for cp in (in_cot, in_gate, in_up):
        cp.start()
    net.barrier()
    xall[r] = nmlp[...]
    g_x = LineGather(net, xall)
    g_x.step(0)
    g_down.start()
    g_x.step(1)
    g_down.pass_x()
    in_cot.wait()
    in_gate.wait()
    in_up.wait()
    g_x.step(2)
    g_down.pass_y()
    g_down.arrive()
    cot2 = call[...].reshape(n_tok, width)

    def back_tile(rows):
        return dot(call[...].reshape(n_tok, width), w_down[rows, :], 1, 1)

    def all_tiles(body):
        @pl.loop(0, tiles)
        def _(t):
            body(t, pl.ds(pl.multiple_of(t * tile, 16), tile), gh.at[t], hid.at[t], gg.at[t], gu.at[t])

        body(tiles, pl.ds(tiles * tile, rest), gh_r, hid_r, gg_r, gu_r)

    def hidden_back(t, rows, gh_t, hid_t, gg_t, gu_t):
        gh_t[...] = back_tile(rows)

    all_tiles(hidden_back)
    g_x.step(3)

    def act(t, rows, gh_t, hid_t, gg_t, gu_t):
        x = xall[...].reshape(n_tok, width)
        gate = dot(x, w_gate[rows, :], 1, 1)
        up = dot(x, w_up[rows, :], 1, 1)
        s = jax.nn.sigmoid(gate)
        silu = gate * s
        back = gh_t[...]
        hid_t[...] = (silu * up).astype(BF)
        gg_t[...] = (back * up * s * (1.0 + gate * (1.0 - s))).astype(BF)
        gu_t[...] = (back * silu).astype(BF)

    all_tiles(act)
    acc[...] = jnp.zeros_like(acc)

    def input_back(t, rows, gh_t, hid_t, gg_t, gu_t):
        acc[...] += dot(gg_t[...], w_gate[rows, :]) + dot(gu_t[...], w_up[rows, :])

    all_tiles(input_back)
    part[...] = acc[...].astype(BF).reshape(R, sub, width)
    rs = LineSum(net, part, rbu, rbd)
    rs.step(0)
    acc[...] = jnp.zeros_like(acc)

    def down(t, rows, gh_t, hid_t, gg_t, gu_t):
        acc[...] += dot(hid_t[...], w_down[rows, :])

    all_tiles(down)
    xall_done = g_x
    xall_done.finish()
    g_down.finish()
    rs.step(1)
    exchange = []

    def hand_over(m, w):
        for i, b in enumerate((net.c + 1 - 2 * lax.rem(net.c, 2), lax.rem(net.across_c + 1 - 2 * lax.rem(net.across_c, 2), 4))):
            cp = net.copy(w.at[:, pl.ds(pl.multiple_of(b * (width // C), 128), width // C)], rx.at[m, i], net.sibling)
            cp.start()
            exchange.append(cp)

    def grad_down(t, rows, gh_t, hid_t, gg_t, gu_t):
        w_down[rows, :] = dot(hid_t[...], call[...].reshape(n_tok, width), 0, 0).astype(BF)

    all_tiles(grad_down)
    hand_over(0, w_down)
    rs.step(2)

    def grad_gate(t, rows, gh_t, hid_t, gg_t, gu_t):
        w_gate[rows, :] = dot(gg_t[...], xall[...].reshape(n_tok, width), 0, 0).astype(BF)

    all_tiles(grad_gate)
    hand_over(1, w_gate)

    def grad_up(t, rows, gh_t, hid_t, gg_t, gu_t):
        w_up[rows, :] = dot(gu_t[...], xall[...].reshape(n_tok, width), 0, 0).astype(BF)

    all_tiles(grad_up)
    hand_over(2, w_up)
    rs.step(3)
    o_gmid[...] = jnp.zeros_like(o_gmid)
    rs.total_into(o_gmid)
    grad = o_gmid[...]
    m = mid[...]
    inv = lax.rsqrt(jnp.mean(m * m, axis=-1, keepdims=True) + epsilon)
    normal = m * inv
    e = grad * gains[0:1, width:]
    back = inv * (e - normal * jnp.mean(e * normal, axis=-1, keepdims=True))
    o_gain[...] = jnp.broadcast_to(jnp.sum(grad * normal, axis=0, keepdims=True), o_gain.shape)
    o_gmid[...] = call[r].astype(F32) + back
    rs.finish()
    part[...] = acc[...].astype(BF).reshape(R, sub, width)
    out_down = net.here(part, o_down)
    out_down.start()
    outs = []
    w = width // C
    for m_i, wref in enumerate((w_down, w_gate, w_up)):
        for i, b in enumerate((c, net.across_c)):
            exchange[2 * m_i + i].wait_recv()
            n_chunk = 5
            rows_n = ff // n_chunk

            @pl.loop(0, n_chunk)
            def _(q):
                rows = pl.ds(pl.multiple_of(q * rows_n, 16), rows_n)
                mine = wref[rows, pl.ds(pl.multiple_of(b * w, 128), w)]
                rx[m_i, i, rows, :] = (mine.astype(F32) + rx[m_i, i, rows, :].astype(F32)).astype(BF)

            cp = net.here(rx.at[m_i, i], o_sum.at[m_i, i])
            cp.start()
            outs.append(cp)
    for cp in exchange:
        cp.wait_send()
    for cp in outs + [out_down]:
        cp.wait()


def feedforward(sizes, nmlp, mid, gains, cot, wg, wu, wd):
    dp, R, C = sizes
    sub, width = nmlp.shape
    n = R * sub
    ff = wd.shape[0]
    tile = 512
    tiles, rest = ff // tile, ff % tile
    shape = jax.ShapeDtypeStruct
    outs = [
        (shape((sub, width), F32), VMEM), (shape((8, width), F32), VMEM),
        (shape((R, sub, width), BF), ANY), (shape((3, 2, ff, width // C), BF), ANY),
    ]
    return pl.pallas_call(
        functools.partial(feedforward_kernel, sizes),
        out_shape=[o for o, _ in outs],
        in_specs=[VMEM, VMEM, VMEM, ANY, ANY, ANY, ANY],
        out_specs=[s for _, s in outs],
        scratch_shapes=[
            pltpu.VMEM((ff, width), BF), pltpu.VMEM((ff, width), BF), pltpu.VMEM((ff, width), BF),
            pltpu.VMEM((R, sub, width), BF), pltpu.VMEM((R, sub, width), BF),
            pltpu.VMEM((tiles, n, tile), F32), pltpu.VMEM((tiles, n, tile), BF),
            pltpu.VMEM((tiles, n, tile), BF), pltpu.VMEM((tiles, n, tile), BF),
            pltpu.VMEM((n, rest), F32), pltpu.VMEM((n, rest), BF),
            pltpu.VMEM((n, rest), BF), pltpu.VMEM((n, rest), BF),
            pltpu.VMEM((n, width), F32), pltpu.VMEM((R, sub, width), BF),
            pltpu.VMEM((R, sub, width), BF), pltpu.VMEM((R, sub, width), BF),
            pltpu.VMEM((3, 2, ff, width // C), BF),
            pltpu.SemaphoreType.DMA((48,)), pltpu.SemaphoreType.DMA((48,)),
            pltpu.SemaphoreType.DMA((24,)),
        ],
        compiler_params=pltpu.CompilerParams(
            collective_id=2, has_side_effects=True, vmem_limit_bytes=VMEM_LIMIT
        ),
        name="feedforward",
    )(nmlp, mid, gains, cot, wg, wu, wd)


def partner(value, axis, mask):
    pairs = [(s, s ^ mask) for s in range(lax.axis_size(axis))]
    return lax.ppermute(value, axis, pairs)


def gather(value, axis, dim=0):
    return lax.all_gather(value, axis, axis=dim, tiled=True)


def scatter_sum(value, axis, dim=0):
    return lax.psum_scatter(value.astype(BF), axis, scatter_dimension=dim, tiled=True)


def features_to_tokens(block):
    cols = lax.axis_size("col")
    sub = block.shape[0] // cols
    out = lax.all_to_all(block.reshape(cols, sub, -1), "col", 0, 0, tiled=True)
    return jnp.moveaxis(out, 0, 1).reshape(sub, -1)


def tokens_to_features(block):
    cols = lax.axis_size("col")
    sub = block.shape[0]
    parts = jnp.moveaxis(block.reshape(sub, cols, -1), 1, 0)
    out = lax.all_to_all(parts, "col", 0, 0, tiled=True)
    return out.reshape(cols * sub, -1)


def rotation(positions):
    half = HEAD // 2
    rates = rope_base ** (-jnp.arange(half, dtype=F32) * (2.0 / HEAD))
    angles = positions.astype(F32)[:, None] * rates[None, :]
    return jnp.cos(angles), jnp.sin(angles)


def rotate(values, cosine, sine):
    half = HEAD // 2
    shaped = values.reshape(values.shape[0], -1, HEAD)
    a, b = shaped[..., :half], shaped[..., half:]
    c, s = cosine[:, None, :], sine[:, None, :]
    turned = jnp.concatenate([a * c - b * s, b * c + a * s], axis=-1)
    return turned.reshape(values.shape)


def norm_back(grad, normal, inverse, gain):
    e = grad * gain
    mean = jnp.mean(e * normal, axis=-1, keepdims=True)
    return inverse * (e - normal * mean), jnp.sum(grad * normal, axis=0)


def on_device(
    tokens_in, seq_lengths, attention_gain, query_weight, query_bias, keyvalue_weight,
    keyvalue_bias, output_weight, feedforward_gain, gate_weight, up_weight, down_weight,
    cotangent,
):
    rows, cols = lax.axis_size("row"), lax.axis_size("col")
    col = lax.axis_index("col")
    row_tokens = tokens_in.shape[0]
    group = row_tokens * rows
    sub = row_tokens // cols
    wq_width = query_weight.shape[1]
    heads = wq_width // HEAD
    is_key = lax.axis_index("row") % 2 == 0
    sizes = (lax.axis_size("dp"), rows, cols)
    width = tokens_in.shape[1] * cols
    places = jnp.arange(group, dtype=jnp.int32)
    ends = jnp.cumsum(seq_lengths[0])
    first = jnp.max(jnp.where(places[:, None] >= ends[None, :-1], ends[None, :-1], 0), axis=1)
    own = lambda v: lax.dynamic_slice_in_dim(v.reshape(rows, cols, sub), col, 1, 1).reshape(-1)
    my_places, my_first = own(places), own(first)
    cosine, sine = rotation(my_places - my_first)
    cos2 = jnp.concatenate([cosine, cosine], axis=1)
    sin2 = jnp.concatenate([-sine, sine], axis=1)
    qpos = jnp.stack([my_first, my_places], axis=1)
    wide = lambda v: jnp.broadcast_to(v.astype(F32)[None], (8, v.shape[0]))
    small = wide(jnp.concatenate([attention_gain, feedforward_gain]))
    (middle, nmlp, gains_all, normed, queries, kv, attended, grad_out_all, w_joint, w_out,
     w_gate, w_up) = attention_forward(
        sizes, tokens_in, cotangent, query_weight, keyvalue_weight, output_weight, gate_weight.T,
        up_weight.T, small, wide(query_bias), wide(keyvalue_bias), cos2, sin2, qpos,
    )
    grad_middle, gain_mlp_part, down_part, block_sums = feedforward(
        sizes, nmlp, middle, gains_all, grad_out_all, w_gate, w_up, down_weight
    )
    gain_mlp_part = gain_mlp_part[0]
    gain_attn, gain_mlp = gains_all[0, :width], gains_all[0, width:]
    inputs = features_to_tokens(tokens_in).astype(F32)
    inverse_attn = lax.rsqrt(jnp.mean(inputs * inputs, axis=-1, keepdims=True) + epsilon)
    normal_attn = inputs * inverse_attn
    normed = normed.reshape(-1, width)
    keys = kv[..., :HEAD].reshape(group, HEAD)
    values = kv[..., HEAD:].reshape(group, HEAD)
    q_heads = queries.reshape(rows, sub, heads, HEAD)
    scale = HEAD ** (-0.5)

    def block_probs(r):
        limit = (r + 1) * row_tokens
        scores = jnp.einsum(
            "qhd,sd->hqs", q_heads[r], keys[:limit], preferred_element_type=F32
        ) * scale
        mine = slice(r * sub, (r + 1) * sub)
        allowed = (places[None, :limit] >= my_first[mine][:, None]) & (
            places[None, :limit] <= my_places[mine][:, None]
        )
        scores = jnp.where(allowed[None], scores, masked_score)
        e = jnp.exp(scores - jnp.max(scores, axis=-1, keepdims=True))
        return e / jnp.sum(e, axis=-1, keepdims=True)

    branch = scatter_sum(down_part.reshape(-1, width), "row").astype(F32)
    layer_out = tokens_to_features((middle + branch).astype(BF))
    grad_middle_all = gather(grad_middle.astype(BF), "row")
    grad_heads = dot(grad_middle_all, w_out, 1, 1).astype(BF).reshape(rows, sub, heads, HEAD)
    gw_out = dot(attended, grad_middle_all, 0, 0)
    dq, dk, dv = [], 0.0, 0.0
    for r in range(rows):
        limit = (r + 1) * row_tokens
        p = block_probs(r)
        pad = ((0, group - limit), (0, 0))
        dv = dv + jnp.pad(jnp.einsum(
            "hqs,qhd->sd", p.astype(BF), grad_heads[r], preferred_element_type=F32), pad)
        g = jnp.einsum("qhd,sd->hqs", grad_heads[r], values[:limit], preferred_element_type=F32)
        ds = (p * (g - jnp.sum(p * g, axis=-1, keepdims=True))).astype(BF)
        dq.append(jnp.einsum("hqs,sd->qhd", ds, keys[:limit], preferred_element_type=F32)
                  .reshape(sub, wq_width) * scale)
        dk = dk + jnp.pad(jnp.einsum(
            "hqs,qhd->sd", ds, q_heads[r], preferred_element_type=F32) * scale, pad)
    dq = jnp.concatenate(dq, axis=0)
    dslots = jnp.concatenate([dk, dv], axis=1)
    dslots = jnp.moveaxis(dslots.reshape(rows, cols, sub, -1), 1, 0).reshape(group, -1)
    dslots = scatter_sum(dslots, "col").astype(F32)
    dturned = jnp.concatenate([dq, dslots[:, :HEAD]], axis=1)
    grad_joint = jnp.concatenate(
        [rotate(dturned, cosine, -sine), dslots[:, HEAD:]], axis=1
    ).astype(BF)
    grad_normed = scatter_sum(dot(grad_joint, w_joint, 1, 1), "row").astype(F32)
    gw_joint = dot(normed, grad_joint, 0, 0)
    g_bias = jnp.sum(grad_joint.astype(F32), axis=0)
    back, gain_attn_part = norm_back(grad_normed, normal_attn, inverse_attn, gain_attn)
    input_grad = tokens_to_features((grad_middle + back).astype(BF))
    across = lambda v: lax.ppermute(v, "col", [(k, (k + 2) % 4) for k in range(4)])
    pair_sum = block_sums[:, 0].astype(F32) + across(block_sums[:, 1]).astype(F32)
    gw_down = scatter_sum(pair_sum[0], "dp").astype(F32)
    gw_gate = scatter_sum(pair_sum[1], "dp", 1).astype(F32).T
    gw_up = scatter_sum(pair_sum[2], "dp", 1).astype(F32).T
    both = lambda v, dim: scatter_sum(scatter_sum(v, "col", dim), "dp").astype(F32)

    def slot_share(v, axis):
        k, w = v[..., wq_width : wq_width + HEAD], v[..., wq_width + HEAD :]
        got = partner(jnp.where(is_key, w, k).astype(BF), "row", 1)
        return jnp.where(is_key, k, w) + got.astype(F32)

    gw_joint = scatter_sum(gw_joint, "col").astype(F32)
    gw_query = scatter_sum(gw_joint[:, :wq_width], "dp").astype(F32)
    gw_keyvalue = scatter_sum(slot_share(gw_joint, 1), "dp").astype(F32)
    g_bias = lax.psum(g_bias, "col")
    g_qb = lax.psum_scatter(g_bias[:wq_width], "dp", scatter_dimension=0, tiled=True)
    g_kvb = slot_share(g_bias, 0)
    g_kvb = lax.psum_scatter(g_kvb, "dp", scatter_dimension=0, tiled=True)
    gains = lax.psum((gain_attn_part, gain_mlp_part), ("dp", "row", "col"))
    mine = lambda v: lax.dynamic_slice_in_dim(v, col * (v.shape[0] // cols), v.shape[0] // cols)
    return (
        layer_out, input_grad, mine(gains[0]), gw_query, g_qb, gw_keyvalue, g_kvb,
        both(gw_out, 1), mine(gains[1]), gw_gate, gw_up, gw_down,
    )


def solution(mesh):
    return jax.shard_map(
        on_device,
        mesh=mesh,
        in_specs=(
            P(("dp", "row"), "col"), P("dp", None), P("col"), P("col", "row"), P("row"),
            P("col", "row"), P("row"), P("row", "col"), P("col"), P("col", "row"),
            P("col", "row"), P("row", "col"), P(("dp", "row"), "col"),
        ),
        out_specs=(
            P(("dp", "row"), "col"), P(("dp", "row"), "col"), P("col"),
            P(("col", "dp"), "row"), P(("row", "dp")), P(("col", "dp"), "row"),
            P(("row", "dp")), P(("row", "dp"), "col"), P("col"), P(("col", "dp"), "row"),
            P(("col", "dp"), "row"), P(("row", "dp"), "col"),
        ),
        check_vma=False,
    )
```

```python
import functools

import jax
import jax.numpy as jnp
from jax import lax
from jax.experimental import pallas as pl
from jax.experimental.pallas import tpu as pltpu
from jax.sharding import PartitionSpec as P

HEAD = 128
epsilon = 1e-06
rope_base = 1000000.0
masked_score = -1e30
BF = jnp.bfloat16
F32 = jnp.float32
MESH = pl.DeviceIdType.MESH
ANY = pl.BlockSpec(memory_space=pl.ANY)
VMEM = pl.BlockSpec(memory_space=pltpu.VMEM)
VMEM_LIMIT = 60 * 2**20


def dot(a, b, ca=1, cb=0):
    return lax.dot_general(a, b, (((ca,), (cb,)), ((), ())), preferred_element_type=F32)


class Net:
    def __init__(self, sizes, send, recv, local):
        self.dp, self.R, self.C = sizes
        self.d = lax.axis_index("dp")
        self.r = lax.axis_index("row")
        self.c = lax.axis_index("col")
        half = self.dp // 2
        self.h = self.d // half
        self.send, self.recv, self.local = send, recv, local
        self.n = 0
        self.n_local = 0
        self.other_h = 1 - self.h
        self.mate = (lax.rem(self.d + half, self.dp), self.r, self.c)
        self.sibling = self.at_col(self.c + 1 - 2 * lax.rem(self.c, 2))
        self.across_c = lax.rem(self.c + 2, 4)
        self.across = self.at_col(self.across_c)

    def at_col(self, c):
        return (self.d, self.r, c)

    def at_row(self, r):
        return (self.d, r, self.c)

    def copy(self, src, dst, dev):
        i = self.n
        self.n += 1
        return pltpu.make_async_remote_copy(
            src_ref=src, dst_ref=dst, send_sem=self.send.at[i], recv_sem=self.recv.at[i],
            device_id=dev, device_id_type=MESH,
        )

    def like(self, copy_index, src, dst, dev):
        return pltpu.make_async_remote_copy(
            src_ref=src, dst_ref=dst, send_sem=self.send.at[copy_index],
            recv_sem=self.recv.at[copy_index], device_id=dev, device_id_type=MESH,
        )

    def here(self, src, dst):
        i = self.n_local
        self.n_local += 1
        return pltpu.make_async_copy(src, dst, self.local.at[i])

    def barrier(self):
        sem = pltpu.get_barrier_semaphore()
        for k in range(1, self.C):
            pl.semaphore_signal(
                sem, inc=1, device_id=self.at_col(lax.rem(self.c + k, self.C)), device_id_type=MESH
            )
        pl.semaphore_signal(sem, inc=1, device_id=self.mate, device_id_type=MESH)

        @pl.when(self.r > 0)
        def _():
            pl.semaphore_signal(sem, inc=1, device_id=self.at_row(self.r - 1), device_id_type=MESH)

        @pl.when(self.r < self.R - 1)
        def _():
            pl.semaphore_signal(sem, inc=1, device_id=self.at_row(self.r + 1), device_id_type=MESH)

        count = self.C + (self.r > 0).astype(jnp.int32) + (self.r < self.R - 1).astype(jnp.int32)
        pl.semaphore_wait(sem, count)


class LineGather:
    def __init__(self, net, buf):
        self.net, self.buf = net, buf
        r, R = net.r, net.R
        self.up_i, self.dn_i = [], []
        for s in range(R - 1):
            self.up_i.append(net.n)
            self.dn_i.append(net.n + 1)
            net.n += 2

    def _up(self, s, shard):
        net = self.net
        b = self.buf.at[jnp.clip(shard, 0, net.R - 1)]
        return net.like(self.up_i[s], b, b, net.at_row(jnp.minimum(net.r + 1, net.R - 1)))

    def _dn(self, s, shard):
        net = self.net
        b = self.buf.at[jnp.clip(shard, 0, net.R - 1)]
        return net.like(self.dn_i[s], b, b, net.at_row(jnp.maximum(net.r - 1, 0)))

    def step(self, s):
        net = self.net
        r, R = net.r, net.R
        if s > 0:

            @pl.when(r - s >= 0)
            def _():
                self._up(s - 1, r - s).wait_recv()

        if s < R - 1:

            @pl.when((r - s >= 0) & (r < R - 1))
            def _():
                self._up(s, r - s).start()

        if s > 0:

            @pl.when(r + s < R)
            def _():
                self._dn(s - 1, r + s).wait_recv()

        if s < R - 1:

            @pl.when((r + s < R) & (r > 0))
            def _():
                self._dn(s, r + s).start()

    def finish(self):
        net = self.net
        r, R = net.r, net.R
        for s in range(R - 1):

            @pl.when((r - s >= 0) & (r < R - 1))
            def _():
                self._up(s, r - s).wait_send()

            @pl.when((r + s < R) & (r > 0))
            def _():
                self._dn(s, r + s).wait_send()


class LineSum:
    def __init__(self, net, part, from_below, from_above):
        self.net, self.part, self.bu, self.bd = net, part, from_below, from_above
        self.base = net.n
        net.n += 2 * net.R

    def _dn(self, j):
        net = self.net
        j = jnp.clip(j, 0, net.R - 1)
        return net.like(
            self.base + j, self.part.at[j], self.bd.at[j], net.at_row(jnp.maximum(net.r - 1, 0))
        )

    def _up(self, j):
        net = self.net
        j = jnp.clip(j, 0, net.R - 1)
        return net.like(
            self.base + net.R + j, self.part.at[j], self.bu.at[j],
            net.at_row(jnp.minimum(net.r + 1, net.R - 1)),
        )

    def _add(self, j, buf):
        self.part[j] = (self.part[j].astype(F32) + buf[j].astype(F32)).astype(BF)

    def step(self, t):
        net = self.net
        r, R = net.r, net.R
        j = t - (R - 1 - r)
        k = R - 1 - (t - r)

        @pl.when((j >= 0) & (r < R - 1))
        def _():
            self._dn(j).wait_recv()

        @pl.when((j >= 0) & (j < r))
        def _():
            @pl.when(r < R - 1)
            def _():
                self._add(j, self.bd)

            self._dn(j).start()

        @pl.when((k <= R - 1) & (r > 0))
        def _():
            self._up(k).wait_recv()

        @pl.when((k <= R - 1) & (k > r))
        def _():
            @pl.when(r > 0)
            def _():
                self._add(k, self.bu)

            self._up(k).start()

    def finish(self):
        net = self.net
        r, R = net.r, net.R
        for j in range(R):

            @pl.when(j < r)
            def _():
                self._dn(j).wait_send()

            @pl.when(j > r)
            def _():
                self._up(j).wait_send()

    def total_into(self, out):
        net = self.net
        r, R = net.r, net.R
        out[...] += self.part[r].astype(F32)

        @pl.when(r < R - 1)
        def _():
            out[...] += self.bd[r].astype(F32)

        @pl.when(r > 0)
        def _():
            out[...] += self.bu[r].astype(F32)


class WeightGather:
    def __init__(self, net, src, full, by_rows, piece=0, pieces=1):
        self.net, self.full, self.by_rows = net, full, by_rows
        if by_rows:
            self.n, self.w = full.shape[0] // net.C, full.shape[1]
        else:
            self.n, self.w = full.shape[0] // pieces, full.shape[1] // net.C
        self.first = piece * self.n
        if src is not None:
            src = src.at[pl.ds(self.first, self.n)]
        c, p, h, o = net.c, net.across_c, net.h, net.other_h
        half = self.n // 2
        self.here = None
        if src is not None:
            self.here = net.here(src, self.view(c, 0, 2))
            own_half = src.at[pl.ds(pl.multiple_of(h * half, 16), half)]
            own = src
        else:
            own_half, own = self.view(c, h, 1), self.view(c, 0, 2)
        self.x = net.copy(own_half, self.view(c, h, 1), net.across)
        self.sib = net.copy(own, self.view(c, 0, 2), net.sibling)
        self.y = net.copy(self.view(p, h, 1), self.view(p, h, 1), net.mate)
        self.sib_h = net.copy(self.view(p, h, 1), self.view(p, h, 1), net.sibling)
        self.sib_o = net.copy(self.view(p, o, 1), self.view(p, o, 1), net.sibling)

    def view(self, b, h, halves):
        half = self.n // 2
        if self.by_rows:
            return self.full.at[pl.ds(pl.multiple_of(b * self.n + h * half, 16), halves * half)]
        return self.full.at[
            pl.ds(pl.multiple_of(self.first + h * half, 16), halves * half),
            pl.ds(pl.multiple_of(b * self.w, 128), self.w),
        ]

    def start(self):
        if self.here is not None:
            self.here.start()
        self.x.start()
        self.sib.start()

    def pass_x(self):
        self.x.wait_recv()
        self.y.start()
        self.sib_h.start()

    def pass_y(self):
        self.y.wait_recv()
        self.sib_o.start()

    def arrive(self):
        if self.here is not None:
            self.here.wait()
        self.sib.wait_recv()
        self.sib_h.wait_recv()
        self.sib_o.wait_recv()

    def finish(self):
        for cp in (self.x, self.sib, self.y, self.sib_h, self.sib_o):
            cp.wait_send()


def turn(values, cos2, sin2):
    heads = []
    for i in range(values.shape[1] // HEAD):
        v = values[:, i * HEAD : (i + 1) * HEAD]
        heads.append(v * cos2 + pltpu.roll(v, HEAD // 2, 1) * sin2)
    return jnp.concatenate(heads, axis=1) if len(heads) > 1 else heads[0]


def attention_kernel(
    sizes,
    tok, cot, wq, wkv, wo, wg, wu, small, qb, kvb, cos2, sin2, qpos,
    o_x, o_mid, o_nmlp, o_gains, o_normed, o_q, o_kv, o_att, o_cot, o_wj, o_wo, o_wg, o_wu,
    xin, cin, gains, kvb2, nall, call, wj, wov, kv, qs, att, part, rbu, rbd, send, recv, local,
):
    net = Net(sizes, send, recv, local)
    R, C, r, c = net.R, net.C, net.r, net.c
    sub, width = nall.shape[1], nall.shape[2]
    block = tok.shape[1]
    row_tok = sub * C
    n_tok = sub * R
    qw = wq.shape[1]
    slot = lax.rem(r, 2)
    partner = net.at_row(r + 1 - 2 * slot)
    net.barrier()

    def spread(src, dst):
        mine = pl.multiple_of(c * sub, sub)
        local_copy = net.here(src.at[pl.ds(mine, sub)], dst.at[c])
        copies = []
        for k in range(1, C):
            to = lax.rem(c + k, C)
            frm = lax.rem(c + C - k, C)
            i = net.n
            net.n += 1
            rows = pl.ds(pl.multiple_of(to * sub, sub), sub)
            copies.append(
                (net.like(i, src.at[rows], dst.at[c], net.at_col(to)),
                 net.like(i, src.at[rows], dst.at[frm], net.at_col(to)))
            )
        return local_copy, copies

    def begin(pair):
        pair[0].start()
        for out, _ in pair[1]:
            out.start()

    def arrived(pair):
        pair[0].wait()
        for _, inc in pair[1]:
            inc.wait_recv()

    tok_in, cot_in = spread(tok, xin), spread(cot, cin)
    begin(tok_in)
    gain_own = net.here(small, gains.at[c])
    gain_own.start()
    gain_copies = []
    for k in range(1, C):
        to, frm = lax.rem(c + k, C), lax.rem(c + C - k, C)
        i = net.n
        net.n += 1
        out = net.like(i, small, gains.at[c], net.at_col(to))
        gain_copies.append((out, net.like(i, small, gains.at[frm], net.at_col(to))))
        out.start()
    own_rows = pl.ds(pl.multiple_of(c * block, block), block)
    col_own = pl.ds(pl.multiple_of(qw + slot * HEAD, HEAD), HEAD)
    col_mate = pl.ds(pl.multiple_of(qw + (1 - slot) * HEAD, HEAD), HEAD)
    kv_x = net.copy(wkv, wj.at[own_rows, col_own], partner)
    kv_in = net.like(net.n - 1, wkv, wj.at[own_rows, col_mate], partner)
    kv_x.start()
    kvb_x = net.copy(kvb, kvb2.at[slot], partner)
    kvb_in = net.like(net.n - 1, kvb, kvb2.at[1 - slot], partner)
    kvb_x.start()
    kvb_own = net.here(kvb, kvb2.at[slot])
    kvb_own.start()
    wq_own = net.here(wq, wj.at[own_rows, pl.ds(0, qw)])
    wq_own.start()
    wkv_own = net.here(wkv, wj.at[own_rows, col_own])
    wkv_own.start()
    g_joint = WeightGather(net, None, wj, True)
    g_out = WeightGather(net, wo, wov, False)
    bulk = [WeightGather(net, w, o, False, i, 2) for w, o in ((wg, o_wg), (wu, o_wu)) for i in (0, 1)]

    arrived(tok_in)
    gain_own.wait()
    for _, inc in gain_copies:
        inc.wait_recv()
    for k in range(C):
        o_gains[:, k * block : (k + 1) * block] = gains[k, :, :block]
        o_gains[:, width + k * block : width + (k + 1) * block] = gains[k, :, block:]
    x = jnp.concatenate([xin[k].astype(F32) for k in range(C)], axis=1)
    o_mid[...] = x
    o_x[...] = x.astype(BF)
    inv = lax.rsqrt(jnp.mean(x * x, axis=-1, keepdims=True) + epsilon)
    nall[r] = (x * inv * o_gains[0:1, :width]).astype(BF)
    g_n = LineGather(net, nall)
    g_n.step(0)
    wq_own.wait()
    wkv_own.wait()
    kv_in.wait_recv()
    g_joint.start()
    g_out.start()
    begin(cot_in)
    g_joint.pass_x()
    g_out.pass_x()
    bulk[0].start()
    g_joint.pass_y()
    g_n.step(1)
    g_out.pass_y()
    bulk[1].start()
    arrived(cot_in)
    for k in range(C):
        call[r, :, k * block : (k + 1) * block] = cin[k]
    g_n.step(2)
    bulk[0].pass_x()
    g_joint.arrive()
    kvb_own.wait()
    kvb_in.wait_recv()
    g_n.step(3)
    g_cot = LineGather(net, call)
    g_cot.step(0)
    bias = jnp.concatenate([qb[0:1, :], kvb2[0, 0:1, :], kvb2[1, 0:1, :]], axis=1)
    joint = dot(nall[...].reshape(n_tok, width), wj[...]) + bias
    key = turn(joint[:, qw : qw + HEAD], cos2[...], sin2[...]).astype(BF)
    kv[:, c, :, :HEAD] = key.reshape(R, sub, HEAD)
    kv[:, c, :, HEAD:] = joint[:, qw + HEAD :].astype(BF).reshape(R, sub, HEAD)
    kv_copies = []
    for k in range(1, C):
        to, frm = lax.rem(c + k, C), lax.rem(c + C - k, C)
        i = net.n
        net.n += 1
        out = net.like(i, kv.at[:, c], kv.at[:, c], net.at_col(to))
        kv_copies.append((out, net.like(i, kv.at[:, frm], kv.at[:, frm], net.at_col(to))))
        out.start()
    qs[...] = turn(joint[:, :qw], cos2[...], sin2[...]).astype(BF)
    out_normed = net.here(nall, o_normed)
    out_normed.start()
    out_wj = net.here(wj, o_wj)
    out_wj.start()
    for _, inc in kv_copies:
        inc.wait_recv()
    bulk[1].pass_x()
    bulk[2].start()
    bulk[3].start()
    bulk[0].pass_y()
    g_cot.step(1)
    out_kv = net.here(kv, o_kv)
    out_kv.start()
    scale = HEAD ** (-0.5)
    for rr in range(R):
        limit = (rr + 1) * row_tok
        keys = kv[: rr + 1, :, :, :HEAD].reshape(limit, HEAD)
        values = kv[: rr + 1, :, :, HEAD:].reshape(limit, HEAD)
        mine = slice(rr * sub, (rr + 1) * sub)
        place = lax.broadcasted_iota(jnp.int32, (sub, limit), 1)
        allowed = (place >= qpos[mine, 0:1]) & (place <= qpos[mine, 1:2])
        for h in range(qw // HEAD):
            cols = slice(h * HEAD, (h + 1) * HEAD)
            s = jnp.where(allowed, dot(qs[mine, cols], keys, 1, 1) * scale, masked_score)
            e = jnp.exp(s - jnp.max(s, axis=-1, keepdims=True))
            p = e * (1.0 / jnp.sum(e, axis=-1, keepdims=True))
            att[mine, cols] = dot(p.astype(BF), values).astype(BF)
    g_out.arrive()
    part[...] = dot(att[...], wov[...]).astype(BF).reshape(R, sub, width)
    rs = LineSum(net, part, rbu, rbd)
    rs.step(0)
    out_q = net.here(qs, o_q)
    out_q.start()
    out_att = net.here(att, o_att)
    out_att.start()
    out_wo = net.here(wov, o_wo)
    out_wo.start()
    g_cot.step(2)
    bulk[1].pass_y()
    bulk[2].pass_x()
    rs.step(1)
    g_cot.step(3)
    out_cot = net.here(call, o_cot)
    out_cot.start()
    bulk[3].pass_x()
    rs.step(2)
    bulk[2].pass_y()
    rs.step(3)
    rs.total_into(o_mid)
    mid = o_mid[...]
    inv = lax.rsqrt(jnp.mean(mid * mid, axis=-1, keepdims=True) + epsilon)
    o_nmlp[...] = (mid * inv * o_gains[0:1, width:]).astype(BF)
    bulk[3].pass_y()
    for g in bulk:
        g.arrive()
    for g in [g_joint, g_out, g_n, g_cot, rs] + bulk:
        g.finish()
    for out, _ in tok_in[1] + cot_in[1] + gain_copies + kv_copies:
        out.wait_send()
    kv_x.wait_send()
    kvb_x.wait_send()
    for cp in (out_normed, out_wj, out_kv, out_q, out_att, out_wo, out_cot):
        cp.wait()


def attention_forward(sizes, tok, cot, wq, wkv, wo, wg, wu, small, qb, kvb, cos2, sin2, qpos):
    dp, R, C = sizes
    sub = tok.shape[0] // C
    block = tok.shape[1]
    width = block * C
    qw, jw = wq.shape[1], wq.shape[1] + 2 * HEAD
    n = sub * R
    ff = wg.shape[0]
    shape = jax.ShapeDtypeStruct
    outs = [
        (shape((sub, width), BF), VMEM),
        (shape((sub, width), F32), VMEM), (shape((sub, width), BF), VMEM),
        (shape((8, 2 * width), F32), VMEM), (shape((R, sub, width), BF), ANY),
        (shape((n, qw), BF), ANY), (shape((R, C, sub, 2 * HEAD), BF), ANY),
        (shape((n, qw), BF), ANY), (shape((R, sub, width), BF), ANY),
        (shape((width, jw), BF), ANY), (shape((qw, width), BF), ANY),
        (shape((ff, width), BF), ANY), (shape((ff, width), BF), ANY),
    ]
    return pl.pallas_call(
        functools.partial(attention_kernel, sizes),
        out_shape=[o for o, _ in outs],
        in_specs=[ANY] * 7 + [VMEM] * 6,
        out_specs=[s for _, s in outs],
        scratch_shapes=[
            pltpu.VMEM((C, sub, block), BF), pltpu.VMEM((C, sub, block), BF),
            pltpu.VMEM((C, 8, 2 * block), F32), pltpu.VMEM((2, 8, HEAD), F32),
            pltpu.VMEM((R, sub, width), BF), pltpu.VMEM((R, sub, width), BF),
            pltpu.VMEM((width, jw), BF), pltpu.VMEM((qw, width), BF),
            pltpu.VMEM((R, C, sub, 2 * HEAD), BF), pltpu.VMEM((n, qw), BF),
            pltpu.VMEM((n, qw), BF), pltpu.VMEM((R, sub, width), BF),
            pltpu.VMEM((R, sub, width), BF), pltpu.VMEM((R, sub, width), BF),
            pltpu.SemaphoreType.DMA((64,)), pltpu.SemaphoreType.DMA((64,)),
            pltpu.SemaphoreType.DMA((24,)),
        ],
        compiler_params=pltpu.CompilerParams(
            collective_id=1, has_side_effects=True, vmem_limit_bytes=VMEM_LIMIT
        ),
        name="attention_forward",
    )(tok, cot, wq, wkv, wo, wg, wu, small, qb, kvb, cos2, sin2, qpos)


def feedforward_kernel(
    sizes,
    nmlp, mid, gains, cot, wg, wu, wd,
    o_gmid, o_gain, o_down, o_sd, o_sg, o_su,
    w_gate, w_up, w_down, xall, call, acc, hid, gg, gu, hid_r, gg_r, gu_r,
    s_hid, s_gg, s_gu, s_hid_r, s_gg_r, s_gu_r, sx, sc, xt, part, rbu, rbd, g,
    send, recv, local,
):
    net = Net(sizes, send, recv, local)
    R, C, r, c = net.R, net.C, net.r, net.c
    sub, width = nmlp.shape
    block = width // C
    n_tok = sub * R
    tiles, _, tile = hid.shape
    rest = hid_r.shape[1]
    wide = width // tile
    own_cols = [pl.ds(pl.multiple_of(b * block, HEAD), block) for b in (c, net.across_c)]
    sib_cols = [
        pl.ds(pl.multiple_of((b + 1 - 2 * lax.rem(b, 2)) * block, HEAD), block)
        for b in (c, net.across_c)
    ]
    parts = [(pl.ds(t * tile, tile), t) for t in range(tiles)] + [(pl.ds(tiles * tile, rest), None)]

    def at(whole, remainder, t):
        return remainder if t is None else whole.at[t]

    g_down = WeightGather(net, wd, w_down, False)
    in_cot = net.here(cot, call)
    in_gate = net.here(wg, w_gate)
    in_up = net.here(wu, w_up)
    for cp in (in_cot, in_gate, in_up):
        cp.start()
    net.barrier()
    xall[r] = nmlp[...]
    g_x = LineGather(net, xall)
    g_x.step(0)
    g_down.start()
    in_cot.wait()
    to_sibling = [net.copy(call.at[:, :, sib_cols[i]], sc.at[i], net.sibling) for i in (0, 1)]
    for cp in to_sibling:
        cp.start()
    g_x.step(1)
    g_down.pass_x()
    in_gate.wait()
    in_up.wait()
    g_x.step(2)
    g_down.pass_y()
    g_down.arrive()

    def hidden_back(rows):
        return dot(call[...].reshape(n_tok, width), w_down[rows, :], 1, 1)

    @pl.loop(0, wide)
    def _(t):
        acc[t] = hidden_back(pl.ds(pl.multiple_of(t * tile, tile), tile))

    g_x.step(3)
    for i in (0, 1):
        cp = net.copy(xall.at[:, :, sib_cols[i]], sx.at[i], net.sibling)
        cp.start()
        to_sibling.append(cp)

    def act(rows, back, t):
        x = xall[...].reshape(n_tok, width)
        gate = dot(x, w_gate[rows, :], 1, 1)
        up = dot(x, w_up[rows, :], 1, 1)
        s = jax.nn.sigmoid(gate)
        silu = gate * s
        at(hid, hid_r, t)[...] = (silu * up).astype(BF)
        at(gg, gg_r, t)[...] = (back * up * s * (1.0 + gate * (1.0 - s))).astype(BF)
        at(gu, gu_r, t)[...] = (back * silu).astype(BF)

    @pl.loop(0, wide)
    def _(t):
        act(pl.ds(pl.multiple_of(t * tile, tile), tile), acc[t], t)

    for rows, t in parts[wide:]:
        act(rows, hidden_back(rows), t)
    for mine, theirs in (
        (hid, s_hid), (gg, s_gg), (gu, s_gu), (hid_r, s_hid_r), (gg_r, s_gg_r), (gu_r, s_gu_r)
    ):
        cp = net.copy(mine, theirs, net.sibling)
        cp.start()
        to_sibling.append(cp)

    def products(n, pairs):
        cols = pl.ds(pl.multiple_of(n * tile, tile), tile)
        total = None
        for rows, t in parts:
            for whole, remainder, w in pairs:
                term = dot(at(whole, remainder, t)[...], w[rows, cols])
                total = term if total is None else total + term
        return cols, total

    @pl.loop(0, wide)
    def _(n):
        cols, total = products(n, ((gg, gg_r, w_gate), (gu, gu_r, w_up)))
        part[:, :, cols] = total.astype(BF).reshape(R, sub, tile)

    rs = LineSum(net, part, rbu, rbd)
    rs.step(0)

    @pl.loop(0, wide)
    def _(n):
        acc[n] = products(n, ((hid, hid_r, w_down),))[1]

    for cp in to_sibling:
        cp.wait_recv()
    rs.step(1)
    g_down.finish()
    outs = []
    sib_cot = [sc[i].reshape(n_tok, block) for i in (0, 1)]
    for rows, t in parts:
        for i in (0, 1):
            own_cot = call[:, :, own_cols[i]].reshape(n_tok, block)
            total = dot(at(hid, hid_r, t)[...], own_cot, 0, 0)
            total = total + dot(at(s_hid, s_hid_r, t)[...], sib_cot[i], 0, 0)
            w_down[rows, i * block : (i + 1) * block] = total.astype(BF)
    for i in (0, 1):
        cp = net.here(w_down.at[:, pl.ds(i * block, block)], o_sd.at[i])
        cp.start()
        outs.append(cp)
    rs.step(2)
    for i in (0, 1):
        xt[i * block : (i + 1) * block, :n_tok] = xall[:, :, own_cols[i]].reshape(n_tok, block).T
        xt[i * block : (i + 1) * block, n_tok:] = sx[i].reshape(n_tok, block).T
    for mine, mine_r, theirs, theirs_r, o in (
        (gg, gg_r, s_gg, s_gg_r, o_sg), (gu, gu_r, s_gu, s_gu_r, o_su)
    ):
        if o is o_su:
            outs.pop().wait()
        for rows, t in parts:
            total = dot(xt[:, :n_tok], at(mine, mine_r, t)[...])
            total = total + dot(xt[:, n_tok:], at(theirs, theirs_r, t)[...])
            g[:, :, rows] = total.astype(BF).reshape(8, g.shape[1], -1)
        cp = net.here(g, o)
        cp.start()
        outs.append(cp)
    rs.step(3)
    o_gmid[...] = jnp.zeros_like(o_gmid)
    rs.total_into(o_gmid)
    grad = o_gmid[...]
    m = mid[...]
    inv = lax.rsqrt(jnp.mean(m * m, axis=-1, keepdims=True) + epsilon)
    normal = m * inv
    e = grad * gains[0:1, width:]
    back = inv * (e - normal * jnp.mean(e * normal, axis=-1, keepdims=True))
    o_gain[...] = jnp.broadcast_to(jnp.sum(grad * normal, axis=0, keepdims=True), o_gain.shape)
    o_gmid[...] = call[r].astype(F32) + back
    rs.finish()
    for n in range(wide):
        part[:, :, n * tile : (n + 1) * tile] = acc[n].astype(BF).reshape(R, sub, tile)
    out_down = net.here(part, o_down)
    out_down.start()
    g_x.finish()
    for cp in to_sibling:
        cp.wait_send()
    for cp in outs + [out_down]:
        cp.wait()


def feedforward(sizes, nmlp, mid, gains, cot, wg, wu, wd):
    dp, R, C = sizes
    sub, width = nmlp.shape
    block = width // C
    n = R * sub
    ff = wd.shape[0]
    tile = 512
    tiles, rest = ff // tile, ff % tile
    shape = jax.ShapeDtypeStruct
    outs = [
        (shape((sub, width), F32), VMEM), (shape((8, width), F32), VMEM),
        (shape((R, sub, width), BF), ANY), (shape((2, ff, block), BF), ANY),
        (shape((8, block // 4, ff), BF), ANY), (shape((8, block // 4, ff), BF), ANY),
    ]
    acts = [pltpu.VMEM((tiles, n, tile), BF)] * 3 + [pltpu.VMEM((n, rest), BF)] * 3
    return pl.pallas_call(
        functools.partial(feedforward_kernel, sizes),
        out_shape=[o for o, _ in outs],
        in_specs=[VMEM, VMEM, VMEM, ANY, ANY, ANY, ANY],
        out_specs=[s for _, s in outs],
        scratch_shapes=[
            pltpu.VMEM((ff, width), BF), pltpu.VMEM((ff, width), BF), pltpu.VMEM((ff, width), BF),
            pltpu.VMEM((R, sub, width), BF), pltpu.VMEM((R, sub, width), BF),
            pltpu.VMEM((width // tile, n, tile), F32), *acts, *acts,
            pltpu.VMEM((2, R, sub, block), BF), pltpu.VMEM((2, R, sub, block), BF),
            pltpu.VMEM((2 * block, 2 * n), BF),
            pltpu.VMEM((R, sub, width), BF), pltpu.VMEM((R, sub, width), BF),
            pltpu.VMEM((R, sub, width), BF),
            pltpu.VMEM((8, block // 4, ff), BF),
            pltpu.SemaphoreType.DMA((40,)), pltpu.SemaphoreType.DMA((40,)),
            pltpu.SemaphoreType.DMA((16,)),
        ],
        compiler_params=pltpu.CompilerParams(
            collective_id=2, has_side_effects=True, vmem_limit_bytes=VMEM_LIMIT
        ),
        name="feedforward",
    )(nmlp, mid, gains, cot, wg, wu, wd)


class BlockSum:
    def __init__(self, net, source, whole, from_x, from_mate, out_own, out_got):
        self.net, self.whole = net, whole
        self.from_x, self.from_mate = from_x, from_mate
        self.out_own, self.out_got = out_own, out_got
        h, o = net.h, net.other_h
        self.first = [net.copy(source.at[4 + 2 * k], from_x.at[k], net.across) for k in (0, 1)]
        self.first += [
            net.copy(source.at[4 * i + 2 * o + 1], from_mate.at[i], net.mate) for i in (0, 1)
        ]
        self.second = [
            net.copy(whole.at[2 * o], out_got.at[0], net.mate),
            net.copy(whole.at[4 + 2 * h + 1], out_got.at[1], net.across),
        ]
        self.keep = net.here(whole.at[pl.ds(2 * h, 2)], out_own)

    def start(self):
        for cp in self.first:
            cp.start()

    def add(self):
        h, whole = self.net.h, self.whole

        def take(i, got):
            whole[i] = (whole[i].astype(F32) + got.astype(F32)).astype(BF)

        for cp in self.first:
            cp.wait_recv()
        for k in (0, 1):
            take(2 * k, self.from_x[k])
        self_b = 2 * h + 1
        for i in (0, 1):
            take(4 * i + self_b, self.from_mate[i])
        for cp in self.second:
            cp.start()
        self.keep.start()

    def finish(self):
        for cp in self.first:
            cp.wait_send()
        for cp in self.second:
            cp.wait_send()
            cp.wait_recv()
        self.keep.wait()


def backward_kernel(
    sizes,
    gmid, x_in, mid, gains, gain_mlp, cos2, sin2, qrow,
    normed, q, kv, att, wj, wo, down, sd, sg, su,
    o_layer, o_input, o_vec, o_j, o_da, o_db, o_ga, o_gb, o_ua, o_ub, o_oa, o_ob,
    mall, nall, qs, kvs, atts, wjs, wos, dpart, drbu, drbd, part, rbu, rbd, grads, dq, dkv, dkv16, dk_in,
    joint, lay,
    s_d, s_g, s_u, x_d, x_g, x_u, y_d, y_g, y_u,
    wjo, wjx, s_j, x_j, y_j, woo, wox, s_o, x_o, y_o, ja, jb, jk, jgot, v1, v1in, v2, v2in,
    send, recv, local,
):
    net = Net(sizes, send, recv, local)
    R, C, r, c = net.R, net.C, net.r, net.c
    sub, width = gmid.shape
    block = width // C
    n_tok = sub * R
    row_tok = sub * C
    qw = qs.shape[1]
    slot = lax.rem(r, 2)
    partner_r = r + 1 - 2 * slot
    loads = [
        net.here(a, b) for a, b in
        ((down, dpart), (sd, s_d), (sg, s_g), (wo, wos), (att, atts), (q, qs), (kv, kvs), (su, s_u),
         (normed, nall), (wj, wjs))
    ]
    for cp in loads:
        cp.start()
    sem = pltpu.get_barrier_semaphore()
    half = net.dp // 2
    others = [(net.d, r, lax.rem(c + k, C)) for k in range(1, C)]
    others += [(net.d, lax.rem(r + k, R), c) for k in range(1, R)]
    others += [(net.mate[0], lax.rem(r + k, R), c) for k in range(R)]
    for dev in others:
        pl.semaphore_signal(sem, inc=1, device_id=dev, device_id_type=MESH)
    pl.semaphore_wait(sem, len(others))

    mall[r] = gmid[...].astype(BF)
    g_m = LineGather(net, mall)
    g_m.step(0)
    sum_d = BlockSum(net, sd, s_d, x_d, y_d, o_da, o_db)
    sum_g = BlockSum(net, sg, s_g, x_g, y_g, o_ga, o_gb)
    sum_u = BlockSum(net, su, s_u, x_u, y_u, o_ua, o_ub)
    sum_d.start()
    sum_g.start()
    loads[0].wait()
    rs_d = LineSum(net, dpart, drbu, drbd)
    rs_d.step(0)
    g_m.step(1)
    rs_d.step(1)
    for cp in loads[1:7]:
        cp.wait()
    sum_d.add()
    sum_u.start()
    g_m.step(2)
    rs_d.step(2)
    g_m.step(3)
    m_all = mall[...].reshape(n_tok, width)
    grads[...] = dot(m_all, wos[...], 1, 1).astype(BF)

    def to_columns(src, dst):
        rows = pl.ds(pl.multiple_of(c * sub, sub), sub)
        mine = net.here(src.at[:, pl.ds(pl.multiple_of(c * block, HEAD), block)], dst.at[rows])
        mine.start()
        pairs = []
        for k in range(1, C):
            to, frm = lax.rem(c + k, C), lax.rem(c + C - k, C)
            i = net.n
            net.n += 1
            cut = src.at[:, pl.ds(pl.multiple_of(to * block, HEAD), block)]
            out = net.like(i, cut, dst.at[rows], net.at_col(to))
            out.start()
            from_rows = pl.ds(pl.multiple_of(frm * sub, sub), sub)
            pairs.append((out, net.like(i, cut, dst.at[from_rows], net.at_col(to))))
        return mine, pairs

    def settle(exchange):
        exchange[0].wait()
        for out, inc in exchange[1]:
            inc.wait_recv()
            out.wait_send()

    sib_blocks = [b + 1 - 2 * lax.rem(b, 2) for b in (c, net.across_c)]
    total = dot(atts[...], m_all, 0, 0)
    for b in range(C):
        woo[4 * b : 4 * b + 4] = (
            total[:, b * block : (b + 1) * block].astype(BF).reshape(4, qw // 4, block)
        )
    out_x = [net.copy(woo.at[pl.ds(4 * b, 4)], wox.at[i], net.sibling) for i, b in enumerate(sib_blocks)]
    for cp in out_x:
        cp.start()
    rs_d.step(3)

    lay[0] = mid[...]
    rs_d.total_into(lay.at[0])
    jk[...] = lay[0].astype(BF)
    layer_x = to_columns(jk, o_layer)

    scale = HEAD ** (-0.5)
    heads = qw // HEAD
    for rr in reversed(range(R)):
        limit = (rr + 1) * row_tok
        keys = kvs[: rr + 1, :, :, :HEAD].reshape(limit, HEAD)
        values = kvs[: rr + 1, :, :, HEAD:].reshape(limit, HEAD)
        mine = slice(rr * sub, (rr + 1) * sub)
        stack = lambda ref: jnp.concatenate(
            [ref[mine, h * HEAD : (h + 1) * HEAD] for h in range(heads)], axis=0
        )
        qh, gh = stack(qs), stack(grads)
        place = lax.broadcasted_iota(jnp.int32, (limit, heads * sub), 0)
        first = jnp.concatenate([qrow[0:1, mine]] * heads, axis=1)
        here = jnp.concatenate([qrow[1:2, mine]] * heads, axis=1)
        s = jnp.where(
            (place >= first) & (place <= here), dot(keys, qh, 1, 1) * scale, masked_score
        )
        e = jnp.exp(s - jnp.max(s, axis=0, keepdims=True))
        p = e * (1.0 / jnp.sum(e, axis=0, keepdims=True))
        g = dot(values, gh, 1, 1)
        ds = (p * (g - jnp.sum(p * g, axis=0, keepdims=True))).astype(BF)
        dv = dot(p.astype(BF), gh)
        dk = dot(ds, qh) * scale
        if rr == R - 1:
            dkv[:, :HEAD] = dk
            dkv[:, HEAD:] = dv
        else:
            dkv[:limit, :HEAD] += dk
            dkv[:limit, HEAD:] += dv
        dqs = dot(ds, keys, 0, 0) * scale
        for h in range(heads):
            dq[mine, h * HEAD : (h + 1) * HEAD] = dqs[h * sub : (h + 1) * sub]
        if rr == R - 1:
            sum_g.add()
        if rr == R - 2:
            for i, b in enumerate((c, net.across_c)):
                out_x[i].wait_recv()
                s_o[4 * i : 4 * i + 4] = (
                    woo[pl.ds(4 * b, 4)].astype(F32) + wox[i].astype(F32)
                ).astype(BF)
    dkv16[...] = dkv[...].astype(BF).reshape(dkv16.shape)
    dk_copies = []
    for k in range(1, C):
        to, frm = lax.rem(c + k, C), lax.rem(c + C - k, C)
        i = net.n
        net.n += 1
        out = net.like(i, dkv16.at[:, to], dk_in.at[c], net.at_col(to))
        out.start()
        dk_copies.append((out, net.like(i, dkv16.at[:, to], dk_in.at[frm], net.at_col(to)), frm))
    sum_o = BlockSum(net, s_o, s_o, x_o, y_o, o_oa, o_ob)
    sum_o.start()
    for cp in loads[7:]:
        cp.wait()
    sum_u.add()
    slots = dkv16[:, c].astype(F32)
    for _, inc, frm in dk_copies:
        inc.wait_recv()
        slots = slots + dk_in[frm].astype(F32)
    slots = slots.reshape(n_tok, 2 * HEAD)
    joint[:, :qw] = turn(dq[...], cos2[...], -sin2[...]).astype(BF)
    joint[:, qw : qw + HEAD] = turn(slots[:, :HEAD], cos2[...], -sin2[...]).astype(BF)
    joint[:, qw + HEAD :] = slots[:, HEAD:].astype(BF)
    part[...] = dot(joint[...], wjs[...], 1, 1).astype(BF).reshape(R, sub, width)
    rs = LineSum(net, part, rbu, rbd)
    rs.step(0)
    total = dot(nall[...].reshape(n_tok, width), joint[...], 0, 0)
    wjo[...] = total.astype(BF).reshape(wjo.shape)
    joint_x = [net.copy(wjo.at[pl.ds(4 * b, 4)], wjx.at[i], net.sibling) for i, b in enumerate(sib_blocks)]
    for cp in joint_x:
        cp.start()
    bias = jnp.sum(joint[...].astype(F32), axis=0, keepdims=True)
    for i, b in enumerate((c, net.across_c)):
        joint_x[i].wait_recv()
        s_j[4 * i : 4 * i + 4] = (
            wjo[pl.ds(4 * b, 4)].astype(F32) + wjx[i].astype(F32)
        ).astype(BF)
    sum_j = BlockSum(net, s_j, s_j, x_j, y_j, ja, jb)
    sum_j.start()
    sum_o.add()
    rs.step(1)
    sum_j.add()
    rs.step(2)
    sum_j.finish()
    own_cols = pl.ds(pl.multiple_of(qw + slot * HEAD, HEAD), HEAD)
    mate_cols = pl.ds(pl.multiple_of(qw + (1 - slot) * HEAD, HEAD), HEAD)
    o_j[:, :, :qw] = ja[:, :, :qw].astype(F32) + jb[:, :, :qw].astype(F32)
    v_mate = ja[:, :, mate_cols].astype(F32) + jb[:, :, mate_cols].astype(F32)
    jgot[0] = v_mate
    slot_x = net.copy(jgot.at[0], jgot.at[1], net.at_row(partner_r))
    slot_x.start()
    rs.step(3)
    lay[1] = jnp.zeros_like(lay[1])
    rs.total_into(lay.at[1])
    grad = lay[1]
    x = x_in[...].astype(F32)
    inv = lax.rsqrt(jnp.mean(x * x, axis=-1, keepdims=True) + epsilon)
    normal = x * inv
    e = grad * gains[0:1, :width]
    back = inv * (e - normal * jnp.mean(e * normal, axis=-1, keepdims=True))
    settle(layer_x)
    jk[...] = (gmid[...] + back).astype(BF)
    input_x = to_columns(jk, o_input)
    gain_attn = jnp.sum(grad * normal, axis=0, keepdims=True)
    for k in range(C):
        cut = slice(k * block, (k + 1) * block)
        v1[k, :, :block] = jnp.broadcast_to(gain_attn[:, cut], (8, block))
        v1[k, :, block : 2 * block] = gain_mlp[:, cut]
        v1[k, :, 2 * block :] = jnp.broadcast_to(bias, (8, bias.shape[1]))
    v_copies = []
    for k in range(1, C):
        to, frm = lax.rem(c + k, C), lax.rem(c + C - k, C)
        i = net.n
        net.n += 1
        out = net.like(i, v1.at[to], v1in.at[c], net.at_col(to))
        out.start()
        v_copies.append((out, net.like(i, v1.at[to], v1in.at[frm], net.at_col(to)), frm))
    total = v1[c]
    for _, inc, frm in v_copies:
        inc.wait_recv()
        total = total + v1in[frm]
    v2[...] = total
    far = []
    for same in (1, 0):
        for k in range(R):
            if same and k == 0:
                continue
            to, frm = lax.rem(r + k, R), lax.rem(r + R - k, R)
            i = net.n
            net.n += 1
            dst_d = net.d if same else net.mate[0]
            hs = net.h if same else net.other_h
            out = net.like(i, v2, v2in.at[net.h, r], (dst_d, to, c))
            out.start()
            far.append((out, net.like(i, v2, v2in.at[hs, frm], (dst_d, to, c))))
    v2in[net.h, r] = total
    slot_x.wait_recv()
    o_j[:, :, qw:] = ja[:, :, own_cols].astype(F32) + jb[:, :, own_cols].astype(F32) + jgot[1]
    for g in (sum_d, sum_g, sum_u, sum_o):
        g.finish()
    for _, inc in far:
        inc.wait_recv()
    gain_sum = v2in[0, 0, :, : 2 * block]
    for hh in (0, 1):
        for k in range(R):
            if hh or k:
                gain_sum = gain_sum + v2in[hh, k, :, : 2 * block]
    o_vec[:, : 2 * block] = gain_sum
    o_vec[:, 2 * block : 2 * block + qw] = (
        v2in[0, r, :, 2 * block : 2 * block + qw] + v2in[1, r, :, 2 * block : 2 * block + qw]
    )
    cols = pl.ds(pl.multiple_of(2 * block + qw + slot * HEAD, HEAD), HEAD)
    o_vec[:, 2 * block + qw :] = (
        v2in[0, r, :, cols] + v2in[1, r, :, cols]
        + v2in[0, partner_r, :, cols] + v2in[1, partner_r, :, cols]
    )
    settle(input_x)
    for g in (g_m, rs_d, rs):
        g.finish()
    for cp in out_x + joint_x + [slot_x]:
        cp.wait_send()
    for cps in dk_copies + v_copies + far:
        cps[0].wait_send()


def backward(sizes, gmid, x_in, mid, gains, gain_mlp, cos2, sin2, qrow, normed, q, kv, att, wj, wo,
             down, sd, sg, su):
    dp, R, C = sizes
    sub, width = gmid.shape
    block = width // C
    n, qw = q.shape
    jw = wj.shape[1]
    ff = sg.shape[2]
    sd = sd.reshape(8, ff // 4, block)
    shape = jax.ShapeDtypeStruct
    d2, g2 = (2, ff // 4, block), (2, block // 4, ff)
    w2, j2 = (2, qw // 4, block), (2, block // 4, jw)
    vec = 2 * block + jw
    outs = [
        (shape((C * sub, block), BF), VMEM), (shape((C * sub, block), BF), VMEM),
        (shape((8, vec - HEAD), F32), VMEM), (shape((2, block // 4, jw - HEAD), F32), VMEM),
        (shape(d2, BF), ANY), (shape(d2, BF), ANY), (shape(g2, BF), ANY), (shape(g2, BF), ANY),
        (shape(g2, BF), ANY), (shape(g2, BF), ANY), (shape(w2, BF), ANY), (shape(w2, BF), ANY),
    ]
    v = pltpu.VMEM
    four = lambda s: (4 * s[0],) + s[1:]
    line = v((R, sub, width), BF)
    return pl.pallas_call(
        functools.partial(backward_kernel, sizes),
        out_shape=[o for o, _ in outs],
        in_specs=[VMEM] * 8 + [ANY] * 10,
        out_specs=[s for _, s in outs],
        scratch_shapes=[
            line, line, v((n, qw), BF), v(kv.shape, BF), v((n, qw), BF), v((width, jw), BF),
            v((qw, width), BF), line, line, line, line, line, line, v((n, qw), BF), v((n, qw), F32),
            v((n * C, 2 * HEAD), F32), v(kv.shape, BF), v((C, R, sub, 2 * HEAD), BF),
            v((n, jw), BF), v((2, sub, width), F32),
            v(four(d2), BF), v(four(g2), BF), v(four(g2), BF), v(d2, BF), v(g2, BF), v(g2, BF),
            v(d2, BF), v(g2, BF), v(g2, BF),
            v((16,) + j2[1:], BF), v((2, 4) + j2[1:], BF), v(four(j2), BF), v(j2, BF), v(j2, BF),
            v((16,) + w2[1:], BF), v((2, 4) + w2[1:], BF), v(four(w2), BF), v(w2, BF), v(w2, BF),
            v(j2, BF), v(j2, BF), v((sub, width), BF), v((2,) + j2[:2] + (HEAD,), F32),
            v((C, 8, vec), F32), v((C, 8, vec), F32), v((8, vec), F32), v((2, R, 8, vec), F32),
            pltpu.SemaphoreType.DMA((88,)), pltpu.SemaphoreType.DMA((88,)),
            pltpu.SemaphoreType.DMA((24,)),
        ],
        compiler_params=pltpu.CompilerParams(
            collective_id=3, has_side_effects=True, vmem_limit_bytes=VMEM_LIMIT
        ),
        name="backward",
    )(gmid, x_in, mid, gains, gain_mlp, cos2, sin2, qrow, normed, q, kv, att, wj, wo, down, sd, sg, su)


def rotation(positions):
    half = HEAD // 2
    rates = rope_base ** (-jnp.arange(half, dtype=F32) * (2.0 / HEAD))
    angles = positions.astype(F32)[:, None] * rates[None, :]
    return jnp.cos(angles), jnp.sin(angles)


def on_device(
    tokens_in, seq_lengths, attention_gain, query_weight, query_bias, keyvalue_weight,
    keyvalue_bias, output_weight, feedforward_gain, gate_weight, up_weight, down_weight,
    cotangent,
):
    sizes = dp, rows, cols = tuple(lax.axis_size(a) for a in ("dp", "row", "col"))
    d, col = lax.axis_index("dp"), lax.axis_index("col")
    group = tokens_in.shape[0] * rows
    sub = tokens_in.shape[0] // cols
    block = tokens_in.shape[1]
    wq_width = query_weight.shape[1]
    r_i = jnp.arange(rows, dtype=jnp.int32)[:, None]
    i_i = jnp.arange(sub, dtype=jnp.int32)[None, :]
    my_places = (r_i * tokens_in.shape[0] + col * sub + i_i).reshape(-1)
    ends = jnp.cumsum(seq_lengths[0])[None, :-1]
    my_first = jnp.max(jnp.where(my_places[:, None] >= ends, ends, 0), axis=1)
    cosine, sine = rotation(my_places - my_first)
    cos2 = jnp.concatenate([cosine, cosine], axis=1)
    sin2 = jnp.concatenate([-sine, sine], axis=1)
    qpos = jnp.stack([my_first, my_places], axis=1)
    qrow = jnp.stack([my_first, my_places] * 4, axis=0)
    wide = lambda v: jnp.broadcast_to(v.astype(F32)[None], (8, v.shape[0]))
    small = wide(jnp.concatenate([attention_gain, feedforward_gain]))
    (x_own, middle, nmlp, gains, normed, queries, kv, attended, cot_all, w_joint, w_out,
     w_gate, w_up) = attention_forward(
        sizes, tokens_in, cotangent, query_weight, keyvalue_weight, output_weight, gate_weight.T,
        up_weight.T, small, wide(query_bias), wide(keyvalue_bias), cos2, sin2, qpos,
    )
    grad_middle, gain_mlp, down_part, sum_down, sum_gate, sum_up = feedforward(
        sizes, nmlp, middle, gains, cot_all, w_gate, w_up, down_weight
    )
    layer_out, input_grad, vec, joint, da, db, ga, gb, ua, ub, oa, ob = backward(
        sizes, grad_middle, x_own, middle, gains, gain_mlp, cos2, sin2, qrow, normed, queries, kv,
        attended, w_joint, w_out, down_part, sum_down, sum_gate, sum_up,
    )
    h = d // (dp // 2)

    def rest_of_dp(v):
        v = v.reshape(-1, v.shape[-1])
        if dp == 2:
            return v
        full = jnp.concatenate([jnp.where(h == 0, v, 0.0), jnp.where(h == 1, v, 0.0)], axis=0)
        return lax.psum_scatter(full, "dp", scatter_dimension=0, tiled=True)

    vec = vec[0]
    if dp > 2:
        vec = lax.psum(jnp.where(h == 0, vec, 0.0), "dp")

    def own_share(v):
        n = v.shape[0] // dp
        return lax.dynamic_slice_in_dim(v, d * n, n)

    both = lambda a, b: rest_of_dp(a.astype(F32) + b.astype(F32))
    joint = rest_of_dp(joint)
    bias = vec[2 * block :]
    return (
        layer_out, input_grad, vec[:block], joint[:, :wq_width], own_share(bias[:wq_width]),
        joint[:, wq_width:], own_share(bias[wq_width:]), both(oa, ob), vec[block : 2 * block],
        both(ga, gb), both(ua, ub), both(da, db),
    )


def solution(mesh):
    return jax.shard_map(
        on_device,
        mesh=mesh,
        in_specs=(
            P(("dp", "row"), "col"), P("dp", None), P("col"), P("col", "row"), P("row"),
            P("col", "row"), P("row"), P("row", "col"), P("col"), P("col", "row"),
            P("col", "row"), P("row", "col"), P(("dp", "row"), "col"),
        ),
        out_specs=(
            P(("dp", "row"), "col"), P(("dp", "row"), "col"), P("col"),
            P(("col", "dp"), "row"), P(("row", "dp")), P(("col", "dp"), "row"),
            P(("row", "dp")), P(("row", "dp"), "col"), P("col"), P(("col", "dp"), "row"),
            P(("col", "dp"), "row"), P(("row", "dp"), "col"),
        ),
        check_vma=False,
    )
```

```python
import functools

import jax
import jax.numpy as jnp
from jax import lax
from jax.experimental import pallas as pl
from jax.experimental.pallas import tpu as pltpu
from jax.sharding import PartitionSpec as P

HEAD = 128
epsilon = 1e-06
rope_base = 1000000.0
masked_score = -1e30
BF = jnp.bfloat16
F32 = jnp.float32
MESH = pl.DeviceIdType.MESH
ANY = pl.BlockSpec(memory_space=pl.ANY)
VMEM = pl.BlockSpec(memory_space=pltpu.VMEM)
SMEM = pl.BlockSpec(memory_space=pltpu.SMEM)
VMEM_LIMIT = 61 * 2**20


def dot(a, b, ca=1, cb=0):
    return lax.dot_general(a, b, (((ca,), (cb,)), ((), ())), preferred_element_type=F32)


class Net:
    def __init__(self, sizes, send, recv, local):
        self.dp, self.R, self.C = sizes
        self.d = lax.axis_index("dp")
        self.r = lax.axis_index("row")
        self.c = lax.axis_index("col")
        half = self.dp // 2
        self.h = self.d // half
        self.send, self.recv, self.local = send, recv, local
        self.n = 0
        self.n_local = 0
        self.other_h = 1 - self.h
        self.mate = (lax.rem(self.d + half, self.dp), self.r, self.c)
        self.sibling = self.at_col(self.c + 1 - 2 * lax.rem(self.c, 2))
        self.across_c = lax.rem(self.c + 2, 4)
        self.across = self.at_col(self.across_c)

    def at_col(self, c):
        return (self.d, self.r, c)

    def at_row(self, r):
        return (self.d, r, self.c)

    def copy(self, src, dst, dev):
        i = self.n
        self.n += 1
        return pltpu.make_async_remote_copy(
            src_ref=src, dst_ref=dst, send_sem=self.send.at[i], recv_sem=self.recv.at[i],
            device_id=dev, device_id_type=MESH,
        )

    def like(self, copy_index, src, dst, dev):
        return pltpu.make_async_remote_copy(
            src_ref=src, dst_ref=dst, send_sem=self.send.at[copy_index],
            recv_sem=self.recv.at[copy_index], device_id=dev, device_id_type=MESH,
        )

    def here(self, src, dst):
        i = self.n_local
        self.n_local += 1
        return pltpu.make_async_copy(src, dst, self.local.at[i])

    def barrier(self):
        sem = pltpu.get_barrier_semaphore()
        for k in range(1, self.C):
            pl.semaphore_signal(
                sem, inc=1, device_id=self.at_col(lax.rem(self.c + k, self.C)), device_id_type=MESH
            )
        pl.semaphore_signal(sem, inc=1, device_id=self.mate, device_id_type=MESH)

        @pl.when(self.r > 0)
        def _():
            pl.semaphore_signal(sem, inc=1, device_id=self.at_row(self.r - 1), device_id_type=MESH)

        @pl.when(self.r < self.R - 1)
        def _():
            pl.semaphore_signal(sem, inc=1, device_id=self.at_row(self.r + 1), device_id_type=MESH)

        count = self.C + (self.r > 0).astype(jnp.int32) + (self.r < self.R - 1).astype(jnp.int32)
        pl.semaphore_wait(sem, count)


class LineGather:
    def __init__(self, net, buf):
        self.net, self.buf = net, buf
        r, R = net.r, net.R
        self.up_i, self.dn_i = [], []
        for s in range(R - 1):
            self.up_i.append(net.n)
            self.dn_i.append(net.n + 1)
            net.n += 2

    def _up(self, s, shard):
        net = self.net
        b = self.buf.at[jnp.clip(shard, 0, net.R - 1)]
        return net.like(self.up_i[s], b, b, net.at_row(jnp.minimum(net.r + 1, net.R - 1)))

    def _dn(self, s, shard):
        net = self.net
        b = self.buf.at[jnp.clip(shard, 0, net.R - 1)]
        return net.like(self.dn_i[s], b, b, net.at_row(jnp.maximum(net.r - 1, 0)))

    def step(self, s):
        net = self.net
        r, R = net.r, net.R
        if s > 0:

            @pl.when(r - s >= 0)
            def _():
                self._up(s - 1, r - s).wait_recv()

        if s < R - 1:

            @pl.when((r - s >= 0) & (r < R - 1))
            def _():
                self._up(s, r - s).start()

        if s > 0:

            @pl.when(r + s < R)
            def _():
                self._dn(s - 1, r + s).wait_recv()

        if s < R - 1:

            @pl.when((r + s < R) & (r > 0))
            def _():
                self._dn(s, r + s).start()

    def finish(self):
        net = self.net
        r, R = net.r, net.R
        for s in range(R - 1):

            @pl.when((r - s >= 0) & (r < R - 1))
            def _():
                self._up(s, r - s).wait_send()

            @pl.when((r + s < R) & (r > 0))
            def _():
                self._dn(s, r + s).wait_send()


class LineSum:
    def __init__(self, net, part, from_below, from_above):
        self.net, self.part, self.bu, self.bd = net, part, from_below, from_above
        self.base = net.n
        net.n += 2 * net.R

    def _dn(self, j):
        net = self.net
        j = jnp.clip(j, 0, net.R - 1)
        return net.like(
            self.base + j, self.part.at[j], self.bd.at[j], net.at_row(jnp.maximum(net.r - 1, 0))
        )

    def _up(self, j):
        net = self.net
        j = jnp.clip(j, 0, net.R - 1)
        return net.like(
            self.base + net.R + j, self.part.at[j], self.bu.at[j],
            net.at_row(jnp.minimum(net.r + 1, net.R - 1)),
        )

    def _add(self, j, buf):
        self.part[j] = (self.part[j].astype(F32) + buf[j].astype(F32)).astype(BF)

    def step(self, t):
        net = self.net
        r, R = net.r, net.R
        j = t - (R - 1 - r)
        k = R - 1 - (t - r)

        @pl.when((j >= 0) & (r < R - 1))
        def _():
            self._dn(j).wait_recv()

        @pl.when((j >= 0) & (j < r))
        def _():
            @pl.when(r < R - 1)
            def _():
                self._add(j, self.bd)

            self._dn(j).start()

        @pl.when((k <= R - 1) & (r > 0))
        def _():
            self._up(k).wait_recv()

        @pl.when((k <= R - 1) & (k > r))
        def _():
            @pl.when(r > 0)
            def _():
                self._add(k, self.bu)

            self._up(k).start()

    def finish(self):
        net = self.net
        r, R = net.r, net.R
        for j in range(R):

            @pl.when(j < r)
            def _():
                self._dn(j).wait_send()

            @pl.when(j > r)
            def _():
                self._up(j).wait_send()

    def total_into(self, out):
        net = self.net
        r, R = net.r, net.R
        out[...] += self.part[r].astype(F32)

        @pl.when(r < R - 1)
        def _():
            out[...] += self.bd[r].astype(F32)

        @pl.when(r > 0)
        def _():
            out[...] += self.bu[r].astype(F32)


class WeightGather:
    def __init__(self, net, src, full, by_rows, piece=0, pieces=1, keep=True):
        self.net, self.full, self.by_rows = net, full, by_rows
        if by_rows:
            self.n, self.w = full.shape[0] // net.C, full.shape[1]
        else:
            self.n, self.w = full.shape[0] // pieces, full.shape[1] // net.C
        self.first = piece * self.n
        if src is not None:
            src = src.at[pl.ds(self.first, self.n)]
        c, p, h, o = net.c, net.across_c, net.h, net.other_h
        half = self.n // 2
        self.here = None
        if src is not None:
            if keep:
                self.here = net.here(src, self.view(c, 0, 2))
            own_half = src.at[pl.ds(pl.multiple_of(h * half, 16), half)]
            own = src
        else:
            own_half, own = self.view(c, h, 1), self.view(c, 0, 2)
        self.x = net.copy(own_half, self.view(c, h, 1), net.across)
        self.sib = net.copy(own, self.view(c, 0, 2), net.sibling)
        self.y = net.copy(self.view(p, h, 1), self.view(p, h, 1), net.mate)
        self.sib_h = net.copy(self.view(p, h, 1), self.view(p, h, 1), net.sibling)
        self.sib_o = net.copy(self.view(p, o, 1), self.view(p, o, 1), net.sibling)

    def view(self, b, h, halves):
        half = self.n // 2
        if self.by_rows:
            return self.full.at[pl.ds(pl.multiple_of(b * self.n + h * half, 16), halves * half)]
        return self.full.at[
            pl.ds(pl.multiple_of(self.first + h * half, 16), halves * half),
            pl.ds(pl.multiple_of(b * self.w, 128), self.w),
        ]

    def start(self):
        if self.here is not None:
            self.here.start()
        self.x.start()
        self.sib.start()

    def pass_x(self):
        self.x.wait_recv()
        self.y.start()
        self.sib_h.start()

    def pass_y(self):
        self.y.wait_recv()
        self.sib_o.start()

    def arrive(self):
        if self.here is not None:
            self.here.wait()
        self.sib.wait_recv()
        self.sib_h.wait_recv()
        self.sib_o.wait_recv()

    def finish(self):
        for cp in (self.x, self.sib, self.y, self.sib_h, self.sib_o):
            cp.wait_send()


class BlockSum:
    def __init__(self, net, source, piece, from_x, from_mate):
        self.net, self.piece = net, piece
        self.from_x, self.from_mate = from_x, from_mate
        o = net.other_h
        self.first = [net.copy(source(1, k, 0), from_x.at[k], net.across) for k in (0, 1)]
        self.first += [net.copy(source(i, o, 1), from_mate.at[i], net.mate) for i in (0, 1)]
        self.second = []

    def start(self):
        for cp in self.first:
            cp.start()

    def add(self):
        h = self.net.h
        for cp in self.first:
            cp.wait_recv()
        for ref, got in (
            (self.piece(0, 0, 0), self.from_x.at[0]), (self.piece(0, 1, 0), self.from_x.at[1]),
            (self.piece(0, h, 1), self.from_mate.at[0]), (self.piece(1, h, 1), self.from_mate.at[1]),
        ):
            ref[...] = (ref[...].astype(F32) + got[...].astype(F32)).astype(BF)

    def pass_on(self, got, to_mate=None, to_across=None):
        net = self.net
        to_mate = self.piece(0, net.other_h, 0) if to_mate is None else to_mate
        to_across = self.piece(1, net.h, 1) if to_across is None else to_across
        self.second = [
            net.copy(to_mate, got.at[0], net.mate), net.copy(to_across, got.at[1], net.across)
        ]
        for cp in self.second:
            cp.start()

    def finish(self):
        for cp in self.first:
            cp.wait_send()
        for cp in self.second:
            cp.wait_send()
            cp.wait_recv()


def leading(ref):
    return lambda i, h, ab: ref.at[4 * i + 2 * h + ab]


def turn(values, cos2, sin2):
    heads = []
    for i in range(values.shape[1] // HEAD):
        v = values[:, i * HEAD : (i + 1) * HEAD]
        heads.append(v * cos2 + pltpu.roll(v, HEAD // 2, 1) * sin2)
    return jnp.concatenate(heads, axis=1) if len(heads) > 1 else heads[0]


def attention_kernel(
    sizes,
    tok, cot, wq, wkv, wo, wg, wu, gain_a, gain_f, qb, kvb, lengths, cos2, sin2,
    o_x, o_mid, o_nmlp, o_gains, o_normed, o_q, o_kv, o_att, o_cot, o_wj, o_wo, o_wg, o_wu,
    xin, cin, small, gains, kvb2, nall, call, wj, wov, kv, qs, att, part, rbu, rbd, send, recv, local,
):
    net = Net(sizes, send, recv, local)
    R, C, r, c = net.R, net.C, net.r, net.c
    sub, width = nall.shape[1], nall.shape[2]
    block = tok.shape[1]
    row_tok = sub * C
    n_tok = sub * R
    qw = wq.shape[1]
    slot = lax.rem(r, 2)
    partner = net.at_row(r + 1 - 2 * slot)
    net.barrier()
    wide = lambda ref: jnp.broadcast_to(ref[...].astype(F32), (8, ref.shape[1]))
    small[:, :block] = wide(gain_a)
    small[:, block:] = wide(gain_f)
    kvb2[slot] = wide(kvb)

    def spread(src, dst):
        mine = pl.multiple_of(c * sub, sub)
        local_copy = net.here(src.at[pl.ds(mine, sub)], dst.at[c])
        copies = []
        for k in range(1, C):
            to = lax.rem(c + k, C)
            frm = lax.rem(c + C - k, C)
            i = net.n
            net.n += 1
            rows = pl.ds(pl.multiple_of(to * sub, sub), sub)
            copies.append(
                (net.like(i, src.at[rows], dst.at[c], net.at_col(to)),
                 net.like(i, src.at[rows], dst.at[frm], net.at_col(to)))
            )
        return local_copy, copies

    def begin(pair):
        pair[0].start()
        for out, _ in pair[1]:
            out.start()

    def arrived(pair):
        pair[0].wait()
        for _, inc in pair[1]:
            inc.wait_recv()

    tok_in, cot_in = spread(tok, xin), spread(cot, cin)
    begin(tok_in)
    gain_own = net.here(small, gains.at[c])
    gain_own.start()
    gain_copies = []
    for k in range(1, C):
        to, frm = lax.rem(c + k, C), lax.rem(c + C - k, C)
        i = net.n
        net.n += 1
        out = net.like(i, small, gains.at[c], net.at_col(to))
        gain_copies.append((out, net.like(i, small, gains.at[frm], net.at_col(to))))
        out.start()
    own_rows = pl.ds(pl.multiple_of(c * block, block), block)
    col_own = pl.ds(pl.multiple_of(qw + slot * HEAD, HEAD), HEAD)
    col_mate = pl.ds(pl.multiple_of(qw + (1 - slot) * HEAD, HEAD), HEAD)
    kv_x = net.copy(wkv, wj.at[own_rows, col_own], partner)
    kv_in = net.like(net.n - 1, wkv, wj.at[own_rows, col_mate], partner)
    kv_x.start()
    kvb_x = net.copy(kvb2.at[slot], kvb2.at[slot], partner)
    kvb_in = net.like(net.n - 1, kvb2.at[slot], kvb2.at[1 - slot], partner)
    kvb_x.start()
    wq_own = net.here(wq, wj.at[own_rows, pl.ds(0, qw)])
    wq_own.start()
    wkv_own = net.here(wkv, wj.at[own_rows, col_own])
    wkv_own.start()
    g_joint = WeightGather(net, None, wj, True)
    g_out = WeightGather(net, wo, wov, False)
    bulk = [WeightGather(net, w, o, False, i, 2, False) for w, o in ((wg, o_wg), (wu, o_wu)) for i in (0, 1)]

    arrived(tok_in)
    gain_own.wait()
    for _, inc in gain_copies:
        inc.wait_recv()
    for k in range(C):
        o_gains[:, k * block : (k + 1) * block] = gains[k, :, :block]
        o_gains[:, width + k * block : width + (k + 1) * block] = gains[k, :, block:]
    x = jnp.concatenate([xin[k].astype(F32) for k in range(C)], axis=1)
    o_mid[...] = x
    o_x[...] = x.astype(BF)
    inv = lax.rsqrt(jnp.mean(x * x, axis=-1, keepdims=True) + epsilon)
    nall[r] = (x * inv * o_gains[0:1, :width]).astype(BF)
    g_n = LineGather(net, nall)
    g_n.step(0)
    wq_own.wait()
    wkv_own.wait()
    kv_in.wait_recv()
    g_joint.start()
    g_out.start()
    begin(cot_in)
    g_joint.pass_x()
    g_out.pass_x()
    bulk[0].start()
    g_joint.pass_y()
    g_n.step(1)
    g_out.pass_y()
    bulk[1].start()
    arrived(cot_in)
    for k in range(C):
        call[r, :, k * block : (k + 1) * block] = cin[k]
    g_n.step(2)
    bulk[0].pass_x()
    g_joint.arrive()
    kvb_in.wait_recv()
    g_n.step(3)
    g_cot = LineGather(net, call)
    g_cot.step(0)
    bias = jnp.concatenate([qb[...].astype(F32), kvb2[0, 0:1, :], kvb2[1, 0:1, :]], axis=1)
    joint = dot(nall[...].reshape(n_tok, width), wj[...]) + bias
    key = turn(joint[:, qw : qw + HEAD], cos2[...], sin2[...]).astype(BF)
    kv[:, c, :, :HEAD] = key.reshape(R, sub, HEAD)
    kv[:, c, :, HEAD:] = joint[:, qw + HEAD :].astype(BF).reshape(R, sub, HEAD)
    sib_c = c + 1 - 2 * lax.rem(c, 2)
    far_c = net.across_c
    far_sib_c = far_c + 1 - 2 * lax.rem(far_c, 2)
    kv_far = net.copy(kv.at[:, c], kv.at[:, c], net.across)
    kv_sib = net.copy(kv.at[:, c], kv.at[:, c], net.sibling)
    kv_pass = net.copy(kv.at[:, far_c], kv.at[:, far_c], net.sibling)
    kv_far.start()
    kv_sib.start()
    qs[...] = turn(joint[:, :qw], cos2[...], sin2[...]).astype(BF)
    out_normed = net.here(nall, o_normed)
    out_normed.start()
    out_wj = net.here(wj, o_wj)
    out_wj.start()
    kv_far.wait_recv()
    kv_pass.start()
    kv_sib.wait_recv()
    kv_pass.wait_recv()
    bulk[1].pass_x()
    bulk[2].start()
    bulk[3].start()
    bulk[0].pass_y()
    g_cot.step(1)
    out_kv = net.here(kv, o_kv)
    out_kv.start()
    scale = HEAD ** (-0.5)
    ends = [lengths[0, 0]]
    for i in range(1, lengths.shape[1] - 1):
        ends.append(ends[-1] + lengths[0, i])
    for rr in range(R):
        limit = (rr + 1) * row_tok
        keys = kv[: rr + 1, :, :, :HEAD].reshape(limit, HEAD)
        values = kv[: rr + 1, :, :, HEAD:].reshape(limit, HEAD)
        mine = slice(rr * sub, (rr + 1) * sub)
        place = lax.broadcasted_iota(jnp.int32, (sub, limit), 1)
        here = rr * row_tok + c * sub + lax.broadcasted_iota(jnp.int32, (sub, 1), 0)
        first = jnp.zeros((sub, 1), jnp.int32)
        for end in ends:
            first = jnp.where(here >= end, end, first)
        allowed = (place >= first) & (place <= here)
        for h in range(qw // HEAD):
            cols = slice(h * HEAD, (h + 1) * HEAD)
            s = jnp.where(allowed, dot(qs[mine, cols], keys, 1, 1) * scale, masked_score)
            e = jnp.exp(s - jnp.max(s, axis=-1, keepdims=True))
            p = e * (1.0 / jnp.sum(e, axis=-1, keepdims=True))
            att[mine, cols] = dot(p.astype(BF), values).astype(BF)
    g_out.arrive()
    part[...] = dot(att[...], wov[...]).astype(BF).reshape(R, sub, width)
    rs = LineSum(net, part, rbu, rbd)
    rs.step(0)
    out_q = net.here(qs, o_q)
    out_q.start()
    out_att = net.here(att, o_att)
    out_att.start()
    out_wo = net.here(wov, o_wo)
    out_wo.start()
    g_cot.step(2)
    bulk[1].pass_y()
    bulk[2].pass_x()
    rs.step(1)
    g_cot.step(3)
    out_cot = net.here(call, o_cot)
    out_cot.start()
    bulk[3].pass_x()
    rs.step(2)
    bulk[2].pass_y()
    rs.step(3)
    rs.total_into(o_mid)
    mid = o_mid[...]
    inv = lax.rsqrt(jnp.mean(mid * mid, axis=-1, keepdims=True) + epsilon)
    o_nmlp[...] = (mid * inv * o_gains[0:1, width:]).astype(BF)
    bulk[3].pass_y()
    for g in bulk:
        g.arrive()
    for g in [g_joint, g_out, g_n, g_cot, rs] + bulk:
        g.finish()
    for out, _ in tok_in[1] + cot_in[1] + gain_copies:
        out.wait_send()
    for cp in (kv_far, kv_sib, kv_pass):
        cp.wait_send()
    kv_x.wait_send()
    kvb_x.wait_send()
    for cp in (out_normed, out_wj, out_kv, out_q, out_att, out_wo, out_cot):
        cp.wait()


def attention_forward(
    sizes, tok, cot, wq, wkv, wo, wg, wu, gain_a, gain_f, qb, kvb, lengths, cos2, sin2
):
    dp, R, C = sizes
    sub = tok.shape[0] // C
    block = tok.shape[1]
    width = block * C
    qw, jw = wq.shape[1], wq.shape[1] + 2 * HEAD
    n = sub * R
    ff = wg.shape[0]
    shape = jax.ShapeDtypeStruct
    outs = [
        (shape((sub, width), BF), VMEM),
        (shape((sub, width), F32), VMEM), (shape((sub, width), BF), VMEM),
        (shape((8, 2 * width), F32), VMEM), (shape((R, sub, width), BF), ANY),
        (shape((n, qw), BF), ANY), (shape((R, C, sub, 2 * HEAD), BF), ANY),
        (shape((n, qw), BF), ANY), (shape((R, sub, width), BF), ANY),
        (shape((width, jw), BF), ANY), (shape((qw, width), BF), ANY),
        (shape((ff, width), BF), ANY), (shape((ff, width), BF), ANY),
    ]
    return pl.pallas_call(
        functools.partial(attention_kernel, sizes),
        out_shape=[o for o, _ in outs],
        in_specs=[ANY] * 7 + [VMEM] * 4 + [SMEM] + [VMEM] * 2,
        out_specs=[s for _, s in outs],
        scratch_shapes=[
            pltpu.VMEM((C, sub, block), BF), pltpu.VMEM((C, sub, block), BF),
            pltpu.VMEM((8, 2 * block), F32), pltpu.VMEM((C, 8, 2 * block), F32), pltpu.VMEM((2, 8, HEAD), F32),
            pltpu.VMEM((R, sub, width), BF), pltpu.VMEM((R, sub, width), BF),
            pltpu.VMEM((width, jw), BF), pltpu.VMEM((qw, width), BF),
            pltpu.VMEM((R, C, sub, 2 * HEAD), BF), pltpu.VMEM((n, qw), BF),
            pltpu.VMEM((n, qw), BF), pltpu.VMEM((R, sub, width), BF),
            pltpu.VMEM((R, sub, width), BF), pltpu.VMEM((R, sub, width), BF),
            pltpu.SemaphoreType.DMA((64,)), pltpu.SemaphoreType.DMA((64,)),
            pltpu.SemaphoreType.DMA((24,)),
        ],
        compiler_params=pltpu.CompilerParams(
            collective_id=1, has_side_effects=True, vmem_limit_bytes=VMEM_LIMIT
        ),
        name="attention_forward",
    )(tok, cot, wq, wkv, wo, wg, wu, gain_a, gain_f, qb, kvb, lengths, cos2, sin2)


def feedforward_kernel(
    sizes,
    nmlp, mid, gains, cot, wg, wu, wd, own_g, own_u,
    o_gmid, o_gain, o_down, o_sd, o_sg, o_su,
    w_gate, w_up, w_down, xall, call, acc, hid, gg, gu, hid_r, gg_r, gu_r,
    s_hid, s_gg, s_gu, s_hid_r, s_gg_r, s_gu_r, sx, sc, xt, part, rbu, rbd, g, x_d, y_d,
    send, recv, local,
):
    net = Net(sizes, send, recv, local)
    R, C, r, c = net.R, net.C, net.r, net.c
    sub, width = nmlp.shape
    block = width // C
    n_tok = sub * R
    tiles, _, tile = hid.shape
    rest = hid_r.shape[1]
    wide = width // tile
    own_cols = [pl.ds(pl.multiple_of(b * block, HEAD), block) for b in (c, net.across_c)]
    sib_cols = [
        pl.ds(pl.multiple_of((b + 1 - 2 * lax.rem(b, 2)) * block, HEAD), block)
        for b in (c, net.across_c)
    ]
    parts = [(pl.ds(t * tile, tile), t) for t in range(tiles)] + [(pl.ds(tiles * tile, rest), None)]

    def at(whole, remainder, t):
        return remainder if t is None else whole.at[t]

    pieces = 5
    g_down = [WeightGather(net, wd, w_down, False, i, pieces) for i in range(pieces)]
    in_cot = net.here(cot, call)
    in_cot.start()
    in_w = []
    for full, own, w in ((wg, own_g, w_gate), (wu, own_u, w_up)):
        for k in range(C):
            cols = pl.ds(pl.multiple_of(lax.rem(c + k, C) * block, HEAD), block)
            cp = net.here(full.at[:, cols] if k else own, w.at[:, cols])
            cp.start()
            in_w.append(cp)
    net.barrier()
    xall[r] = nmlp[...]
    g_x = LineGather(net, xall)
    g_x.step(0)
    g_down[0].start()
    g_down[1].start()
    in_cot.wait()
    to_sibling = [net.copy(call.at[:, :, sib_cols[i]], sc.at[i], net.sibling) for i in (0, 1)]
    for cp in to_sibling:
        cp.start()
    g_down[0].pass_x()
    g_down[2].start()
    g_down[1].pass_x()
    g_down[3].start()
    g_down[0].pass_y()
    g_x.step(1)
    for cp in in_w:
        cp.wait()
    g_down[2].pass_x()
    g_down[4].start()
    g_down[1].pass_y()
    g_down[3].pass_x()
    g_down[2].pass_y()
    g_x.step(2)
    g_down[4].pass_x()
    g_down[3].pass_y()

    def hidden_back(rows):
        return dot(call[...].reshape(n_tok, width), w_down[rows, :], 1, 1)

    g_down[0].arrive()
    for t in range(wide):
        g_down[t + 1].arrive()
        acc[t] = hidden_back(pl.ds(t * tile, tile))
    g_down[4].pass_y()
    g_x.step(3)
    for i in (0, 1):
        cp = net.copy(xall.at[:, :, sib_cols[i]], sx.at[i], net.sibling)
        cp.start()
        to_sibling.append(cp)

    g_down[4].arrive()

    def act(rows, back, t):
        x = xall[...].reshape(n_tok, width)
        gate = dot(x, w_gate[rows, :], 1, 1)
        up = dot(x, w_up[rows, :], 1, 1)
        s = jax.nn.sigmoid(gate)
        silu = gate * s
        at(hid, hid_r, t)[...] = (silu * up).astype(BF)
        at(gg, gg_r, t)[...] = (back * up * s * (1.0 + gate * (1.0 - s))).astype(BF)
        at(gu, gu_r, t)[...] = (back * silu).astype(BF)

    @pl.loop(0, wide)
    def _(t):
        act(pl.ds(pl.multiple_of(t * tile, tile), tile), acc[t], t)

    for rows, t in parts[wide:]:
        act(rows, hidden_back(rows), t)
    for mine, theirs in (
        (hid, s_hid), (gg, s_gg), (gu, s_gu), (hid_r, s_hid_r), (gg_r, s_gg_r), (gu_r, s_gu_r)
    ):
        cp = net.copy(mine, theirs, net.sibling)
        cp.start()
        to_sibling.append(cp)

    def products(n, pairs, tokens):
        cols = pl.ds(pl.multiple_of(n * tile, tile), tile)
        total = None
        for rows, t in parts:
            for whole, remainder, w in pairs:
                term = dot(at(whole, remainder, t)[tokens], w[rows, cols])
                total = term if total is None else total + term
        return cols, total

    half_rows = R // 2
    far_half = 1 - r // half_rows

    def input_back(half):
        tokens = pl.ds(pl.multiple_of(half * half_rows * sub, 16), half_rows * sub)

        @pl.loop(0, wide)
        def _(n):
            cols, total = products(n, ((gg, gg_r, w_gate), (gu, gu_r, w_up)), tokens)
            part[pl.ds(half * half_rows, half_rows), :, cols] = (
                total.astype(BF).reshape(half_rows, sub, tile)
            )

    input_back(far_half)
    rs = LineSum(net, part, rbu, rbd)
    rs.step(0)
    input_back(1 - far_half)
    for g_piece in g_down:
        g_piece.finish()
    for cp in to_sibling:
        cp.wait_recv()

    @pl.loop(0, wide)
    def _(n):
        acc[n] = products(n, ((hid, hid_r, w_down),), pl.ds(0, n_tok))[1]

    rs.step(1)
    outs = []
    sib_cot = [sc[i].reshape(n_tok, block) for i in (0, 1)]
    for rows, t in parts:
        for i in (0, 1):
            own_cot = call[:, :, own_cols[i]].reshape(n_tok, block)
            total = dot(at(hid, hid_r, t)[...], own_cot, 0, 0)
            total = total + dot(at(s_hid, s_hid_r, t)[...], sib_cot[i], 0, 0)
            w_down[rows, i * block : (i + 1) * block] = total.astype(BF)
    eighth = w_down.shape[0] // 4
    down_piece = lambda i, h, ab: w_down.at[
        pl.ds(pl.multiple_of((2 * h + ab) * eighth, 16), eighth), pl.ds(i * block, block)
    ]
    sum_d = BlockSum(net, down_piece, down_piece, x_d, y_d)
    sum_d.start()
    rs.step(2)
    for i in (0, 1):
        xt[i * block : (i + 1) * block, :n_tok] = xall[:, :, own_cols[i]].reshape(n_tok, block).T
        xt[i * block : (i + 1) * block, n_tok:] = sx[i].reshape(n_tok, block).T
    for mine, mine_r, theirs, theirs_r, o in (
        (gg, gg_r, s_gg, s_gg_r, o_sg), (gu, gu_r, s_gu, s_gu_r, o_su)
    ):
        if outs:
            outs.pop().wait()
        for rows, t in parts:
            total = dot(xt[:, :n_tok], at(mine, mine_r, t)[...])
            total = total + dot(xt[:, n_tok:], at(theirs, theirs_r, t)[...])
            g[:, :, rows] = total.astype(BF).reshape(8, g.shape[1], -1)
        cp = net.here(g, o)
        cp.start()
        outs.append(cp)
    rs.step(3)
    o_gmid[...] = jnp.zeros_like(o_gmid)
    rs.total_into(o_gmid)
    grad = o_gmid[...]
    m = mid[...]
    inv = lax.rsqrt(jnp.mean(m * m, axis=-1, keepdims=True) + epsilon)
    normal = m * inv
    e = grad * gains[0:1, width:]
    back = inv * (e - normal * jnp.mean(e * normal, axis=-1, keepdims=True))
    o_gain[...] = jnp.broadcast_to(jnp.sum(grad * normal, axis=0, keepdims=True), o_gain.shape)
    o_gmid[...] = call[r].astype(F32) + back
    rs.finish()
    for n in range(wide):
        part[:, :, n * tile : (n + 1) * tile] = acc[n].astype(BF).reshape(R, sub, tile)
    out_down = net.here(part, o_down)
    out_down.start()
    sum_d.add()
    for k, ref in enumerate(
        (down_piece(0, net.h, 0), down_piece(0, net.h, 1), down_piece(0, net.other_h, 0),
         down_piece(1, net.h, 1))
    ):
        cp = net.here(ref, o_sd.at[k])
        cp.start()
        outs.append(cp)
    sum_d.finish()
    g_x.finish()
    for cp in to_sibling:
        cp.wait_send()
    for cp in outs + [out_down]:
        cp.wait()


def feedforward(sizes, nmlp, mid, gains, cot, wg, wu, wd, own_g, own_u):
    dp, R, C = sizes
    sub, width = nmlp.shape
    block = width // C
    n = R * sub
    ff = wd.shape[0]
    tile = 512
    tiles, rest = ff // tile, ff % tile
    shape = jax.ShapeDtypeStruct
    outs = [
        (shape((sub, width), F32), VMEM), (shape((8, width), F32), VMEM),
        (shape((R, sub, width), BF), ANY), (shape((4, ff // 4, block), BF), ANY),
        (shape((8, block // 4, ff), BF), ANY), (shape((8, block // 4, ff), BF), ANY),
    ]
    acts = [pltpu.VMEM((tiles, n, tile), BF)] * 3 + [pltpu.VMEM((n, rest), BF)] * 3
    return pl.pallas_call(
        functools.partial(feedforward_kernel, sizes),
        out_shape=[o for o, _ in outs],
        in_specs=[VMEM] * 3 + [ANY] * 6,
        out_specs=[s for _, s in outs],
        scratch_shapes=[
            pltpu.VMEM((ff, width), BF), pltpu.VMEM((ff, width), BF), pltpu.VMEM((ff, width), BF),
            pltpu.VMEM((R, sub, width), BF), pltpu.VMEM((R, sub, width), BF),
            pltpu.VMEM((width // tile, n, tile), F32), *acts, *acts,
            pltpu.VMEM((2, R, sub, block), BF), pltpu.VMEM((2, R, sub, block), BF),
            pltpu.VMEM((2 * block, 2 * n), BF),
            pltpu.VMEM((R, sub, width), BF), pltpu.VMEM((R, sub, width), BF),
            pltpu.VMEM((R, sub, width), BF),
            pltpu.VMEM((8, block // 4, ff), BF),
            pltpu.VMEM((2, ff // 4, block), BF), pltpu.VMEM((2, ff // 4, block), BF),
            pltpu.SemaphoreType.DMA((64,)), pltpu.SemaphoreType.DMA((64,)),
            pltpu.SemaphoreType.DMA((32,)),
        ],
        compiler_params=pltpu.CompilerParams(
            collective_id=2, has_side_effects=True, vmem_limit_bytes=VMEM_LIMIT
        ),
        name="feedforward",
    )(nmlp, mid, gains, cot, wg, wu, wd, own_g, own_u)


def backward_kernel(
    sizes,
    gmid, x_in, mid, gains, gain_mlp, lengths, cos2, sin2,
    normed, q, kv, att, wj, wo, down, sd, sg, su,
    o_layer, o_input, o_vec, o_j, o_db, o_ga, o_gb, o_ua, o_ub, o_oa, o_ob,
    mall, nall, qs, kvs, atts, wjs, wos, dpart, drbu, drbd, part, rbu, rbd, grads, dq, dkv, dkv16, dk_sib, dk_in,
    joint, lay,
    s_g, s_u, x_g, x_u, y_g, y_u,
    wjo, wjx, s_j, x_j, y_j, woo, wox, s_o, x_o, y_o, jb, jk, jgot, v1, v1in, v2, v2in,
    send, recv, local,
):
    net = Net(sizes, send, recv, local)
    R, C, r, c = net.R, net.C, net.r, net.c
    sub, width = gmid.shape
    block = width // C
    n_tok = sub * R
    row_tok = sub * C
    qw = qs.shape[1]
    slot = lax.rem(r, 2)
    partner_r = r + 1 - 2 * slot
    loads = [
        net.here(a, b) for a, b in
        ((wo, wos), (att, atts), (q, qs), (kv, kvs), (down, dpart), (sg, s_g), (su, s_u),
         (normed, nall), (wj, wjs))
    ]
    for cp in loads:
        cp.start()
    sem = pltpu.get_barrier_semaphore()
    half = net.dp // 2
    others = [(net.d, r, lax.rem(c + k, C)) for k in range(1, C)]
    others += [(net.d, lax.rem(r + k, R), c) for k in range(1, R)]
    others += [(net.mate[0], lax.rem(r + k, R), c) for k in range(R)]
    for dev in others:
        pl.semaphore_signal(sem, inc=1, device_id=dev, device_id_type=MESH)
    pl.semaphore_wait(sem, len(others))

    mall[r] = gmid[...].astype(BF)
    g_m = LineGather(net, mall)
    g_m.step(0)
    sum_d = [net.copy(sd.at[2], o_db.at[0], net.mate), net.copy(sd.at[3], o_db.at[1], net.across)]
    for cp in sum_d:
        cp.start()
    sum_g = BlockSum(net, leading(sg), leading(s_g), x_g, y_g)
    sum_u = BlockSum(net, leading(su), leading(s_u), x_u, y_u)
    sum_g.start()
    g_m.step(1)
    for cp in loads[:6]:
        cp.wait()
    g_m.step(2)
    g_m.step(3)
    rs_d = LineSum(net, dpart, drbu, drbd)
    rs_d.step(0)
    m_all = mall[...].reshape(n_tok, width)
    grads[...] = dot(m_all, wos[...], 1, 1).astype(BF)

    def to_columns(src, dst):
        rows = pl.ds(pl.multiple_of(c * sub, sub), sub)
        mine = net.here(src.at[:, pl.ds(pl.multiple_of(c * block, HEAD), block)], dst.at[rows])
        mine.start()
        pairs = []
        for k in range(1, C):
            to, frm = lax.rem(c + k, C), lax.rem(c + C - k, C)
            i = net.n
            net.n += 1
            cut = src.at[:, pl.ds(pl.multiple_of(to * block, HEAD), block)]
            out = net.like(i, cut, dst.at[rows], net.at_col(to))
            out.start()
            from_rows = pl.ds(pl.multiple_of(frm * sub, sub), sub)
            pairs.append((out, net.like(i, cut, dst.at[from_rows], net.at_col(to))))
        return mine, pairs

    def settle(exchange):
        exchange[0].wait()
        for out, inc in exchange[1]:
            inc.wait_recv()
            out.wait_send()

    sib_blocks = [b + 1 - 2 * lax.rem(b, 2) for b in (c, net.across_c)]
    total = dot(atts[...], m_all, 0, 0)
    for b in range(C):
        woo[4 * b : 4 * b + 4] = (
            total[:, b * block : (b + 1) * block].astype(BF).reshape(4, qw // 4, block)
        )
    out_x = [net.copy(woo.at[pl.ds(4 * b, 4)], wox.at[i], net.sibling) for i, b in enumerate(sib_blocks)]
    for cp in out_x:
        cp.start()
    scale = HEAD ** (-0.5)
    heads = qw // HEAD
    ends = [lengths[0, 0]]
    for i in range(1, lengths.shape[1] - 1):
        ends.append(ends[-1] + lengths[0, i])
    for rr in reversed(range(R)):
        limit = (rr + 1) * row_tok
        keys = kvs[: rr + 1, :, :, :HEAD].reshape(limit, HEAD)
        values = kvs[: rr + 1, :, :, HEAD:].reshape(limit, HEAD)
        mine = slice(rr * sub, (rr + 1) * sub)
        stack = lambda ref: jnp.concatenate(
            [ref[mine, h * HEAD : (h + 1) * HEAD] for h in range(heads)], axis=0
        )
        qh, gh = stack(qs), stack(grads)
        place = lax.broadcasted_iota(jnp.int32, (limit, heads * sub), 0)
        lane = lax.broadcasted_iota(jnp.int32, (1, heads * sub), 1)
        here = rr * row_tok + c * sub + lax.rem(lane, sub)
        first = jnp.zeros_like(here)
        for end in ends:
            first = jnp.where(here >= end, end, first)
        s = jnp.where(
            (place >= first) & (place <= here), dot(keys, qh, 1, 1) * scale, masked_score
        )
        e = jnp.exp(s - jnp.max(s, axis=0, keepdims=True))
        p = e * (1.0 / jnp.sum(e, axis=0, keepdims=True))
        g = dot(values, gh, 1, 1)
        ds = (p * (g - jnp.sum(p * g, axis=0, keepdims=True))).astype(BF)
        dv = dot(p.astype(BF), gh)
        dk = dot(ds, qh) * scale
        if rr == R - 1:
            dkv[:, :HEAD] = dk
            dkv[:, HEAD:] = dv
        else:
            dkv[:limit, :HEAD] += dk
            dkv[:limit, HEAD:] += dv
        dqs = dot(ds, keys, 0, 0) * scale
        for h in range(heads):
            dq[mine, h * HEAD : (h + 1) * HEAD] = dqs[h * sub : (h + 1) * sub]
        if rr == R - 1:
            sum_g.add()
            sum_g.pass_on(o_gb)
            sum_u.start()
            rs_d.step(1)
        if rr == R - 2:
            rs_d.step(2)
            for i, b in enumerate((c, net.across_c)):
                out_x[i].wait_recv()
                s_o[4 * i : 4 * i + 4] = (
                    woo[pl.ds(4 * b, 4)].astype(F32) + wox[i].astype(F32)
                ).astype(BF)
        if rr == 0:
            rs_d.step(3)
    sib_c = c + 1 - 2 * lax.rem(c, 2)
    far_c = net.across_c
    far_sib_c = far_c + 1 - 2 * lax.rem(far_c, 2)
    dkv16[...] = dkv[...].astype(BF).reshape(dkv16.shape)
    dk_copies = [
        net.copy(dkv16.at[:, far_sib_c], dk_sib.at[1], net.sibling),
        net.copy(dkv16.at[:, sib_c], dk_sib.at[0], net.sibling),
    ]
    for cp in dk_copies:
        cp.start()
    dk_copies[0].wait_recv()
    dk_in[0] = (dkv16[:, far_c].astype(F32) + dk_sib[1].astype(F32)).astype(BF)
    dk_copies.append(net.copy(dk_in.at[0], dk_in.at[1], net.across))
    dk_copies[2].start()
    lay[0] = mid[...]
    rs_d.total_into(lay.at[0])
    jk[...] = lay[0].astype(BF)
    sum_o = BlockSum(net, leading(s_o), leading(s_o), x_o, y_o)
    sum_o.start()
    for cp in loads[6:]:
        cp.wait()
    slots = dkv16[:, c].astype(F32)
    dk_copies[1].wait_recv()
    slots = slots + dk_sib[0].astype(F32)
    dk_copies[2].wait_recv()
    slots = slots + dk_in[1].astype(F32)
    slots = slots.reshape(n_tok, 2 * HEAD)
    joint[:, :qw] = turn(dq[...], cos2[...], -sin2[...]).astype(BF)
    joint[:, qw : qw + HEAD] = turn(slots[:, :HEAD], cos2[...], -sin2[...]).astype(BF)
    joint[:, qw + HEAD :] = slots[:, HEAD:].astype(BF)
    part[...] = dot(joint[...], wjs[...], 1, 1).astype(BF).reshape(R, sub, width)
    rs = LineSum(net, part, rbu, rbd)
    rs.step(0)
    total = dot(nall[...].reshape(n_tok, width), joint[...], 0, 0)
    wjo[...] = total.astype(BF).reshape(wjo.shape)
    joint_x = [net.copy(wjo.at[pl.ds(4 * b, 4)], wjx.at[i], net.sibling) for i, b in enumerate(sib_blocks)]
    for cp in joint_x:
        cp.start()
    bias = jnp.sum(joint[...].astype(F32), axis=0, keepdims=True)
    for i, b in enumerate((c, net.across_c)):
        joint_x[i].wait_recv()
        s_j[4 * i : 4 * i + 4] = (
            wjo[pl.ds(4 * b, 4)].astype(F32) + wjx[i].astype(F32)
        ).astype(BF)
    sum_j = BlockSum(net, leading(s_j), leading(s_j), x_j, y_j)
    sum_j.start()
    layer_x = to_columns(jk, o_layer)
    sum_o.add()
    sum_o.pass_on(o_ob)
    rs.step(1)
    sum_u.add()
    sum_u.pass_on(o_ub)
    sum_j.add()
    sum_j.pass_on(jb)
    keeps = [
        net.here(src.at[pl.ds(2 * net.h, 2)], dst)
        for src, dst in ((s_g, o_ga), (s_u, o_ua), (s_o, o_oa))
    ]
    for cp in keeps:
        cp.start()
    rs.step(2)
    sum_j.finish()
    ja = s_j.at[pl.ds(2 * net.h, 2)]
    own_cols = pl.ds(pl.multiple_of(qw + slot * HEAD, HEAD), HEAD)
    mate_cols = pl.ds(pl.multiple_of(qw + (1 - slot) * HEAD, HEAD), HEAD)
    o_j[:, :, :qw] = ja[:, :, :qw].astype(F32) + jb[:, :, :qw].astype(F32)
    v_mate = ja[:, :, mate_cols].astype(F32) + jb[:, :, mate_cols].astype(F32)
    jgot[0] = v_mate
    slot_x = net.copy(jgot.at[0], jgot.at[1], net.at_row(partner_r))
    slot_x.start()
    rs.step(3)
    lay[1] = jnp.zeros_like(lay[1])
    rs.total_into(lay.at[1])
    grad = lay[1]
    x = x_in[...].astype(F32)
    inv = lax.rsqrt(jnp.mean(x * x, axis=-1, keepdims=True) + epsilon)
    normal = x * inv
    e = grad * gains[0:1, :width]
    back = inv * (e - normal * jnp.mean(e * normal, axis=-1, keepdims=True))
    settle(layer_x)
    jk[...] = (gmid[...] + back).astype(BF)
    input_x = to_columns(jk, o_input)
    gain_attn = jnp.sum(grad * normal, axis=0, keepdims=True)
    for k in range(C):
        cut = slice(k * block, (k + 1) * block)
        v1[k, :, :block] = jnp.broadcast_to(gain_attn[:, cut], (8, block))
        v1[k, :, block : 2 * block] = gain_mlp[:, cut]
        v1[k, :, 2 * block :] = jnp.broadcast_to(bias, (8, bias.shape[1]))
    v_copies = []
    for k in range(1, C):
        to, frm = lax.rem(c + k, C), lax.rem(c + C - k, C)
        i = net.n
        net.n += 1
        out = net.like(i, v1.at[to], v1in.at[c], net.at_col(to))
        out.start()
        v_copies.append((out, net.like(i, v1.at[to], v1in.at[frm], net.at_col(to)), frm))
    total = v1[c]
    for _, inc, frm in v_copies:
        inc.wait_recv()
        total = total + v1in[frm]
    v2[...] = total
    far = []
    for same in (1, 0):
        for k in range(R):
            if same and k == 0:
                continue
            to, frm = lax.rem(r + k, R), lax.rem(r + R - k, R)
            i = net.n
            net.n += 1
            dst_d = net.d if same else net.mate[0]
            hs = net.h if same else net.other_h
            out = net.like(i, v2, v2in.at[net.h, r], (dst_d, to, c))
            out.start()
            far.append((out, net.like(i, v2, v2in.at[hs, frm], (dst_d, to, c))))
    v2in[net.h, r] = total
    slot_x.wait_recv()
    o_j[:, :, qw:] = ja[:, :, own_cols].astype(F32) + jb[:, :, own_cols].astype(F32) + jgot[1]
    for g in (sum_g, sum_u, sum_o):
        g.finish()
    for cp in sum_d:
        cp.wait()
    for cp in keeps:
        cp.wait()
    for _, inc in far:
        inc.wait_recv()
    gain_sum = v2in[0, 0, :, : 2 * block]
    for hh in (0, 1):
        for k in range(R):
            if hh or k:
                gain_sum = gain_sum + v2in[hh, k, :, : 2 * block]
    o_vec[:, : 2 * block] = gain_sum
    o_vec[:, 2 * block : 2 * block + qw] = (
        v2in[0, r, :, 2 * block : 2 * block + qw] + v2in[1, r, :, 2 * block : 2 * block + qw]
    )
    cols = pl.ds(pl.multiple_of(2 * block + qw + slot * HEAD, HEAD), HEAD)
    o_vec[:, 2 * block + qw :] = (
        v2in[0, r, :, cols] + v2in[1, r, :, cols]
        + v2in[0, partner_r, :, cols] + v2in[1, partner_r, :, cols]
    )
    settle(input_x)
    for g in (g_m, rs_d, rs):
        g.finish()
    for cp in out_x + joint_x + [slot_x]:
        cp.wait_send()
    for cp in dk_copies:
        cp.wait_send()
    for cps in v_copies + far:
        cps[0].wait_send()


def backward(sizes, gmid, x_in, mid, gains, gain_mlp, lengths, cos2, sin2, normed, q, kv, att, wj, wo,
             down, sd, sg, su):
    dp, R, C = sizes
    sub, width = gmid.shape
    block = width // C
    n, qw = q.shape
    jw = wj.shape[1]
    ff = sg.shape[2]
    shape = jax.ShapeDtypeStruct
    d2, g2 = (2, ff // 4, block), (2, block // 4, ff)
    w2, j2 = (2, qw // 4, block), (2, block // 4, jw)
    vec = 2 * block + jw
    outs = [
        (shape((C * sub, block), BF), VMEM), (shape((C * sub, block), BF), VMEM),
        (shape((8, vec - HEAD), F32), VMEM), (shape((2, block // 4, jw - HEAD), F32), VMEM),
        (shape(d2, BF), ANY), (shape(g2, BF), ANY), (shape(g2, BF), ANY),
        (shape(g2, BF), ANY), (shape(g2, BF), ANY), (shape(w2, BF), ANY), (shape(w2, BF), ANY),
    ]
    v = pltpu.VMEM
    four = lambda s: (4 * s[0],) + s[1:]
    line = v((R, sub, width), BF)
    return pl.pallas_call(
        functools.partial(backward_kernel, sizes),
        out_shape=[o for o, _ in outs],
        in_specs=[VMEM] * 5 + [SMEM] + [VMEM] * 2 + [ANY] * 10,
        out_specs=[s for _, s in outs],
        scratch_shapes=[
            line, line, v((n, qw), BF), v(kv.shape, BF), v((n, qw), BF), v((width, jw), BF),
            v((qw, width), BF), line, line, line, line, line, line, v((n, qw), BF), v((n, qw), F32),
            v((n * C, 2 * HEAD), F32), v(kv.shape, BF), v((2, R, sub, 2 * HEAD), BF),
            v((2, R, sub, 2 * HEAD), BF),
            v((n, jw), BF), v((2, sub, width), F32),
            v(four(g2), BF), v(four(g2), BF), v(g2, BF), v(g2, BF), v(g2, BF), v(g2, BF),
            v((16,) + j2[1:], BF), v((2, 4) + j2[1:], BF), v(four(j2), BF), v(j2, BF), v(j2, BF),
            v((16,) + w2[1:], BF), v((2, 4) + w2[1:], BF), v(four(w2), BF), v(w2, BF), v(w2, BF),
            v(j2, BF), v((sub, width), BF), v((2,) + j2[:2] + (HEAD,), F32),
            v((C, 8, vec), F32), v((C, 8, vec), F32), v((8, vec), F32), v((2, R, 8, vec), F32),
            pltpu.SemaphoreType.DMA((88,)), pltpu.SemaphoreType.DMA((88,)),
            pltpu.SemaphoreType.DMA((24,)),
        ],
        compiler_params=pltpu.CompilerParams(
            collective_id=3, has_side_effects=True, vmem_limit_bytes=VMEM_LIMIT
        ),
        name="backward",
    )(gmid, x_in, mid, gains, gain_mlp, lengths, cos2, sin2, normed, q, kv, att, wj, wo, down, sd, sg, su)


def on_device(
    tokens_in, seq_lengths, attention_gain, query_weight, query_bias, keyvalue_weight,
    keyvalue_bias, output_weight, feedforward_gain, gate_weight, up_weight, down_weight,
    cotangent,
):
    sizes = dp, rows, cols = tuple(lax.axis_size(a) for a in ("dp", "row", "col"))
    d, col = lax.axis_index("dp"), lax.axis_index("col")
    sub = tokens_in.shape[0] // cols
    block = tokens_in.shape[1]
    wq_width = query_weight.shape[1]
    r_i = jnp.arange(rows, dtype=jnp.int32)[:, None]
    i_i = jnp.arange(sub, dtype=jnp.int32)[None, :]
    places = (r_i * tokens_in.shape[0] + col * sub + i_i).reshape(-1, 1)
    first, end = jnp.zeros_like(places), 0
    for i in range(seq_lengths.shape[1] - 1):
        end = end + seq_lengths[0, i]
        first = jnp.where(places >= end, end, first)
    lane = jnp.arange(HEAD, dtype=jnp.int32)[None, :]
    rates = rope_base ** (-(lane % (HEAD // 2)).astype(F32) * (2.0 / HEAD))
    angles = (places - first).astype(F32) * rates
    cos2 = jnp.cos(angles)
    sin2 = jnp.sin(angles) * jnp.where(lane < HEAD // 2, -1.0, 1.0)
    one = lambda v: v.reshape(1, -1)
    (x_own, middle, nmlp, gains, normed, queries, kv, attended, cot_all, w_joint, w_out,
     w_gate, w_up) = attention_forward(
        sizes, tokens_in, cotangent, query_weight, keyvalue_weight, output_weight, gate_weight.T,
        up_weight.T, one(attention_gain), one(feedforward_gain), one(query_bias),
        one(keyvalue_bias), seq_lengths, cos2, sin2,
    )
    grad_middle, gain_mlp, down_part, sum_down, sum_gate, sum_up = feedforward(
        sizes, nmlp, middle, gains, cot_all, w_gate, w_up, down_weight, gate_weight.T, up_weight.T
    )
    layer_out, input_grad, vec, joint, db, ga, gb, ua, ub, oa, ob = backward(
        sizes, grad_middle, x_own, middle, gains, gain_mlp, seq_lengths, cos2, sin2, normed, queries, kv,
        attended, w_joint, w_out, down_part, sum_down, sum_gate, sum_up,
    )
    h = d // (dp // 2)

    def rest_of_dp(v):
        v = v.reshape(-1, v.shape[-1])
        if dp == 2:
            return v
        full = jnp.concatenate([jnp.where(h == 0, v, 0.0), jnp.where(h == 1, v, 0.0)], axis=0)
        return lax.psum_scatter(full, "dp", scatter_dimension=0, tiled=True)

    vec = vec[0]
    if dp > 2:
        vec = lax.psum(jnp.where(h == 0, vec, 0.0), "dp")

    def own_share(v):
        n = v.shape[0] // dp
        return lax.dynamic_slice_in_dim(v, d * n, n)

    both = lambda a, b: rest_of_dp(a.astype(F32) + b.astype(F32))
    joint = rest_of_dp(joint)
    bias = vec[2 * block :]
    return (
        layer_out, input_grad, vec[:block], joint[:, :wq_width], own_share(bias[:wq_width]),
        joint[:, wq_width:], own_share(bias[wq_width:]), both(oa, ob), vec[block : 2 * block],
        both(ga, gb), both(ua, ub), both(sum_down[:2], db),
    )


def solution(mesh):
    return jax.shard_map(
        on_device,
        mesh=mesh,
        in_specs=(
            P(("dp", "row"), "col"), P("dp", None), P("col"), P("col", "row"), P("row"),
            P("col", "row"), P("row"), P("row", "col"), P("col"), P("col", "row"),
            P("col", "row"), P("row", "col"), P(("dp", "row"), "col"),
        ),
        out_specs=(
            P(("dp", "row"), "col"), P(("dp", "row"), "col"), P("col"),
            P(("col", "dp"), "row"), P(("row", "dp")), P(("col", "dp"), "row"),
            P(("row", "dp")), P(("row", "dp"), "col"), P("col"), P(("col", "dp"), "row"),
            P(("col", "dp"), "row"), P(("row", "dp"), "col"),
        ),
        check_vma=False,
    )
```

```python
import functools

import jax
import jax.numpy as jnp
from jax import lax
from jax.experimental import pallas as pl
from jax.experimental.pallas import tpu as pltpu
from jax.sharding import PartitionSpec as P

HEAD = 128
epsilon = 1e-06
rope_base = 1000000.0
masked_score = -1e30
BF = jnp.bfloat16
F32 = jnp.float32
MESH = pl.DeviceIdType.MESH
ANY = pl.BlockSpec(memory_space=pl.ANY)
VMEM = pl.BlockSpec(memory_space=pltpu.VMEM)
SMEM = pl.BlockSpec(memory_space=pltpu.SMEM)
VMEM_LIMIT = 61 * 2**20


def dot(a, b, ca=1, cb=0):
    return lax.dot_general(a, b, (((ca,), (cb,)), ((), ())), preferred_element_type=F32)


class Net:
    def __init__(self, sizes, send, recv, local):
        self.dp, self.R, self.C = sizes
        self.d = lax.axis_index("dp")
        self.r = lax.axis_index("row")
        self.c = lax.axis_index("col")
        half = self.dp // 2
        self.h = self.d // half
        self.send, self.recv, self.local = send, recv, local
        self.n = 0
        self.n_local = 0
        self.other_h = 1 - self.h
        self.mate = (lax.rem(self.d + half, self.dp), self.r, self.c)
        self.sibling = self.at_col(self.c + 1 - 2 * lax.rem(self.c, 2))
        self.across_c = lax.rem(self.c + 2, 4)
        self.across = self.at_col(self.across_c)

    def at_col(self, c):
        return (self.d, self.r, c)

    def at_row(self, r):
        return (self.d, r, self.c)

    def copy(self, src, dst, dev):
        i = self.n
        self.n += 1
        return pltpu.make_async_remote_copy(
            src_ref=src, dst_ref=dst, send_sem=self.send.at[i], recv_sem=self.recv.at[i],
            device_id=dev, device_id_type=MESH,
        )

    def like(self, copy_index, src, dst, dev):
        return pltpu.make_async_remote_copy(
            src_ref=src, dst_ref=dst, send_sem=self.send.at[copy_index],
            recv_sem=self.recv.at[copy_index], device_id=dev, device_id_type=MESH,
        )

    def here(self, src, dst):
        i = self.n_local
        self.n_local += 1
        return pltpu.make_async_copy(src, dst, self.local.at[i])

    def barrier(self):
        sem = pltpu.get_barrier_semaphore()
        for k in range(1, self.C):
            pl.semaphore_signal(
                sem, inc=1, device_id=self.at_col(lax.rem(self.c + k, self.C)), device_id_type=MESH
            )
        pl.semaphore_signal(sem, inc=1, device_id=self.mate, device_id_type=MESH)

        @pl.when(self.r > 0)
        def _():
            pl.semaphore_signal(sem, inc=1, device_id=self.at_row(self.r - 1), device_id_type=MESH)

        @pl.when(self.r < self.R - 1)
        def _():
            pl.semaphore_signal(sem, inc=1, device_id=self.at_row(self.r + 1), device_id_type=MESH)

        count = self.C + (self.r > 0).astype(jnp.int32) + (self.r < self.R - 1).astype(jnp.int32)
        pl.semaphore_wait(sem, count)


PARTS = 2


def shard(buf, j, q, parts):
    if len(buf.shape) == 4:
        return buf.at[q, j]
    n = buf.shape[1] // parts
    return buf.at[j, pl.ds(q * n, n)]


class LineGather:
    def __init__(self, net, buf, parts=PARTS):
        self.net, self.buf, self.parts = net, buf, parts
        self.base = net.n
        net.n += 2 * (net.R - 1) * parts

    def _copy(self, up, s, q, j):
        net = self.net
        b = shard(self.buf, jnp.clip(j, 0, net.R - 1), q, self.parts)
        to = jnp.minimum(net.r + 1, net.R - 1) if up else jnp.maximum(net.r - 1, 0)
        return net.like(self.base + 2 * (s * self.parts + q) + up, b, b, net.at_row(to))

    def step(self, s, which=None):
        net = self.net
        r, R = net.r, net.R
        for q in range(self.parts) if which is None else which:
            if s > 0:

                @pl.when(r - s >= 0)
                def _():
                    self._copy(1, s - 1, q, r - s).wait_recv()

            if s < R - 1:

                @pl.when((r - s >= 0) & (r < R - 1))
                def _():
                    self._copy(1, s, q, r - s).start()

            if s > 0:

                @pl.when(r + s < R)
                def _():
                    self._copy(0, s - 1, q, r + s).wait_recv()

            if s < R - 1:

                @pl.when((r + s < R) & (r > 0))
                def _():
                    self._copy(0, s, q, r + s).start()

    def finish(self):
        net = self.net
        r, R = net.r, net.R
        for s in range(R - 1):
            for q in range(self.parts):

                @pl.when((r - s >= 0) & (r < R - 1))
                def _():
                    self._copy(1, s, q, r - s).wait_send()

                @pl.when((r + s < R) & (r > 0))
                def _():
                    self._copy(0, s, q, r + s).wait_send()


class LineSum:
    def __init__(self, net, part, from_below, from_above, parts=PARTS):
        self.net, self.part, self.bu, self.bd, self.parts = net, part, from_below, from_above, parts
        self.base = net.n
        net.n += 2 * net.R * parts

    def _at(self, buf, j, q):
        return shard(buf, j, q, self.parts)

    def _copy(self, up, j, q):
        net = self.net
        j = jnp.clip(j, 0, net.R - 1)
        to = jnp.minimum(net.r + 1, net.R - 1) if up else jnp.maximum(net.r - 1, 0)
        return net.like(
            self.base + (2 * q + up) * net.R + j, self._at(self.part, j, q),
            self._at(self.bu if up else self.bd, j, q), net.at_row(to),
        )

    def _add(self, j, q, buf):
        mine, got = self._at(self.part, j, q), self._at(buf, j, q)
        mine[...] = (mine[...].astype(F32) + got[...].astype(F32)).astype(BF)

    def step(self, t, which=None):
        net = self.net
        r, R = net.r, net.R
        j = t - (R - 1 - r)
        k = R - 1 - (t - r)
        for q in range(self.parts) if which is None else which:

            @pl.when((j >= 0) & (r < R - 1))
            def _():
                self._copy(0, j, q).wait_recv()

            @pl.when((j >= 0) & (j < r))
            def _():
                @pl.when(r < R - 1)
                def _():
                    self._add(j, q, self.bd)

                self._copy(0, j, q).start()

            @pl.when((k <= R - 1) & (r > 0))
            def _():
                self._copy(1, k, q).wait_recv()

            @pl.when((k <= R - 1) & (k > r))
            def _():
                @pl.when(r > 0)
                def _():
                    self._add(k, q, self.bu)

                self._copy(1, k, q).start()

    def finish(self):
        net = self.net
        r, R = net.r, net.R
        for j in range(R):
            for q in range(self.parts):

                @pl.when(j < r)
                def _():
                    self._copy(0, j, q).wait_send()

                @pl.when(j > r)
                def _():
                    self._copy(1, j, q).wait_send()

    def total_into(self, out):
        net = self.net
        r, R = net.r, net.R
        n = out.shape[0] // self.parts
        for q in range(self.parts):
            mine = out.at[pl.ds(q * n, n)]
            mine[...] += self._at(self.part, r, q)[...].astype(F32)

            @pl.when(r < R - 1)
            def _():
                mine[...] += self._at(self.bd, r, q)[...].astype(F32)

            @pl.when(r > 0)
            def _():
                mine[...] += self._at(self.bu, r, q)[...].astype(F32)


class WeightGather:
    def __init__(self, net, src, full, by_rows, piece=0, pieces=1, keep=True):
        self.net, self.full, self.by_rows = net, full, by_rows
        if by_rows:
            self.n, self.w = full.shape[0] // net.C, full.shape[1]
        else:
            self.n, self.w = full.shape[0] // pieces, full.shape[1] // net.C
        self.first = piece * self.n
        if src is not None:
            src = src.at[pl.ds(self.first, self.n)]
        c, p, h, o = net.c, net.across_c, net.h, net.other_h
        half = self.n // 2
        self.here = None
        if src is not None:
            if keep:
                self.here = net.here(src, self.view(c, 0, 2))
            own_half = src.at[pl.ds(pl.multiple_of(h * half, 16), half)]
            own = src
        else:
            own_half, own = self.view(c, h, 1), self.view(c, 0, 2)
        self.x = net.copy(own_half, self.view(c, h, 1), net.across)
        self.sib = net.copy(own, self.view(c, 0, 2), net.sibling)
        self.y = net.copy(self.view(p, h, 1), self.view(p, h, 1), net.mate)
        self.sib_h = net.copy(self.view(p, h, 1), self.view(p, h, 1), net.sibling)
        self.sib_o = net.copy(self.view(p, o, 1), self.view(p, o, 1), net.sibling)

    def view(self, b, h, halves):
        half = self.n // 2
        if self.by_rows:
            return self.full.at[pl.ds(pl.multiple_of(b * self.n + h * half, 16), halves * half)]
        return self.full.at[
            pl.ds(pl.multiple_of(self.first + h * half, 16), halves * half),
            pl.ds(pl.multiple_of(b * self.w, 128), self.w),
        ]

    def start(self):
        if self.here is not None:
            self.here.start()
        self.x.start()
        self.sib.start()

    def pass_x(self):
        self.x.wait_recv()
        self.y.start()
        self.sib_h.start()

    def pass_y(self):
        self.y.wait_recv()
        self.sib_o.start()

    def arrive(self):
        if self.here is not None:
            self.here.wait()
        self.sib.wait_recv()
        self.sib_h.wait_recv()
        self.sib_o.wait_recv()

    def finish(self):
        for cp in (self.x, self.sib, self.y, self.sib_h, self.sib_o):
            cp.wait_send()


class BlockSum:
    def __init__(self, net, source, piece, from_x, from_mate):
        self.net, self.piece = net, piece
        self.from_x, self.from_mate = from_x, from_mate
        o = net.other_h
        self.first = [net.copy(source(1, k, 0), from_x.at[k], net.across) for k in (0, 1)]
        self.first += [net.copy(source(i, o, 1), from_mate.at[i], net.mate) for i in (0, 1)]
        self.second = []

    def start(self):
        for cp in self.first:
            cp.start()

    def add(self):
        h = self.net.h
        for cp in self.first:
            cp.wait_recv()
        for ref, got in (
            (self.piece(0, 0, 0), self.from_x.at[0]), (self.piece(0, 1, 0), self.from_x.at[1]),
            (self.piece(0, h, 1), self.from_mate.at[0]), (self.piece(1, h, 1), self.from_mate.at[1]),
        ):
            ref[...] = (ref[...].astype(F32) + got[...].astype(F32)).astype(BF)

    def pass_on(self, got):
        net = self.net
        cut, rest = self.from_x.shape[1], self.from_mate.shape[1]
        self.second = [
            net.copy(self.piece(0, net.other_h, 0), got.at[pl.ds(0, cut)], net.mate),
            net.copy(self.piece(1, net.h, 1), got.at[pl.ds(cut, rest)], net.across),
        ]
        for cp in self.second:
            cp.start()

    def finish(self):
        for cp in self.first:
            cp.wait_send()
        for cp in self.second:
            cp.wait_send()
            cp.wait_recv()


def halves(ref, cut):
    def piece(i, h, ab):
        rows = pl.ds(cut, ref.shape[1] - cut) if ab else pl.ds(0, cut)
        return ref.at[2 * i + h, rows]

    return piece


def third(rows):
    return rows // 3 // 16 * 16


def turn(values, cos2, sin2):
    heads = []
    for i in range(values.shape[1] // HEAD):
        v = values[:, i * HEAD : (i + 1) * HEAD]
        heads.append(v * cos2 + pltpu.roll(v, HEAD // 2, 1) * sin2)
    return jnp.concatenate(heads, axis=1) if len(heads) > 1 else heads[0]


def attention_kernel(
    sizes,
    tok, cot, wq, wkv, wo, wg, wu, vectors, lengths, turns,
    o_x, o_mid, o_nmlp, o_gains, o_normed, o_q, o_kv, o_att, o_cot, o_wj, o_wo, o_wg, o_wu,
    xin, cin, small, gains, kvb2, nall, call, wj, wov, kv, qs, att, part, rbu, rbd, send, recv, local,
):
    net = Net(sizes, send, recv, local)
    R, C, r, c = net.R, net.C, net.r, net.c
    sub, width = nall.shape[1], nall.shape[2]
    block = tok.shape[1]
    row_tok = sub * C
    n_tok = sub * R
    qw = wq.shape[1]
    slot = lax.rem(r, 2)
    partner = net.at_row(r + 1 - 2 * slot)
    net.barrier()
    small[...] = vectors[:, : 2 * block]
    kvb2[slot] = vectors[:, 2 * block + qw :]
    cos2, sin2 = turns.at[:, pl.ds(0, HEAD)], turns.at[:, pl.ds(HEAD, HEAD)]

    def spread(src, dst):
        mine = pl.multiple_of(c * sub, sub)
        local_copy = net.here(src.at[pl.ds(mine, sub)], dst.at[c])
        copies = []
        for k in range(1, C):
            to = lax.rem(c + k, C)
            frm = lax.rem(c + C - k, C)
            i = net.n
            net.n += 1
            rows = pl.ds(pl.multiple_of(to * sub, sub), sub)
            copies.append(
                (net.like(i, src.at[rows], dst.at[c], net.at_col(to)),
                 net.like(i, src.at[rows], dst.at[frm], net.at_col(to)))
            )
        return local_copy, copies

    def begin(pair):
        pair[0].start()
        for out, _ in pair[1]:
            out.start()

    def arrived(pair):
        pair[0].wait()
        for _, inc in pair[1]:
            inc.wait_recv()

    tok_in, cot_in = spread(tok, xin), spread(cot, cin)
    begin(tok_in)
    gain_own = net.here(small, gains.at[c])
    gain_own.start()
    gain_copies = []
    for k in range(1, C):
        to, frm = lax.rem(c + k, C), lax.rem(c + C - k, C)
        i = net.n
        net.n += 1
        out = net.like(i, small, gains.at[c], net.at_col(to))
        gain_copies.append((out, net.like(i, small, gains.at[frm], net.at_col(to))))
        out.start()
    own_rows = pl.ds(pl.multiple_of(c * block, block), block)
    col_own = pl.ds(pl.multiple_of(qw + slot * HEAD, HEAD), HEAD)
    col_mate = pl.ds(pl.multiple_of(qw + (1 - slot) * HEAD, HEAD), HEAD)
    kv_x = net.copy(wkv, wj.at[own_rows, col_own], partner)
    kv_in = net.like(net.n - 1, wkv, wj.at[own_rows, col_mate], partner)
    kv_x.start()
    kvb_x = net.copy(kvb2.at[slot], kvb2.at[slot], partner)
    kvb_in = net.like(net.n - 1, kvb2.at[slot], kvb2.at[1 - slot], partner)
    kvb_x.start()
    wq_own = net.here(wq, wj.at[own_rows, pl.ds(0, qw)])
    wq_own.start()
    wkv_own = net.here(wkv, wj.at[own_rows, col_own])
    wkv_own.start()
    g_joint = WeightGather(net, None, wj, True)
    g_out = WeightGather(net, wo, wov, False)
    bulk = [WeightGather(net, w, o, False, i, 2, False) for w, o in ((wg, o_wg), (wu, o_wu)) for i in (0, 1)]

    arrived(tok_in)
    gain_own.wait()
    for _, inc in gain_copies:
        inc.wait_recv()
    for k in range(C):
        o_gains[:, k * block : (k + 1) * block] = gains[k, :, :block]
        o_gains[:, width + k * block : width + (k + 1) * block] = gains[k, :, block:]
    x = jnp.concatenate([xin[k].astype(F32) for k in range(C)], axis=1)
    o_mid[...] = x
    o_x[...] = x.astype(BF)
    inv = lax.rsqrt(jnp.mean(x * x, axis=-1, keepdims=True) + epsilon)
    nall[r] = (x * inv * o_gains[0:1, :width]).astype(BF)
    g_n = LineGather(net, nall)
    g_n.step(0)
    wq_own.wait()
    wkv_own.wait()
    kv_in.wait_recv()
    g_joint.start()
    g_out.start()
    begin(cot_in)
    bulk[0].start()
    bulk[1].start()
    g_joint.pass_x()
    g_out.pass_x()
    g_n.step(1)
    g_joint.pass_y()
    g_out.pass_y()
    arrived(cot_in)
    for k in range(C):
        call[r, :, k * block : (k + 1) * block] = cin[k]
    g_n.step(2)
    bulk[0].pass_x()
    g_joint.arrive()
    kvb_in.wait_recv()
    g_n.step(3)
    g_cot = LineGather(net, call)
    g_cot.step(0)
    bias = jnp.concatenate([vectors[0:1, 2 * block : 2 * block + qw], kvb2[0, 0:1, :], kvb2[1, 0:1, :]], axis=1)
    joint = dot(nall[...].reshape(n_tok, width), wj[...]) + bias
    key = turn(joint[:, qw : qw + HEAD], cos2[...], sin2[...]).astype(BF)
    kv[:, c, :, :HEAD] = key.reshape(R, sub, HEAD)
    kv[:, c, :, HEAD:] = joint[:, qw + HEAD :].astype(BF).reshape(R, sub, HEAD)
    sib_c = c + 1 - 2 * lax.rem(c, 2)
    far_c = net.across_c
    far_sib_c = far_c + 1 - 2 * lax.rem(far_c, 2)
    kv_far = net.copy(kv.at[:, c], kv.at[:, c], net.across)
    kv_sib = net.copy(kv.at[:, c], kv.at[:, c], net.sibling)
    kv_pass = net.copy(kv.at[:, far_c], kv.at[:, far_c], net.sibling)
    kv_far.start()
    kv_sib.start()
    qs[...] = turn(joint[:, :qw], cos2[...], sin2[...]).astype(BF)
    out_normed = net.here(nall, o_normed)
    out_normed.start()
    out_wj = net.here(wj, o_wj)
    out_wj.start()
    kv_far.wait_recv()
    kv_pass.start()
    kv_sib.wait_recv()
    kv_pass.wait_recv()
    bulk[1].pass_x()
    bulk[2].start()
    bulk[3].start()
    bulk[0].pass_y()
    g_cot.step(1)
    out_kv = net.here(kv, o_kv)
    out_kv.start()
    scale = HEAD ** (-0.5)
    ends = [lengths[0, 0]]
    for i in range(1, lengths.shape[1] - 1):
        ends.append(ends[-1] + lengths[0, i])
    for rr in range(R):
        limit = (rr + 1) * row_tok
        keys = kv[: rr + 1, :, :, :HEAD].reshape(limit, HEAD)
        values = kv[: rr + 1, :, :, HEAD:].reshape(limit, HEAD)
        mine = slice(rr * sub, (rr + 1) * sub)
        place = lax.broadcasted_iota(jnp.int32, (sub, limit), 1)
        here = rr * row_tok + c * sub + lax.broadcasted_iota(jnp.int32, (sub, 1), 0)
        first = jnp.zeros((sub, 1), jnp.int32)
        for end in ends:
            first = jnp.where(here >= end, end, first)
        allowed = (place >= first) & (place <= here)
        for h in range(qw // HEAD):
            cols = slice(h * HEAD, (h + 1) * HEAD)
            s = jnp.where(allowed, dot(qs[mine, cols], keys, 1, 1) * scale, masked_score)
            e = jnp.exp(s - jnp.max(s, axis=-1, keepdims=True))
            p = e * (1.0 / jnp.sum(e, axis=-1, keepdims=True))
            att[mine, cols] = dot(p.astype(BF), values).astype(BF)
    g_out.arrive()
    part[...] = dot(att[...], wov[...]).astype(BF).reshape(R, sub, width)
    rs = LineSum(net, part, rbu, rbd)
    rs.step(0)
    out_q = net.here(qs, o_q)
    out_q.start()
    out_att = net.here(att, o_att)
    out_att.start()
    out_wo = net.here(wov, o_wo)
    out_wo.start()
    g_cot.step(2)
    bulk[1].pass_y()
    bulk[2].pass_x()
    rs.step(1)
    g_cot.step(3)
    out_cot = net.here(call, o_cot)
    out_cot.start()
    bulk[3].pass_x()
    rs.step(2)
    bulk[2].pass_y()
    rs.step(3)
    rs.total_into(o_mid)
    mid = o_mid[...]
    inv = lax.rsqrt(jnp.mean(mid * mid, axis=-1, keepdims=True) + epsilon)
    o_nmlp[...] = (mid * inv * o_gains[0:1, width:]).astype(BF)
    bulk[3].pass_y()
    for g in bulk:
        g.arrive()
    for g in [g_joint, g_out, g_n, g_cot, rs] + bulk:
        g.finish()
    for out, _ in tok_in[1] + cot_in[1] + gain_copies:
        out.wait_send()
    for cp in (kv_far, kv_sib, kv_pass):
        cp.wait_send()
    kv_x.wait_send()
    kvb_x.wait_send()
    for cp in (out_normed, out_wj, out_kv, out_q, out_att, out_wo, out_cot):
        cp.wait()


def attention_forward(
    sizes, tok, cot, wq, wkv, wo, wg, wu, vectors, lengths, turns
):
    dp, R, C = sizes
    sub = tok.shape[0] // C
    block = tok.shape[1]
    width = block * C
    qw, jw = wq.shape[1], wq.shape[1] + 2 * HEAD
    n = sub * R
    ff = wg.shape[0]
    shape = jax.ShapeDtypeStruct
    outs = [
        (shape((sub, width), BF), VMEM),
        (shape((sub, width), F32), VMEM), (shape((sub, width), BF), VMEM),
        (shape((8, 2 * width), F32), VMEM), (shape((R, sub, width), BF), ANY),
        (shape((n, qw), BF), ANY), (shape((R, C, sub, 2 * HEAD), BF), ANY),
        (shape((n, qw), BF), ANY), (shape((R, sub, width), BF), ANY),
        (shape((width, jw), BF), ANY), (shape((qw, width), BF), ANY),
        (shape((ff, width), BF), ANY), (shape((ff, width), BF), ANY),
    ]
    return pl.pallas_call(
        functools.partial(attention_kernel, sizes),
        out_shape=[o for o, _ in outs],
        in_specs=[ANY] * 7 + [VMEM, SMEM, VMEM],
        out_specs=[s for _, s in outs],
        scratch_shapes=[
            pltpu.VMEM((C, sub, block), BF), pltpu.VMEM((C, sub, block), BF),
            pltpu.VMEM((8, 2 * block), F32), pltpu.VMEM((C, 8, 2 * block), F32), pltpu.VMEM((2, 8, HEAD), F32),
            pltpu.VMEM((R, sub, width), BF), pltpu.VMEM((R, sub, width), BF),
            pltpu.VMEM((width, jw), BF), pltpu.VMEM((qw, width), BF),
            pltpu.VMEM((R, C, sub, 2 * HEAD), BF), pltpu.VMEM((n, qw), BF),
            pltpu.VMEM((n, qw), BF), pltpu.VMEM((R, sub, width), BF),
            pltpu.VMEM((R, sub, width), BF), pltpu.VMEM((R, sub, width), BF),
            pltpu.SemaphoreType.DMA((128,)), pltpu.SemaphoreType.DMA((128,)),
            pltpu.SemaphoreType.DMA((24,)),
        ],
        compiler_params=pltpu.CompilerParams(
            collective_id=1, has_side_effects=True, vmem_limit_bytes=VMEM_LIMIT
        ),
        name="attention_forward",
    )(tok, cot, wq, wkv, wo, wg, wu, vectors, lengths, turns)


def feedforward_kernel(
    sizes,
    nmlp, mid, gains, cot, wg, wu, wd, own_g, own_u,
    o_gmid, o_gain, o_down, o_sd, o_sm, o_sx, o_sg, o_su,
    w_gate, w_up, w_down, xall, call, acc, hid, gg, gu, cc, sx, xt, part, rbu, rbd, dpart, g, x_d, y_d,
    send, recv, local,
):
    net = Net(sizes, send, recv, local)
    R, C, r, c = net.R, net.C, net.r, net.c
    sub, width = nmlp.shape
    block = width // C
    n_tok = sub * R
    n_part = n_tok // PARTS
    n = sub // PARTS
    ff = w_gate.shape[0]
    tile = acc.shape[2]
    wide = width // tile
    tiles = [(f, min(tile, ff - f)) for f in range(0, ff, tile)]
    own_cols = [pl.ds(pl.multiple_of(b * block, HEAD), block) for b in (c, net.across_c)]
    sib_cols = [
        pl.ds(pl.multiple_of((b + 1 - 2 * lax.rem(b, 2)) * block, HEAD), block)
        for b in (c, net.across_c)
    ]
    pieces = 5
    g_down = [WeightGather(net, wd, w_down, False, i, pieces) for i in range(pieces)]
    in_cot = [net.here(cot.at[:, pl.ds(q * n, n)], call.at[q]) for q in range(PARTS)]
    for cp in in_cot:
        cp.start()
    in_w = []
    for full, own, w in ((wg, own_g, w_gate), (wu, own_u, w_up)):
        for k in range(C):
            cols = pl.ds(pl.multiple_of(lax.rem(c + k, C) * block, HEAD), block)
            cp = net.here(full.at[:, cols] if k else own, w.at[:, cols])
            cp.start()
            in_w.append(cp)
    for q in range(PARTS):
        xall[q, r] = nmlp[q * n : (q + 1) * n]
    net.barrier()
    g_x = LineGather(net, xall)
    g_x.step(0)
    g_down[0].start()
    g_down[1].start()
    for cp in in_cot:
        cp.wait()
    to_sibling = []

    def hand(src, dst):
        cp = net.copy(src, dst, net.sibling)
        cp.start()
        to_sibling.append(cp)

    for i in (0, 1):
        hand(call.at[:, :, :, sib_cols[i]], cc.at[1, :, :, :, pl.ds(i * block, block)])
        cc[0, :, :, :, i * block : (i + 1) * block] = call[:, :, :, own_cols[i]]

    def hidden_back(f, count):
        return dot(call[...].reshape(n_tok, width), w_down[f : f + count, :], 1, 1)

    def pass_x(i):
        g_down[i].pass_x()
        if i + 2 < pieces:
            g_down[i + 2].start()

    pass_x(0)
    g_x.step(1, (0,))
    pass_x(1)
    g_down[0].pass_y()
    pass_x(2)
    g_x.step(2, (0,))
    g_x.step(1, (1,))
    g_down[1].pass_y()
    pass_x(3)
    g_down[0].arrive()
    g_down[1].arrive()
    acc[0] = hidden_back(0, tile)
    g_down[2].pass_y()
    g_x.step(3, (0,))
    pass_x(4)
    for cp in in_w:
        cp.wait()

    def act(q, t):
        f, count = tiles[t]
        rows = slice(f, f + count)
        mine = slice(q * n_part, (q + 1) * n_part)
        x = xall[q].reshape(n_part, width)
        gate = dot(x, w_gate[rows, :], 1, 1)
        up = dot(x, w_up[rows, :], 1, 1)
        if t < wide:
            back = acc[t, mine]
        else:
            back = dot(call[q].reshape(n_part, width), w_down[rows, :], 1, 1)
        s = jax.nn.sigmoid(gate)
        silu = gate * s
        hid[mine, rows] = (silu * up).astype(BF)
        gg[mine, rows] = (back * up * s * (1.0 + gate * (1.0 - s))).astype(BF)
        gu[mine, rows] = (back * silu).astype(BF)

    act(0, 0)
    g_down[3].pass_y()
    g_down[2].arrive()
    acc[1] = hidden_back(tile, tile)
    act(0, 1)
    g_x.step(2, (1,))
    g_down[3].arrive()
    acc[2] = hidden_back(2 * tile, tile)
    act(0, 2)
    g_down[4].pass_y()
    g_down[4].arrive()
    for t in range(wide, len(tiles)):
        act(0, t)
    g_x.step(3, (1,))

    def hand_acts(q):
        mine, theirs = pl.ds(q * n_part, n_part), pl.ds(n_tok + q * n_part, n_part)
        for ref in (hid, gg, gu):
            hand(ref.at[mine], ref.at[theirs])

    def input_back(q):
        mine = slice(q * n_part, (q + 1) * n_part)

        @pl.loop(0, wide)
        def _(i):
            cols = pl.ds(pl.multiple_of(i * tile, tile), tile)
            total = dot(gg[mine, :], w_gate[:, cols]) + dot(gu[mine, :], w_up[:, cols])
            part[q, :, :, cols] = total.astype(BF).reshape(R, n, tile)

    hand_acts(0)
    input_back(0)
    rs = LineSum(net, part, rbu, rbd)
    rs.step(0, (0,))
    for i in (0, 1):
        hand(xall.at[:, :, :, sib_cols[i]], sx.at[i])
    for t in range(len(tiles)):
        act(1, t)
        if t == 3:
            rs.step(1, (0,))
    hand_acts(1)
    input_back(1)
    rs.step(0, (1,))
    rs.step(2, (0,))
    for g_piece in g_down:
        g_piece.finish()
    for cp in to_sibling:
        cp.wait_recv()
    outs = []
    for f, count in tiles:
        total = dot(hid[:, f : f + count], cc[...].reshape(2 * n_tok, 2 * block), 0, 0)
        w_gate[f : f + count, : 2 * block] = total.astype(BF)
    half_ff = ff // 2
    cut = x_d.shape[1]

    def down_piece(i, h, ab):
        first, count = (cut, half_ff - cut) if ab else (0, cut)
        return w_gate.at[
            pl.ds(pl.multiple_of(h * half_ff + first, 16), count), pl.ds(i * block, block)
        ]

    sum_d = BlockSum(net, down_piece, down_piece, x_d, y_d)
    sum_d.start()
    rs.step(1, (1,))
    rs.step(3, (0,))

    @pl.loop(0, wide)
    def _(i):
        cols = pl.ds(pl.multiple_of(i * tile, tile), tile)
        total = dot(hid[:n_tok, :], w_down[:, cols])
        dpart[:, :, :, cols] = total.astype(BF).reshape(PARTS, R, n, tile)

    rs.step(2, (1,))
    out_down = [net.here(dpart.at[q], o_down.at[:, pl.ds(q * n, n)]) for q in range(PARTS)]
    for cp in out_down:
        cp.start()
    for i in (0, 1):
        rows = slice(i * block, (i + 1) * block)
        xt[rows, :n_tok] = xall[:, :, :, own_cols[i]].reshape(n_tok, block).T
        xt[rows, n_tok:] = sx[i].reshape(n_tok, block).T
    for src, o in ((gg, o_sg), (gu, o_su)):
        if outs:
            outs.pop().wait()
        for f, count in tiles:
            total = dot(xt[...], src[:, f : f + count])
            g[:, :, f : f + count] = total.astype(BF).reshape(4, g.shape[1], count)
        cp = net.here(g, o)
        cp.start()
        outs.append(cp)
        if src is gg:
            rs.step(3, (1,))
    o_gmid[...] = jnp.zeros_like(o_gmid)
    rs.total_into(o_gmid)
    grad = o_gmid[...]
    m = mid[...]
    inv = lax.rsqrt(jnp.mean(m * m, axis=-1, keepdims=True) + epsilon)
    normal = m * inv
    e = grad * gains[0:1, width:]
    back = inv * (e - normal * jnp.mean(e * normal, axis=-1, keepdims=True))
    o_gain[...] = jnp.broadcast_to(jnp.sum(grad * normal, axis=0, keepdims=True), o_gain.shape)
    for q in range(PARTS):
        rows = slice(q * n, (q + 1) * n)
        o_gmid[rows] = call[q, r].astype(F32) + back[rows]
    rs.finish()
    sum_d.add()
    own_half = w_gate.at[
        pl.ds(pl.multiple_of(net.h * half_ff, 16), half_ff), pl.ds(0, block)
    ]
    for src, dst in (
        (own_half, o_sd), (down_piece(0, net.other_h, 0), o_sm), (down_piece(1, net.h, 1), o_sx)
    ):
        cp = net.here(src, dst)
        cp.start()
        outs.append(cp)
    sum_d.finish()
    g_x.finish()
    for cp in to_sibling:
        cp.wait_send()
    for cp in outs + out_down:
        cp.wait()


def feedforward(sizes, nmlp, mid, gains, cot, wg, wu, wd, own_g, own_u):
    dp, R, C = sizes
    sub, width = nmlp.shape
    block = width // C
    n_tok = R * sub
    ff = wd.shape[0]
    tile = 512
    cut = ff // 4
    shape = jax.ShapeDtypeStruct
    outs = [
        (shape((sub, width), F32), VMEM), (shape((8, width), F32), VMEM),
        (shape((R, sub, width), BF), ANY), (shape((ff // 2, block), BF), ANY),
        (shape((cut, block), BF), ANY), (shape((ff // 2 - cut, block), BF), ANY),
        (shape((4, block // 2, ff), BF), ANY), (shape((4, block // 2, ff), BF), ANY),
    ]
    v = pltpu.VMEM
    line = v((PARTS, R, sub // PARTS, width), BF)
    acts = v((2 * n_tok, ff), BF)
    weight = v((ff, width), BF)
    return pl.pallas_call(
        functools.partial(feedforward_kernel, sizes),
        out_shape=[o for o, _ in outs],
        in_specs=[VMEM] * 3 + [ANY] * 6,
        out_specs=[s for _, s in outs],
        scratch_shapes=[
            weight, weight, weight, line, line, v((width // tile, n_tok, tile), F32), acts, acts, acts,
            v((2, PARTS, R, sub // PARTS, 2 * block), BF), v((2, PARTS, R, sub // PARTS, block), BF),
            v((2 * block, 2 * n_tok), BF), line, line, line, line, v((4, block // 2, ff), BF),
            v((2, cut, block), BF), v((2, ff // 2 - cut, block), BF),
            pltpu.SemaphoreType.DMA((128,)), pltpu.SemaphoreType.DMA((128,)),
            pltpu.SemaphoreType.DMA((32,)),
        ],
        compiler_params=pltpu.CompilerParams(
            collective_id=2, has_side_effects=True, vmem_limit_bytes=VMEM_LIMIT
        ),
        name="feedforward",
    )(nmlp, mid, gains, cot, wg, wu, wd, own_g, own_u)


def backward_kernel(
    sizes,
    gmid, x_in, mid, gains, gain_mlp, lengths, turns,
    normed, q, kv, att, wj, wo, down, sm, sx, sg, su,
    o_layer, o_input, o_vec, o_j, o_db, o_ga, o_gb, o_ua, o_ub, o_oa, o_ob,
    mall, nall, qs, kvs, atts, wjs, wos, dpart, drbu, drbd, part, rbu, rbd, grads, dq, dkv, dkv16, dk_sib, dk_in,
    joint, lay,
    s_g, s_u, x_g, x_u, y_g, y_u,
    wjo, wjx, s_j, x_j, y_j, woo, wox, s_o, x_o, y_o, jb, jk, jk2, jgot, v1, v1in, v2, v2in,
    send, recv, local,
):
    net = Net(sizes, send, recv, local)
    R, C, r, c = net.R, net.C, net.r, net.c
    sub, width = gmid.shape
    block = width // C
    n_tok = sub * R
    row_tok = sub * C
    qw = qs.shape[1]
    slot = lax.rem(r, 2)
    cos2, sin2 = turns.at[:, pl.ds(0, HEAD)], turns.at[:, pl.ds(HEAD, HEAD)]
    partner_r = r + 1 - 2 * slot
    loads = [
        net.here(a, b) for a, b in
        ((wo, wos), (att, atts), (q, qs), (kv, kvs), (down, dpart), (sg, s_g), (su, s_u),
         (normed, nall), (wj, wjs))
    ]
    for cp in loads:
        cp.start()
    sem = pltpu.get_barrier_semaphore()
    half = net.dp // 2
    others = [(net.d, r, lax.rem(c + k, C)) for k in range(1, C)]
    others += [(net.d, lax.rem(r + k, R), c) for k in range(1, R)]
    others += [(net.mate[0], lax.rem(r + k, R), c) for k in range(R)]
    for dev in others:
        pl.semaphore_signal(sem, inc=1, device_id=dev, device_id_type=MESH)
    pl.semaphore_wait(sem, len(others))

    mall[r] = gmid[...].astype(BF)
    g_m = LineGather(net, mall)
    g_m.step(0)
    cut_d, rest_d = sm.shape[0], sx.shape[0]
    sum_d = [
        net.copy(sm, o_db.at[pl.ds(0, cut_d)], net.mate),
        net.copy(sx, o_db.at[pl.ds(cut_d, rest_d)], net.across),
    ]
    for cp in sum_d:
        cp.start()
    sum_g = BlockSum(net, halves(sg, x_g.shape[1]), halves(s_g, x_g.shape[1]), x_g, y_g)
    sum_u = BlockSum(net, halves(su, x_u.shape[1]), halves(s_u, x_u.shape[1]), x_u, y_u)
    sum_g.start()
    sum_u.start()
    g_m.step(1)
    for cp in loads[:6]:
        cp.wait()
    g_m.step(2)
    g_m.step(3)
    rs_d = LineSum(net, dpart, drbu, drbd)
    rs_d.step(0)
    m_all = mall[...].reshape(n_tok, width)
    grads[...] = dot(m_all, wos[...], 1, 1).astype(BF)

    def to_columns(src, dst):
        rows = pl.ds(pl.multiple_of(c * sub, sub), sub)
        mine = net.here(src.at[:, pl.ds(pl.multiple_of(c * block, HEAD), block)], dst.at[rows])
        mine.start()
        pairs = []
        for k in range(1, C):
            to, frm = lax.rem(c + k, C), lax.rem(c + C - k, C)
            i = net.n
            net.n += 1
            cut = src.at[:, pl.ds(pl.multiple_of(to * block, HEAD), block)]
            out = net.like(i, cut, dst.at[rows], net.at_col(to))
            out.start()
            from_rows = pl.ds(pl.multiple_of(frm * sub, sub), sub)
            pairs.append((out, net.like(i, cut, dst.at[from_rows], net.at_col(to))))
        return mine, pairs

    def settle(exchange):
        exchange[0].wait()
        for out, inc in exchange[1]:
            inc.wait_recv()
            out.wait_send()

    sib_blocks = [b + 1 - 2 * lax.rem(b, 2) for b in (c, net.across_c)]
    total = dot(atts[...], m_all, 0, 0)
    for b in range(C):
        woo[2 * b : 2 * b + 2] = (
            total[:, b * block : (b + 1) * block].astype(BF).reshape(2, qw // 2, block)
        )
    out_x = [net.copy(woo.at[pl.ds(2 * b, 2)], wox.at[i], net.sibling) for i, b in enumerate(sib_blocks)]
    for cp in out_x:
        cp.start()
    scale = HEAD ** (-0.5)
    heads = qw // HEAD
    ends = [lengths[0, 0]]
    for i in range(1, lengths.shape[1] - 1):
        ends.append(ends[-1] + lengths[0, i])
    for rr in reversed(range(R)):
        limit = (rr + 1) * row_tok
        keys = kvs[: rr + 1, :, :, :HEAD].reshape(limit, HEAD)
        values = kvs[: rr + 1, :, :, HEAD:].reshape(limit, HEAD)
        mine = slice(rr * sub, (rr + 1) * sub)
        stack = lambda ref: jnp.concatenate(
            [ref[mine, h * HEAD : (h + 1) * HEAD] for h in range(heads)], axis=0
        )
        qh, gh = stack(qs), stack(grads)
        place = lax.broadcasted_iota(jnp.int32, (limit, heads * sub), 0)
        lane = lax.broadcasted_iota(jnp.int32, (1, heads * sub), 1)
        here = rr * row_tok + c * sub + lax.rem(lane, sub)
        first = jnp.zeros_like(here)
        for end in ends:
            first = jnp.where(here >= end, end, first)
        s = jnp.where(
            (place >= first) & (place <= here), dot(keys, qh, 1, 1) * scale, masked_score
        )
        e = jnp.exp(s - jnp.max(s, axis=0, keepdims=True))
        p = e * (1.0 / jnp.sum(e, axis=0, keepdims=True))
        g = dot(values, gh, 1, 1)
        ds = (p * (g - jnp.sum(p * g, axis=0, keepdims=True))).astype(BF)
        dv = dot(p.astype(BF), gh)
        dk = dot(ds, qh) * scale
        if rr == R - 1:
            dkv[:, :HEAD] = dk
            dkv[:, HEAD:] = dv
        else:
            dkv[:limit, :HEAD] += dk
            dkv[:limit, HEAD:] += dv
        dqs = dot(ds, keys, 0, 0) * scale
        for h in range(heads):
            dq[mine, h * HEAD : (h + 1) * HEAD] = dqs[h * sub : (h + 1) * sub]
        if rr == R - 2:
            rs_d.step(1)
            for i, b in enumerate((c, net.across_c)):
                out_x[i].wait_recv()
                s_o[2 * i : 2 * i + 2] = (
                    woo[pl.ds(2 * b, 2)].astype(F32) + wox[i].astype(F32)
                ).astype(BF)
    sib_c = c + 1 - 2 * lax.rem(c, 2)
    far_c = net.across_c
    far_sib_c = far_c + 1 - 2 * lax.rem(far_c, 2)
    dkv16[...] = dkv[...].astype(BF).reshape(dkv16.shape)
    dk_copies = [
        net.copy(dkv16.at[:, far_sib_c], dk_sib.at[1], net.sibling),
        net.copy(dkv16.at[:, sib_c], dk_sib.at[0], net.sibling),
    ]
    for cp in dk_copies:
        cp.start()
    dk_copies[0].wait_recv()
    dk_in[0] = (dkv16[:, far_c].astype(F32) + dk_sib[1].astype(F32)).astype(BF)
    dk_copies.append(net.copy(dk_in.at[0], dk_in.at[1], net.across))
    dk_copies[2].start()
    sum_o = BlockSum(net, halves(s_o, x_o.shape[1]), halves(s_o, x_o.shape[1]), x_o, y_o)
    sum_o.start()
    rs_d.step(2)
    for cp in loads[6:]:
        cp.wait()
    sum_g.add()
    sum_g.pass_on(o_gb)
    slots = dkv16[:, c].astype(F32)
    dk_copies[1].wait_recv()
    slots = slots + dk_sib[0].astype(F32)
    dk_copies[2].wait_recv()
    slots = slots + dk_in[1].astype(F32)
    slots = slots.reshape(n_tok, 2 * HEAD)
    joint[:, :qw] = turn(dq[...], cos2[...], -sin2[...]).astype(BF)
    joint[:, qw : qw + HEAD] = turn(slots[:, :HEAD], cos2[...], -sin2[...]).astype(BF)
    joint[:, qw + HEAD :] = slots[:, HEAD:].astype(BF)
    part[...] = dot(joint[...], wjs[...], 1, 1).astype(BF).reshape(R, sub, width)
    rs = LineSum(net, part, rbu, rbd)
    rs.step(0)
    total = dot(nall[...].reshape(n_tok, width), joint[...], 0, 0)
    wjo[...] = total.astype(BF).reshape(wjo.shape)
    joint_x = [net.copy(wjo.at[pl.ds(2 * b, 2)], wjx.at[i], net.sibling) for i, b in enumerate(sib_blocks)]
    for cp in joint_x:
        cp.start()
    bias = jnp.sum(joint[...].astype(F32), axis=0, keepdims=True)
    for i, b in enumerate((c, net.across_c)):
        joint_x[i].wait_recv()
        s_j[2 * i : 2 * i + 2] = (
            wjo[pl.ds(2 * b, 2)].astype(F32) + wjx[i].astype(F32)
        ).astype(BF)
    sum_j = BlockSum(net, halves(s_j, x_j.shape[1]), halves(s_j, x_j.shape[1]), x_j, y_j)
    sum_j.start()
    sum_u.add()
    sum_u.pass_on(o_ub)
    rs_d.step(3)
    lay[0] = mid[...]
    rs_d.total_into(lay.at[0])
    jk[...] = lay[0].astype(BF)
    rs.step(1)
    sum_o.add()
    sum_o.pass_on(o_ob)
    rs.step(2)
    sum_j.add()
    sum_j.pass_on(jb)
    layer_x = to_columns(jk, o_layer)
    keeps = [
        net.here(src.at[net.h], dst)
        for src, dst in ((s_g, o_ga), (s_u, o_ua), (s_o, o_oa))
    ]
    for cp in keeps:
        cp.start()
    rs.step(3)
    lay[1] = jnp.zeros_like(lay[1])
    rs.total_into(lay.at[1])
    grad = lay[1]
    x = x_in[...].astype(F32)
    inv = lax.rsqrt(jnp.mean(x * x, axis=-1, keepdims=True) + epsilon)
    normal = x * inv
    e = grad * gains[0:1, :width]
    back = inv * (e - normal * jnp.mean(e * normal, axis=-1, keepdims=True))
    gain_attn = jnp.sum(grad * normal, axis=0, keepdims=True)
    for k in range(C):
        cut = slice(k * block, (k + 1) * block)
        v1[k, :, :block] = jnp.broadcast_to(gain_attn[:, cut], (8, block))
        v1[k, :, block : 2 * block] = gain_mlp[:, cut]
        v1[k, :, 2 * block :] = jnp.broadcast_to(bias, (8, bias.shape[1]))
    v_copies = []
    for k in range(1, C):
        to, frm = lax.rem(c + k, C), lax.rem(c + C - k, C)
        i = net.n
        net.n += 1
        out = net.like(i, v1.at[to], v1in.at[c], net.at_col(to))
        out.start()
        v_copies.append((out, net.like(i, v1.at[to], v1in.at[frm], net.at_col(to)), frm))
    jk2[...] = (gmid[...] + back).astype(BF)
    input_x = to_columns(jk2, o_input)
    sum_j.finish()
    ja = s_j.at[net.h]
    own_cols = pl.ds(pl.multiple_of(qw + slot * HEAD, HEAD), HEAD)
    mate_cols = pl.ds(pl.multiple_of(qw + (1 - slot) * HEAD, HEAD), HEAD)
    jgot[0] = ja[:, mate_cols].astype(F32) + jb[:, mate_cols].astype(F32)
    slot_x = net.copy(jgot.at[0], jgot.at[1], net.at_row(partner_r))
    slot_x.start()
    o_j[:, :qw] = ja[:, :qw].astype(F32) + jb[:, :qw].astype(F32)
    total = v1[c]
    for _, inc, frm in v_copies:
        inc.wait_recv()
        total = total + v1in[frm]
    v2[...] = total
    far = []
    for same in (1, 0):
        for k in range(R):
            if same and k == 0:
                continue
            to, frm = lax.rem(r + k, R), lax.rem(r + R - k, R)
            i = net.n
            net.n += 1
            dst_d = net.d if same else net.mate[0]
            hs = net.h if same else net.other_h
            out = net.like(i, v2, v2in.at[net.h, r], (dst_d, to, c))
            out.start()
            far.append((out, net.like(i, v2, v2in.at[hs, frm], (dst_d, to, c))))
    v2in[net.h, r] = total
    slot_x.wait_recv()
    o_j[:, qw:] = ja[:, own_cols].astype(F32) + jb[:, own_cols].astype(F32) + jgot[1]
    for g in (sum_g, sum_u, sum_o):
        g.finish()
    for cp in sum_d:
        cp.wait()
    for cp in keeps:
        cp.wait()
    for _, inc in far:
        inc.wait_recv()
    gain_sum = v2in[0, 0, :, : 2 * block]
    for hh in (0, 1):
        for k in range(R):
            if hh or k:
                gain_sum = gain_sum + v2in[hh, k, :, : 2 * block]
    o_vec[:, : 2 * block] = gain_sum
    o_vec[:, 2 * block : 2 * block + qw] = (
        v2in[0, r, :, 2 * block : 2 * block + qw] + v2in[1, r, :, 2 * block : 2 * block + qw]
    )
    cols = pl.ds(pl.multiple_of(2 * block + qw + slot * HEAD, HEAD), HEAD)
    o_vec[:, 2 * block + qw :] = (
        v2in[0, r, :, cols] + v2in[1, r, :, cols]
        + v2in[0, partner_r, :, cols] + v2in[1, partner_r, :, cols]
    )
    settle(layer_x)
    settle(input_x)
    for g in (g_m, rs_d, rs):
        g.finish()
    for cp in out_x + joint_x + [slot_x]:
        cp.wait_send()
    for cp in dk_copies:
        cp.wait_send()
    for cps in v_copies + far:
        cps[0].wait_send()


def backward(sizes, gmid, x_in, mid, gains, gain_mlp, lengths, turns, normed, q, kv, att, wj, wo,
             down, sm, sx, sg, su):
    dp, R, C = sizes
    sub, width = gmid.shape
    block = width // C
    n, qw = q.shape
    jw = wj.shape[1]
    ff = sg.shape[2]
    shape = jax.ShapeDtypeStruct
    d2, g2, w2, j2 = (ff // 2, block), (block // 2, ff), (qw // 2, block), (block // 2, jw)
    vec = 2 * block + jw
    outs = [
        (shape((C * sub, block), BF), VMEM), (shape((C * sub, block), BF), VMEM),
        (shape((8, vec - HEAD), F32), VMEM), (shape((block // 2, jw - HEAD), F32), VMEM),
        (shape(d2, BF), ANY), (shape(g2, BF), ANY), (shape(g2, BF), ANY),
        (shape(g2, BF), ANY), (shape(g2, BF), ANY), (shape(w2, BF), ANY), (shape(w2, BF), ANY),
    ]
    v = pltpu.VMEM
    four = lambda s: v((4,) + s, BF)

    def landing(s):
        cut = third(s[0])
        return [v((2, cut) + s[1:], BF), v((2, s[0] - cut) + s[1:], BF)]

    x_g, y_g = landing(g2)
    x_o, y_o = landing(w2)
    x_j, y_j = landing(j2)
    line = v((R, sub, width), BF)
    return pl.pallas_call(
        functools.partial(backward_kernel, sizes),
        out_shape=[o for o, _ in outs],
        in_specs=[VMEM] * 5 + [SMEM, VMEM] + [ANY] * 11,
        out_specs=[s for _, s in outs],
        scratch_shapes=[
            line, line, v((n, qw), BF), v(kv.shape, BF), v((n, qw), BF), v((width, jw), BF),
            v((qw, width), BF), line, line, line, line, line, line, v((n, qw), BF), v((n, qw), F32),
            v((n * C, 2 * HEAD), F32), v(kv.shape, BF), v((2, R, sub, 2 * HEAD), BF),
            v((2, R, sub, 2 * HEAD), BF),
            v((n, jw), BF), v((2, sub, width), F32),
            four(g2), four(g2), x_g, x_g, y_g, y_g,
            v((8,) + j2, BF), v((2, 2) + j2, BF), four(j2), x_j, y_j,
            v((8,) + w2, BF), v((2, 2) + w2, BF), four(w2), x_o, y_o,
            v(j2, BF), v((sub, width), BF), v((sub, width), BF), v((2, j2[0], HEAD), F32),
            v((C, 8, vec), F32), v((C, 8, vec), F32), v((8, vec), F32), v((2, R, 8, vec), F32),
            pltpu.SemaphoreType.DMA((128,)), pltpu.SemaphoreType.DMA((128,)),
            pltpu.SemaphoreType.DMA((24,)),
        ],
        compiler_params=pltpu.CompilerParams(
            collective_id=3, has_side_effects=True, vmem_limit_bytes=VMEM_LIMIT
        ),
        name="backward",
    )(gmid, x_in, mid, gains, gain_mlp, lengths, turns, normed, q, kv, att, wj, wo, down, sm, sx, sg, su)


def finish_kernel(
    d, layer, inp, vec, joint, da, db, ga, gb, ua, ub, oa, ob,
    o_layer, o_input, o_again, o_q, o_qb, o_kv, o_kvb, o_out, o_fgain, o_gate, o_up, o_down,
    a0, a1, a2, b0, b1, b2, f0, f1, f2, sem_in, sem_out,
):
    work = ((da, db, a0, b0, f0, o_down), (ga, gb, a1, b1, f1, o_gate), (ua, ub, a2, b2, f2, o_up))
    loads = []
    for i, (a, b, av, bv, _, _) in enumerate(work):
        pair = [
            pltpu.make_async_copy(a, av, sem_in.at[2 * i]),
            pltpu.make_async_copy(b, bv, sem_in.at[2 * i + 1]),
        ]
        for cp in pair:
            cp.start()
        loads.append(pair)
    block = layer.shape[1]
    qw = oa.shape[0] * 2
    o_layer[...] = layer[...]
    o_input[...] = inp[...]
    o_out[...] = oa[...].astype(F32) + ob[...].astype(F32)
    o_q[...] = joint[:, :qw]
    o_kv[...] = joint[:, qw:]
    second = d[0, 0] == 1
    o_again[...] = vec[0:1, :block]
    o_fgain[...] = vec[0:1, block : 2 * block]
    bias = vec[0:1, 2 * block :]
    pick = lambda v: jnp.where(second, v[:, v.shape[1] // 2 :], v[:, : v.shape[1] // 2])
    o_qb[...] = pick(bias[:, :qw])
    o_kvb[...] = pick(bias[:, qw:])
    outs = []
    for i, (_, _, av, bv, f, o) in enumerate(work):
        for cp in loads[i]:
            cp.wait()
        f[...] = av[...].astype(F32) + bv[...].astype(F32)
        cp = pltpu.make_async_copy(f, o, sem_out.at[i])
        cp.start()
        outs.append(cp)
    for cp in outs:
        cp.wait()


def finish(d, layer, inp, vec, joint, da, db, ga, gb, ua, ub, oa, ob):
    block, qw, kvw = layer.shape[1], oa.shape[0] * 2, joint.shape[1] - oa.shape[0] * 2
    f32 = lambda *s: jax.ShapeDtypeStruct(s, F32)
    like = lambda v: jax.ShapeDtypeStruct(v.shape, F32)
    outs = [
        (jax.ShapeDtypeStruct(layer.shape, BF), VMEM), (jax.ShapeDtypeStruct(inp.shape, BF), VMEM),
        (f32(1, block), VMEM), (f32(joint.shape[0], qw), VMEM), (f32(1, qw // 2), VMEM),
        (f32(joint.shape[0], kvw), VMEM), (f32(1, kvw // 2), VMEM), (like(oa), VMEM),
        (f32(1, block), VMEM), (like(ga), ANY), (like(ua), ANY), (like(da), ANY),
    ]
    v = pltpu.VMEM
    return pl.pallas_call(
        finish_kernel,
        out_shape=[o for o, _ in outs],
        in_specs=[SMEM] + [VMEM] * 4 + [ANY] * 6 + [VMEM] * 2,
        out_specs=[s for _, s in outs],
        scratch_shapes=[
            v(da.shape, BF), v(ga.shape, BF), v(ua.shape, BF), v(da.shape, BF), v(ga.shape, BF),
            v(ua.shape, BF), v(da.shape, F32), v(ga.shape, F32), v(ua.shape, F32),
            pltpu.SemaphoreType.DMA((6,)), pltpu.SemaphoreType.DMA((3,)),
        ],
        compiler_params=pltpu.CompilerParams(vmem_limit_bytes=VMEM_LIMIT),
        name="finish",
    )(d, layer, inp, vec, joint, da, db, ga, gb, ua, ub, oa, ob)


def on_device(
    tokens_in, seq_lengths, attention_gain, query_weight, query_bias, keyvalue_weight,
    keyvalue_bias, output_weight, feedforward_gain, gate_weight, up_weight, down_weight,
    cotangent,
):
    sizes = dp, rows, cols = tuple(lax.axis_size(a) for a in ("dp", "row", "col"))
    d, col = lax.axis_index("dp"), lax.axis_index("col")
    sub = tokens_in.shape[0] // cols
    block = tokens_in.shape[1]
    wq_width = query_weight.shape[1]
    r_i = jnp.arange(rows, dtype=jnp.int32)[:, None]
    i_i = jnp.arange(sub, dtype=jnp.int32)[None, :]
    places = (r_i * tokens_in.shape[0] + col * sub + i_i).reshape(-1, 1)
    first, end = jnp.zeros_like(places), 0
    for i in range(seq_lengths.shape[1] - 1):
        end = end + seq_lengths[0, i]
        first = jnp.where(places >= end, end, first)
    lane = jnp.arange(HEAD, dtype=jnp.int32)[None, :]
    rates = rope_base ** (-(lane % (HEAD // 2)).astype(F32) * (2.0 / HEAD))
    angles = (places - first).astype(F32) * rates
    sign = jnp.where(lane < HEAD // 2, -1.0, 1.0)
    turns = jnp.concatenate([jnp.cos(angles), jnp.sin(angles) * sign], axis=1)
    vectors = jnp.concatenate([attention_gain, feedforward_gain, query_bias, keyvalue_bias])
    vectors = jnp.broadcast_to(vectors.astype(F32)[None], (8, vectors.shape[0]))
    (x_own, middle, nmlp, gains, normed, queries, kv, attended, cot_all, w_joint, w_out,
     w_gate, w_up) = attention_forward(
        sizes, tokens_in, cotangent, query_weight, keyvalue_weight, output_weight, gate_weight.T,
        up_weight.T, vectors, seq_lengths, turns,
    )
    grad_middle, gain_mlp, down_part, da, sum_mate, sum_across, sum_gate, sum_up = feedforward(
        sizes, nmlp, middle, gains, cot_all, w_gate, w_up, down_weight, gate_weight.T, up_weight.T
    )
    layer_out, input_grad, vec, joint, db, ga, gb, ua, ub, oa, ob = backward(
        sizes, grad_middle, x_own, middle, gains, gain_mlp, seq_lengths, turns, normed, queries, kv,
        attended, w_joint, w_out, down_part, sum_mate, sum_across, sum_gate, sum_up,
    )
    if dp == 2:
        out = finish(
            d.reshape(1, 1), layer_out, input_grad, vec, joint, da, db, ga, gb, ua, ub, oa, ob
        )
        return tuple(v.reshape(-1) if v.shape[0] == 1 else v for v in out)
    h = d // (dp // 2)

    def rest_of_dp(v):
        full = jnp.concatenate([jnp.where(h == 0, v, 0.0), jnp.where(h == 1, v, 0.0)], axis=0)
        return lax.psum_scatter(full, "dp", scatter_dimension=0, tiled=True)

    vec = lax.psum(jnp.where(h == 0, vec[0], 0.0), "dp")

    def own_share(v):
        n = v.shape[0] // dp
        return lax.dynamic_slice_in_dim(v, d * n, n)

    both = lambda a, b: rest_of_dp(a.astype(F32) + b.astype(F32))
    joint = rest_of_dp(joint)
    bias = vec[2 * block :]
    return (
        layer_out, input_grad, vec[:block], joint[:, :wq_width], own_share(bias[:wq_width]),
        joint[:, wq_width:], own_share(bias[wq_width:]), both(oa, ob), vec[block : 2 * block],
        both(ga, gb), both(ua, ub), both(da, db),
    )


def solution(mesh):
    return jax.shard_map(
        on_device,
        mesh=mesh,
        in_specs=(
            P(("dp", "row"), "col"), P("dp", None), P("col"), P("col", "row"), P("row"),
            P("col", "row"), P("row"), P("row", "col"), P("col"), P("col", "row"),
            P("col", "row"), P("row", "col"), P(("dp", "row"), "col"),
        ),
        out_specs=(
            P(("dp", "row"), "col"), P(("dp", "row"), "col"), P("col"),
            P(("col", "dp"), "row"), P(("row", "dp")), P(("col", "dp"), "row"),
            P(("row", "dp")), P(("row", "dp"), "col"), P("col"), P(("col", "dp"), "row"),
            P(("col", "dp"), "row"), P(("row", "dp"), "col"),
        ),
        check_vma=False,
    )
```

```python
import functools

import jax
import jax.numpy as jnp
import numpy as np
from jax import lax
from jax.experimental import pallas as pl
from jax.experimental.pallas import tpu as pltpu
from jax.sharding import PartitionSpec as P

HEAD = 128
epsilon = 1e-06
rope_base = 1000000.0
masked_score = -1e30
BF = jnp.bfloat16
F32 = jnp.float32
MESH = pl.DeviceIdType.MESH
ANY = pl.BlockSpec(memory_space=pl.ANY)
VMEM = pl.BlockSpec(memory_space=pltpu.VMEM)
SMEM = pl.BlockSpec(memory_space=pltpu.SMEM)
VMEM_LIMIT = 63 * 2**20


def dot(a, b, ca=1, cb=0):
    return lax.dot_general(a, b, (((ca,), (cb,)), ((), ())), preferred_element_type=F32)


class Net:
    def __init__(self, sizes, send, recv, local):
        self.dp, self.R, self.C = sizes
        self.d = lax.axis_index("dp")
        self.r = lax.axis_index("row")
        self.c = lax.axis_index("col")
        half = self.dp // 2
        self.h = self.d // half
        self.send, self.recv, self.local = send, recv, local
        self.n = 0
        self.n_local = 0
        self.other_h = 1 - self.h
        self.mate = (lax.rem(self.d + half, self.dp), self.r, self.c)
        self.sibling = self.at_col(self.c + 1 - 2 * lax.rem(self.c, 2))
        self.across_c = lax.rem(self.c + 2, 4)
        self.across = self.at_col(self.across_c)

    def at_col(self, c):
        return (self.d, self.r, c)

    def at_row(self, r):
        return (self.d, r, self.c)

    def copy(self, src, dst, dev):
        i = self.n
        self.n += 1
        return pltpu.make_async_remote_copy(
            src_ref=src, dst_ref=dst, send_sem=self.send.at[i], recv_sem=self.recv.at[i],
            device_id=dev, device_id_type=MESH,
        )

    def like(self, copy_index, src, dst, dev):
        return pltpu.make_async_remote_copy(
            src_ref=src, dst_ref=dst, send_sem=self.send.at[copy_index],
            recv_sem=self.recv.at[copy_index], device_id=dev, device_id_type=MESH,
        )

    def here(self, src, dst):
        i = self.n_local
        self.n_local += 1
        return pltpu.make_async_copy(src, dst, self.local.at[i])

    def barrier(self):
        sem = pltpu.get_barrier_semaphore()
        for k in range(1, self.C):
            pl.semaphore_signal(
                sem, inc=1, device_id=self.at_col(lax.rem(self.c + k, self.C)), device_id_type=MESH
            )
        pl.semaphore_signal(sem, inc=1, device_id=self.mate, device_id_type=MESH)

        @pl.when(self.r > 0)
        def _():
            pl.semaphore_signal(sem, inc=1, device_id=self.at_row(self.r - 1), device_id_type=MESH)

        @pl.when(self.r < self.R - 1)
        def _():
            pl.semaphore_signal(sem, inc=1, device_id=self.at_row(self.r + 1), device_id_type=MESH)

        count = self.C + (self.r > 0).astype(jnp.int32) + (self.r < self.R - 1).astype(jnp.int32)
        pl.semaphore_wait(sem, count)


PARTS = 2


def shard(buf, j, q, parts):
    if len(buf.shape) == 4:
        return buf.at[q, j]
    n = buf.shape[1] // parts
    return buf.at[j, pl.ds(q * n, n)]


class LineGather:
    def __init__(self, net, buf, parts=PARTS):
        self.net, self.buf, self.parts = net, buf, parts
        self.base = net.n
        net.n += 2 * (net.R - 1) * parts

    def _copy(self, up, s, q, j):
        net = self.net
        b = shard(self.buf, jnp.clip(j, 0, net.R - 1), q, self.parts)
        to = jnp.minimum(net.r + 1, net.R - 1) if up else jnp.maximum(net.r - 1, 0)
        return net.like(self.base + 2 * (s * self.parts + q) + up, b, b, net.at_row(to))

    def step(self, s, which=None):
        net = self.net
        r, R = net.r, net.R
        for q in range(self.parts) if which is None else which:
            if s > 0:

                @pl.when(r - s >= 0)
                def _():
                    self._copy(1, s - 1, q, r - s).wait_recv()

            if s < R - 1:

                @pl.when((r - s >= 0) & (r < R - 1))
                def _():
                    self._copy(1, s, q, r - s).start()

            if s > 0:

                @pl.when(r + s < R)
                def _():
                    self._copy(0, s - 1, q, r + s).wait_recv()

            if s < R - 1:

                @pl.when((r + s < R) & (r > 0))
                def _():
                    self._copy(0, s, q, r + s).start()

    def finish(self):
        net = self.net
        r, R = net.r, net.R
        for s in range(R - 1):
            for q in range(self.parts):

                @pl.when((r - s >= 0) & (r < R - 1))
                def _():
                    self._copy(1, s, q, r - s).wait_send()

                @pl.when((r + s < R) & (r > 0))
                def _():
                    self._copy(0, s, q, r + s).wait_send()


class LineSum:
    def __init__(self, net, part, from_below, from_above, parts=PARTS):
        self.net, self.part, self.bu, self.bd, self.parts = net, part, from_below, from_above, parts
        self.base = net.n
        net.n += 2 * net.R * parts

    def _at(self, buf, j, q):
        return shard(buf, j, q, self.parts)

    def _copy(self, up, j, q):
        net = self.net
        j = jnp.clip(j, 0, net.R - 1)
        to = jnp.minimum(net.r + 1, net.R - 1) if up else jnp.maximum(net.r - 1, 0)
        return net.like(
            self.base + (2 * q + up) * net.R + j, self._at(self.part, j, q),
            self._at(self.bu if up else self.bd, j, q), net.at_row(to),
        )

    def _add(self, j, q, buf):
        mine, got = self._at(self.part, j, q), self._at(buf, j, q)
        mine[...] = (mine[...].astype(F32) + got[...].astype(F32)).astype(BF)

    def step(self, t, which=None):
        net = self.net
        r, R = net.r, net.R
        j = t - (R - 1 - r)
        k = R - 1 - (t - r)
        for q in range(self.parts) if which is None else which:

            @pl.when((j >= 0) & (r < R - 1))
            def _():
                self._copy(0, j, q).wait_recv()

            @pl.when((j >= 0) & (j < r))
            def _():
                @pl.when(r < R - 1)
                def _():
                    self._add(j, q, self.bd)

                self._copy(0, j, q).start()

            @pl.when((k <= R - 1) & (r > 0))
            def _():
                self._copy(1, k, q).wait_recv()

            @pl.when((k <= R - 1) & (k > r))
            def _():
                @pl.when(r > 0)
                def _():
                    self._add(k, q, self.bu)

                self._copy(1, k, q).start()

    def finish(self):
        net = self.net
        r, R = net.r, net.R
        for j in range(R):
            for q in range(self.parts):

                @pl.when(j < r)
                def _():
                    self._copy(0, j, q).wait_send()

                @pl.when(j > r)
                def _():
                    self._copy(1, j, q).wait_send()

    def total_into(self, out):
        net = self.net
        r, R = net.r, net.R
        n = out.shape[0] // self.parts
        for q in range(self.parts):
            mine = out.at[pl.ds(q * n, n)]
            mine[...] += self._at(self.part, r, q)[...].astype(F32)

            @pl.when(r < R - 1)
            def _():
                mine[...] += self._at(self.bd, r, q)[...].astype(F32)

            @pl.when(r > 0)
            def _():
                mine[...] += self._at(self.bu, r, q)[...].astype(F32)


class WeightGather:
    def __init__(self, net, src, full, by_rows, piece=0, pieces=1, keep=True):
        self.net, self.full, self.by_rows = net, full, by_rows
        if by_rows:
            self.n, self.w = full.shape[0] // net.C, full.shape[1]
        else:
            self.n, self.w = full.shape[0] // pieces, full.shape[1] // net.C
        self.first = piece * self.n
        if src is not None:
            src = src.at[pl.ds(self.first, self.n)]
        c, p, h, o = net.c, net.across_c, net.h, net.other_h
        half = self.n // 2
        self.here = None
        if src is not None:
            if keep:
                self.here = net.here(src, self.view(c, 0, 2))
            own_half = src.at[pl.ds(pl.multiple_of(h * half, 16), half)]
            own = src
        else:
            own_half, own = self.view(c, h, 1), self.view(c, 0, 2)
        self.x = net.copy(own_half, self.view(c, h, 1), net.across)
        self.sib = net.copy(own, self.view(c, 0, 2), net.sibling)
        self.y = net.copy(self.view(p, h, 1), self.view(p, h, 1), net.mate)
        self.sib_h = net.copy(self.view(p, h, 1), self.view(p, h, 1), net.sibling)
        self.sib_o = net.copy(self.view(p, o, 1), self.view(p, o, 1), net.sibling)

    def view(self, b, h, halves):
        half = self.n // 2
        if self.by_rows:
            return self.full.at[pl.ds(pl.multiple_of(b * self.n + h * half, 16), halves * half)]
        return self.full.at[
            pl.ds(pl.multiple_of(self.first + h * half, 16), halves * half),
            pl.ds(pl.multiple_of(b * self.w, 128), self.w),
        ]

    def start(self):
        if self.here is not None:
            self.here.start()
        self.x.start()
        self.sib.start()

    def pass_x(self):
        self.x.wait_recv()
        self.y.start()
        self.sib_h.start()

    def pass_y(self):
        self.y.wait_recv()
        self.sib_o.start()

    def arrive(self):
        if self.here is not None:
            self.here.wait()
        self.sib.wait_recv()
        self.sib_h.wait_recv()
        self.sib_o.wait_recv()

    def finish(self):
        for cp in (self.x, self.sib, self.y, self.sib_h, self.sib_o):
            cp.wait_send()


class BlockSum:
    def __init__(self, net, source, piece, from_x, from_mate):
        self.net, self.piece = net, piece
        self.from_x, self.from_mate = from_x, from_mate
        o = net.other_h
        self.first = [net.copy(source(1, k, 0), from_x.at[k], net.across) for k in (0, 1)]
        self.first += [net.copy(source(i, o, 1), from_mate.at[i], net.mate) for i in (0, 1)]
        self.second = []

    def start(self):
        for cp in self.first:
            cp.start()

    def add(self):
        h = self.net.h
        for cp in self.first:
            cp.wait_recv()
        for ref, got in (
            (self.piece(0, 0, 0), self.from_x.at[0]), (self.piece(0, 1, 0), self.from_x.at[1]),
            (self.piece(0, h, 1), self.from_mate.at[0]), (self.piece(1, h, 1), self.from_mate.at[1]),
        ):
            ref[...] = (ref[...].astype(F32) + got[...].astype(F32)).astype(BF)

    def pass_on(self, got):
        net = self.net
        cut, rest = self.from_x.shape[1], self.from_mate.shape[1]
        self.second = [
            net.copy(self.piece(0, net.other_h, 0), got.at[pl.ds(0, cut)], net.mate),
            net.copy(self.piece(1, net.h, 1), got.at[pl.ds(cut, rest)], net.across),
        ]
        for cp in self.second:
            cp.start()

    def finish(self):
        for cp in self.first:
            cp.wait_send()
        for cp in self.second:
            cp.wait_send()
            cp.wait_recv()


def halves(ref, cut):
    def piece(i, h, ab):
        rows = pl.ds(cut, ref.shape[1] - cut) if ab else pl.ds(0, cut)
        return ref.at[2 * i + h, rows]

    return piece


def x_first(rows):
    return rows * 5 // 12 // 16 * 16


def turn(values, cos2, sin2):
    heads = []
    for i in range(values.shape[1] // HEAD):
        v = values[:, i * HEAD : (i + 1) * HEAD]
        heads.append(v * cos2 + pltpu.roll(v, HEAD // 2, 1) * sin2)
    return jnp.concatenate(heads, axis=1) if len(heads) > 1 else heads[0]


def attention_kernel(
    sizes,
    tok, cot, wq, wkv, wo, wg, wu, gain_a, gain_f, qb, kvb, lengths, rates,
    out_x, out_mid, out_nmlp, out_gains, out_turns, o_normed, o_q, o_kv, o_att, o_cot, o_wj, o_wo, o_wg, o_wu,
    xin, cin, small, gains, kvb2, nall, call, wj, wov, kv, qs, att, part, rbu, rbd, o_x, o_mid, o_nmlp, o_gains, turns,
    send, recv, local,
):
    net = Net(sizes, send, recv, local)
    R, C, r, c = net.R, net.C, net.r, net.c
    sub, width = nall.shape[1], nall.shape[2]
    block = tok.shape[1]
    row_tok = sub * C
    n_tok = sub * R
    qw = wq.shape[1]
    slot = lax.rem(r, 2)
    partner = net.at_row(r + 1 - 2 * slot)
    wide = lambda ref: jnp.broadcast_to(ref[...].astype(F32).reshape(1, ref.shape[0]), (8, ref.shape[0]))
    small[:, :block] = wide(gain_a)
    small[:, block:] = wide(gain_f)
    kvb2[slot] = wide(kvb)
    net.barrier()
    cos2, sin2 = turns.at[:, pl.ds(0, HEAD)], turns.at[:, pl.ds(HEAD, HEAD)]
    ends = [lengths[0, 0]]
    for i in range(1, lengths.shape[1] - 1):
        ends.append(ends[-1] + lengths[0, i])

    def place_of(rr):
        here = rr * row_tok + c * sub + lax.broadcasted_iota(jnp.int32, (sub, 1), 0)
        first = jnp.zeros((sub, 1), jnp.int32)
        for end in ends:
            first = jnp.where(here >= end, end, first)
        return here, first

    def spread(src, dst):
        mine = pl.multiple_of(c * sub, sub)
        local_copy = net.here(src.at[pl.ds(mine, sub)], dst.at[c])
        copies = []
        for k in range(1, C):
            to = lax.rem(c + k, C)
            frm = lax.rem(c + C - k, C)
            i = net.n
            net.n += 1
            rows = pl.ds(pl.multiple_of(to * sub, sub), sub)
            copies.append(
                (net.like(i, src.at[rows], dst.at[c], net.at_col(to)),
                 net.like(i, src.at[rows], dst.at[frm], net.at_col(to)))
            )
        return local_copy, copies

    def begin(pair):
        pair[0].start()
        for out, _ in pair[1]:
            out.start()

    def arrived(pair):
        pair[0].wait()
        for _, inc in pair[1]:
            inc.wait_recv()

    tok_in, cot_in = spread(tok, xin), spread(cot, cin)
    gain_own = net.here(small, gains.at[c])
    gain_own.start()
    gain_copies = []
    for k in range(1, C):
        to, frm = lax.rem(c + k, C), lax.rem(c + C - k, C)
        i = net.n
        net.n += 1
        out = net.like(i, small, gains.at[c], net.at_col(to))
        gain_copies.append((out, net.like(i, small, gains.at[frm], net.at_col(to))))
        out.start()
    begin(tok_in)
    own_rows = pl.ds(pl.multiple_of(c * block, block), block)
    col_own = pl.ds(pl.multiple_of(qw + slot * HEAD, HEAD), HEAD)
    col_mate = pl.ds(pl.multiple_of(qw + (1 - slot) * HEAD, HEAD), HEAD)
    kv_x = net.copy(wkv, wj.at[own_rows, col_own], partner)
    kv_in = net.like(net.n - 1, wkv, wj.at[own_rows, col_mate], partner)
    kv_x.start()
    kvb_x = net.copy(kvb2.at[slot], kvb2.at[slot], partner)
    kvb_in = net.like(net.n - 1, kvb2.at[slot], kvb2.at[1 - slot], partner)
    kvb_x.start()
    wq_own = net.here(wq, wj.at[own_rows, pl.ds(0, qw)])
    wq_own.start()
    wkv_own = net.here(wkv, wj.at[own_rows, col_own])
    wkv_own.start()
    g_joint = WeightGather(net, None, wj, True)
    g_out = WeightGather(net, wo, wov, False)
    bulk = [WeightGather(net, w, o, False, i, 2, False) for w, o in ((wg, o_wg), (wu, o_wu)) for i in (0, 1)]

    wq_own.wait()
    wkv_own.wait()
    kv_in.wait_recv()
    g_joint.start()
    g_out.start()
    begin(cot_in)
    bulk[0].start()
    bulk[1].start()

    arrived(tok_in)
    gain_own.wait()
    for _, inc in gain_copies:
        inc.wait_recv()
    for k in range(C):
        o_gains[:, k * block : (k + 1) * block] = gains[k, :, :block]
        o_gains[:, width + k * block : width + (k + 1) * block] = gains[k, :, block:]
    x = jnp.concatenate([xin[k].astype(F32) for k in range(C)], axis=1)
    o_mid[...] = x
    o_x[...] = x.astype(BF)
    inv = lax.rsqrt(jnp.mean(x * x, axis=-1, keepdims=True) + epsilon)
    nall[r] = (x * inv * o_gains[0:1, :width]).astype(BF)
    g_n = LineGather(net, nall)
    g_n.step(0)
    g_joint.pass_x()
    g_out.pass_x()
    g_n.step(1)
    g_joint.pass_y()
    g_out.pass_y()
    arrived(cot_in)
    for k in range(C):
        call[r, :, k * block : (k + 1) * block] = cin[k]
    lane = lax.broadcasted_iota(jnp.int32, (1, HEAD), 1)
    for rr in range(R):
        here, first = place_of(rr)
        angle = (here - first).astype(F32) * rates[...]
        mine = slice(rr * sub, (rr + 1) * sub)
        cos2[mine, :] = jnp.cos(angle)
        sin2[mine, :] = jnp.where(lane < HEAD // 2, -1.0, 1.0) * jnp.sin(angle)
    g_n.step(2)
    bulk[0].pass_x()
    g_joint.arrive()
    kvb_in.wait_recv()
    g_n.step(3)
    g_cot = LineGather(net, call)
    g_cot.step(0)
    bias = jnp.concatenate([wide(qb)[0:1], kvb2[0, 0:1, :], kvb2[1, 0:1, :]], axis=1)
    joint = dot(nall[...].reshape(n_tok, width), wj[...]) + bias
    key = turn(joint[:, qw : qw + HEAD], cos2[...], sin2[...]).astype(BF)
    kv[:, c, :, :HEAD] = key.reshape(R, sub, HEAD)
    kv[:, c, :, HEAD:] = joint[:, qw + HEAD :].astype(BF).reshape(R, sub, HEAD)
    sib_c = c + 1 - 2 * lax.rem(c, 2)
    far_c = net.across_c
    far_sib_c = far_c + 1 - 2 * lax.rem(far_c, 2)
    kv_far = net.copy(kv.at[:, c], kv.at[:, c], net.across)
    kv_sib = net.copy(kv.at[:, c], kv.at[:, c], net.sibling)
    kv_pass = net.copy(kv.at[:, far_c], kv.at[:, far_c], net.sibling)
    kv_far.start()
    kv_sib.start()
    qs[...] = turn(joint[:, :qw], cos2[...], sin2[...]).astype(BF)
    tail = [net.here(o_x, out_x), net.here(o_gains, out_gains), net.here(turns, out_turns)]
    for cp in tail:
        cp.start()
    out_normed = net.here(nall, o_normed)
    out_normed.start()
    out_wj = net.here(wj, o_wj)
    out_wj.start()
    kv_far.wait_recv()
    kv_pass.start()
    kv_sib.wait_recv()
    kv_pass.wait_recv()
    bulk[1].pass_x()
    bulk[2].start()
    bulk[3].start()
    bulk[0].pass_y()
    g_cot.step(1)
    out_kv = net.here(kv, o_kv)
    out_kv.start()
    scale = HEAD ** (-0.5)
    for rr in range(R):
        limit = (rr + 1) * row_tok
        keys = kv[: rr + 1, :, :, :HEAD].reshape(limit, HEAD)
        values = kv[: rr + 1, :, :, HEAD:].reshape(limit, HEAD)
        mine = slice(rr * sub, (rr + 1) * sub)
        place = lax.broadcasted_iota(jnp.int32, (sub, limit), 1)
        here, first = place_of(rr)
        allowed = (place >= first) & (place <= here)
        for h in range(qw // HEAD):
            cols = slice(h * HEAD, (h + 1) * HEAD)
            s = jnp.where(allowed, dot(qs[mine, cols], keys, 1, 1) * scale, masked_score)
            e = jnp.exp(s - jnp.max(s, axis=-1, keepdims=True))
            p = e * (1.0 / jnp.sum(e, axis=-1, keepdims=True))
            att[mine, cols] = dot(p.astype(BF), values).astype(BF)
    g_out.arrive()
    part[...] = dot(att[...], wov[...]).astype(BF).reshape(R, sub, width)
    rs = LineSum(net, part, rbu, rbd)
    rs.step(0)
    out_q = net.here(qs, o_q)
    out_q.start()
    out_att = net.here(att, o_att)
    out_att.start()
    out_wo = net.here(wov, o_wo)
    out_wo.start()
    g_cot.step(2)
    bulk[1].pass_y()
    bulk[2].pass_x()
    rs.step(1)
    g_cot.step(3)
    out_cot = net.here(call, o_cot)
    out_cot.start()
    bulk[3].pass_x()
    rs.step(2)
    bulk[2].pass_y()
    rs.step(3)
    rs.total_into(o_mid)
    mid = o_mid[...]
    inv = lax.rsqrt(jnp.mean(mid * mid, axis=-1, keepdims=True) + epsilon)
    o_nmlp[...] = (mid * inv * o_gains[0:1, width:]).astype(BF)
    for src, dst in ((o_mid, out_mid), (o_nmlp, out_nmlp)):
        cp = net.here(src, dst)
        cp.start()
        tail.append(cp)
    bulk[3].pass_y()
    for g in bulk:
        g.arrive()
    for g in [g_joint, g_out, g_n, g_cot, rs] + bulk:
        g.finish()
    for out, _ in tok_in[1] + cot_in[1] + gain_copies:
        out.wait_send()
    for cp in (kv_far, kv_sib, kv_pass):
        cp.wait_send()
    kv_x.wait_send()
    kvb_x.wait_send()
    for cp in tail + [out_normed, out_wj, out_kv, out_q, out_att, out_wo, out_cot]:
        cp.wait()


def attention_forward(
    sizes, tok, cot, wq, wkv, wo, wg, wu, gain_a, gain_f, qb, kvb, lengths, rates
):
    dp, R, C = sizes
    sub = tok.shape[0] // C
    block = tok.shape[1]
    width = block * C
    qw, jw = wq.shape[1], wq.shape[1] + 2 * HEAD
    n = sub * R
    ff = wg.shape[0]
    shape = jax.ShapeDtypeStruct
    outs = [
        (shape((sub, width), BF), ANY),
        (shape((sub, width), F32), ANY), (shape((sub, width), BF), ANY),
        (shape((8, 2 * width), F32), ANY), (shape((n, 2 * HEAD), F32), ANY),
        (shape((R, sub, width), BF), ANY),
        (shape((n, qw), BF), ANY), (shape((R, C, sub, 2 * HEAD), BF), ANY),
        (shape((n, qw), BF), ANY), (shape((R, sub, width), BF), ANY),
        (shape((width, jw), BF), ANY), (shape((qw, width), BF), ANY),
        (shape((ff, width), BF), ANY), (shape((ff, width), BF), ANY),
    ]
    return pl.pallas_call(
        functools.partial(attention_kernel, sizes),
        out_shape=[o for o, _ in outs],
        in_specs=[ANY] * 7 + [VMEM] * 4 + [SMEM, VMEM],
        out_specs=[s for _, s in outs],
        scratch_shapes=[
            pltpu.VMEM((C, sub, block), BF), pltpu.VMEM((C, sub, block), BF),
            pltpu.VMEM((8, 2 * block), F32), pltpu.VMEM((C, 8, 2 * block), F32), pltpu.VMEM((2, 8, HEAD), F32),
            pltpu.VMEM((R, sub, width), BF), pltpu.VMEM((R, sub, width), BF),
            pltpu.VMEM((width, jw), BF), pltpu.VMEM((qw, width), BF),
            pltpu.VMEM((R, C, sub, 2 * HEAD), BF), pltpu.VMEM((n, qw), BF),
            pltpu.VMEM((n, qw), BF), pltpu.VMEM((R, sub, width), BF),
            pltpu.VMEM((R, sub, width), BF), pltpu.VMEM((R, sub, width), BF),
            pltpu.VMEM((sub, width), BF), pltpu.VMEM((sub, width), F32),
            pltpu.VMEM((sub, width), BF), pltpu.VMEM((8, 2 * width), F32),
            pltpu.VMEM((n, 2 * HEAD), F32),
            pltpu.SemaphoreType.DMA((128,)), pltpu.SemaphoreType.DMA((128,)),
            pltpu.SemaphoreType.DMA((32,)),
        ],
        compiler_params=pltpu.CompilerParams(
            collective_id=1, has_side_effects=True, vmem_limit_bytes=VMEM_LIMIT
        ),
        name="attention_forward",
    )(tok, cot, wq, wkv, wo, wg, wu, gain_a, gain_f, qb, kvb, lengths, rates)


def feedforward_kernel(
    sizes,
    nmlp, in_mid, in_gains, cot, wg, wu, wd, own_g, own_u,
    out_gmid, out_gain, o_down, o_sd, o_sm, o_sx, o_sg, o_su,
    w_gate, w_up, w_down, xall, call, acc, hid, gg, gu, cc, sx, xt, part, rbu, rbd, dpart, g, x_d, y_d, o_gmid, o_gain, mid, gains,
    send, recv, local,
):
    net = Net(sizes, send, recv, local)
    R, C, r, c = net.R, net.C, net.r, net.c
    sub, width = nmlp.shape
    block = width // C
    n_tok = sub * R
    n_part = n_tok // PARTS
    n = sub // PARTS
    ff = w_gate.shape[0]
    tile = acc.shape[2]
    wide = width // tile
    own_cols = [pl.ds(pl.multiple_of(b * block, HEAD), block) for b in (c, net.across_c)]
    pieces = 5
    g_down = [WeightGather(net, wd, w_down, False, i, pieces) for i in range(pieces)]
    in_x = [net.here(nmlp.at[pl.ds(q * n, n)], xall.at[q, r]) for q in range(PARTS)]
    in_norm = [net.here(in_mid, mid), net.here(in_gains, gains)]
    for cp in in_x + in_norm:
        cp.start()
    in_cot = [net.here(cot.at[:, pl.ds(q * n, n)], call.at[q]) for q in range(PARTS)]
    for cp in in_cot:
        cp.start()
    in_w = []
    for full, own, w in ((wg, own_g, w_gate), (wu, own_u, w_up)):
        for k in range(C):
            cols = pl.ds(pl.multiple_of(lax.rem(c + k, C) * block, HEAD), block)
            cp = net.here(full.at[:, cols] if k else own, w.at[:, cols])
            cp.start()
            in_w.append(cp)
    if hid.shape[1] > ff:
        for ref in (hid, gg, gu):
            ref[:n_tok, ff:] = jnp.zeros((n_tok, hid.shape[1] - ff), BF)
    net.barrier()
    for cp in in_x:
        cp.wait()
    g_x = LineGather(net, xall)
    g_x.step(0)
    g_down[0].start()
    g_down[1].start()
    for cp in in_cot:
        cp.wait()
    to_sibling = []

    def hand(src, dst):
        cp = net.copy(src, dst, net.sibling)
        cp.start()
        to_sibling.append(cp)

    hand(call, dpart)
    for i in (0, 1):
        cc[0, :, :, :, i * block : (i + 1) * block] = call[:, :, :, own_cols[i]]

    def pass_x(i):
        g_down[i].pass_x()
        if i + 2 < pieces:
            g_down[i + 2].start()

    acts_out = [
        [
            net.copy(
                ref.at[pl.ds(q * n_part, n_part)], ref.at[pl.ds(n_tok + q * n_part, n_part)],
                net.sibling,
            )
            for ref in (hid, gg, gu)
        ]
        for q in range(PARTS)
    ]
    x_out = net.copy(xall, sx, net.sibling)
    to_sibling += [cp for pair in acts_out for cp in pair] + [x_out]
    rs = LineSum(net, part, rbu, rbd)
    full = ff // tile
    rest = pl.ds(full * tile, ff - full * tile)

    def act(q, rows, back):
        mine = pl.ds(pl.multiple_of(q * n_part, n_part), n_part)
        x = xall[q].reshape(n_part, width)
        gate = dot(x, w_gate[rows, :], 1, 1)
        up = dot(x, w_up[rows, :], 1, 1)
        s = jax.nn.sigmoid(gate)
        silu = gate * s
        hid[mine, rows] = (silu * up).astype(BF)
        gg[mine, rows] = (back * up * s * (1.0 + gate * (1.0 - s))).astype(BF)
        gu[mine, rows] = (back * silu).astype(BF)

    pass_x(0)
    g_x.step(1, (0,))
    pass_x(1)
    g_down[0].pass_y()
    pass_x(2)
    g_x.step(2, (0,))
    g_x.step(1, (1,))
    g_down[1].pass_y()
    pass_x(3)
    g_down[0].arrive()
    g_down[1].arrive()

    @pl.loop(0, PARTS)
    def _(q):
        @pl.loop(0, full)
        def _(t):
            rows = pl.ds(pl.multiple_of(t * tile, tile), tile)

            @pl.when(q == 0)
            def _():
                @pl.when(t == 1)
                def _():
                    g_down[3].pass_y()
                    g_down[2].arrive()

                @pl.when(t == 2)
                def _():
                    g_x.step(2, (1,))
                    g_down[3].arrive()

                @pl.when(t == 3)
                def _():
                    g_down[4].pass_y()
                    g_down[4].arrive()

                acc[t] = dot(call[...].reshape(n_tok, width), w_down[rows, :], 1, 1)

                @pl.when(t == 0)
                def _():
                    g_down[2].pass_y()
                    g_x.step(3, (0,))
                    pass_x(4)
                    for cp in in_w:
                        cp.wait()

            act(q, rows, acc[t, pl.ds(pl.multiple_of(q * n_part, n_part), n_part)])

            @pl.when((q == 1) & (t == full - 1))
            def _():
                rs.step(1, (0,))

        act(q, rest, dot(call[q].reshape(n_part, width), w_down[rest, :], 1, 1))

        @pl.when(q == 0)
        def _():
            g_x.step(3, (1,))

        for k in range(PARTS):

            @pl.when(q == k)
            def _():
                for cp in acts_out[k]:
                    cp.start()

        mine = pl.ds(pl.multiple_of(q * n_part, n_part), n_part)

        @pl.loop(0, wide)
        def _(i):
            cols = pl.ds(pl.multiple_of(i * tile, tile), tile)
            total = dot(gg[mine, :ff], w_gate[:, cols]) + dot(gu[mine, :ff], w_up[:, cols])
            part[q, :, :, cols] = total.astype(BF).reshape(R, n, tile)

        @pl.when(q == 0)
        def _():
            rs.step(0, (0,))
            x_out.start()

        @pl.when(q == 1)
        def _():
            rs.step(0, (1,))
            rs.step(2, (0,))

    for g_piece in g_down:
        g_piece.finish()
    for cp in to_sibling:
        cp.wait_recv()
    for i in (0, 1):
        cc[1, :, :, :, i * block : (i + 1) * block] = dpart[:, :, :, own_cols[i]]
    outs = []

    def all_tiles(body):
        @pl.loop(0, full)
        def _(t):
            body(pl.ds(pl.multiple_of(t * tile, tile), tile))

        body(rest)

    def down_grad(rows):
        total = dot(hid[:, rows], cc[...].reshape(2 * n_tok, 2 * block), 0, 0)
        w_gate[rows, : 2 * block] = total.astype(BF)

    all_tiles(down_grad)
    half_ff = ff // 2
    cut = x_d.shape[1]

    def down_piece(i, h, ab):
        first, count = (cut, half_ff - cut) if ab else (0, cut)
        return w_gate.at[
            pl.ds(pl.multiple_of(h * half_ff + first, 16), count), pl.ds(i * block, block)
        ]

    sum_d = BlockSum(net, down_piece, down_piece, x_d, y_d)
    sum_d.start()
    rs.step(1, (1,))
    rs.step(3, (0,))

    @pl.loop(0, wide)
    def _(i):
        cols = pl.ds(pl.multiple_of(i * tile, tile), tile)
        total = dot(hid[:n_tok, :ff], w_down[:, cols])
        dpart[:, :, :, cols] = total.astype(BF).reshape(PARTS, R, n, tile)

    rs.step(2, (1,))
    out_down = [net.here(dpart.at[q], o_down.at[:, pl.ds(q * n, n)]) for q in range(PARTS)]
    for cp in out_down:
        cp.start()
    for i in (0, 1):
        rows = slice(i * block, (i + 1) * block)
        xt[rows, :n_tok] = xall[:, :, :, own_cols[i]].reshape(n_tok, block).T
        xt[rows, n_tok:] = sx[:, :, :, own_cols[i]].reshape(n_tok, block).T
    for src, o in ((gg, o_sg), (gu, o_su)):
        if outs:
            outs.pop().wait()

        def grad(cols):
            total = dot(xt[...], src[:, cols])
            g[:, :, cols] = total.astype(BF).reshape(4, g.shape[1], cols.size)

        all_tiles(grad)
        cp = net.here(g, o)
        cp.start()
        outs.append(cp)
        if src is gg:
            rs.step(3, (1,))
    o_gmid[...] = jnp.zeros_like(o_gmid)
    rs.total_into(o_gmid)
    for cp in in_norm:
        cp.wait()
    grad = o_gmid[...]
    m = mid[...]
    inv = lax.rsqrt(jnp.mean(m * m, axis=-1, keepdims=True) + epsilon)
    normal = m * inv
    e = grad * gains[0:1, width:]
    back = inv * (e - normal * jnp.mean(e * normal, axis=-1, keepdims=True))
    o_gain[...] = jnp.broadcast_to(jnp.sum(grad * normal, axis=0, keepdims=True), o_gain.shape)
    for q in range(PARTS):
        rows = slice(q * n, (q + 1) * n)
        o_gmid[rows] = call[q, r].astype(F32) + back[rows]
    for src, dst in ((o_gmid, out_gmid), (o_gain, out_gain)):
        cp = net.here(src, dst)
        cp.start()
        outs.append(cp)
    rs.finish()
    sum_d.add()
    own_half = w_gate.at[
        pl.ds(pl.multiple_of(net.h * half_ff, 16), half_ff), pl.ds(0, block)
    ]
    for src, dst in (
        (own_half, o_sd), (down_piece(0, net.other_h, 0), o_sm), (down_piece(1, net.h, 1), o_sx)
    ):
        cp = net.here(src, dst)
        cp.start()
        outs.append(cp)
    sum_d.finish()
    g_x.finish()
    for cp in to_sibling:
        cp.wait_send()
    for cp in outs + out_down:
        cp.wait()


def feedforward(sizes, nmlp, mid, gains, cot, wg, wu, wd, own_g, own_u):
    dp, R, C = sizes
    sub, width = nmlp.shape
    block = width // C
    n_tok = R * sub
    ff = wd.shape[0]
    tile = 512
    cut = ff // 4
    shape = jax.ShapeDtypeStruct
    outs = [
        (shape((sub, width), F32), ANY), (shape((8, width), F32), ANY),
        (shape((R, sub, width), BF), ANY), (shape((ff // 2, block), BF), ANY),
        (shape((cut, block), BF), ANY), (shape((ff // 2 - cut, block), BF), ANY),
        (shape((4, block // 2, ff), BF), ANY), (shape((4, block // 2, ff), BF), ANY),
    ]
    v = pltpu.VMEM
    line = v((PARTS, R, sub // PARTS, width), BF)
    acts = v((2 * n_tok, -(-ff // HEAD) * HEAD), BF)
    weight = v((ff, width), BF)
    return pl.pallas_call(
        functools.partial(feedforward_kernel, sizes),
        out_shape=[o for o, _ in outs],
        in_specs=[ANY] * 9,
        out_specs=[s for _, s in outs],
        scratch_shapes=[
            weight, weight, weight, line, line, v((ff // tile, n_tok, tile), F32), acts, acts, acts,
            v((2, PARTS, R, sub // PARTS, 2 * block), BF), line,
            v((2 * block, 2 * n_tok), BF), line, line, line, line, v((4, block // 2, ff), BF),
            v((2, cut, block), BF), v((2, ff // 2 - cut, block), BF),
            v((sub, width), F32), v((8, width), F32), v((sub, width), F32), v((8, 2 * width), F32),
            pltpu.SemaphoreType.DMA((128,)), pltpu.SemaphoreType.DMA((128,)),
            pltpu.SemaphoreType.DMA((32,)),
        ],
        compiler_params=pltpu.CompilerParams(
            collective_id=2, has_side_effects=True, vmem_limit_bytes=VMEM_LIMIT
        ),
        name="feedforward",
    )(nmlp, mid, gains, cot, wg, wu, wd, own_g, own_u)


def backward_kernel(
    sizes,
    in_gmid, in_x, in_mid, in_gains, in_gain_mlp, lengths, in_turns,
    normed, q, kv, att, wj, wo, down, sm, sx, sg, su,
    o_layer, o_input, out_vec, out_j, o_db, o_ga, o_gb, o_ua, o_ub, o_oa, o_ob,
    mall, nall, qs, kvs, atts, wjs, wos, dpart, drbu, drbd, part, rbu, rbd, grads, dq, dkv, dkv16, dk_sib, dk_in,
    joint, lay,
    s_g, s_u, x_g, x_u, y_g, y_u,
    wjo, wjx, s_j, x_j, y_j, woo, wox, s_o, x_o, y_o, jb, jk, jk2, jgot, v1, v1in, v2, v2in, o_vec, o_j,
    gmid, x_in, mid, gains, gain_mlp, turns,
    send, recv, local,
):
    net = Net(sizes, send, recv, local)
    R, C, r, c = net.R, net.C, net.r, net.c
    sub, width = in_gmid.shape
    block = width // C
    n_tok = sub * R
    row_tok = sub * C
    qw = qs.shape[1]
    slot = lax.rem(r, 2)
    cos2, sin2 = turns.at[:, pl.ds(0, HEAD)], turns.at[:, pl.ds(HEAD, HEAD)]
    partner_r = r + 1 - 2 * slot
    small_loads = [
        net.here(a, b) for a, b in
        ((in_gmid, gmid), (in_x, x_in), (in_mid, mid), (in_gains, gains), (in_gain_mlp, gain_mlp),
         (in_turns, turns))
    ]
    for cp in small_loads:
        cp.start()
    loads = [
        net.here(a, b) for a, b in
        ((wo, wos), (att, atts), (q, qs), (kv, kvs), (down, dpart), (sg, s_g), (su, s_u),
         (normed, nall), (wj, wjs))
    ]
    for cp in loads:
        cp.start()
    sem = pltpu.get_barrier_semaphore()
    half = net.dp // 2
    others = [(net.d, r, lax.rem(c + k, C)) for k in range(1, C)]
    others += [(net.d, lax.rem(r + k, R), c) for k in range(1, R)]
    others += [(net.mate[0], lax.rem(r + k, R), c) for k in range(R)]
    for dev in others:
        pl.semaphore_signal(sem, inc=1, device_id=dev, device_id_type=MESH)
    pl.semaphore_wait(sem, len(others))

    small_loads[0].wait()
    mall[r] = gmid[...].astype(BF)
    g_m = LineGather(net, mall)
    g_m.step(0)
    sum_g = BlockSum(net, halves(sg, x_g.shape[1]), halves(s_g, x_g.shape[1]), x_g, y_g)
    sum_u = BlockSum(net, halves(su, x_u.shape[1]), halves(s_u, x_u.shape[1]), x_u, y_u)
    sum_g.start()
    sum_u.start()
    g_m.step(1)
    for cp in loads[:6] + small_loads[1:]:
        cp.wait()
    g_m.step(2)
    sum_g.add()
    sum_g.pass_on(o_gb)
    g_m.step(3)
    rs_d = LineSum(net, dpart, drbu, drbd)
    rs_d.step(0)
    m_all = mall[...].reshape(n_tok, width)
    grads[...] = dot(m_all, wos[...], 1, 1).astype(BF)

    def to_columns(src, dst):
        rows = pl.ds(pl.multiple_of(c * sub, sub), sub)
        mine = net.here(src.at[:, pl.ds(pl.multiple_of(c * block, HEAD), block)], dst.at[rows])
        mine.start()
        pairs = []
        for k in range(1, C):
            to, frm = lax.rem(c + k, C), lax.rem(c + C - k, C)
            i = net.n
            net.n += 1
            cut = src.at[:, pl.ds(pl.multiple_of(to * block, HEAD), block)]
            out = net.like(i, cut, dst.at[rows], net.at_col(to))
            out.start()
            from_rows = pl.ds(pl.multiple_of(frm * sub, sub), sub)
            pairs.append((out, net.like(i, cut, dst.at[from_rows], net.at_col(to))))
        return mine, pairs

    def settle(exchange):
        exchange[0].wait()
        for out, inc in exchange[1]:
            inc.wait_recv()
            out.wait_send()

    sib_blocks = [b + 1 - 2 * lax.rem(b, 2) for b in (c, net.across_c)]
    total = dot(atts[...], m_all, 0, 0)
    for b in range(C):
        woo[2 * b : 2 * b + 2] = (
            total[:, b * block : (b + 1) * block].astype(BF).reshape(2, qw // 2, block)
        )
    out_x = [net.copy(woo.at[pl.ds(2 * b, 2)], wox.at[i], net.sibling) for i, b in enumerate(sib_blocks)]
    for cp in out_x:
        cp.start()
    scale = HEAD ** (-0.5)
    heads = qw // HEAD
    ends = [lengths[0, 0]]
    for i in range(1, lengths.shape[1] - 1):
        ends.append(ends[-1] + lengths[0, i])
    for rr in reversed(range(R)):
        limit = (rr + 1) * row_tok
        keys = kvs[: rr + 1, :, :, :HEAD].reshape(limit, HEAD)
        values = kvs[: rr + 1, :, :, HEAD:].reshape(limit, HEAD)
        mine = slice(rr * sub, (rr + 1) * sub)
        stack = lambda ref: jnp.concatenate(
            [ref[mine, h * HEAD : (h + 1) * HEAD] for h in range(heads)], axis=0
        )
        qh, gh = stack(qs), stack(grads)
        place = lax.broadcasted_iota(jnp.int32, (limit, heads * sub), 0)
        lane = lax.broadcasted_iota(jnp.int32, (1, heads * sub), 1)
        here = rr * row_tok + c * sub + lax.rem(lane, sub)
        first = jnp.zeros_like(here)
        for end in ends:
            first = jnp.where(here >= end, end, first)
        s = jnp.where(
            (place >= first) & (place <= here), dot(keys, qh, 1, 1) * scale, masked_score
        )
        e = jnp.exp(s - jnp.max(s, axis=0, keepdims=True))
        p = e * (1.0 / jnp.sum(e, axis=0, keepdims=True))
        g = dot(values, gh, 1, 1)
        ds = (p * (g - jnp.sum(p * g, axis=0, keepdims=True))).astype(BF)
        dv = dot(p.astype(BF), gh)
        dk = dot(ds, qh) * scale
        if rr == R - 1:
            dkv[:, :HEAD] = dk
            dkv[:, HEAD:] = dv
        else:
            dkv[:limit, :HEAD] += dk
            dkv[:limit, HEAD:] += dv
        dqs = dot(ds, keys, 0, 0) * scale
        for h in range(heads):
            dq[mine, h * HEAD : (h + 1) * HEAD] = dqs[h * sub : (h + 1) * sub]
        if rr == R - 2:
            rs_d.step(1)
            for i, b in enumerate((c, net.across_c)):
                out_x[i].wait_recv()
                s_o[2 * i : 2 * i + 2] = (
                    woo[pl.ds(2 * b, 2)].astype(F32) + wox[i].astype(F32)
                ).astype(BF)
    sib_c = c + 1 - 2 * lax.rem(c, 2)
    far_c = net.across_c
    far_sib_c = far_c + 1 - 2 * lax.rem(far_c, 2)
    dkv16[...] = dkv[...].astype(BF).reshape(dkv16.shape)
    dk_copies = [
        net.copy(dkv16.at[:, far_sib_c], dk_sib.at[1], net.sibling),
        net.copy(dkv16.at[:, sib_c], dk_sib.at[0], net.sibling),
    ]
    for cp in dk_copies:
        cp.start()
    dk_copies[0].wait_recv()
    dk_in[0] = (dkv16[:, far_c].astype(F32) + dk_sib[1].astype(F32)).astype(BF)
    dk_copies.append(net.copy(dk_in.at[0], dk_in.at[1], net.across))
    dk_copies[2].start()
    sum_o = BlockSum(net, halves(s_o, x_o.shape[1]), halves(s_o, x_o.shape[1]), x_o, y_o)
    sum_o.start()
    rs_d.step(2)
    for cp in loads[6:]:
        cp.wait()
    sum_u.add()
    sum_u.pass_on(o_ub)
    cut_d, rest_d = sm.shape[0], sx.shape[0]
    sum_d = [
        net.copy(sx, o_db.at[pl.ds(cut_d, rest_d)], net.across),
        net.copy(sm, o_db.at[pl.ds(0, cut_d)], net.mate),
    ]
    slots = dkv16[:, c].astype(F32)
    dk_copies[1].wait_recv()
    slots = slots + dk_sib[0].astype(F32)
    dk_copies[2].wait_recv()
    slots = slots + dk_in[1].astype(F32)
    slots = slots.reshape(n_tok, 2 * HEAD)
    joint[:, :qw] = turn(dq[...], cos2[...], -sin2[...]).astype(BF)
    joint[:, qw : qw + HEAD] = turn(slots[:, :HEAD], cos2[...], -sin2[...]).astype(BF)
    joint[:, qw + HEAD :] = slots[:, HEAD:].astype(BF)
    part[...] = dot(joint[...], wjs[...], 1, 1).astype(BF).reshape(R, sub, width)
    rs = LineSum(net, part, rbu, rbd)
    rs.step(0)
    total = dot(nall[...].reshape(n_tok, width), joint[...], 0, 0)
    wjo[...] = total.astype(BF).reshape(wjo.shape)
    joint_x = [net.copy(wjo.at[pl.ds(2 * b, 2)], wjx.at[i], net.sibling) for i, b in enumerate(sib_blocks)]
    for cp in joint_x:
        cp.start()
    bias = jnp.sum(joint[...].astype(F32), axis=0, keepdims=True)
    for i, b in enumerate((c, net.across_c)):
        joint_x[i].wait_recv()
        s_j[2 * i : 2 * i + 2] = (
            wjo[pl.ds(2 * b, 2)].astype(F32) + wjx[i].astype(F32)
        ).astype(BF)
    sum_j = BlockSum(net, halves(s_j, x_j.shape[1]), halves(s_j, x_j.shape[1]), x_j, y_j)
    sum_j.start()
    rs_d.step(3)
    lay[0] = mid[...]
    rs_d.total_into(lay.at[0])
    jk[...] = lay[0].astype(BF)
    layer_x = to_columns(jk, o_layer)
    sum_d[0].start()
    rs.step(1)
    sum_o.add()
    sum_o.pass_on(o_ob)
    rs.step(2)
    sum_j.add()
    sum_j.pass_on(jb)
    sum_d[1].start()
    keeps = [
        net.here(src.at[net.h], dst)
        for src, dst in ((s_g, o_ga), (s_u, o_ua), (s_o, o_oa))
    ]
    for cp in keeps:
        cp.start()
    rs.step(3)
    lay[1] = jnp.zeros_like(lay[1])
    rs.total_into(lay.at[1])
    grad = lay[1]
    x = x_in[...].astype(F32)
    inv = lax.rsqrt(jnp.mean(x * x, axis=-1, keepdims=True) + epsilon)
    normal = x * inv
    e = grad * gains[0:1, :width]
    back = inv * (e - normal * jnp.mean(e * normal, axis=-1, keepdims=True))
    gain_attn = jnp.sum(grad * normal, axis=0, keepdims=True)
    for k in range(C):
        cut = slice(k * block, (k + 1) * block)
        v1[k, :, :block] = jnp.broadcast_to(gain_attn[:, cut], (8, block))
        v1[k, :, block : 2 * block] = gain_mlp[:, cut]
        v1[k, :, 2 * block :] = jnp.broadcast_to(bias, (8, bias.shape[1]))
    v_copies = []
    for k in range(1, C):
        to, frm = lax.rem(c + k, C), lax.rem(c + C - k, C)
        i = net.n
        net.n += 1
        out = net.like(i, v1.at[to], v1in.at[c], net.at_col(to))
        out.start()
        v_copies.append((out, net.like(i, v1.at[to], v1in.at[frm], net.at_col(to)), frm))
    jk2[...] = (gmid[...] + back).astype(BF)
    input_x = to_columns(jk2, o_input)
    sum_j.finish()
    ja = s_j.at[net.h]
    own_cols = pl.ds(pl.multiple_of(qw + slot * HEAD, HEAD), HEAD)
    mate_cols = pl.ds(pl.multiple_of(qw + (1 - slot) * HEAD, HEAD), HEAD)
    jgot[0] = ja[:, mate_cols].astype(F32) + jb[:, mate_cols].astype(F32)
    slot_x = net.copy(jgot.at[0], jgot.at[1], net.at_row(partner_r))
    slot_x.start()
    o_j[:, :qw] = ja[:, :qw].astype(F32) + jb[:, :qw].astype(F32)
    total = v1[c]
    for _, inc, frm in v_copies:
        inc.wait_recv()
        total = total + v1in[frm]
    v2[...] = total
    far = []
    for same in (1, 0):
        for k in range(R):
            if same and k == 0:
                continue
            to, frm = lax.rem(r + k, R), lax.rem(r + R - k, R)
            i = net.n
            net.n += 1
            dst_d = net.d if same else net.mate[0]
            hs = net.h if same else net.other_h
            out = net.like(i, v2, v2in.at[net.h, r], (dst_d, to, c))
            out.start()
            far.append((out, net.like(i, v2, v2in.at[hs, frm], (dst_d, to, c))))
    v2in[net.h, r] = total
    slot_x.wait_recv()
    o_j[:, qw:] = ja[:, own_cols].astype(F32) + jb[:, own_cols].astype(F32) + jgot[1]
    tail = [net.here(o_j, out_j)]
    tail[0].start()
    for g in (sum_g, sum_u, sum_o):
        g.finish()
    for cp in sum_d:
        cp.wait()
    for cp in keeps:
        cp.wait()
    for _, inc in far:
        inc.wait_recv()
    gain_sum = v2in[0, 0, :, : 2 * block]
    for hh in (0, 1):
        for k in range(R):
            if hh or k:
                gain_sum = gain_sum + v2in[hh, k, :, : 2 * block]
    o_vec[:, : 2 * block] = gain_sum
    o_vec[:, 2 * block : 2 * block + qw] = (
        v2in[0, r, :, 2 * block : 2 * block + qw] + v2in[1, r, :, 2 * block : 2 * block + qw]
    )
    cols = pl.ds(pl.multiple_of(2 * block + qw + slot * HEAD, HEAD), HEAD)
    o_vec[:, 2 * block + qw :] = (
        v2in[0, r, :, cols] + v2in[1, r, :, cols]
        + v2in[0, partner_r, :, cols] + v2in[1, partner_r, :, cols]
    )
    tail.append(net.here(o_vec, out_vec))
    tail[1].start()
    settle(layer_x)
    settle(input_x)
    for g in (g_m, rs_d, rs):
        g.finish()
    for cp in out_x + joint_x + [slot_x]:
        cp.wait_send()
    for cp in dk_copies:
        cp.wait_send()
    for cps in v_copies + far:
        cps[0].wait_send()
    for cp in tail:
        cp.wait()


def backward(sizes, gmid, x_in, mid, gains, gain_mlp, lengths, turns, normed, q, kv, att, wj, wo,
             down, sm, sx, sg, su):
    dp, R, C = sizes
    sub, width = gmid.shape
    block = width // C
    n, qw = q.shape
    jw = wj.shape[1]
    ff = sg.shape[2]
    shape = jax.ShapeDtypeStruct
    d2, g2, w2, j2 = (ff // 2, block), (block // 2, ff), (qw // 2, block), (block // 2, jw)
    vec = 2 * block + jw
    outs = [
        (shape((C * sub, block), BF), ANY), (shape((C * sub, block), BF), ANY),
        (shape((8, vec - HEAD), F32), ANY), (shape((block // 2, jw - HEAD), F32), ANY),
        (shape(d2, BF), ANY), (shape(g2, BF), ANY), (shape(g2, BF), ANY),
        (shape(g2, BF), ANY), (shape(g2, BF), ANY), (shape(w2, BF), ANY), (shape(w2, BF), ANY),
    ]
    v = pltpu.VMEM
    four = lambda s: v((4,) + s, BF)

    def landing(s):
        cut = x_first(s[0])
        return [v((2, cut) + s[1:], BF), v((2, s[0] - cut) + s[1:], BF)]

    x_g, y_g = landing(g2)
    x_o, y_o = landing(w2)
    x_j, y_j = landing(j2)
    line = v((R, sub, width), BF)
    return pl.pallas_call(
        functools.partial(backward_kernel, sizes),
        out_shape=[o for o, _ in outs],
        in_specs=[ANY] * 5 + [SMEM] + [ANY] * 12,
        out_specs=[s for _, s in outs],
        scratch_shapes=[
            line, line, v((n, qw), BF), v(kv.shape, BF), v((n, qw), BF), v((width, jw), BF),
            v((qw, width), BF), line, line, line, line, line, line, v((n, qw), BF), v((n, qw), F32),
            v((n * C, 2 * HEAD), F32), v(kv.shape, BF), v((2, R, sub, 2 * HEAD), BF),
            v((2, R, sub, 2 * HEAD), BF),
            v((n, jw), BF), v((2, sub, width), F32),
            four(g2), four(g2), x_g, x_g, y_g, y_g,
            v((8,) + j2, BF), v((2, 2) + j2, BF), four(j2), x_j, y_j,
            v((8,) + w2, BF), v((2, 2) + w2, BF), four(w2), x_o, y_o,
            v(j2, BF), v((sub, width), BF), v((sub, width), BF), v((2, j2[0], HEAD), F32),
            v((C, 8, vec), F32), v((C, 8, vec), F32), v((8, vec), F32), v((2, R, 8, vec), F32),
            v((8, vec - HEAD), F32), v((block // 2, jw - HEAD), F32),
            v(gmid.shape, F32), v(x_in.shape, BF), v(mid.shape, F32), v(gains.shape, F32),
            v(gain_mlp.shape, F32), v(turns.shape, F32),
            pltpu.SemaphoreType.DMA((128,)), pltpu.SemaphoreType.DMA((128,)),
            pltpu.SemaphoreType.DMA((32,)),
        ],
        compiler_params=pltpu.CompilerParams(
            collective_id=3, has_side_effects=True, vmem_limit_bytes=VMEM_LIMIT
        ),
        name="backward",
    )(gmid, x_in, mid, gains, gain_mlp, lengths, turns, normed, q, kv, att, wj, wo, down, sm, sx, sg, su)

def finish_kernel(
    d, vec, joint, da, db, ga, gb, ua, ub, oa, ob, layer, inp,
    o_again, o_fgain, o_qb, o_kvb, o_q, o_kv, o_out, o_gate, o_up, o_down, o_layer, o_input,
    vec_v, joint_v, da_v, db_v, ga_v, gb_v, ua_v, ub_v, oa_v, ob_v,
    layer_v, inp_v, again_v, fgain_v, qb_v, kvb_v, q_v, kv_v, out_v, gate_v, up_v, down_v, sem_in, sem_out,
):
    pairs = (
        (vec, vec_v), (joint, joint_v), (oa, oa_v), (ob, ob_v), (da, da_v), (db, db_v),
        (ga, ga_v), (gb, gb_v), (ua, ua_v), (ub, ub_v), (layer, layer_v), (inp, inp_v),
    )
    loads = [pltpu.make_async_copy(s, t, sem_in.at[i]) for i, (s, t) in enumerate(pairs)]
    for cp in loads:
        cp.start()
    stores = []

    def store(src, dst):
        cp = pltpu.make_async_copy(src, dst, sem_out.at[len(stores)])
        cp.start()
        stores.append(cp)

    block, qw = o_again.shape[0], o_q.shape[1]
    loads[0].wait()
    second = d[0, 0] == 1
    again_v[...] = vec_v[0, :block]
    fgain_v[...] = vec_v[0, block : 2 * block]
    bias = vec_v[0:1, 2 * block :]
    pick = lambda v: jnp.where(second, v[:, v.shape[1] // 2 :], v[:, : v.shape[1] // 2])
    qb_v[...] = pick(bias[:, :qw])[0]
    kvb_v[...] = pick(bias[:, qw:])[0]
    for src, dst in ((again_v, o_again), (fgain_v, o_fgain), (qb_v, o_qb), (kvb_v, o_kvb)):
        store(src, dst)
    loads[1].wait()
    q_v[...] = joint_v[:, :qw]
    kv_v[...] = joint_v[:, qw:]
    store(q_v, o_q)
    store(kv_v, o_kv)
    for i, (a, b, f, o) in enumerate(
        ((oa_v, ob_v, out_v, o_out), (da_v, db_v, down_v, o_down), (ga_v, gb_v, gate_v, o_gate),
         (ua_v, ub_v, up_v, o_up))
    ):
        loads[2 + 2 * i].wait()
        loads[3 + 2 * i].wait()
        f[...] = a[...].astype(F32) + b[...].astype(F32)
        store(f, o)
    for i, (src, dst) in enumerate(((layer_v, o_layer), (inp_v, o_input))):
        loads[10 + i].wait()
        store(src, dst)
    for cp in stores:
        cp.wait()


def finish(d, layer, inp, vec, joint, da, db, ga, gb, ua, ub, oa, ob):
    block, qw, kvw = layer.shape[1], oa.shape[0] * 2, joint.shape[1] - oa.shape[0] * 2
    f32 = lambda *s: jax.ShapeDtypeStruct(s, F32)
    like = lambda v: jax.ShapeDtypeStruct(v.shape, F32)
    results = [
        f32(block), f32(block), f32(qw // 2), f32(kvw // 2), f32(joint.shape[0], qw),
        f32(joint.shape[0], kvw), like(oa), like(ga), like(ua), like(da),
    ]
    v = lambda a: pltpu.VMEM(a.shape, a.dtype)
    out = pl.pallas_call(
        finish_kernel,
        out_shape=results + [jax.ShapeDtypeStruct(a.shape, BF) for a in (layer, inp)],
        in_specs=[SMEM] + [ANY] * 12,
        out_specs=[ANY] * 12,
        scratch_shapes=[v(a) for a in (vec, joint, da, db, ga, gb, ua, ub, oa, ob, layer, inp)]
        + [v(a) for a in results]
        + [pltpu.SemaphoreType.DMA((12,)), pltpu.SemaphoreType.DMA((12,))],
        compiler_params=pltpu.CompilerParams(vmem_limit_bytes=VMEM_LIMIT),
        name="finish",
    )(d, vec, joint, da, db, ga, gb, ua, ub, oa, ob, layer, inp)
    again, fgain, q_bias, kv_bias, q, kv, o, gate, up, down, layer, inp = out
    return layer, inp, again, q, q_bias, kv, kv_bias, o, fgain, gate, up, down


def on_device(
    tokens_in, seq_lengths, attention_gain, query_weight, query_bias, keyvalue_weight,
    keyvalue_bias, output_weight, feedforward_gain, gate_weight, up_weight, down_weight,
    cotangent,
):
    sizes = dp, rows, cols = tuple(lax.axis_size(a) for a in ("dp", "row", "col"))
    d, col = lax.axis_index("dp"), lax.axis_index("col")
    sub = tokens_in.shape[0] // cols
    block = tokens_in.shape[1]
    wq_width = query_weight.shape[1]
    lane = np.arange(HEAD) % (HEAD // 2)
    rates = jnp.asarray((rope_base ** (-lane * (2.0 / HEAD))).astype(np.float32)[None])
    (x_own, middle, nmlp, gains, turns, normed, queries, kv, attended, cot_all, w_joint, w_out,
     w_gate, w_up) = attention_forward(
        sizes, tokens_in, cotangent, query_weight, keyvalue_weight, output_weight, gate_weight.T,
        up_weight.T, attention_gain, feedforward_gain, query_bias, keyvalue_bias, seq_lengths, rates,
    )
    grad_middle, gain_mlp, down_part, da, sum_mate, sum_across, sum_gate, sum_up = feedforward(
        sizes, nmlp, middle, gains, cot_all, w_gate, w_up, down_weight, gate_weight.T, up_weight.T
    )
    layer_out, input_grad, vec, joint, db, ga, gb, ua, ub, oa, ob = backward(
        sizes, grad_middle, x_own, middle, gains, gain_mlp, seq_lengths, turns, normed, queries, kv,
        attended, w_joint, w_out, down_part, sum_mate, sum_across, sum_gate, sum_up,
    )
    if dp == 2:
        return finish(
            d.reshape(1, 1), layer_out, input_grad, vec, joint, da, db, ga, gb, ua, ub, oa, ob
        )
    h = d // (dp // 2)

    def rest_of_dp(v):
        full = jnp.concatenate([jnp.where(h == 0, v, 0.0), jnp.where(h == 1, v, 0.0)], axis=0)
        return lax.psum_scatter(full, "dp", scatter_dimension=0, tiled=True)

    vec = lax.psum(jnp.where(h == 0, vec[0], 0.0), "dp")

    def own_share(v):
        n = v.shape[0] // dp
        return lax.dynamic_slice_in_dim(v, d * n, n)

    both = lambda a, b: rest_of_dp(a.astype(F32) + b.astype(F32))
    joint = rest_of_dp(joint)
    bias = vec[2 * block :]
    return (
        layer_out, input_grad, vec[:block], joint[:, :wq_width], own_share(bias[:wq_width]),
        joint[:, wq_width:], own_share(bias[wq_width:]), both(oa, ob), vec[block : 2 * block],
        both(ga, gb), both(ua, ub), both(da, db),
    )


def solution(mesh):
    return jax.shard_map(
        on_device,
        mesh=mesh,
        in_specs=(
            P(("dp", "row"), "col"), P("dp", None), P("col"), P("col", "row"), P("row"),
            P("col", "row"), P("row"), P("row", "col"), P("col"), P("col", "row"),
            P("col", "row"), P("row", "col"), P(("dp", "row"), "col"),
        ),
        out_specs=(
            P(("dp", "row"), "col"), P(("dp", "row"), "col"), P("col"),
            P(("col", "dp"), "row"), P(("row", "dp")), P(("col", "dp"), "row"),
            P(("row", "dp")), P(("row", "dp"), "col"), P("col"), P(("col", "dp"), "row"),
            P(("col", "dp"), "row"), P(("row", "dp"), "col"),
        ),
        check_vma=False,
    )
```

```python
import functools

import jax
import jax.numpy as jnp
import numpy as np
from jax import lax
from jax.experimental import pallas as pl
from jax.experimental.pallas import tpu as pltpu
from jax.sharding import PartitionSpec as P

HEAD = 128
epsilon = 1e-06
rope_base = 1000000.0
masked_score = -1e30
BF = jnp.bfloat16
F32 = jnp.float32
MESH = pl.DeviceIdType.MESH
ANY = pl.BlockSpec(memory_space=pl.ANY)
VMEM = pl.BlockSpec(memory_space=pltpu.VMEM)
SMEM = pl.BlockSpec(memory_space=pltpu.SMEM)
VMEM_LIMIT = 63 * 2**20


def dot(a, b, ca=1, cb=0):
    return lax.dot_general(a, b, (((ca,), (cb,)), ((), ())), preferred_element_type=F32)


class Net:
    def __init__(self, sizes, send, recv, local):
        self.dp, self.R, self.C = sizes
        self.d = lax.axis_index("dp")
        self.r = lax.axis_index("row")
        self.c = lax.axis_index("col")
        half = self.dp // 2
        self.h = self.d // half
        self.send, self.recv, self.local = send, recv, local
        self.n = 0
        self.n_local = 0
        self.other_h = 1 - self.h
        self.mate = (lax.rem(self.d + half, self.dp), self.r, self.c)
        self.sibling = self.at_col(self.c + 1 - 2 * lax.rem(self.c, 2))
        self.across_c = lax.rem(self.c + 2, 4)
        self.across = self.at_col(self.across_c)

    def at_col(self, c):
        return (self.d, self.r, c)

    def at_row(self, r):
        return (self.d, r, self.c)

    def copy(self, src, dst, dev):
        i = self.n
        self.n += 1
        return pltpu.make_async_remote_copy(
            src_ref=src, dst_ref=dst, send_sem=self.send.at[i], recv_sem=self.recv.at[i],
            device_id=dev, device_id_type=MESH,
        )

    def like(self, copy_index, src, dst, dev):
        return pltpu.make_async_remote_copy(
            src_ref=src, dst_ref=dst, send_sem=self.send.at[copy_index],
            recv_sem=self.recv.at[copy_index], device_id=dev, device_id_type=MESH,
        )

    def here(self, src, dst):
        i = self.n_local
        self.n_local += 1
        return pltpu.make_async_copy(src, dst, self.local.at[i])

    def barrier(self):
        sem = pltpu.get_barrier_semaphore()
        for k in range(1, self.C):
            pl.semaphore_signal(
                sem, inc=1, device_id=self.at_col(lax.rem(self.c + k, self.C)), device_id_type=MESH
            )
        pl.semaphore_signal(sem, inc=1, device_id=self.mate, device_id_type=MESH)

        @pl.when(self.r > 0)
        def _():
            pl.semaphore_signal(sem, inc=1, device_id=self.at_row(self.r - 1), device_id_type=MESH)

        @pl.when(self.r < self.R - 1)
        def _():
            pl.semaphore_signal(sem, inc=1, device_id=self.at_row(self.r + 1), device_id_type=MESH)

        count = self.C + (self.r > 0).astype(jnp.int32) + (self.r < self.R - 1).astype(jnp.int32)
        pl.semaphore_wait(sem, count)


PARTS = 2


def shard(buf, j, q, parts):
    if len(buf.shape) == 4:
        return buf.at[q, j]
    n = buf.shape[1] // parts
    return buf.at[j, pl.ds(q * n, n)]


class LineGather:
    def __init__(self, net, buf, parts=PARTS):
        self.net, self.buf, self.parts = net, buf, parts
        self.base = net.n
        net.n += 2 * (net.R - 1) * parts

    def _copy(self, up, s, q, j):
        net = self.net
        b = shard(self.buf, jnp.clip(j, 0, net.R - 1), q, self.parts)
        to = jnp.minimum(net.r + 1, net.R - 1) if up else jnp.maximum(net.r - 1, 0)
        return net.like(self.base + 2 * (s * self.parts + q) + up, b, b, net.at_row(to))

    def step(self, s, which=None):
        net = self.net
        r, R = net.r, net.R
        for q in range(self.parts) if which is None else which:
            if s > 0:

                @pl.when(r - s >= 0)
                def _():
                    self._copy(1, s - 1, q, r - s).wait_recv()

            if s < R - 1:

                @pl.when((r - s >= 0) & (r < R - 1))
                def _():
                    self._copy(1, s, q, r - s).start()

            if s > 0:

                @pl.when(r + s < R)
                def _():
                    self._copy(0, s - 1, q, r + s).wait_recv()

            if s < R - 1:

                @pl.when((r + s < R) & (r > 0))
                def _():
                    self._copy(0, s, q, r + s).start()

    def finish(self):
        net = self.net
        r, R = net.r, net.R
        for s in range(R - 1):
            for q in range(self.parts):

                @pl.when((r - s >= 0) & (r < R - 1))
                def _():
                    self._copy(1, s, q, r - s).wait_send()

                @pl.when((r + s < R) & (r > 0))
                def _():
                    self._copy(0, s, q, r + s).wait_send()


class LineSum:
    def __init__(self, net, part, from_below, from_above, parts=PARTS):
        self.net, self.part, self.bu, self.bd, self.parts = net, part, from_below, from_above, parts
        self.base = net.n
        net.n += 2 * net.R * parts

    def _at(self, buf, j, q):
        return shard(buf, j, q, self.parts)

    def _copy(self, up, j, q):
        net = self.net
        j = jnp.clip(j, 0, net.R - 1)
        to = jnp.minimum(net.r + 1, net.R - 1) if up else jnp.maximum(net.r - 1, 0)
        return net.like(
            self.base + (2 * q + up) * net.R + j, self._at(self.part, j, q),
            self._at(self.bu if up else self.bd, j, q), net.at_row(to),
        )

    def _add(self, j, q, buf):
        mine, got = self._at(self.part, j, q), self._at(buf, j, q)
        mine[...] = (mine[...].astype(F32) + got[...].astype(F32)).astype(BF)

    def step(self, t, which=None):
        net = self.net
        r, R = net.r, net.R
        j = t - (R - 1 - r)
        k = R - 1 - (t - r)
        for q in range(self.parts) if which is None else which:

            @pl.when((j >= 0) & (r < R - 1))
            def _():
                self._copy(0, j, q).wait_recv()

            @pl.when((j >= 0) & (j < r))
            def _():
                @pl.when(r < R - 1)
                def _():
                    self._add(j, q, self.bd)

                self._copy(0, j, q).start()

            @pl.when((k <= R - 1) & (r > 0))
            def _():
                self._copy(1, k, q).wait_recv()

            @pl.when((k <= R - 1) & (k > r))
            def _():
                @pl.when(r > 0)
                def _():
                    self._add(k, q, self.bu)

                self._copy(1, k, q).start()

    def finish(self):
        net = self.net
        r, R = net.r, net.R
        for j in range(R):
            for q in range(self.parts):

                @pl.when(j < r)
                def _():
                    self._copy(0, j, q).wait_send()

                @pl.when(j > r)
                def _():
                    self._copy(1, j, q).wait_send()

    def total_into(self, out):
        net = self.net
        r, R = net.r, net.R
        n = out.shape[0] // self.parts
        for q in range(self.parts):
            mine = out.at[pl.ds(q * n, n)]
            mine[...] += self._at(self.part, r, q)[...].astype(F32)

            @pl.when(r < R - 1)
            def _():
                mine[...] += self._at(self.bd, r, q)[...].astype(F32)

            @pl.when(r > 0)
            def _():
                mine[...] += self._at(self.bu, r, q)[...].astype(F32)


class WeightGather:
    def __init__(self, net, src, full, by_rows, piece=0, pieces=1, keep=True):
        self.net, self.full, self.by_rows = net, full, by_rows
        if by_rows:
            self.n, self.w = full.shape[0] // net.C, full.shape[1]
        else:
            self.n, self.w = full.shape[0] // pieces, full.shape[1] // net.C
        self.first = piece * self.n
        if src is not None:
            src = src.at[pl.ds(self.first, self.n)]
        c, p, h, o = net.c, net.across_c, net.h, net.other_h
        half = self.n // 2
        self.here = None
        if src is not None:
            if keep:
                self.here = net.here(src, self.view(c, 0, 2))
            own_half = src.at[pl.ds(pl.multiple_of(h * half, 16), half)]
            own = src
        else:
            own_half, own = self.view(c, h, 1), self.view(c, 0, 2)
        self.x = net.copy(own_half, self.view(c, h, 1), net.across)
        self.sib = net.copy(own, self.view(c, 0, 2), net.sibling)
        self.y = net.copy(self.view(p, h, 1), self.view(p, h, 1), net.mate)
        self.sib_h = net.copy(self.view(p, h, 1), self.view(p, h, 1), net.sibling)
        self.sib_o = net.copy(self.view(p, o, 1), self.view(p, o, 1), net.sibling)

    def view(self, b, h, halves):
        half = self.n // 2
        if self.by_rows:
            return self.full.at[pl.ds(pl.multiple_of(b * self.n + h * half, 16), halves * half)]
        return self.full.at[
            pl.ds(pl.multiple_of(self.first + h * half, 16), halves * half),
            pl.ds(pl.multiple_of(b * self.w, 128), self.w),
        ]

    def start(self):
        if self.here is not None:
            self.here.start()
        self.x.start()
        self.sib.start()

    def pass_x(self):
        self.x.wait_recv()
        self.y.start()
        self.sib_h.start()

    def pass_y(self):
        self.y.wait_recv()
        self.sib_o.start()

    def arrive(self):
        if self.here is not None:
            self.here.wait()
        self.sib.wait_recv()
        self.sib_h.wait_recv()
        self.sib_o.wait_recv()

    def finish(self):
        for cp in (self.x, self.sib, self.y, self.sib_h, self.sib_o):
            cp.wait_send()


class BlockSum:
    def __init__(self, net, source, piece, from_x, from_mate):
        self.net, self.piece = net, piece
        self.from_x, self.from_mate = from_x, from_mate
        o = net.other_h
        self.first = [net.copy(source(1, k, 0), from_x.at[k], net.across) for k in (0, 1)]
        self.first += [net.copy(source(i, o, 1), from_mate.at[i], net.mate) for i in (0, 1)]
        self.second = []

    def start(self):
        for cp in self.first:
            cp.start()

    def add(self):
        h = self.net.h
        for cp in self.first:
            cp.wait_recv()
        for ref, got in (
            (self.piece(0, 0, 0), self.from_x.at[0]), (self.piece(0, 1, 0), self.from_x.at[1]),
            (self.piece(0, h, 1), self.from_mate.at[0]), (self.piece(1, h, 1), self.from_mate.at[1]),
        ):
            ref[...] = (ref[...].astype(F32) + got[...].astype(F32)).astype(BF)

    def pass_on(self, got, which=(0, 1)):
        net = self.net
        cut, rest = self.from_x.shape[1], self.from_mate.shape[1]
        for k in which:
            if k == 0:
                cp = net.copy(self.piece(0, net.other_h, 0), got.at[pl.ds(0, cut)], net.mate)
            else:
                cp = net.copy(self.piece(1, net.h, 1), got.at[pl.ds(cut, rest)], net.across)
            cp.start()
            self.second.append(cp)

    def finish(self):
        for cp in self.first:
            cp.wait_send()
        for cp in self.second:
            cp.wait_send()
            cp.wait_recv()


def halves(ref, cut):
    def piece(i, h, ab):
        rows = pl.ds(cut, ref.shape[1] - cut) if ab else pl.ds(0, cut)
        return ref.at[2 * i + h, rows]

    return piece


def x_first(rows):
    return rows * 5 // 12 // 16 * 16


def turn(values, cos2, sin2):
    heads = []
    for i in range(values.shape[1] // HEAD):
        v = values[:, i * HEAD : (i + 1) * HEAD]
        heads.append(v * cos2 + pltpu.roll(v, HEAD // 2, 1) * sin2)
    return jnp.concatenate(heads, axis=1) if len(heads) > 1 else heads[0]


def attention_kernel(
    sizes,
    tok, cot, wq, wkv, wo, wg, wu, gain_a, gain_f, qb, kvb, lengths, rates,
    out_x, out_mid, out_nmlp, out_gains, out_turns, o_normed, o_q, o_kv, o_att, o_cot, o_wj, o_wo, o_wg, o_wu,
    xin, cin, small, gains, kvb2, nall, call, wj, wov, kv, qs, att, part, rbu, rbd, o_x, o_mid, o_nmlp, o_gains, turns,
    send, recv, local,
):
    net = Net(sizes, send, recv, local)
    R, C, r, c = net.R, net.C, net.r, net.c
    sub, width = nall.shape[1], nall.shape[2]
    block = tok.shape[1]
    row_tok = sub * C
    n_tok = sub * R
    qw = wq.shape[1]
    slot = lax.rem(r, 2)
    partner = net.at_row(r + 1 - 2 * slot)
    wide = lambda ref: jnp.broadcast_to(ref[...].astype(F32).reshape(1, ref.shape[0]), (8, ref.shape[0]))
    small[:, :block] = wide(gain_a)
    small[:, block:] = wide(gain_f)
    kvb2[slot] = wide(kvb)
    net.barrier()
    cos2, sin2 = turns.at[:, pl.ds(0, HEAD)], turns.at[:, pl.ds(HEAD, HEAD)]
    ends = [lengths[0, 0]]
    for i in range(1, lengths.shape[1] - 1):
        ends.append(ends[-1] + lengths[0, i])

    def place_of(rr):
        here = rr * row_tok + c * sub + lax.broadcasted_iota(jnp.int32, (sub, 1), 0)
        first = jnp.zeros((sub, 1), jnp.int32)
        for end in ends:
            first = jnp.where(here >= end, end, first)
        return here, first

    def spread(src, dst):
        mine = pl.multiple_of(c * sub, sub)
        local_copy = net.here(src.at[pl.ds(mine, sub)], dst.at[c])
        copies = []
        for k in range(1, C):
            to = lax.rem(c + k, C)
            frm = lax.rem(c + C - k, C)
            i = net.n
            net.n += 1
            rows = pl.ds(pl.multiple_of(to * sub, sub), sub)
            copies.append(
                (net.like(i, src.at[rows], dst.at[c], net.at_col(to)),
                 net.like(i, src.at[rows], dst.at[frm], net.at_col(to)))
            )
        return local_copy, copies

    def begin(pair):
        pair[0].start()
        for out, _ in pair[1]:
            out.start()

    def arrived(pair):
        pair[0].wait()
        for _, inc in pair[1]:
            inc.wait_recv()

    tok_in, cot_in = spread(tok, xin), spread(cot, cin)
    gain_own = net.here(small, gains.at[c])
    gain_own.start()
    gain_copies = []
    for k in range(1, C):
        to, frm = lax.rem(c + k, C), lax.rem(c + C - k, C)
        i = net.n
        net.n += 1
        out = net.like(i, small, gains.at[c], net.at_col(to))
        gain_copies.append((out, net.like(i, small, gains.at[frm], net.at_col(to))))
        out.start()
    begin(tok_in)
    own_rows = pl.ds(pl.multiple_of(c * block, block), block)
    col_own = pl.ds(pl.multiple_of(qw + slot * HEAD, HEAD), HEAD)
    col_mate = pl.ds(pl.multiple_of(qw + (1 - slot) * HEAD, HEAD), HEAD)
    kv_x = net.copy(wkv, wj.at[own_rows, col_own], partner)
    kv_in = net.like(net.n - 1, wkv, wj.at[own_rows, col_mate], partner)
    kv_x.start()
    kvb_x = net.copy(kvb2.at[slot], kvb2.at[slot], partner)
    kvb_in = net.like(net.n - 1, kvb2.at[slot], kvb2.at[1 - slot], partner)
    kvb_x.start()
    wq_own = net.here(wq, wj.at[own_rows, pl.ds(0, qw)])
    wq_own.start()
    wkv_own = net.here(wkv, wj.at[own_rows, col_own])
    wkv_own.start()
    g_joint = WeightGather(net, None, wj, True)
    g_out = WeightGather(net, wo, wov, False)
    bulk = [WeightGather(net, w, o, False, i, 2, False) for w, o in ((wg, o_wg), (wu, o_wu)) for i in (0, 1)]

    wq_own.wait()
    wkv_own.wait()
    kv_in.wait_recv()
    g_joint.start()
    g_out.start()
    begin(cot_in)
    bulk[0].start()
    bulk[1].start()

    arrived(tok_in)
    gain_own.wait()
    for _, inc in gain_copies:
        inc.wait_recv()
    for k in range(C):
        o_gains[:, k * block : (k + 1) * block] = gains[k, :, :block]
        o_gains[:, width + k * block : width + (k + 1) * block] = gains[k, :, block:]
    x = jnp.concatenate([xin[k].astype(F32) for k in range(C)], axis=1)
    o_mid[...] = x
    o_x[...] = x.astype(BF)
    inv = lax.rsqrt(jnp.mean(x * x, axis=-1, keepdims=True) + epsilon)
    nall[r] = (x * inv * o_gains[0:1, :width]).astype(BF)
    g_n = LineGather(net, nall)
    g_n.step(0)
    g_joint.pass_x()
    g_out.pass_x()
    g_n.step(1)
    g_joint.pass_y()
    g_out.pass_y()
    arrived(cot_in)
    for k in range(C):
        call[r, :, k * block : (k + 1) * block] = cin[k]
    lane = lax.broadcasted_iota(jnp.int32, (1, HEAD), 1)
    for rr in range(R):
        here, first = place_of(rr)
        angle = (here - first).astype(F32) * rates[...]
        mine = slice(rr * sub, (rr + 1) * sub)
        cos2[mine, :] = jnp.cos(angle)
        sin2[mine, :] = jnp.where(lane < HEAD // 2, -1.0, 1.0) * jnp.sin(angle)
    g_n.step(2)
    bulk[0].pass_x()
    g_joint.arrive()
    kvb_in.wait_recv()
    g_n.step(3)
    g_cot = LineGather(net, call)
    g_cot.step(0)
    bias = jnp.concatenate([wide(qb)[0:1], kvb2[0, 0:1, :], kvb2[1, 0:1, :]], axis=1)
    joint = dot(nall[...].reshape(n_tok, width), wj[...]) + bias
    key = turn(joint[:, qw : qw + HEAD], cos2[...], sin2[...]).astype(BF)
    kv[:, c, :, :HEAD] = key.reshape(R, sub, HEAD)
    kv[:, c, :, HEAD:] = joint[:, qw + HEAD :].astype(BF).reshape(R, sub, HEAD)
    sib_c = c + 1 - 2 * lax.rem(c, 2)
    far_c = net.across_c
    far_sib_c = far_c + 1 - 2 * lax.rem(far_c, 2)
    kv_far = net.copy(kv.at[:, c], kv.at[:, c], net.across)
    kv_sib = net.copy(kv.at[:, c], kv.at[:, c], net.sibling)
    kv_pass = net.copy(kv.at[:, far_c], kv.at[:, far_c], net.sibling)
    kv_far.start()
    kv_sib.start()
    qs[...] = turn(joint[:, :qw], cos2[...], sin2[...]).astype(BF)
    tail = [net.here(o_x, out_x), net.here(o_gains, out_gains), net.here(turns, out_turns)]
    for cp in tail:
        cp.start()
    out_normed = net.here(nall, o_normed)
    out_normed.start()
    out_wj = net.here(wj, o_wj)
    out_wj.start()
    kv_far.wait_recv()
    kv_pass.start()
    kv_sib.wait_recv()
    kv_pass.wait_recv()
    bulk[1].pass_x()
    bulk[2].start()
    bulk[3].start()
    bulk[0].pass_y()
    g_cot.step(1)
    out_kv = net.here(kv, o_kv)
    out_kv.start()
    scale = HEAD ** (-0.5)
    g_out.arrive()
    rs = LineSum(net, part, rbu, rbd)
    for rr in [R - 1, 0] + list(range(R - 2, 0, -1)):
        limit = (rr + 1) * row_tok
        keys = kv[: rr + 1, :, :, :HEAD].reshape(limit, HEAD)
        values = kv[: rr + 1, :, :, HEAD:].reshape(limit, HEAD)
        mine = slice(rr * sub, (rr + 1) * sub)
        place = lax.broadcasted_iota(jnp.int32, (sub, limit), 1)
        here, first = place_of(rr)
        allowed = (place >= first) & (place <= here)
        for h in range(qw // HEAD):
            cols = slice(h * HEAD, (h + 1) * HEAD)
            s = jnp.where(allowed, dot(qs[mine, cols], keys, 1, 1) * scale, masked_score)
            e = jnp.exp(s - jnp.max(s, axis=-1, keepdims=True))
            p = e * (1.0 / jnp.sum(e, axis=-1, keepdims=True))
            att[mine, cols] = dot(p.astype(BF), values).astype(BF)
        part[rr] = dot(att[mine, :], wov[...]).astype(BF)
        if rr == 0:
            rs.step(0)
    out_q = net.here(qs, o_q)
    out_q.start()
    out_att = net.here(att, o_att)
    out_att.start()
    out_wo = net.here(wov, o_wo)
    out_wo.start()
    g_cot.step(2)
    bulk[1].pass_y()
    bulk[2].pass_x()
    rs.step(1)
    g_cot.step(3)
    out_cot = net.here(call, o_cot)
    out_cot.start()
    bulk[3].pass_x()
    rs.step(2)
    bulk[2].pass_y()
    rs.step(3)
    rs.total_into(o_mid)
    mid = o_mid[...]
    inv = lax.rsqrt(jnp.mean(mid * mid, axis=-1, keepdims=True) + epsilon)
    o_nmlp[...] = (mid * inv * o_gains[0:1, width:]).astype(BF)
    for src, dst in ((o_mid, out_mid), (o_nmlp, out_nmlp)):
        cp = net.here(src, dst)
        cp.start()
        tail.append(cp)
    bulk[3].pass_y()
    for g in bulk:
        g.arrive()
    for g in [g_joint, g_out, g_n, g_cot, rs] + bulk:
        g.finish()
    for out, _ in tok_in[1] + cot_in[1] + gain_copies:
        out.wait_send()
    for cp in (kv_far, kv_sib, kv_pass):
        cp.wait_send()
    kv_x.wait_send()
    kvb_x.wait_send()
    for cp in tail + [out_normed, out_wj, out_kv, out_q, out_att, out_wo, out_cot]:
        cp.wait()


def attention_forward(
    sizes, tok, cot, wq, wkv, wo, wg, wu, gain_a, gain_f, qb, kvb, lengths, rates
):
    dp, R, C = sizes
    sub = tok.shape[0] // C
    block = tok.shape[1]
    width = block * C
    qw, jw = wq.shape[1], wq.shape[1] + 2 * HEAD
    n = sub * R
    ff = wg.shape[0]
    shape = jax.ShapeDtypeStruct
    outs = [
        (shape((sub, width), BF), ANY),
        (shape((sub, width), F32), ANY), (shape((sub, width), BF), ANY),
        (shape((8, 2 * width), F32), ANY), (shape((n, 2 * HEAD), F32), ANY),
        (shape((R, sub, width), BF), ANY),
        (shape((n, qw), BF), ANY), (shape((R, C, sub, 2 * HEAD), BF), ANY),
        (shape((n, qw), BF), ANY), (shape((R, sub, width), BF), ANY),
        (shape((width, jw), BF), ANY), (shape((qw, width), BF), ANY),
        (shape((ff, width), BF), ANY), (shape((ff, width), BF), ANY),
    ]
    return pl.pallas_call(
        functools.partial(attention_kernel, sizes),
        out_shape=[o for o, _ in outs],
        in_specs=[ANY] * 7 + [VMEM] * 4 + [SMEM, VMEM],
        out_specs=[s for _, s in outs],
        scratch_shapes=[
            pltpu.VMEM((C, sub, block), BF), pltpu.VMEM((C, sub, block), BF),
            pltpu.VMEM((8, 2 * block), F32), pltpu.VMEM((C, 8, 2 * block), F32), pltpu.VMEM((2, 8, HEAD), F32),
            pltpu.VMEM((R, sub, width), BF), pltpu.VMEM((R, sub, width), BF),
            pltpu.VMEM((width, jw), BF), pltpu.VMEM((qw, width), BF),
            pltpu.VMEM((R, C, sub, 2 * HEAD), BF), pltpu.VMEM((n, qw), BF),
            pltpu.VMEM((n, qw), BF), pltpu.VMEM((R, sub, width), BF),
            pltpu.VMEM((R, sub, width), BF), pltpu.VMEM((R, sub, width), BF),
            pltpu.VMEM((sub, width), BF), pltpu.VMEM((sub, width), F32),
            pltpu.VMEM((sub, width), BF), pltpu.VMEM((8, 2 * width), F32),
            pltpu.VMEM((n, 2 * HEAD), F32),
            pltpu.SemaphoreType.DMA((128,)), pltpu.SemaphoreType.DMA((128,)),
            pltpu.SemaphoreType.DMA((32,)),
        ],
        compiler_params=pltpu.CompilerParams(
            collective_id=1, has_side_effects=True, vmem_limit_bytes=VMEM_LIMIT
        ),
        name="attention_forward",
    )(tok, cot, wq, wkv, wo, wg, wu, gain_a, gain_f, qb, kvb, lengths, rates)


def feedforward_kernel(
    sizes,
    nmlp, in_mid, in_gains, cot, wg, wu, wd, own_g, own_u,
    out_gmid, out_gain, o_down, o_sd, o_sm, o_sx, o_sg, o_gu, o_xt,
    w_gate, w_up, w_down, xall, call, acc, hid, gg, gu, cc, sx, xt, part, rbu, rbd, dpart, g, x_d, y_d, o_gmid, o_gain, mid, gains,
    send, recv, local,
):
    net = Net(sizes, send, recv, local)
    R, C, r, c = net.R, net.C, net.r, net.c
    sub, width = nmlp.shape
    block = width // C
    n_tok = sub * R
    n_part = n_tok // PARTS
    n = sub // PARTS
    ff = w_gate.shape[0]
    tile = acc.shape[2]
    wide = width // tile
    own_cols = [pl.ds(pl.multiple_of(b * block, HEAD), block) for b in (c, net.across_c)]
    pieces = 5
    g_down = [WeightGather(net, wd, w_down, False, i, pieces) for i in range(pieces)]
    in_x = [net.here(nmlp.at[pl.ds(q * n, n)], xall.at[q, r]) for q in range(PARTS)]
    in_norm = [net.here(in_mid, mid), net.here(in_gains, gains)]
    for cp in in_x + in_norm:
        cp.start()
    in_cot = [net.here(cot.at[:, pl.ds(q * n, n)], call.at[q]) for q in range(PARTS)]
    for cp in in_cot:
        cp.start()
    in_w = []
    for full, own, w in ((wg, own_g, w_gate), (wu, own_u, w_up)):
        for k in range(C):
            cols = pl.ds(pl.multiple_of(lax.rem(c + k, C) * block, HEAD), block)
            cp = net.here(full.at[:, cols] if k else own, w.at[:, cols])
            cp.start()
            in_w.append(cp)
    if hid.shape[1] > ff:
        for ref in (hid, gg, gu):
            ref[:n_tok, ff:] = jnp.zeros((n_tok, hid.shape[1] - ff), BF)
    net.barrier()
    for cp in in_x:
        cp.wait()
    g_x = LineGather(net, xall)
    g_x.step(0, (0,))
    g_down[0].start()
    g_down[1].start()
    for cp in in_cot:
        cp.wait()
    to_sibling = []

    def hand(src, dst):
        cp = net.copy(src, dst, net.sibling)
        cp.start()
        to_sibling.append(cp)

    hand(call, dpart)
    for i in (0, 1):
        cc[0, :, :, :, i * block : (i + 1) * block] = call[:, :, :, own_cols[i]]

    def pass_x(i):
        g_down[i].pass_x()
        if i + 2 < pieces:
            g_down[i + 2].start()

    acts_out = [
        [
            net.copy(
                ref.at[pl.ds(q * n_part, n_part)], ref.at[pl.ds(n_tok + q * n_part, n_part)],
                net.sibling,
            )
            for ref in (hid, gg, gu)
        ]
        for q in range(PARTS)
    ]
    x_out = net.copy(xall, sx, net.sibling)
    to_sibling += [cp for pair in acts_out for cp in pair] + [x_out]
    rs = LineSum(net, part, rbu, rbd)
    full = ff // tile
    rest = pl.ds(full * tile, ff - full * tile)

    def act(q, rows, back):
        mine = pl.ds(pl.multiple_of(q * n_part, n_part), n_part)
        x = xall[q].reshape(n_part, width)
        gate = dot(x, w_gate[rows, :], 1, 1)
        up = dot(x, w_up[rows, :], 1, 1)
        s = jax.nn.sigmoid(gate)
        silu = gate * s
        hid[mine, rows] = (silu * up).astype(BF)
        gg[mine, rows] = (back * up * s * (1.0 + gate * (1.0 - s))).astype(BF)
        gu[mine, rows] = (back * silu).astype(BF)

    pass_x(0)
    g_x.step(1, (0,))
    g_x.step(0, (1,))
    pass_x(1)
    g_down[0].pass_y()
    pass_x(2)
    g_x.step(2, (0,))
    g_x.step(1, (1,))
    g_down[1].pass_y()
    pass_x(3)
    g_down[0].arrive()
    g_down[1].arrive()

    @pl.loop(0, PARTS)
    def _(q):
        @pl.loop(0, full)
        def _(t):
            rows = pl.ds(pl.multiple_of(t * tile, tile), tile)

            @pl.when(q == 0)
            def _():
                @pl.when(t == 1)
                def _():
                    g_down[3].pass_y()
                    g_down[2].arrive()

                @pl.when(t == 2)
                def _():
                    g_x.step(2, (1,))
                    g_down[3].arrive()

                @pl.when(t == 3)
                def _():
                    g_down[4].pass_y()
                    g_down[4].arrive()

                acc[t] = dot(call[...].reshape(n_tok, width), w_down[rows, :], 1, 1)

                @pl.when(t == 0)
                def _():
                    g_down[2].pass_y()
                    g_x.step(3, (0,))
                    pass_x(4)
                    for cp in in_w:
                        cp.wait()

            act(q, rows, acc[t, pl.ds(pl.multiple_of(q * n_part, n_part), n_part)])

            @pl.when((q == 1) & (t == full - 1))
            def _():
                rs.step(1, (0,))

        act(q, rest, dot(call[q].reshape(n_part, width), w_down[rest, :], 1, 1))

        @pl.when(q == 0)
        def _():
            g_x.step(3, (1,))

        for k in range(PARTS):

            @pl.when(q == k)
            def _():
                for cp in acts_out[k]:
                    cp.start()

        mine = pl.ds(pl.multiple_of(q * n_part, n_part), n_part)

        @pl.loop(0, wide)
        def _(i):
            cols = pl.ds(pl.multiple_of(i * tile, tile), tile)
            total = dot(gg[mine, :ff], w_gate[:, cols]) + dot(gu[mine, :ff], w_up[:, cols])
            part[q, :, :, cols] = total.astype(BF).reshape(R, n, tile)

        @pl.when(q == 0)
        def _():
            rs.step(0, (0,))
            x_out.start()

        @pl.when(q == 1)
        def _():
            rs.step(0, (1,))
            rs.step(2, (0,))

    for g_piece in g_down:
        g_piece.finish()
    for cp in to_sibling:
        cp.wait_recv()
    outs = [net.here(gu, o_gu)]
    outs[0].start()
    for i in (0, 1):
        cc[1, :, :, :, i * block : (i + 1) * block] = dpart[:, :, :, own_cols[i]]

    def all_tiles(body):
        @pl.loop(0, full)
        def _(t):
            body(pl.ds(pl.multiple_of(t * tile, tile), tile))

        body(rest)

    def down_grad(rows):
        total = dot(hid[:, rows], cc[...].reshape(2 * n_tok, 2 * block), 0, 0)
        w_gate[rows, : 2 * block] = total.astype(BF)

    all_tiles(down_grad)
    half_ff = ff // 2
    cut = x_d.shape[1]

    def down_piece(i, h, ab):
        first, count = (cut, half_ff - cut) if ab else (0, cut)
        return w_gate.at[
            pl.ds(pl.multiple_of(h * half_ff + first, 16), count), pl.ds(i * block, block)
        ]

    sum_d = BlockSum(net, down_piece, down_piece, x_d, y_d)
    sum_d.start()
    rs.step(1, (1,))
    rs.step(3, (0,))

    @pl.loop(0, wide)
    def _(i):
        cols = pl.ds(pl.multiple_of(i * tile, tile), tile)
        total = dot(hid[:n_tok, :ff], w_down[:, cols])
        dpart[:, :, :, cols] = total.astype(BF).reshape(PARTS, R, n, tile)

    rs.step(2, (1,))
    out_down = [net.here(dpart.at[q], o_down.at[:, pl.ds(q * n, n)]) for q in range(PARTS)]
    for cp in out_down:
        cp.start()
    for i in (0, 1):
        rows = slice(i * block, (i + 1) * block)
        xt[rows, :n_tok] = xall[:, :, :, own_cols[i]].reshape(n_tok, block).T
        xt[rows, n_tok:] = sx[:, :, :, own_cols[i]].reshape(n_tok, block).T
    def gate_grad(cols):
        total = dot(xt[...], gg[:, cols])
        g[:, :, cols] = total.astype(BF).reshape(4, g.shape[1], cols.size)

    all_tiles(gate_grad)
    for src, dst in ((g, o_sg), (xt, o_xt)):
        cp = net.here(src, dst)
        cp.start()
        outs.append(cp)
    rs.step(3, (1,))
    o_gmid[...] = jnp.zeros_like(o_gmid)
    rs.total_into(o_gmid)
    for cp in in_norm:
        cp.wait()
    grad = o_gmid[...]
    m = mid[...]
    inv = lax.rsqrt(jnp.mean(m * m, axis=-1, keepdims=True) + epsilon)
    normal = m * inv
    e = grad * gains[0:1, width:]
    back = inv * (e - normal * jnp.mean(e * normal, axis=-1, keepdims=True))
    o_gain[...] = jnp.broadcast_to(jnp.sum(grad * normal, axis=0, keepdims=True), o_gain.shape)
    for q in range(PARTS):
        rows = slice(q * n, (q + 1) * n)
        o_gmid[rows] = call[q, r].astype(F32) + back[rows]
    for src, dst in ((o_gmid, out_gmid), (o_gain, out_gain)):
        cp = net.here(src, dst)
        cp.start()
        outs.append(cp)
    rs.finish()
    sum_d.add()
    own_half = w_gate.at[
        pl.ds(pl.multiple_of(net.h * half_ff, 16), half_ff), pl.ds(0, block)
    ]
    for src, dst in (
        (own_half, o_sd), (down_piece(0, net.other_h, 0), o_sm), (down_piece(1, net.h, 1), o_sx)
    ):
        cp = net.here(src, dst)
        cp.start()
        outs.append(cp)
    sum_d.finish()
    g_x.finish()
    for cp in to_sibling:
        cp.wait_send()
    for cp in outs + out_down:
        cp.wait()


def feedforward(sizes, nmlp, mid, gains, cot, wg, wu, wd, own_g, own_u):
    dp, R, C = sizes
    sub, width = nmlp.shape
    block = width // C
    n_tok = R * sub
    ff = wd.shape[0]
    tile = 512
    cut = ff // 4
    shape = jax.ShapeDtypeStruct
    outs = [
        (shape((sub, width), F32), ANY), (shape((8, width), F32), ANY),
        (shape((R, sub, width), BF), ANY), (shape((ff // 2, block), BF), ANY),
        (shape((cut, block), BF), ANY), (shape((ff // 2 - cut, block), BF), ANY),
        (shape((4, block // 2, ff), BF), ANY),
        (shape((2 * n_tok, -(-ff // HEAD) * HEAD), BF), ANY),
        (shape((2 * block, 2 * n_tok), BF), ANY),
    ]
    v = pltpu.VMEM
    line = v((PARTS, R, sub // PARTS, width), BF)
    acts = v((2 * n_tok, -(-ff // HEAD) * HEAD), BF)
    weight = v((ff, width), BF)
    return pl.pallas_call(
        functools.partial(feedforward_kernel, sizes),
        out_shape=[o for o, _ in outs],
        in_specs=[ANY] * 9,
        out_specs=[s for _, s in outs],
        scratch_shapes=[
            weight, weight, weight, line, line, v((ff // tile, n_tok, tile), F32), acts, acts, acts,
            v((2, PARTS, R, sub // PARTS, 2 * block), BF), line,
            v((2 * block, 2 * n_tok), BF), line, line, line, line, v((4, block // 2, ff), BF),
            v((2, cut, block), BF), v((2, ff // 2 - cut, block), BF),
            v((sub, width), F32), v((8, width), F32), v((sub, width), F32), v((8, 2 * width), F32),
            pltpu.SemaphoreType.DMA((128,)), pltpu.SemaphoreType.DMA((128,)),
            pltpu.SemaphoreType.DMA((32,)),
        ],
        compiler_params=pltpu.CompilerParams(
            collective_id=2, has_side_effects=True, vmem_limit_bytes=VMEM_LIMIT
        ),
        name="feedforward",
    )(nmlp, mid, gains, cot, wg, wu, wd, own_g, own_u)


def backward_kernel(
    sizes,
    in_gmid, in_x, in_mid, in_gains, in_gain_mlp, lengths, in_turns,
    normed, q, kv, att, wj, wo, down, sm, sx, sg, up_grads, xt_in,
    o_layer, o_input, out_vec, out_j, o_db, o_ga, o_gb, o_ua, o_ub, o_oa, o_ob,
    mall, nall, qs, kvs, atts, wjs, wos, dpart, drbu, drbd, part, rbu, rbd, grads, dq, dkv, dkv16, dk_sib, dk_in,
    joint, lay,
    s_g, s_u, x_g, x_u, y_g, y_u,
    wjo, wjx, s_j, x_j, y_j, woo, wox, s_o, x_o, y_o, jb, jk, jk2, jgot, v1, v1in, v2, v2in, o_vec, o_j,
    gmid, x_in, mid, gains, gain_mlp, turns, gu, xt,
    send, recv, local,
):
    net = Net(sizes, send, recv, local)
    R, C, r, c = net.R, net.C, net.r, net.c
    sub, width = in_gmid.shape
    block = width // C
    n_tok = sub * R
    row_tok = sub * C
    qw = qs.shape[1]
    slot = lax.rem(r, 2)
    cos2, sin2 = turns.at[:, pl.ds(0, HEAD)], turns.at[:, pl.ds(HEAD, HEAD)]
    partner_r = r + 1 - 2 * slot
    small_loads = [
        net.here(a, b) for a, b in
        ((in_gmid, gmid), (in_x, x_in), (in_mid, mid), (in_gains, gains), (in_gain_mlp, gain_mlp),
         (in_turns, turns))
    ]
    up_loads = [net.here(up_grads, gu), net.here(xt_in, xt)]
    for cp in small_loads + up_loads:
        cp.start()
    loads = [
        net.here(a, b) for a, b in
        ((wo, wos), (att, atts), (q, qs), (kv, kvs), (down, dpart), (sg, s_g),
         (normed, nall), (wj, wjs))
    ]
    for cp in loads:
        cp.start()
    sem = pltpu.get_barrier_semaphore()
    half = net.dp // 2
    others = [(net.d, r, lax.rem(c + k, C)) for k in range(1, C)]
    others += [(net.d, lax.rem(r + k, R), c) for k in range(1, R)]
    others += [(net.mate[0], lax.rem(r + k, R), c) for k in range(R)]
    for dev in others:
        pl.semaphore_signal(sem, inc=1, device_id=dev, device_id_type=MESH)
    pl.semaphore_wait(sem, len(others))

    small_loads[0].wait()
    mall[r] = gmid[...].astype(BF)
    g_m = LineGather(net, mall)
    g_m.step(0)
    sum_g = BlockSum(net, halves(sg, x_g.shape[1]), halves(s_g, x_g.shape[1]), x_g, y_g)
    sum_u = BlockSum(net, halves(s_u, x_u.shape[1]), halves(s_u, x_u.shape[1]), x_u, y_u)
    sum_g.start()
    for cp in up_loads:
        cp.wait()
    ff = s_u.shape[2]

    def up_tile(cols):
        total = dot(xt[...], gu[:, cols])
        s_u[:, :, cols] = total.astype(BF).reshape(4, s_u.shape[1], cols.size)

    @pl.loop(0, ff // 512)
    def _(t):
        up_tile(pl.ds(pl.multiple_of(t * 512, 512), 512))

    up_tile(pl.ds(ff // 512 * 512, ff % 512))
    sum_u.start()
    cut_d, rest_d = sm.shape[0], sx.shape[0]
    sum_d = [
        net.copy(sx, o_db.at[pl.ds(cut_d, rest_d)], net.across),
        net.copy(sm, o_db.at[pl.ds(0, cut_d)], net.mate),
    ]
    sum_d[0].start()
    g_m.step(1)
    for cp in loads[:6] + small_loads[1:]:
        cp.wait()
    g_m.step(2)
    sum_g.add()
    sum_g.pass_on(o_gb, (0,))
    g_m.step(3)
    rs_d = LineSum(net, dpart, drbu, drbd)
    rs_d.step(0)
    m_all = mall[...].reshape(n_tok, width)
    grads[...] = dot(m_all, wos[...], 1, 1).astype(BF)

    def to_columns(src, dst):
        rows = pl.ds(pl.multiple_of(c * sub, sub), sub)
        mine = net.here(src.at[:, pl.ds(pl.multiple_of(c * block, HEAD), block)], dst.at[rows])
        mine.start()
        pairs = []
        for k in range(1, C):
            to, frm = lax.rem(c + k, C), lax.rem(c + C - k, C)
            i = net.n
            net.n += 1
            cut = src.at[:, pl.ds(pl.multiple_of(to * block, HEAD), block)]
            out = net.like(i, cut, dst.at[rows], net.at_col(to))
            out.start()
            from_rows = pl.ds(pl.multiple_of(frm * sub, sub), sub)
            pairs.append((out, net.like(i, cut, dst.at[from_rows], net.at_col(to))))
        return mine, pairs

    def settle(exchange):
        exchange[0].wait()
        for out, inc in exchange[1]:
            inc.wait_recv()
            out.wait_send()

    sib_blocks = [b + 1 - 2 * lax.rem(b, 2) for b in (c, net.across_c)]
    total = dot(atts[...], m_all, 0, 0)
    for b in range(C):
        woo[2 * b : 2 * b + 2] = (
            total[:, b * block : (b + 1) * block].astype(BF).reshape(2, qw // 2, block)
        )
    out_x = [net.copy(woo.at[pl.ds(2 * b, 2)], wox.at[i], net.sibling) for i, b in enumerate(sib_blocks)]
    for cp in out_x:
        cp.start()
    scale = HEAD ** (-0.5)
    heads = qw // HEAD
    ends = [lengths[0, 0]]
    for i in range(1, lengths.shape[1] - 1):
        ends.append(ends[-1] + lengths[0, i])
    for rr in reversed(range(R)):
        limit = (rr + 1) * row_tok
        keys = kvs[: rr + 1, :, :, :HEAD].reshape(limit, HEAD)
        values = kvs[: rr + 1, :, :, HEAD:].reshape(limit, HEAD)
        mine = slice(rr * sub, (rr + 1) * sub)
        stack = lambda ref: jnp.concatenate(
            [ref[mine, h * HEAD : (h + 1) * HEAD] for h in range(heads)], axis=0
        )
        qh, gh = stack(qs), stack(grads)
        place = lax.broadcasted_iota(jnp.int32, (limit, heads * sub), 0)
        lane = lax.broadcasted_iota(jnp.int32, (1, heads * sub), 1)
        here = rr * row_tok + c * sub + lax.rem(lane, sub)
        first = jnp.zeros_like(here)
        for end in ends:
            first = jnp.where(here >= end, end, first)
        s = jnp.where(
            (place >= first) & (place <= here), dot(keys, qh, 1, 1) * scale, masked_score
        )
        e = jnp.exp(s - jnp.max(s, axis=0, keepdims=True))
        p = e * (1.0 / jnp.sum(e, axis=0, keepdims=True))
        g = dot(values, gh, 1, 1)
        ds = (p * (g - jnp.sum(p * g, axis=0, keepdims=True))).astype(BF)
        dv = dot(p.astype(BF), gh)
        dk = dot(ds, qh) * scale
        if rr == R - 1:
            dkv[:, :HEAD] = dk
            dkv[:, HEAD:] = dv
        else:
            dkv[:limit, :HEAD] += dk
            dkv[:limit, HEAD:] += dv
        dqs = dot(ds, keys, 0, 0) * scale
        for h in range(heads):
            dq[mine, h * HEAD : (h + 1) * HEAD] = dqs[h * sub : (h + 1) * sub]
        if rr == R - 2:
            rs_d.step(1)
            for i, b in enumerate((c, net.across_c)):
                out_x[i].wait_recv()
                s_o[2 * i : 2 * i + 2] = (
                    woo[pl.ds(2 * b, 2)].astype(F32) + wox[i].astype(F32)
                ).astype(BF)
    sib_c = c + 1 - 2 * lax.rem(c, 2)
    far_c = net.across_c
    far_sib_c = far_c + 1 - 2 * lax.rem(far_c, 2)
    dkv16[...] = dkv[...].astype(BF).reshape(dkv16.shape)
    dk_copies = [
        net.copy(dkv16.at[:, far_sib_c], dk_sib.at[1], net.sibling),
        net.copy(dkv16.at[:, sib_c], dk_sib.at[0], net.sibling),
    ]
    for cp in dk_copies:
        cp.start()
    dk_copies[0].wait_recv()
    dk_in[0] = (dkv16[:, far_c].astype(F32) + dk_sib[1].astype(F32)).astype(BF)
    dk_copies.append(net.copy(dk_in.at[0], dk_in.at[1], net.across))
    dk_copies[2].start()
    sum_g.pass_on(o_gb, (1,))
    sum_o = BlockSum(net, halves(s_o, x_o.shape[1]), halves(s_o, x_o.shape[1]), x_o, y_o)
    sum_o.start()
    rs_d.step(2)
    for cp in loads[6:]:
        cp.wait()
    slots = dkv16[:, c].astype(F32)
    dk_copies[1].wait_recv()
    slots = slots + dk_sib[0].astype(F32)
    dk_copies[2].wait_recv()
    slots = slots + dk_in[1].astype(F32)
    slots = slots.reshape(n_tok, 2 * HEAD)
    joint[:, :qw] = turn(dq[...], cos2[...], -sin2[...]).astype(BF)
    joint[:, qw : qw + HEAD] = turn(slots[:, :HEAD], cos2[...], -sin2[...]).astype(BF)
    joint[:, qw + HEAD :] = slots[:, HEAD:].astype(BF)
    part[...] = dot(joint[...], wjs[...], 1, 1).astype(BF).reshape(R, sub, width)
    rs = LineSum(net, part, rbu, rbd)
    rs.step(0)
    sum_u.add()
    sum_u.pass_on(o_ub)
    total = dot(nall[...].reshape(n_tok, width), joint[...], 0, 0)
    wjo[...] = total.astype(BF).reshape(wjo.shape)
    joint_x = [net.copy(wjo.at[pl.ds(2 * b, 2)], wjx.at[i], net.sibling) for i, b in enumerate(sib_blocks)]
    for cp in joint_x:
        cp.start()
    bias = jnp.sum(joint[...].astype(F32), axis=0, keepdims=True)
    for i, b in enumerate((c, net.across_c)):
        joint_x[i].wait_recv()
        s_j[2 * i : 2 * i + 2] = (
            wjo[pl.ds(2 * b, 2)].astype(F32) + wjx[i].astype(F32)
        ).astype(BF)
    sum_j = BlockSum(net, halves(s_j, x_j.shape[1]), halves(s_j, x_j.shape[1]), x_j, y_j)
    sum_j.start()
    rs_d.step(3)
    lay[0] = mid[...]
    rs_d.total_into(lay.at[0])
    jk[...] = lay[0].astype(BF)
    rs.step(1)
    sum_o.add()
    sum_o.pass_on(o_ob)
    rs.step(2)
    sum_j.add()
    sum_j.pass_on(jb)
    keeps = [
        net.here(src.at[net.h], dst)
        for src, dst in ((s_g, o_ga), (s_u, o_ua), (s_o, o_oa))
    ]
    for cp in keeps:
        cp.start()
    rs.step(3)
    lay[1] = jnp.zeros_like(lay[1])
    rs.total_into(lay.at[1])
    grad = lay[1]
    x = x_in[...].astype(F32)
    inv = lax.rsqrt(jnp.mean(x * x, axis=-1, keepdims=True) + epsilon)
    normal = x * inv
    e = grad * gains[0:1, :width]
    back = inv * (e - normal * jnp.mean(e * normal, axis=-1, keepdims=True))
    gain_attn = jnp.sum(grad * normal, axis=0, keepdims=True)
    for k in range(C):
        cut = slice(k * block, (k + 1) * block)
        v1[k, :, :block] = jnp.broadcast_to(gain_attn[:, cut], (8, block))
        v1[k, :, block : 2 * block] = gain_mlp[:, cut]
        v1[k, :, 2 * block :] = jnp.broadcast_to(bias, (8, bias.shape[1]))
    v_copies = []
    for k in range(1, C):
        to, frm = lax.rem(c + k, C), lax.rem(c + C - k, C)
        i = net.n
        net.n += 1
        out = net.like(i, v1.at[to], v1in.at[c], net.at_col(to))
        out.start()
        v_copies.append((out, net.like(i, v1.at[to], v1in.at[frm], net.at_col(to)), frm))
    jk2[...] = (gmid[...] + back).astype(BF)
    input_x = to_columns(jk2, o_input)
    layer_x = to_columns(jk, o_layer)
    sum_d[1].start()
    sum_j.finish()
    ja = s_j.at[net.h]
    own_cols = pl.ds(pl.multiple_of(qw + slot * HEAD, HEAD), HEAD)
    mate_cols = pl.ds(pl.multiple_of(qw + (1 - slot) * HEAD, HEAD), HEAD)
    jgot[0] = ja[:, mate_cols].astype(F32) + jb[:, mate_cols].astype(F32)
    slot_x = net.copy(jgot.at[0], jgot.at[1], net.at_row(partner_r))
    slot_x.start()
    o_j[:, :qw] = ja[:, :qw].astype(F32) + jb[:, :qw].astype(F32)
    total = v1[c]
    for _, inc, frm in v_copies:
        inc.wait_recv()
        total = total + v1in[frm]
    v2[...] = total
    far = []
    for same in (1, 0):
        for k in range(R):
            if same and k == 0:
                continue
            to, frm = lax.rem(r + k, R), lax.rem(r + R - k, R)
            i = net.n
            net.n += 1
            dst_d = net.d if same else net.mate[0]
            hs = net.h if same else net.other_h
            out = net.like(i, v2, v2in.at[net.h, r], (dst_d, to, c))
            out.start()
            far.append((out, net.like(i, v2, v2in.at[hs, frm], (dst_d, to, c))))
    v2in[net.h, r] = total
    slot_x.wait_recv()
    o_j[:, qw:] = ja[:, own_cols].astype(F32) + jb[:, own_cols].astype(F32) + jgot[1]
    tail = [net.here(o_j, out_j)]
    tail[0].start()
    for g in (sum_g, sum_u, sum_o):
        g.finish()
    for cp in sum_d:
        cp.wait()
    for cp in keeps:
        cp.wait()
    for _, inc in far:
        inc.wait_recv()
    gain_sum = v2in[0, 0, :, : 2 * block]
    for hh in (0, 1):
        for k in range(R):
            if hh or k:
                gain_sum = gain_sum + v2in[hh, k, :, : 2 * block]
    o_vec[:, : 2 * block] = gain_sum
    o_vec[:, 2 * block : 2 * block + qw] = (
        v2in[0, r, :, 2 * block : 2 * block + qw] + v2in[1, r, :, 2 * block : 2 * block + qw]
    )
    cols = pl.ds(pl.multiple_of(2 * block + qw + slot * HEAD, HEAD), HEAD)
    o_vec[:, 2 * block + qw :] = (
        v2in[0, r, :, cols] + v2in[1, r, :, cols]
        + v2in[0, partner_r, :, cols] + v2in[1, partner_r, :, cols]
    )
    tail.append(net.here(o_vec, out_vec))
    tail[1].start()
    settle(layer_x)
    settle(input_x)
    for g in (g_m, rs_d, rs):
        g.finish()
    for cp in out_x + joint_x + [slot_x]:
        cp.wait_send()
    for cp in dk_copies:
        cp.wait_send()
    for cps in v_copies + far:
        cps[0].wait_send()
    for cp in tail:
        cp.wait()


def backward(sizes, gmid, x_in, mid, gains, gain_mlp, lengths, turns, normed, q, kv, att, wj, wo,
             down, sm, sx, sg, up_grads, xt):
    dp, R, C = sizes
    sub, width = gmid.shape
    block = width // C
    n, qw = q.shape
    jw = wj.shape[1]
    ff = sg.shape[2]
    shape = jax.ShapeDtypeStruct
    d2, g2, w2, j2 = (ff // 2, block), (block // 2, ff), (qw // 2, block), (block // 2, jw)
    vec = 2 * block + jw
    outs = [
        (shape((C * sub, block), BF), ANY), (shape((C * sub, block), BF), ANY),
        (shape((8, vec - HEAD), F32), ANY), (shape((block // 2, jw - HEAD), F32), ANY),
        (shape(d2, BF), ANY), (shape(g2, BF), ANY), (shape(g2, BF), ANY),
        (shape(g2, BF), ANY), (shape(g2, BF), ANY), (shape(w2, BF), ANY), (shape(w2, BF), ANY),
    ]
    v = pltpu.VMEM
    four = lambda s: v((4,) + s, BF)

    def landing(s):
        cut = x_first(s[0])
        return [v((2, cut) + s[1:], BF), v((2, s[0] - cut) + s[1:], BF)]

    x_g, y_g = landing(g2)
    x_o, y_o = landing(w2)
    x_j, y_j = landing(j2)
    line = v((R, sub, width), BF)
    return pl.pallas_call(
        functools.partial(backward_kernel, sizes),
        out_shape=[o for o, _ in outs],
        in_specs=[ANY] * 5 + [SMEM] + [ANY] * 13,
        out_specs=[s for _, s in outs],
        scratch_shapes=[
            line, line, v((n, qw), BF), v(kv.shape, BF), v((n, qw), BF), v((width, jw), BF),
            v((qw, width), BF), line, line, line, line, line, line, v((n, qw), BF), v((n, qw), F32),
            v((n * C, 2 * HEAD), F32), v(kv.shape, BF), v((2, R, sub, 2 * HEAD), BF),
            v((2, R, sub, 2 * HEAD), BF),
            v((n, jw), BF), v((2, sub, width), F32),
            four(g2), four(g2), x_g, x_g, y_g, y_g,
            v((8,) + j2, BF), v((2, 2) + j2, BF), four(j2), x_j, y_j,
            v((8,) + w2, BF), v((2, 2) + w2, BF), four(w2), x_o, y_o,
            v(j2, BF), v((sub, width), BF), v((sub, width), BF), v((2, j2[0], HEAD), F32),
            v((C, 8, vec), F32), v((C, 8, vec), F32), v((8, vec), F32), v((2, R, 8, vec), F32),
            v((8, vec - HEAD), F32), v((block // 2, jw - HEAD), F32),
            v(gmid.shape, F32), v(x_in.shape, BF), v(mid.shape, F32), v(gains.shape, F32),
            v(gain_mlp.shape, F32), v(turns.shape, F32), v(up_grads.shape, BF), v(xt.shape, BF),
            pltpu.SemaphoreType.DMA((128,)), pltpu.SemaphoreType.DMA((128,)),
            pltpu.SemaphoreType.DMA((32,)),
        ],
        compiler_params=pltpu.CompilerParams(
            collective_id=3, has_side_effects=True, vmem_limit_bytes=VMEM_LIMIT
        ),
        name="backward",
    )(gmid, x_in, mid, gains, gain_mlp, lengths, turns, normed, q, kv, att, wj, wo, down, sm, sx, sg, up_grads, xt)

def finish_kernel(
    d, vec, joint, da, db, ga, gb, ua, ub, oa, ob, layer, inp,
    o_again, o_fgain, o_qb, o_kvb, o_q, o_kv, o_out, o_gate, o_up, o_down, o_layer, o_input,
    vec_v, joint_v, da_v, db_v, ga_v, gb_v, ua_v, ub_v, oa_v, ob_v,
    layer_v, inp_v, again_v, fgain_v, qb_v, kvb_v, q_v, kv_v, out_v, gate_v, up_v, down_v, sem_in, sem_out,
):
    pairs = (
        (vec, vec_v), (joint, joint_v), (oa, oa_v), (ob, ob_v), (da, da_v), (db, db_v),
        (ga, ga_v), (gb, gb_v), (ua, ua_v), (ub, ub_v), (layer, layer_v), (inp, inp_v),
    )
    loads = [pltpu.make_async_copy(s, t, sem_in.at[i]) for i, (s, t) in enumerate(pairs)]
    for cp in loads:
        cp.start()
    stores = []

    def store(src, dst):
        cp = pltpu.make_async_copy(src, dst, sem_out.at[len(stores)])
        cp.start()
        stores.append(cp)

    block, qw = o_again.shape[0], o_q.shape[1]
    loads[0].wait()
    second = d[0, 0] == 1
    again_v[...] = vec_v[0, :block]
    fgain_v[...] = vec_v[0, block : 2 * block]
    bias = vec_v[0:1, 2 * block :]
    pick = lambda v: jnp.where(second, v[:, v.shape[1] // 2 :], v[:, : v.shape[1] // 2])
    qb_v[...] = pick(bias[:, :qw])[0]
    kvb_v[...] = pick(bias[:, qw:])[0]
    for src, dst in ((again_v, o_again), (fgain_v, o_fgain), (qb_v, o_qb), (kvb_v, o_kvb)):
        store(src, dst)
    loads[1].wait()
    q_v[...] = joint_v[:, :qw]
    kv_v[...] = joint_v[:, qw:]
    store(q_v, o_q)
    store(kv_v, o_kv)
    for i, (a, b, f, o) in enumerate(
        ((oa_v, ob_v, out_v, o_out), (da_v, db_v, down_v, o_down), (ga_v, gb_v, gate_v, o_gate),
         (ua_v, ub_v, up_v, o_up))
    ):
        loads[2 + 2 * i].wait()
        loads[3 + 2 * i].wait()
        f[...] = a[...].astype(F32) + b[...].astype(F32)
        store(f, o)
    for i, (src, dst) in enumerate(((layer_v, o_layer), (inp_v, o_input))):
        loads[10 + i].wait()
        store(src, dst)
    for cp in stores:
        cp.wait()


def finish(d, layer, inp, vec, joint, da, db, ga, gb, ua, ub, oa, ob):
    block, qw, kvw = layer.shape[1], oa.shape[0] * 2, joint.shape[1] - oa.shape[0] * 2
    f32 = lambda *s: jax.ShapeDtypeStruct(s, F32)
    like = lambda v: jax.ShapeDtypeStruct(v.shape, F32)
    results = [
        f32(block), f32(block), f32(qw // 2), f32(kvw // 2), f32(joint.shape[0], qw),
        f32(joint.shape[0], kvw), like(oa), like(ga), like(ua), like(da),
    ]
    v = lambda a: pltpu.VMEM(a.shape, a.dtype)
    out = pl.pallas_call(
        finish_kernel,
        out_shape=results + [jax.ShapeDtypeStruct(a.shape, BF) for a in (layer, inp)],
        in_specs=[SMEM] + [ANY] * 12,
        out_specs=[ANY] * 12,
        scratch_shapes=[v(a) for a in (vec, joint, da, db, ga, gb, ua, ub, oa, ob, layer, inp)]
        + [v(a) for a in results]
        + [pltpu.SemaphoreType.DMA((12,)), pltpu.SemaphoreType.DMA((12,))],
        compiler_params=pltpu.CompilerParams(vmem_limit_bytes=VMEM_LIMIT),
        name="finish",
    )(d, vec, joint, da, db, ga, gb, ua, ub, oa, ob, layer, inp)
    again, fgain, q_bias, kv_bias, q, kv, o, gate, up, down, layer, inp = out
    return layer, inp, again, q, q_bias, kv, kv_bias, o, fgain, gate, up, down


def on_device(
    tokens_in, seq_lengths, attention_gain, query_weight, query_bias, keyvalue_weight,
    keyvalue_bias, output_weight, feedforward_gain, gate_weight, up_weight, down_weight,
    cotangent,
):
    sizes = dp, rows, cols = tuple(lax.axis_size(a) for a in ("dp", "row", "col"))
    d, col = lax.axis_index("dp"), lax.axis_index("col")
    sub = tokens_in.shape[0] // cols
    block = tokens_in.shape[1]
    wq_width = query_weight.shape[1]
    lane = np.arange(HEAD) % (HEAD // 2)
    rates = jnp.asarray((rope_base ** (-lane * (2.0 / HEAD))).astype(np.float32)[None])
    (x_own, middle, nmlp, gains, turns, normed, queries, kv, attended, cot_all, w_joint, w_out,
     w_gate, w_up) = attention_forward(
        sizes, tokens_in, cotangent, query_weight, keyvalue_weight, output_weight, gate_weight.T,
        up_weight.T, attention_gain, feedforward_gain, query_bias, keyvalue_bias, seq_lengths, rates,
    )
    grad_middle, gain_mlp, down_part, da, sum_mate, sum_across, sum_gate, up_grads, up_tokens = feedforward(
        sizes, nmlp, middle, gains, cot_all, w_gate, w_up, down_weight, gate_weight.T, up_weight.T
    )
    layer_out, input_grad, vec, joint, db, ga, gb, ua, ub, oa, ob = backward(
        sizes, grad_middle, x_own, middle, gains, gain_mlp, seq_lengths, turns, normed, queries, kv,
        attended, w_joint, w_out, down_part, sum_mate, sum_across, sum_gate,
        up_grads, up_tokens,
    )
    if dp == 2:
        return finish(
            d.reshape(1, 1), layer_out, input_grad, vec, joint, da, db, ga, gb, ua, ub, oa, ob
        )
    h = d // (dp // 2)

    def rest_of_dp(v):
        full = jnp.concatenate([jnp.where(h == 0, v, 0.0), jnp.where(h == 1, v, 0.0)], axis=0)
        return lax.psum_scatter(full, "dp", scatter_dimension=0, tiled=True)

    vec = lax.psum(jnp.where(h == 0, vec[0], 0.0), "dp")

    def own_share(v):
        n = v.shape[0] // dp
        return lax.dynamic_slice_in_dim(v, d * n, n)

    both = lambda a, b: rest_of_dp(a.astype(F32) + b.astype(F32))
    joint = rest_of_dp(joint)
    bias = vec[2 * block :]
    return (
        layer_out, input_grad, vec[:block], joint[:, :wq_width], own_share(bias[:wq_width]),
        joint[:, wq_width:], own_share(bias[wq_width:]), both(oa, ob), vec[block : 2 * block],
        both(ga, gb), both(ua, ub), both(da, db),
    )


def solution(mesh):
    return jax.shard_map(
        on_device,
        mesh=mesh,
        in_specs=(
            P(("dp", "row"), "col"), P("dp", None), P("col"), P("col", "row"), P("row"),
            P("col", "row"), P("row"), P("row", "col"), P("col"), P("col", "row"),
            P("col", "row"), P("row", "col"), P(("dp", "row"), "col"),
        ),
        out_specs=(
            P(("dp", "row"), "col"), P(("dp", "row"), "col"), P("col"),
            P(("col", "dp"), "row"), P(("row", "dp")), P(("col", "dp"), "row"),
            P(("row", "dp")), P(("row", "dp"), "col"), P("col"), P(("col", "dp"), "row"),
            P(("col", "dp"), "row"), P(("row", "dp"), "col"),
        ),
        check_vma=False,
    )
```

```python
import functools

import jax
import jax.numpy as jnp
import numpy as np
from jax import lax
from jax.experimental import pallas as pl
from jax.experimental.pallas import tpu as pltpu
from jax.sharding import PartitionSpec as P

HEAD = 128
epsilon = 1e-06
rope_base = 1000000.0
masked_score = -1e30
BF = jnp.bfloat16
F32 = jnp.float32
MESH = pl.DeviceIdType.MESH
ANY = pl.BlockSpec(memory_space=pl.ANY)
VMEM = pl.BlockSpec(memory_space=pltpu.VMEM)
SMEM = pl.BlockSpec(memory_space=pltpu.SMEM)
VMEM_LIMIT = 63 * 2**20


def dot(a, b, ca=1, cb=0):
    return lax.dot_general(a, b, (((ca,), (cb,)), ((), ())), preferred_element_type=F32)


class Net:
    def __init__(self, sizes, send, recv, local):
        self.dp, self.R, self.C = sizes
        self.d = lax.axis_index("dp")
        self.r = lax.axis_index("row")
        self.c = lax.axis_index("col")
        half = self.dp // 2
        self.h = self.d // half
        self.send, self.recv, self.local = send, recv, local
        self.n = 0
        self.n_local = 0
        self.other_h = 1 - self.h
        self.mate = (lax.rem(self.d + half, self.dp), self.r, self.c)
        self.sibling = self.at_col(self.c + 1 - 2 * lax.rem(self.c, 2))
        self.across_c = lax.rem(self.c + 2, 4)
        self.across = self.at_col(self.across_c)

    def at_col(self, c):
        return (self.d, self.r, c)

    def at_row(self, r):
        return (self.d, r, self.c)

    def copy(self, src, dst, dev):
        i = self.n
        self.n += 1
        return pltpu.make_async_remote_copy(
            src_ref=src, dst_ref=dst, send_sem=self.send.at[i], recv_sem=self.recv.at[i],
            device_id=dev, device_id_type=MESH,
        )

    def like(self, copy_index, src, dst, dev):
        return pltpu.make_async_remote_copy(
            src_ref=src, dst_ref=dst, send_sem=self.send.at[copy_index],
            recv_sem=self.recv.at[copy_index], device_id=dev, device_id_type=MESH,
        )

    def here(self, src, dst):
        i = self.n_local
        self.n_local += 1
        return pltpu.make_async_copy(src, dst, self.local.at[i])

    def arrive(self):
        sem = pltpu.get_barrier_semaphore()
        for k in range(1, self.C):
            pl.semaphore_signal(
                sem, inc=1, device_id=self.at_col(lax.rem(self.c + k, self.C)), device_id_type=MESH
            )
        pl.semaphore_signal(sem, inc=1, device_id=self.mate, device_id_type=MESH)

        @pl.when(self.r > 0)
        def _():
            pl.semaphore_signal(sem, inc=1, device_id=self.at_row(self.r - 1), device_id_type=MESH)

        @pl.when(self.r < self.R - 1)
        def _():
            pl.semaphore_signal(sem, inc=1, device_id=self.at_row(self.r + 1), device_id_type=MESH)

    def barrier(self):
        sem = pltpu.get_barrier_semaphore()
        count = self.C + (self.r > 0).astype(jnp.int32) + (self.r < self.R - 1).astype(jnp.int32)
        pl.semaphore_wait(sem, count)


PARTS = 2


def shard(buf, j, q, parts):
    if len(buf.shape) == 4:
        return buf.at[q, j]
    n = buf.shape[1] // parts
    return buf.at[j, pl.ds(q * n, n)]


class LineGather:
    def __init__(self, net, buf, parts=PARTS):
        self.net, self.buf, self.parts = net, buf, parts
        self.base = net.n
        net.n += 2 * (net.R - 1) * parts

    def _copy(self, up, s, q, j):
        net = self.net
        b = shard(self.buf, jnp.clip(j, 0, net.R - 1), q, self.parts)
        to = jnp.minimum(net.r + 1, net.R - 1) if up else jnp.maximum(net.r - 1, 0)
        return net.like(self.base + 2 * (s * self.parts + q) + up, b, b, net.at_row(to))

    def step(self, s, which=None):
        net = self.net
        r, R = net.r, net.R
        for q in range(self.parts) if which is None else which:
            if s > 0:

                @pl.when(r - s >= 0)
                def _():
                    self._copy(1, s - 1, q, r - s).wait_recv()

            if s < R - 1:

                @pl.when((r - s >= 0) & (r < R - 1))
                def _():
                    self._copy(1, s, q, r - s).start()

            if s > 0:

                @pl.when(r + s < R)
                def _():
                    self._copy(0, s - 1, q, r + s).wait_recv()

            if s < R - 1:

                @pl.when((r + s < R) & (r > 0))
                def _():
                    self._copy(0, s, q, r + s).start()

    def finish(self):
        net = self.net
        r, R = net.r, net.R
        for s in range(R - 1):
            for q in range(self.parts):

                @pl.when((r - s >= 0) & (r < R - 1))
                def _():
                    self._copy(1, s, q, r - s).wait_send()

                @pl.when((r + s < R) & (r > 0))
                def _():
                    self._copy(0, s, q, r + s).wait_send()


class LineSum:
    def __init__(self, net, part, from_below, from_above, parts=PARTS):
        self.net, self.part, self.bu, self.bd, self.parts = net, part, from_below, from_above, parts
        self.base = net.n
        net.n += 2 * net.R * parts

    def _at(self, buf, j, q):
        return shard(buf, j, q, self.parts)

    def _copy(self, up, j, q):
        net = self.net
        j = jnp.clip(j, 0, net.R - 1)
        to = jnp.minimum(net.r + 1, net.R - 1) if up else jnp.maximum(net.r - 1, 0)
        return net.like(
            self.base + (2 * q + up) * net.R + j, self._at(self.part, j, q),
            self._at(self.bu if up else self.bd, j, q), net.at_row(to),
        )

    def _add(self, j, q, buf):
        mine, got = self._at(self.part, j, q), self._at(buf, j, q)
        mine[...] = (mine[...].astype(F32) + got[...].astype(F32)).astype(BF)

    def step(self, t, which=None):
        net = self.net
        r, R = net.r, net.R
        j = t - (R - 1 - r)
        k = R - 1 - (t - r)
        for q in range(self.parts) if which is None else which:

            @pl.when((j >= 0) & (r < R - 1))
            def _():
                self._copy(0, j, q).wait_recv()

            @pl.when((j >= 0) & (j < r))
            def _():
                @pl.when(r < R - 1)
                def _():
                    self._add(j, q, self.bd)

                self._copy(0, j, q).start()

            @pl.when((k <= R - 1) & (r > 0))
            def _():
                self._copy(1, k, q).wait_recv()

            @pl.when((k <= R - 1) & (k > r))
            def _():
                @pl.when(r > 0)
                def _():
                    self._add(k, q, self.bu)

                self._copy(1, k, q).start()

    def finish(self):
        net = self.net
        r, R = net.r, net.R
        for j in range(R):
            for q in range(self.parts):

                @pl.when(j < r)
                def _():
                    self._copy(0, j, q).wait_send()

                @pl.when(j > r)
                def _():
                    self._copy(1, j, q).wait_send()

    def total_into(self, out):
        net = self.net
        r, R = net.r, net.R
        n = out.shape[0] // self.parts
        for q in range(self.parts):
            mine = out.at[pl.ds(q * n, n)]
            mine[...] += self._at(self.part, r, q)[...].astype(F32)

            @pl.when(r < R - 1)
            def _():
                mine[...] += self._at(self.bd, r, q)[...].astype(F32)

            @pl.when(r > 0)
            def _():
                mine[...] += self._at(self.bu, r, q)[...].astype(F32)


class WeightGather:
    def __init__(self, net, src, full, by_rows, piece=0, pieces=1, keep=True):
        self.net, self.full, self.by_rows = net, full, by_rows
        if by_rows:
            self.n, self.w = full.shape[0] // net.C, full.shape[1]
        else:
            self.n, self.w = full.shape[0] // pieces, full.shape[1] // net.C
        self.first = piece * self.n
        if src is not None:
            src = src.at[pl.ds(self.first, self.n)]
        c, p, h, o = net.c, net.across_c, net.h, net.other_h
        half = self.n // 2
        self.here = None
        if src is not None:
            if keep:
                self.here = net.here(src, self.view(c, 0, 2))
            own_half = src.at[pl.ds(pl.multiple_of(h * half, 16), half)]
            own = src
        else:
            own_half, own = self.view(c, h, 1), self.view(c, 0, 2)
        self.x = net.copy(own_half, self.view(c, h, 1), net.across)
        self.sib = net.copy(own, self.view(c, 0, 2), net.sibling)
        self.y = net.copy(self.view(p, h, 1), self.view(p, h, 1), net.mate)
        self.sib_h = net.copy(self.view(p, h, 1), self.view(p, h, 1), net.sibling)
        self.sib_o = net.copy(self.view(p, o, 1), self.view(p, o, 1), net.sibling)

    def view(self, b, h, halves):
        half = self.n // 2
        if self.by_rows:
            return self.full.at[pl.ds(pl.multiple_of(b * self.n + h * half, 16), halves * half)]
        return self.full.at[
            pl.ds(pl.multiple_of(self.first + h * half, 16), halves * half),
            pl.ds(pl.multiple_of(b * self.w, 128), self.w),
        ]

    def start(self):
        if self.here is not None:
            self.here.start()
        self.x.start()
        self.sib.start()

    def pass_x(self):
        self.x.wait_recv()
        self.y.start()
        self.sib_h.start()

    def pass_y(self):
        self.y.wait_recv()
        self.sib_o.start()

    def arrive(self):
        if self.here is not None:
            self.here.wait()
        self.sib.wait_recv()
        self.sib_h.wait_recv()
        self.sib_o.wait_recv()

    def finish(self):
        for cp in (self.x, self.sib, self.y, self.sib_h, self.sib_o):
            cp.wait_send()


class BlockSum:
    def __init__(self, net, source, piece, from_x, from_mate):
        self.net, self.piece = net, piece
        self.from_x, self.from_mate = from_x, from_mate
        o = net.other_h
        self.first = [net.copy(source(1, k, 0), from_x.at[k], net.across) for k in (0, 1)]
        self.first += [net.copy(source(i, o, 1), from_mate.at[i], net.mate) for i in (0, 1)]
        self.second = []

    def start(self):
        for cp in self.first:
            cp.start()

    def add(self):
        h = self.net.h
        for cp in self.first:
            cp.wait_recv()
        for ref, got in (
            (self.piece(0, 0, 0), self.from_x.at[0]), (self.piece(0, 1, 0), self.from_x.at[1]),
            (self.piece(0, h, 1), self.from_mate.at[0]), (self.piece(1, h, 1), self.from_mate.at[1]),
        ):
            ref[...] = (ref[...].astype(F32) + got[...].astype(F32)).astype(BF)

    def pass_on(self, got, which=(0, 1)):
        net = self.net
        cut, rest = self.from_x.shape[1], self.from_mate.shape[1]
        for k in which:
            if k == 0:
                cp = net.copy(self.piece(0, net.other_h, 0), got.at[pl.ds(0, cut)], net.mate)
            else:
                cp = net.copy(self.piece(1, net.h, 1), got.at[pl.ds(cut, rest)], net.across)
            cp.start()
            self.second.append(cp)

    def finish(self):
        for cp in self.first:
            cp.wait_send()
        for cp in self.second:
            cp.wait_send()
            cp.wait_recv()


def halves(ref, cut):
    def piece(i, h, ab):
        rows = pl.ds(cut, ref.shape[1] - cut) if ab else pl.ds(0, cut)
        return ref.at[2 * i + h, rows]

    return piece


def x_first(rows):
    return rows * 5 // 12 // 16 * 16


def turn(values, cos2, sin2):
    heads = []
    for i in range(values.shape[1] // HEAD):
        v = values[:, i * HEAD : (i + 1) * HEAD]
        heads.append(v * cos2 + pltpu.roll(v, HEAD // 2, 1) * sin2)
    return jnp.concatenate(heads, axis=1) if len(heads) > 1 else heads[0]


def attention_kernel(
    sizes,
    tok, cot, wq, wkv, wo, wg, wu, gain_a, gain_f, qb, kvb, lengths, rates,
    out_x, out_mid, out_nmlp, out_gains, out_turns, o_normed, o_q, o_kv, o_att, o_cot, o_wj, o_wo, o_wg, o_wu,
    xin, cin, small, gains, kvb2, nall, call, wj, wov, kv, qs, att, part, rbu, rbd, o_x, o_mid, o_nmlp, o_gains, turns,
    send, recv, local,
):
    net = Net(sizes, send, recv, local)
    net.arrive()
    R, C, r, c = net.R, net.C, net.r, net.c
    sub, width = nall.shape[1], nall.shape[2]
    block = tok.shape[1]
    row_tok = sub * C
    n_tok = sub * R
    qw = wq.shape[1]
    slot = lax.rem(r, 2)
    partner = net.at_row(r + 1 - 2 * slot)
    line = lambda ref: ref[...].astype(F32).reshape(1, ref.shape[0])
    small[:, :block] = line(gain_a)
    small[:, block:] = line(gain_f)
    kvb2[slot] = line(kvb)
    net.barrier()
    cos2, sin2 = turns.at[:, pl.ds(0, HEAD)], turns.at[:, pl.ds(HEAD, HEAD)]
    ends = [lengths[0, 0]]
    for i in range(1, lengths.shape[1] - 1):
        ends.append(ends[-1] + lengths[0, i])

    def place_of(rr):
        here = rr * row_tok + c * sub + lax.broadcasted_iota(jnp.int32, (sub, 1), 0)
        first = jnp.zeros((sub, 1), jnp.int32)
        for end in ends:
            first = jnp.where(here >= end, end, first)
        return here, first

    def spread(src, dst):
        mine = pl.multiple_of(c * sub, sub)
        local_copy = net.here(src.at[pl.ds(mine, sub)], dst.at[c])
        copies = []
        for k in range(1, C):
            to = lax.rem(c + k, C)
            frm = lax.rem(c + C - k, C)
            i = net.n
            net.n += 1
            rows = pl.ds(pl.multiple_of(to * sub, sub), sub)
            copies.append(
                (net.like(i, src.at[rows], dst.at[c], net.at_col(to)),
                 net.like(i, src.at[rows], dst.at[frm], net.at_col(to)))
            )
        return local_copy, copies

    def begin(pair):
        pair[0].start()
        for out, _ in pair[1]:
            out.start()

    def arrived(pair):
        pair[0].wait()
        for _, inc in pair[1]:
            inc.wait_recv()

    tok_in, cot_in = spread(tok, xin), spread(cot, cin)
    gain_own = net.here(small, gains.at[c])
    gain_own.start()
    gain_copies = []
    for k in range(1, C):
        to, frm = lax.rem(c + k, C), lax.rem(c + C - k, C)
        i = net.n
        net.n += 1
        out = net.like(i, small, gains.at[c], net.at_col(to))
        gain_copies.append((out, net.like(i, small, gains.at[frm], net.at_col(to))))
        out.start()
    begin(tok_in)
    own_rows = pl.ds(pl.multiple_of(c * block, block), block)
    col_own = pl.ds(pl.multiple_of(qw + slot * HEAD, HEAD), HEAD)
    col_mate = pl.ds(pl.multiple_of(qw + (1 - slot) * HEAD, HEAD), HEAD)
    kv_x = net.copy(wkv, wj.at[own_rows, col_own], partner)
    kv_in = net.like(net.n - 1, wkv, wj.at[own_rows, col_mate], partner)
    kv_x.start()
    kvb_x = net.copy(kvb2.at[slot], kvb2.at[slot], partner)
    kvb_in = net.like(net.n - 1, kvb2.at[slot], kvb2.at[1 - slot], partner)
    kvb_x.start()
    wq_own = net.here(wq, wj.at[own_rows, pl.ds(0, qw)])
    wq_own.start()
    wkv_own = net.here(wkv, wj.at[own_rows, col_own])
    wkv_own.start()
    g_joint = WeightGather(net, None, wj, True)
    g_out = WeightGather(net, wo, wov, False)
    bulk = [WeightGather(net, w, o, False, i, 2, False) for w, o in ((wg, o_wg), (wu, o_wu)) for i in (0, 1)]

    wq_own.wait()
    wkv_own.wait()
    kv_in.wait_recv()
    g_joint.start()
    g_out.start()
    begin(cot_in)
    bulk[0].start()
    bulk[1].start()

    arrived(tok_in)
    gain_own.wait()
    for _, inc in gain_copies:
        inc.wait_recv()
    for k in range(C):
        o_gains[:, k * block : (k + 1) * block] = gains[k, :, :block]
        o_gains[:, width + k * block : width + (k + 1) * block] = gains[k, :, block:]
    x = jnp.concatenate([xin[k].astype(F32) for k in range(C)], axis=1)
    o_mid[...] = x
    o_x[...] = x.astype(BF)
    inv = lax.rsqrt(jnp.mean(x * x, axis=-1, keepdims=True) + epsilon)
    nall[r] = (x * inv * o_gains[0:1, :width]).astype(BF)
    g_n = LineGather(net, nall)
    g_n.step(0)
    g_joint.pass_x()
    g_out.pass_x()
    g_n.step(1)
    g_joint.pass_y()
    g_out.pass_y()
    arrived(cot_in)
    for k in range(C):
        call[r, :, k * block : (k + 1) * block] = cin[k]
    lane = lax.broadcasted_iota(jnp.int32, (1, HEAD), 1)
    for rr in range(R):
        here, first = place_of(rr)
        angle = (here - first).astype(F32) * rates[...]
        mine = slice(rr * sub, (rr + 1) * sub)
        cos2[mine, :] = jnp.cos(angle)
        sin2[mine, :] = jnp.where(lane < HEAD // 2, -1.0, 1.0) * jnp.sin(angle)
    g_n.step(2)
    bulk[0].pass_x()
    g_joint.arrive()
    kvb_in.wait_recv()
    bias = jnp.concatenate([line(qb), kvb2[0], kvb2[1]], axis=1)
    n = sub // PARTS
    kv_far, kv_sib, kv_pass = [], [], []
    for q in range(PARTS):
        g_n.step(3, (q,))
        spots = [slice(rr * sub + q * n, rr * sub + (q + 1) * n) for rr in range(R)]
        cos_q, sin_q = (jnp.concatenate([t[p, :] for p in spots], axis=0) for t in (cos2, sin2))
        some = slice(q * n, (q + 1) * n)
        joint = dot(nall[:, some, :].reshape(R * n, width), wj[...]) + bias
        kv[:, c, some, :HEAD] = turn(joint[:, qw : qw + HEAD], cos_q, sin_q).astype(BF).reshape(R, n, HEAD)
        kv[:, c, some, HEAD:] = joint[:, qw + HEAD :].astype(BF).reshape(R, n, HEAD)
        own, far = (kv.at[:, k, pl.ds(q * n, n)] for k in (c, net.across_c))
        kv_far.append(net.copy(own, own, net.across))
        kv_sib.append(net.copy(own, own, net.sibling))
        kv_pass.append(net.copy(far, far, net.sibling))
        kv_far[q].start()
        kv_sib[q].start()
        queries = turn(joint[:, :qw], cos_q, sin_q).astype(BF)
        for rr, p in enumerate(spots):
            qs[p, :] = queries[rr * n : (rr + 1) * n]
    g_cot = LineGather(net, call)
    g_cot.step(0)
    tail = [net.here(o_x, out_x), net.here(o_gains, out_gains), net.here(turns, out_turns)]
    for cp in tail:
        cp.start()
    out_normed = net.here(nall, o_normed)
    out_normed.start()
    out_wj = net.here(wj, o_wj)
    out_wj.start()
    bulk[0].pass_y()
    bulk[1].pass_x()
    bulk[2].start()
    bulk[3].start()
    for q in range(PARTS):
        kv_far[q].wait_recv()
        kv_pass[q].start()
    for cp in kv_sib + kv_pass:
        cp.wait_recv()
    g_cot.step(1)
    out_kv = net.here(kv, o_kv)
    out_kv.start()
    scale = HEAD ** (-0.5)
    g_out.arrive()
    rs = LineSum(net, part, rbu, rbd)
    for rr in [R - 1, 0] + list(range(R - 2, 0, -1)):
        limit = (rr + 1) * row_tok
        keys = kv[: rr + 1, :, :, :HEAD].reshape(limit, HEAD)
        values = kv[: rr + 1, :, :, HEAD:].reshape(limit, HEAD)
        mine = slice(rr * sub, (rr + 1) * sub)
        place = lax.broadcasted_iota(jnp.int32, (sub, limit), 1)
        here, first = place_of(rr)
        allowed = (place >= first) & (place <= here)
        for h in range(qw // HEAD):
            cols = slice(h * HEAD, (h + 1) * HEAD)
            s = jnp.where(allowed, dot(qs[mine, cols], keys, 1, 1) * scale, masked_score)
            e = jnp.exp(s - jnp.max(s, axis=-1, keepdims=True))
            p = e * (1.0 / jnp.sum(e, axis=-1, keepdims=True))
            att[mine, cols] = dot(p.astype(BF), values).astype(BF)
        part[rr] = dot(att[mine, :], wov[...]).astype(BF)
        if rr == 0:
            rs.step(0)
    out_q = net.here(qs, o_q)
    out_q.start()
    out_att = net.here(att, o_att)
    out_att.start()
    out_wo = net.here(wov, o_wo)
    out_wo.start()
    bulk[2].pass_x()
    g_cot.step(2)
    bulk[1].pass_y()
    rs.step(1)
    bulk[3].pass_x()
    g_cot.step(3)
    out_cot = net.here(call, o_cot)
    out_cot.start()
    rs.step(2)
    bulk[2].pass_y()
    rs.step(3)
    rs.total_into(o_mid)
    mid = o_mid[...]
    inv = lax.rsqrt(jnp.mean(mid * mid, axis=-1, keepdims=True) + epsilon)
    o_nmlp[...] = (mid * inv * o_gains[0:1, width:]).astype(BF)
    for src, dst in ((o_mid, out_mid), (o_nmlp, out_nmlp)):
        cp = net.here(src, dst)
        cp.start()
        tail.append(cp)
    bulk[3].pass_y()
    for g in bulk:
        g.arrive()
    for g in [g_joint, g_out, g_n, g_cot, rs] + bulk:
        g.finish()
    for out, _ in tok_in[1] + cot_in[1] + gain_copies:
        out.wait_send()
    for cp in kv_far + kv_sib + kv_pass:
        cp.wait_send()
    kv_x.wait_send()
    kvb_x.wait_send()
    for cp in tail + [out_normed, out_wj, out_kv, out_q, out_att, out_wo, out_cot]:
        cp.wait()


def attention_forward(
    sizes, tok, cot, wq, wkv, wo, wg, wu, gain_a, gain_f, qb, kvb, lengths, rates
):
    dp, R, C = sizes
    sub = tok.shape[0] // C
    block = tok.shape[1]
    width = block * C
    qw, jw = wq.shape[1], wq.shape[1] + 2 * HEAD
    n = sub * R
    ff = wg.shape[0]
    shape = jax.ShapeDtypeStruct
    outs = [
        (shape((sub, width), BF), ANY),
        (shape((sub, width), F32), ANY), (shape((sub, width), BF), ANY),
        (shape((1, 2 * width), F32), ANY), (shape((n, 2 * HEAD), F32), ANY),
        (shape((R, sub, width), BF), ANY),
        (shape((n, qw), BF), ANY), (shape((R, C, sub, 2 * HEAD), BF), ANY),
        (shape((n, qw), BF), ANY), (shape((R, sub, width), BF), ANY),
        (shape((width, jw), BF), ANY), (shape((qw, width), BF), ANY),
        (shape((ff, width), BF), ANY), (shape((ff, width), BF), ANY),
    ]
    return pl.pallas_call(
        functools.partial(attention_kernel, sizes),
        out_shape=[o for o, _ in outs],
        in_specs=[ANY] * 7 + [VMEM] * 4 + [SMEM, VMEM],
        out_specs=[s for _, s in outs],
        scratch_shapes=[
            pltpu.VMEM((C, sub, block), BF), pltpu.VMEM((C, sub, block), BF),
            pltpu.VMEM((1, 2 * block), F32), pltpu.VMEM((C, 1, 2 * block), F32), pltpu.VMEM((2, 1, HEAD), F32),
            pltpu.VMEM((R, sub, width), BF), pltpu.VMEM((R, sub, width), BF),
            pltpu.VMEM((width, jw), BF), pltpu.VMEM((qw, width), BF),
            pltpu.VMEM((R, C, sub, 2 * HEAD), BF), pltpu.VMEM((n, qw), BF),
            pltpu.VMEM((n, qw), BF), pltpu.VMEM((R, sub, width), BF),
            pltpu.VMEM((R, sub, width), BF), pltpu.VMEM((R, sub, width), BF),
            pltpu.VMEM((sub, width), BF), pltpu.VMEM((sub, width), F32),
            pltpu.VMEM((sub, width), BF), pltpu.VMEM((1, 2 * width), F32),
            pltpu.VMEM((n, 2 * HEAD), F32),
            pltpu.SemaphoreType.DMA((128,)), pltpu.SemaphoreType.DMA((128,)),
            pltpu.SemaphoreType.DMA((32,)),
        ],
        compiler_params=pltpu.CompilerParams(
            collective_id=1, has_side_effects=True, vmem_limit_bytes=VMEM_LIMIT
        ),
        name="attention_forward",
    )(tok, cot, wq, wkv, wo, wg, wu, gain_a, gain_f, qb, kvb, lengths, rates)


def feedforward_kernel(
    sizes,
    nmlp, in_mid, in_gains, cot, wg, wu, wd, own_g, own_u,
    out_gmid, out_gain, o_down, o_sd, o_sm, o_sx, o_sg, o_gu, o_xt,
    w_gate, w_up, w_down, xall, call, acc, hid, gg, gu, cc, sx, xt, part, rbu, rbd, dpart, g, x_d, y_d, o_gmid, o_gain, mid, gains,
    send, recv, local,
):
    net = Net(sizes, send, recv, local)
    net.arrive()
    R, C, r, c = net.R, net.C, net.r, net.c
    sub, width = nmlp.shape
    block = width // C
    n_tok = sub * R
    n_part = n_tok // PARTS
    n = sub // PARTS
    ff = w_gate.shape[0]
    tile = acc.shape[2]
    wide = width // tile
    own_cols = [pl.ds(pl.multiple_of(b * block, HEAD), block) for b in (c, net.across_c)]
    pieces = 5
    g_down = [WeightGather(net, wd, w_down, False, i, pieces) for i in range(pieces)]
    in_x = [net.here(nmlp.at[pl.ds(q * n, n)], xall.at[q, r]) for q in range(PARTS)]
    in_norm = [net.here(in_mid, mid), net.here(in_gains, gains)]
    for cp in in_x + in_norm:
        cp.start()
    in_cot = [net.here(cot.at[:, pl.ds(q * n, n)], call.at[q]) for q in range(PARTS)]
    for cp in in_cot:
        cp.start()
    in_w = []
    for full, own, w in ((wg, own_g, w_gate), (wu, own_u, w_up)):
        for k in range(C):
            cols = pl.ds(pl.multiple_of(lax.rem(c + k, C) * block, HEAD), block)
            cp = net.here(full.at[:, cols] if k else own, w.at[:, cols])
            cp.start()
            in_w.append(cp)
    if hid.shape[1] > ff:
        for ref in (hid, gg, gu):
            ref[:n_tok, ff:] = jnp.zeros((n_tok, hid.shape[1] - ff), BF)
    net.barrier()
    for cp in in_x:
        cp.wait()
    g_x = LineGather(net, xall)
    g_x.step(0, (0,))
    g_down[0].start()
    g_down[1].start()
    for cp in in_cot:
        cp.wait()
    to_sibling = []

    def hand(src, dst):
        cp = net.copy(src, dst, net.sibling)
        cp.start()
        to_sibling.append(cp)

    hand(call, dpart)
    for i in (0, 1):
        cc[0, :, :, :, i * block : (i + 1) * block] = call[:, :, :, own_cols[i]]

    def pass_x(i):
        g_down[i].pass_x()
        if i + 2 < pieces:
            g_down[i + 2].start()

    acts_out = [
        [
            net.copy(
                ref.at[pl.ds(q * n_part, n_part)], ref.at[pl.ds(n_tok + q * n_part, n_part)],
                net.sibling,
            )
            for ref in (hid, gg, gu)
        ]
        for q in range(PARTS)
    ]
    x_out = net.copy(xall, sx, net.sibling)
    to_sibling += [cp for pair in acts_out for cp in pair] + [x_out]
    rs = LineSum(net, part, rbu, rbd)
    full = ff // tile
    rest = pl.ds(full * tile, ff - full * tile)

    def act(q, rows, back):
        mine = pl.ds(pl.multiple_of(q * n_part, n_part), n_part)
        x = xall[q].reshape(n_part, width)
        gate = dot(x, w_gate[rows, :], 1, 1)
        up = dot(x, w_up[rows, :], 1, 1)
        s = jax.nn.sigmoid(gate)
        silu = gate * s
        hid[mine, rows] = (silu * up).astype(BF)
        gg[mine, rows] = (back * up * s * (1.0 + gate * (1.0 - s))).astype(BF)
        gu[mine, rows] = (back * silu).astype(BF)

    pass_x(0)
    g_x.step(1, (0,))
    g_x.step(0, (1,))
    pass_x(1)
    g_down[0].pass_y()
    pass_x(2)
    g_x.step(2, (0,))
    g_down[1].pass_y()
    pass_x(3)

    def hidden_back(t):
        rows = pl.ds(pl.multiple_of(t * tile, tile), tile)
        acc[t] = dot(call[...].reshape(n_tok, width), w_down[rows, :], 1, 1)

    @pl.loop(0, 2)
    def _(t):
        @pl.when(t == 0)
        def _():
            g_down[0].arrive()
            g_down[1].arrive()

        @pl.when(t == 1)
        def _():
            g_x.step(1, (1,))
            g_down[2].pass_y()
            g_down[2].arrive()

        hidden_back(t)

    for cp in in_w:
        cp.wait()
    pass_x(4)
    g_x.step(3, (0,))

    @pl.loop(0, PARTS)
    def _(q):
        @pl.loop(0, full)
        def _(t):
            rows = pl.ds(pl.multiple_of(t * tile, tile), tile)

            @pl.when((q == 0) & (t >= 2))
            def _():
                @pl.when(t == 2)
                def _():
                    g_x.step(2, (1,))
                    g_down[3].pass_y()
                    g_down[3].arrive()

                @pl.when(t == 3)
                def _():
                    g_down[4].pass_y()
                    g_down[4].arrive()

                hidden_back(t)

            act(q, rows, acc[t, pl.ds(pl.multiple_of(q * n_part, n_part), n_part)])

            @pl.when((q == 1) & (t == full - 1))
            def _():
                rs.step(1, (0,))

        act(q, rest, dot(call[q].reshape(n_part, width), w_down[rest, :], 1, 1))

        @pl.when(q == 0)
        def _():
            g_x.step(3, (1,))

        for k in range(PARTS):

            @pl.when(q == k)
            def _():
                for cp in acts_out[k]:
                    cp.start()

        mine = pl.ds(pl.multiple_of(q * n_part, n_part), n_part)

        @pl.loop(0, wide)
        def _(i):
            cols = pl.ds(pl.multiple_of(i * tile, tile), tile)
            total = dot(gg[mine, :ff], w_gate[:, cols]) + dot(gu[mine, :ff], w_up[:, cols])
            part[q, :, :, cols] = total.astype(BF).reshape(R, n, tile)

        @pl.when(q == 0)
        def _():
            rs.step(0, (0,))
            x_out.start()

        @pl.when(q == 1)
        def _():
            rs.step(0, (1,))
            rs.step(2, (0,))

    for g_piece in g_down:
        g_piece.finish()
    for cp in to_sibling:
        cp.wait_recv()
    outs = [net.here(gu, o_gu)]
    outs[0].start()
    for i in (0, 1):
        cc[1, :, :, :, i * block : (i + 1) * block] = dpart[:, :, :, own_cols[i]]

    def all_tiles(body):
        @pl.loop(0, full)
        def _(t):
            body(pl.ds(pl.multiple_of(t * tile, tile), tile))

        body(rest)

    def down_grad(rows):
        total = dot(hid[:, rows], cc[...].reshape(2 * n_tok, 2 * block), 0, 0)
        w_gate[rows, : 2 * block] = total.astype(BF)

    all_tiles(down_grad)
    half_ff = ff // 2
    cut = x_d.shape[1]

    def down_piece(i, h, ab):
        first, count = (cut, half_ff - cut) if ab else (0, cut)
        return w_gate.at[
            pl.ds(pl.multiple_of(h * half_ff + first, 16), count), pl.ds(i * block, block)
        ]

    sum_d = BlockSum(net, down_piece, down_piece, x_d, y_d)
    sum_d.start()
    rs.step(1, (1,))
    rs.step(3, (0,))

    @pl.loop(0, wide)
    def _(i):
        cols = pl.ds(pl.multiple_of(i * tile, tile), tile)
        total = dot(hid[:n_tok, :ff], w_down[:, cols])
        dpart[:, :, :, cols] = total.astype(BF).reshape(PARTS, R, n, tile)

    rs.step(2, (1,))
    out_down = [net.here(dpart.at[q], o_down.at[:, pl.ds(q * n, n)]) for q in range(PARTS)]
    for cp in out_down:
        cp.start()
    for i in (0, 1):
        rows = slice(i * block, (i + 1) * block)
        xt[rows, :n_tok] = xall[:, :, :, own_cols[i]].reshape(n_tok, block).T
        xt[rows, n_tok:] = sx[:, :, :, own_cols[i]].reshape(n_tok, block).T
    def gate_grad(cols):
        total = dot(xt[...], gg[:, cols])
        g[:, :, cols] = total.astype(BF).reshape(4, g.shape[1], cols.size)

    all_tiles(gate_grad)
    for src, dst in ((g, o_sg), (xt, o_xt)):
        cp = net.here(src, dst)
        cp.start()
        outs.append(cp)
    rs.step(3, (1,))
    o_gmid[...] = jnp.zeros_like(o_gmid)
    rs.total_into(o_gmid)
    for cp in in_norm:
        cp.wait()
    grad = o_gmid[...]
    m = mid[...]
    inv = lax.rsqrt(jnp.mean(m * m, axis=-1, keepdims=True) + epsilon)
    normal = m * inv
    e = grad * gains[0:1, width:]
    back = inv * (e - normal * jnp.mean(e * normal, axis=-1, keepdims=True))
    o_gain[...] = jnp.sum(grad * normal, axis=0, keepdims=True)
    for q in range(PARTS):
        rows = slice(q * n, (q + 1) * n)
        o_gmid[rows] = call[q, r].astype(F32) + back[rows]
    for src, dst in ((o_gmid, out_gmid), (o_gain, out_gain)):
        cp = net.here(src, dst)
        cp.start()
        outs.append(cp)
    rs.finish()
    sum_d.add()
    own_half = w_gate.at[
        pl.ds(pl.multiple_of(net.h * half_ff, 16), half_ff), pl.ds(0, block)
    ]
    for src, dst in (
        (own_half, o_sd), (down_piece(0, net.other_h, 0), o_sm), (down_piece(1, net.h, 1), o_sx)
    ):
        cp = net.here(src, dst)
        cp.start()
        outs.append(cp)
    sum_d.finish()
    g_x.finish()
    for cp in to_sibling:
        cp.wait_send()
    for cp in outs + out_down:
        cp.wait()


def feedforward(sizes, nmlp, mid, gains, cot, wg, wu, wd, own_g, own_u):
    dp, R, C = sizes
    sub, width = nmlp.shape
    block = width // C
    n_tok = R * sub
    ff = wd.shape[0]
    tile = 512
    cut = ff // 4
    shape = jax.ShapeDtypeStruct
    outs = [
        (shape((sub, width), F32), ANY), (shape((1, width), F32), ANY),
        (shape((R, sub, width), BF), ANY), (shape((ff // 2, block), BF), ANY),
        (shape((cut, block), BF), ANY), (shape((ff // 2 - cut, block), BF), ANY),
        (shape((4, block // 2, ff), BF), ANY),
        (shape((2 * n_tok, -(-ff // HEAD) * HEAD), BF), ANY),
        (shape((2 * block, 2 * n_tok), BF), ANY),
    ]
    v = pltpu.VMEM
    line = v((PARTS, R, sub // PARTS, width), BF)
    acts = v((2 * n_tok, -(-ff // HEAD) * HEAD), BF)
    weight = v((ff, width), BF)
    return pl.pallas_call(
        functools.partial(feedforward_kernel, sizes),
        out_shape=[o for o, _ in outs],
        in_specs=[ANY] * 9,
        out_specs=[s for _, s in outs],
        scratch_shapes=[
            weight, weight, weight, line, line, v((ff // tile, n_tok, tile), F32), acts, acts, acts,
            v((2, PARTS, R, sub // PARTS, 2 * block), BF), line,
            v((2 * block, 2 * n_tok), BF), line, line, line, line, v((4, block // 2, ff), BF),
            v((2, cut, block), BF), v((2, ff // 2 - cut, block), BF),
            v((sub, width), F32), v((1, width), F32), v((sub, width), F32), v((1, 2 * width), F32),
            pltpu.SemaphoreType.DMA((128,)), pltpu.SemaphoreType.DMA((128,)),
            pltpu.SemaphoreType.DMA((32,)),
        ],
        compiler_params=pltpu.CompilerParams(
            collective_id=2, has_side_effects=True, vmem_limit_bytes=VMEM_LIMIT
        ),
        name="feedforward",
    )(nmlp, mid, gains, cot, wg, wu, wd, own_g, own_u)


def backward_kernel(
    sizes,
    in_gmid, in_x, in_mid, in_gains, in_gain_mlp, lengths, in_turns,
    normed, q, kv, att, wj, wo, down, sm, sx, sg, up_grads, xt_in,
    o_layer, o_input, out_vec, out_j, o_db, o_ga, o_gb, o_ua, o_ub, o_oa, o_ob,
    mall, nall, qs, kvs, atts, wjs, wos, dpart, drbu, drbd, part, rbu, rbd, grads, dq, dkv, dkv16, dk_sib, dk_in,
    joint, lay,
    s_g, s_u, x_g, x_u, y_g, y_u,
    wjo, wjx, s_j, x_j, y_j, woo, wox, s_o, x_o, y_o, jb, jk, jk2, jgot, v1, v1in, v2, v2in, o_vec, o_j,
    gmid, x_in, mid, gains, gain_mlp, turns, gu, xt,
    send, recv, local,
):
    net = Net(sizes, send, recv, local)
    R, C, r, c = net.R, net.C, net.r, net.c
    sem = pltpu.get_barrier_semaphore()
    half = net.dp // 2
    others = [(net.d, r, lax.rem(c + k, C)) for k in range(1, C)]
    others += [(net.d, lax.rem(r + k, R), c) for k in range(1, R)]
    others += [(net.mate[0], lax.rem(r + k, R), c) for k in range(R)]
    for dev in others:
        pl.semaphore_signal(sem, inc=1, device_id=dev, device_id_type=MESH)
    R, C, r, c = net.R, net.C, net.r, net.c
    sub, width = in_gmid.shape
    block = width // C
    n_tok = sub * R
    row_tok = sub * C
    qw = qs.shape[1]
    slot = lax.rem(r, 2)
    cos2, sin2 = turns.at[:, pl.ds(0, HEAD)], turns.at[:, pl.ds(HEAD, HEAD)]
    partner_r = r + 1 - 2 * slot
    small_loads = [
        net.here(a, b) for a, b in
        ((in_gmid, gmid), (in_x, x_in), (in_mid, mid), (in_gains, gains), (in_gain_mlp, gain_mlp),
         (in_turns, turns))
    ]
    up_loads = [net.here(up_grads, gu), net.here(xt_in, xt)]
    for cp in small_loads + up_loads:
        cp.start()
    loads = [
        net.here(a, b) for a, b in
        ((wo, wos), (att, atts), (q, qs), (kv, kvs), (down, dpart), (sg, s_g),
         (normed, nall), (wj, wjs))
    ]
    for cp in loads:
        cp.start()
    pl.semaphore_wait(sem, len(others))

    small_loads[0].wait()
    mall[r] = gmid[...].astype(BF)
    g_m = LineGather(net, mall)
    g_m.step(0)
    sum_g = BlockSum(net, halves(sg, x_g.shape[1]), halves(s_g, x_g.shape[1]), x_g, y_g)
    sum_u = BlockSum(net, halves(s_u, x_u.shape[1]), halves(s_u, x_u.shape[1]), x_u, y_u)
    sum_g.start()
    for cp in up_loads:
        cp.wait()
    ff = s_u.shape[2]

    def up_tile(cols):
        total = dot(xt[...], gu[:, cols])
        s_u[:, :, cols] = total.astype(BF).reshape(4, s_u.shape[1], cols.size)

    @pl.loop(0, ff // 512)
    def _(t):
        up_tile(pl.ds(pl.multiple_of(t * 512, 512), 512))

    up_tile(pl.ds(ff // 512 * 512, ff % 512))
    sum_u.start()
    cut_d, rest_d = sm.shape[0], sx.shape[0]
    sum_d = [
        net.copy(sx, o_db.at[pl.ds(cut_d, rest_d)], net.across),
        net.copy(sm, o_db.at[pl.ds(0, cut_d)], net.mate),
    ]
    sum_d[0].start()
    g_m.step(1)
    for cp in loads[:6] + small_loads[1:]:
        cp.wait()
    g_m.step(2)
    sum_g.add()
    sum_g.pass_on(o_gb, (0,))
    g_m.step(3)
    rs_d = LineSum(net, dpart, drbu, drbd)
    rs_d.step(0)
    m_all = mall[...].reshape(n_tok, width)
    grads[...] = dot(m_all, wos[...], 1, 1).astype(BF)

    def to_columns(src, dst):
        rows = pl.ds(pl.multiple_of(c * sub, sub), sub)
        mine = net.here(src.at[:, pl.ds(pl.multiple_of(c * block, HEAD), block)], dst.at[rows])
        mine.start()
        pairs = []
        for k in range(1, C):
            to, frm = lax.rem(c + k, C), lax.rem(c + C - k, C)
            i = net.n
            net.n += 1
            cut = src.at[:, pl.ds(pl.multiple_of(to * block, HEAD), block)]
            out = net.like(i, cut, dst.at[rows], net.at_col(to))
            out.start()
            from_rows = pl.ds(pl.multiple_of(frm * sub, sub), sub)
            pairs.append((out, net.like(i, cut, dst.at[from_rows], net.at_col(to))))
        return mine, pairs

    def settle(exchange):
        exchange[0].wait()
        for out, inc in exchange[1]:
            inc.wait_recv()
            out.wait_send()

    sib_blocks = [b + 1 - 2 * lax.rem(b, 2) for b in (c, net.across_c)]
    total = dot(atts[...], m_all, 0, 0)
    for b in range(C):
        woo[2 * b : 2 * b + 2] = (
            total[:, b * block : (b + 1) * block].astype(BF).reshape(2, qw // 2, block)
        )
    out_x = [net.copy(woo.at[pl.ds(2 * b, 2)], wox.at[i], net.sibling) for i, b in enumerate(sib_blocks)]
    for cp in out_x:
        cp.start()
    scale = HEAD ** (-0.5)
    heads = qw // HEAD
    ends = [lengths[0, 0]]
    for i in range(1, lengths.shape[1] - 1):
        ends.append(ends[-1] + lengths[0, i])
    for rr in reversed(range(R)):
        limit = (rr + 1) * row_tok
        keys = kvs[: rr + 1, :, :, :HEAD].reshape(limit, HEAD)
        values = kvs[: rr + 1, :, :, HEAD:].reshape(limit, HEAD)
        mine = slice(rr * sub, (rr + 1) * sub)
        stack = lambda ref: jnp.concatenate(
            [ref[mine, h * HEAD : (h + 1) * HEAD] for h in range(heads)], axis=0
        )
        qh, gh = stack(qs), stack(grads)
        place = lax.broadcasted_iota(jnp.int32, (limit, heads * sub), 0)
        lane = lax.broadcasted_iota(jnp.int32, (1, heads * sub), 1)
        here = rr * row_tok + c * sub + lax.rem(lane, sub)
        first = jnp.zeros_like(here)
        for end in ends:
            first = jnp.where(here >= end, end, first)
        s = jnp.where(
            (place >= first) & (place <= here), dot(keys, qh, 1, 1) * scale, masked_score
        )
        e = jnp.exp(s - jnp.max(s, axis=0, keepdims=True))
        p = e * (1.0 / jnp.sum(e, axis=0, keepdims=True))
        g = dot(values, gh, 1, 1)
        ds = (p * (g - jnp.sum(p * g, axis=0, keepdims=True))).astype(BF)
        dv = dot(p.astype(BF), gh)
        dk = dot(ds, qh) * scale
        if rr == R - 1:
            dkv[:, :HEAD] = dk
            dkv[:, HEAD:] = dv
        else:
            dkv[:limit, :HEAD] += dk
            dkv[:limit, HEAD:] += dv
        dqs = dot(ds, keys, 0, 0) * scale
        for h in range(heads):
            dq[mine, h * HEAD : (h + 1) * HEAD] = dqs[h * sub : (h + 1) * sub]
        if rr == R - 2:
            rs_d.step(1)
            for i, b in enumerate((c, net.across_c)):
                out_x[i].wait_recv()
                s_o[2 * i : 2 * i + 2] = (
                    woo[pl.ds(2 * b, 2)].astype(F32) + wox[i].astype(F32)
                ).astype(BF)
    sib_c = c + 1 - 2 * lax.rem(c, 2)
    far_c = net.across_c
    far_sib_c = far_c + 1 - 2 * lax.rem(far_c, 2)
    dkv16[...] = dkv[...].astype(BF).reshape(dkv16.shape)
    dk_copies = [
        net.copy(dkv16.at[:, far_sib_c], dk_sib.at[1], net.sibling),
        net.copy(dkv16.at[:, sib_c], dk_sib.at[0], net.sibling),
    ]
    for cp in dk_copies:
        cp.start()
    dk_copies[0].wait_recv()
    dk_in[0] = (dkv16[:, far_c].astype(F32) + dk_sib[1].astype(F32)).astype(BF)
    dk_copies.append(net.copy(dk_in.at[0], dk_in.at[1], net.across))
    dk_copies[2].start()
    sum_g.pass_on(o_gb, (1,))
    sum_o = BlockSum(net, halves(s_o, x_o.shape[1]), halves(s_o, x_o.shape[1]), x_o, y_o)
    sum_o.start()
    rs_d.step(2)
    for cp in loads[6:]:
        cp.wait()
    slots = dkv16[:, c].astype(F32)
    dk_copies[1].wait_recv()
    slots = slots + dk_sib[0].astype(F32)
    dk_copies[2].wait_recv()
    slots = slots + dk_in[1].astype(F32)
    slots = slots.reshape(n_tok, 2 * HEAD)
    joint[:, :qw] = turn(dq[...], cos2[...], -sin2[...]).astype(BF)
    joint[:, qw : qw + HEAD] = turn(slots[:, :HEAD], cos2[...], -sin2[...]).astype(BF)
    joint[:, qw + HEAD :] = slots[:, HEAD:].astype(BF)
    part[...] = dot(joint[...], wjs[...], 1, 1).astype(BF).reshape(R, sub, width)
    rs = LineSum(net, part, rbu, rbd)
    rs.step(0)
    total = dot(nall[...].reshape(n_tok, width), joint[...], 0, 0)
    wjo[...] = total.astype(BF).reshape(wjo.shape)
    joint_x = [net.copy(wjo.at[pl.ds(2 * b, 2)], wjx.at[i], net.sibling) for i, b in enumerate(sib_blocks)]
    for cp in joint_x:
        cp.start()
    bias = jnp.sum(joint[...].astype(F32), axis=0, keepdims=True)
    for i, b in enumerate((c, net.across_c)):
        joint_x[i].wait_recv()
        s_j[2 * i : 2 * i + 2] = (
            wjo[pl.ds(2 * b, 2)].astype(F32) + wjx[i].astype(F32)
        ).astype(BF)
    sum_j = BlockSum(net, halves(s_j, x_j.shape[1]), halves(s_j, x_j.shape[1]), x_j, y_j)
    sum_j.start()
    sum_u.add()
    sum_u.pass_on(o_ub)
    rs_d.step(3)
    lay[0] = mid[...]
    rs_d.total_into(lay.at[0])
    jk[...] = lay[0].astype(BF)
    rs.step(1)
    sum_o.add()
    sum_o.pass_on(o_ob)
    rs.step(2)
    sum_j.add()
    sum_j.pass_on(jb)
    sum_d[1].start()
    keeps = [
        net.here(src.at[net.h], dst)
        for src, dst in ((s_g, o_ga), (s_u, o_ua), (s_o, o_oa))
    ]
    for cp in keeps:
        cp.start()
    rs.step(3)
    lay[1] = jnp.zeros_like(lay[1])
    rs.total_into(lay.at[1])
    grad = lay[1]
    x = x_in[...].astype(F32)
    inv = lax.rsqrt(jnp.mean(x * x, axis=-1, keepdims=True) + epsilon)
    normal = x * inv
    e = grad * gains[0:1, :width]
    back = inv * (e - normal * jnp.mean(e * normal, axis=-1, keepdims=True))
    gain_attn = jnp.sum(grad * normal, axis=0, keepdims=True)
    for k in range(C):
        cut = slice(k * block, (k + 1) * block)
        v1[k, :, :block] = gain_attn[:, cut]
        v1[k, :, block : 2 * block] = gain_mlp[:, cut]
        v1[k, :, 2 * block :] = bias
    v_copies = []
    for k in range(1, C):
        to, frm = lax.rem(c + k, C), lax.rem(c + C - k, C)
        i = net.n
        net.n += 1
        out = net.like(i, v1.at[to], v1in.at[c], net.at_col(to))
        out.start()
        v_copies.append((out, net.like(i, v1.at[to], v1in.at[frm], net.at_col(to)), frm))
    jk2[...] = (gmid[...] + back).astype(BF)
    input_x = to_columns(jk2, o_input)
    layer_x = to_columns(jk, o_layer)
    sum_j.finish()
    ja = s_j.at[net.h]
    own_cols = pl.ds(pl.multiple_of(qw + slot * HEAD, HEAD), HEAD)
    mate_cols = pl.ds(pl.multiple_of(qw + (1 - slot) * HEAD, HEAD), HEAD)
    jgot[0] = ja[:, mate_cols].astype(F32) + jb[:, mate_cols].astype(F32)
    slot_x = net.copy(jgot.at[0], jgot.at[1], net.at_row(partner_r))
    slot_x.start()
    o_j[:, :qw] = ja[:, :qw].astype(F32) + jb[:, :qw].astype(F32)
    total = v1[c]
    for _, inc, frm in v_copies:
        inc.wait_recv()
        total = total + v1in[frm]
    v2[...] = total
    far = []
    for same in (1, 0):
        for k in range(R):
            if same and k == 0:
                continue
            to, frm = lax.rem(r + k, R), lax.rem(r + R - k, R)
            i = net.n
            net.n += 1
            dst_d = net.d if same else net.mate[0]
            hs = net.h if same else net.other_h
            out = net.like(i, v2, v2in.at[net.h, r], (dst_d, to, c))
            out.start()
            far.append((out, net.like(i, v2, v2in.at[hs, frm], (dst_d, to, c))))
    v2in[net.h, r] = total
    slot_x.wait_recv()
    o_j[:, qw:] = ja[:, own_cols].astype(F32) + jb[:, own_cols].astype(F32) + jgot[1]
    tail = [net.here(o_j, out_j)]
    tail[0].start()
    for g in (sum_g, sum_u, sum_o):
        g.finish()
    for cp in sum_d:
        cp.wait()
    for cp in keeps:
        cp.wait()
    for _, inc in far:
        inc.wait_recv()
    gain_sum = v2in[0, 0, :, : 2 * block]
    for hh in (0, 1):
        for k in range(R):
            if hh or k:
                gain_sum = gain_sum + v2in[hh, k, :, : 2 * block]
    o_vec[:, : 2 * block] = gain_sum
    o_vec[:, 2 * block : 2 * block + qw] = (
        v2in[0, r, :, 2 * block : 2 * block + qw] + v2in[1, r, :, 2 * block : 2 * block + qw]
    )
    cols = pl.ds(pl.multiple_of(2 * block + qw + slot * HEAD, HEAD), HEAD)
    o_vec[:, 2 * block + qw :] = (
        v2in[0, r, :, cols] + v2in[1, r, :, cols]
        + v2in[0, partner_r, :, cols] + v2in[1, partner_r, :, cols]
    )
    tail.append(net.here(o_vec, out_vec))
    tail[1].start()
    settle(layer_x)
    settle(input_x)
    for g in (g_m, rs_d, rs):
        g.finish()
    for cp in out_x + joint_x + [slot_x]:
        cp.wait_send()
    for cp in dk_copies:
        cp.wait_send()
    for cps in v_copies + far:
        cps[0].wait_send()
    for cp in tail:
        cp.wait()


def backward(sizes, gmid, x_in, mid, gains, gain_mlp, lengths, turns, normed, q, kv, att, wj, wo,
             down, sm, sx, sg, up_grads, xt):
    dp, R, C = sizes
    sub, width = gmid.shape
    block = width // C
    n, qw = q.shape
    jw = wj.shape[1]
    ff = sg.shape[2]
    shape = jax.ShapeDtypeStruct
    d2, g2, w2, j2 = (ff // 2, block), (block // 2, ff), (qw // 2, block), (block // 2, jw)
    vec = 2 * block + jw
    outs = [
        (shape((C * sub, block), BF), ANY), (shape((C * sub, block), BF), ANY),
        (shape((1, vec - HEAD), F32), ANY), (shape((block // 2, jw - HEAD), F32), ANY),
        (shape(d2, BF), ANY), (shape(g2, BF), ANY), (shape(g2, BF), ANY),
        (shape(g2, BF), ANY), (shape(g2, BF), ANY), (shape(w2, BF), ANY), (shape(w2, BF), ANY),
    ]
    v = pltpu.VMEM
    four = lambda s: v((4,) + s, BF)

    def landing(s):
        cut = x_first(s[0])
        return [v((2, cut) + s[1:], BF), v((2, s[0] - cut) + s[1:], BF)]

    x_g, y_g = landing(g2)
    x_o, y_o = landing(w2)
    x_j, y_j = landing(j2)
    line = v((R, sub, width), BF)
    return pl.pallas_call(
        functools.partial(backward_kernel, sizes),
        out_shape=[o for o, _ in outs],
        in_specs=[ANY] * 5 + [SMEM] + [ANY] * 13,
        out_specs=[s for _, s in outs],
        scratch_shapes=[
            line, line, v((n, qw), BF), v(kv.shape, BF), v((n, qw), BF), v((width, jw), BF),
            v((qw, width), BF), line, line, line, line, line, line, v((n, qw), BF), v((n, qw), F32),
            v((n * C, 2 * HEAD), F32), v(kv.shape, BF), v((2, R, sub, 2 * HEAD), BF),
            v((2, R, sub, 2 * HEAD), BF),
            v((n, jw), BF), v((2, sub, width), F32),
            four(g2), four(g2), x_g, x_g, y_g, y_g,
            v((8,) + j2, BF), v((2, 2) + j2, BF), four(j2), x_j, y_j,
            v((8,) + w2, BF), v((2, 2) + w2, BF), four(w2), x_o, y_o,
            v(j2, BF), v((sub, width), BF), v((sub, width), BF), v((2, j2[0], HEAD), F32),
            v((C, 1, vec), F32), v((C, 1, vec), F32), v((1, vec), F32), v((2, R, 1, vec), F32),
            v((1, vec - HEAD), F32), v((block // 2, jw - HEAD), F32),
            v(gmid.shape, F32), v(x_in.shape, BF), v(mid.shape, F32), v(gains.shape, F32),
            v(gain_mlp.shape, F32), v(turns.shape, F32), v(up_grads.shape, BF), v(xt.shape, BF),
            pltpu.SemaphoreType.DMA((128,)), pltpu.SemaphoreType.DMA((128,)),
            pltpu.SemaphoreType.DMA((32,)),
        ],
        compiler_params=pltpu.CompilerParams(
            collective_id=3, has_side_effects=True, vmem_limit_bytes=VMEM_LIMIT
        ),
        name="backward",
    )(gmid, x_in, mid, gains, gain_mlp, lengths, turns, normed, q, kv, att, wj, wo, down, sm, sx, sg, up_grads, xt)

def finish_kernel(
    d, vec, joint, da, db, ga, gb, ua, ub, oa, ob, layer, inp,
    o_again, o_fgain, o_qb, o_kvb, o_q, o_kv, o_out, o_gate, o_up, o_down, o_layer, o_input,
    vec_v, joint_v, da_v, db_v, ga_v, gb_v, ua_v, ub_v, oa_v, ob_v,
    layer_v, inp_v, again_v, fgain_v, qb_v, kvb_v, q_v, kv_v, out_v, gate_v, up_v, down_v, sem_in, sem_out,
):
    pairs = (
        (vec, vec_v), (joint, joint_v), (oa, oa_v), (ob, ob_v), (da, da_v), (db, db_v),
        (ga, ga_v), (gb, gb_v), (ua, ua_v), (ub, ub_v), (layer, layer_v), (inp, inp_v),
    )
    loads = [pltpu.make_async_copy(s, t, sem_in.at[i]) for i, (s, t) in enumerate(pairs)]
    for cp in loads:
        cp.start()
    stores = []

    def store(src, dst):
        cp = pltpu.make_async_copy(src, dst, sem_out.at[len(stores)])
        cp.start()
        stores.append(cp)

    block, qw = o_again.shape[0], o_q.shape[1]
    loads[0].wait()
    second = d[0, 0] == 1
    again_v[...] = vec_v[0, :block]
    fgain_v[...] = vec_v[0, block : 2 * block]
    bias = vec_v[0:1, 2 * block :]
    pick = lambda v: jnp.where(second, v[:, v.shape[1] // 2 :], v[:, : v.shape[1] // 2])
    qb_v[...] = pick(bias[:, :qw])[0]
    kvb_v[...] = pick(bias[:, qw:])[0]
    for src, dst in ((again_v, o_again), (fgain_v, o_fgain), (qb_v, o_qb), (kvb_v, o_kvb)):
        store(src, dst)
    loads[1].wait()
    q_v[...] = joint_v[:, :qw]
    kv_v[...] = joint_v[:, qw:]
    store(q_v, o_q)
    store(kv_v, o_kv)
    for i, (a, b, f, o) in enumerate(
        ((oa_v, ob_v, out_v, o_out), (da_v, db_v, down_v, o_down), (ga_v, gb_v, gate_v, o_gate),
         (ua_v, ub_v, up_v, o_up))
    ):
        loads[2 + 2 * i].wait()
        loads[3 + 2 * i].wait()
        f[...] = a[...].astype(F32) + b[...].astype(F32)
        store(f, o)
    for i, (src, dst) in enumerate(((layer_v, o_layer), (inp_v, o_input))):
        loads[10 + i].wait()
        store(src, dst)
    for cp in stores:
        cp.wait()


def finish(d, layer, inp, vec, joint, da, db, ga, gb, ua, ub, oa, ob):
    block, qw, kvw = layer.shape[1], oa.shape[0] * 2, joint.shape[1] - oa.shape[0] * 2
    f32 = lambda *s: jax.ShapeDtypeStruct(s, F32)
    like = lambda v: jax.ShapeDtypeStruct(v.shape, F32)
    results = [
        f32(block), f32(block), f32(qw // 2), f32(kvw // 2), f32(joint.shape[0], qw),
        f32(joint.shape[0], kvw), like(oa), like(ga), like(ua), like(da),
    ]
    v = lambda a: pltpu.VMEM(a.shape, a.dtype)
    out = pl.pallas_call(
        finish_kernel,
        out_shape=results + [jax.ShapeDtypeStruct(a.shape, BF) for a in (layer, inp)],
        in_specs=[SMEM] + [ANY] * 12,
        out_specs=[ANY] * 12,
        scratch_shapes=[v(a) for a in (vec, joint, da, db, ga, gb, ua, ub, oa, ob, layer, inp)]
        + [v(a) for a in results]
        + [pltpu.SemaphoreType.DMA((12,)), pltpu.SemaphoreType.DMA((12,))],
        compiler_params=pltpu.CompilerParams(vmem_limit_bytes=VMEM_LIMIT),
        name="finish",
    )(d, vec, joint, da, db, ga, gb, ua, ub, oa, ob, layer, inp)
    again, fgain, q_bias, kv_bias, q, kv, o, gate, up, down, layer, inp = out
    return layer, inp, again, q, q_bias, kv, kv_bias, o, fgain, gate, up, down


def on_device(
    tokens_in, seq_lengths, attention_gain, query_weight, query_bias, keyvalue_weight,
    keyvalue_bias, output_weight, feedforward_gain, gate_weight, up_weight, down_weight,
    cotangent,
):
    sizes = dp, rows, cols = tuple(lax.axis_size(a) for a in ("dp", "row", "col"))
    d, col = lax.axis_index("dp"), lax.axis_index("col")
    sub = tokens_in.shape[0] // cols
    block = tokens_in.shape[1]
    wq_width = query_weight.shape[1]
    lane = np.arange(HEAD) % (HEAD // 2)
    rates = jnp.asarray((rope_base ** (-lane * (2.0 / HEAD))).astype(np.float32)[None])
    (x_own, middle, nmlp, gains, turns, normed, queries, kv, attended, cot_all, w_joint, w_out,
     w_gate, w_up) = attention_forward(
        sizes, tokens_in, cotangent, query_weight, keyvalue_weight, output_weight, gate_weight.T,
        up_weight.T, attention_gain, feedforward_gain, query_bias, keyvalue_bias, seq_lengths, rates,
    )
    grad_middle, gain_mlp, down_part, da, sum_mate, sum_across, sum_gate, up_grads, up_tokens = feedforward(
        sizes, nmlp, middle, gains, cot_all, w_gate, w_up, down_weight, gate_weight.T, up_weight.T
    )
    layer_out, input_grad, vec, joint, db, ga, gb, ua, ub, oa, ob = backward(
        sizes, grad_middle, x_own, middle, gains, gain_mlp, seq_lengths, turns, normed, queries, kv,
        attended, w_joint, w_out, down_part, sum_mate, sum_across, sum_gate,
        up_grads, up_tokens,
    )
    if dp == 2:
        return finish(
            d.reshape(1, 1), layer_out, input_grad, vec, joint, da, db, ga, gb, ua, ub, oa, ob
        )
    h = d // (dp // 2)

    def rest_of_dp(v):
        full = jnp.concatenate([jnp.where(h == 0, v, 0.0), jnp.where(h == 1, v, 0.0)], axis=0)
        return lax.psum_scatter(full, "dp", scatter_dimension=0, tiled=True)

    vec = lax.psum(jnp.where(h == 0, vec[0], 0.0), "dp")

    def own_share(v):
        n = v.shape[0] // dp
        return lax.dynamic_slice_in_dim(v, d * n, n)

    both = lambda a, b: rest_of_dp(a.astype(F32) + b.astype(F32))
    joint = rest_of_dp(joint)
    bias = vec[2 * block :]
    return (
        layer_out, input_grad, vec[:block], joint[:, :wq_width], own_share(bias[:wq_width]),
        joint[:, wq_width:], own_share(bias[wq_width:]), both(oa, ob), vec[block : 2 * block],
        both(ga, gb), both(ua, ub), both(da, db),
    )


def solution(mesh):
    return jax.shard_map(
        on_device,
        mesh=mesh,
        in_specs=(
            P(("dp", "row"), "col"), P("dp", None), P("col"), P("col", "row"), P("row"),
            P("col", "row"), P("row"), P("row", "col"), P("col"), P("col", "row"),
            P("col", "row"), P("row", "col"), P(("dp", "row"), "col"),
        ),
        out_specs=(
            P(("dp", "row"), "col"), P(("dp", "row"), "col"), P("col"),
            P(("col", "dp"), "row"), P(("row", "dp")), P(("col", "dp"), "row"),
            P(("row", "dp")), P(("row", "dp"), "col"), P("col"), P(("col", "dp"), "row"),
            P(("col", "dp"), "row"), P(("row", "dp"), "col"),
        ),
        check_vma=False,
    )
```

```python
import functools

import jax
import jax.numpy as jnp
import numpy as np
from jax import lax
from jax.experimental import pallas as pl
from jax.experimental.pallas import tpu as pltpu
from jax.sharding import PartitionSpec as P

HEAD = 128
epsilon = 1e-06
rope_base = 1000000.0
masked_score = -1e30
BF = jnp.bfloat16
F32 = jnp.float32
MESH = pl.DeviceIdType.MESH
ANY = pl.BlockSpec(memory_space=pl.ANY)
VMEM = pl.BlockSpec(memory_space=pltpu.VMEM)
SMEM = pl.BlockSpec(memory_space=pltpu.SMEM)
VMEM_LIMIT = 63 * 2**20


def dot(a, b, ca=1, cb=0):
    return lax.dot_general(a, b, (((ca,), (cb,)), ((), ())), preferred_element_type=F32)


class Net:
    def __init__(self, sizes, send, recv, local):
        self.dp, self.R, self.C = sizes
        self.d = lax.axis_index("dp")
        self.r = lax.axis_index("row")
        self.c = lax.axis_index("col")
        half = self.dp // 2
        self.h = self.d // half
        self.send, self.recv, self.local = send, recv, local
        self.n = 0
        self.n_local = 0
        self.other_h = 1 - self.h
        self.mate = (lax.rem(self.d + half, self.dp), self.r, self.c)
        self.sibling = self.at_col(self.c + 1 - 2 * lax.rem(self.c, 2))
        self.across_c = lax.rem(self.c + 2, 4)
        self.across = self.at_col(self.across_c)

    def at_col(self, c):
        return (self.d, self.r, c)

    def at_row(self, r):
        return (self.d, r, self.c)

    def copy(self, src, dst, dev):
        i = self.n
        self.n += 1
        return pltpu.make_async_remote_copy(
            src_ref=src, dst_ref=dst, send_sem=self.send.at[i], recv_sem=self.recv.at[i],
            device_id=dev, device_id_type=MESH,
        )

    def like(self, copy_index, src, dst, dev):
        return pltpu.make_async_remote_copy(
            src_ref=src, dst_ref=dst, send_sem=self.send.at[copy_index],
            recv_sem=self.recv.at[copy_index], device_id=dev, device_id_type=MESH,
        )

    def here(self, src, dst):
        i = self.n_local
        self.n_local += 1
        return pltpu.make_async_copy(src, dst, self.local.at[i])

    def arrive(self):
        sem = pltpu.get_barrier_semaphore()
        for k in range(1, self.C):
            pl.semaphore_signal(
                sem, inc=1, device_id=self.at_col(lax.rem(self.c + k, self.C)), device_id_type=MESH
            )
        pl.semaphore_signal(sem, inc=1, device_id=self.mate, device_id_type=MESH)

        @pl.when(self.r > 0)
        def _():
            pl.semaphore_signal(sem, inc=1, device_id=self.at_row(self.r - 1), device_id_type=MESH)

        @pl.when(self.r < self.R - 1)
        def _():
            pl.semaphore_signal(sem, inc=1, device_id=self.at_row(self.r + 1), device_id_type=MESH)

    def barrier(self):
        sem = pltpu.get_barrier_semaphore()
        count = self.C + (self.r > 0).astype(jnp.int32) + (self.r < self.R - 1).astype(jnp.int32)
        pl.semaphore_wait(sem, count)


PARTS = 2
PIECES = 5
EARLY = 3


def shard(buf, j, q, parts):
    if len(buf.shape) == 4:
        return buf.at[q, j]
    n = buf.shape[1] // parts
    return buf.at[j, pl.ds(q * n, n)]


class LineGather:
    def __init__(self, net, buf, parts=PARTS):
        self.net, self.buf, self.parts = net, buf, parts
        self.base = net.n
        net.n += 2 * (net.R - 1) * parts

    def _copy(self, up, s, q, j):
        net = self.net
        b = shard(self.buf, jnp.clip(j, 0, net.R - 1), q, self.parts)
        to = jnp.minimum(net.r + 1, net.R - 1) if up else jnp.maximum(net.r - 1, 0)
        return net.like(self.base + 2 * (s * self.parts + q) + up, b, b, net.at_row(to))

    def step(self, s, which=None):
        net = self.net
        r, R = net.r, net.R
        for q in range(self.parts) if which is None else which:
            if s > 0:

                @pl.when(r - s >= 0)
                def _():
                    self._copy(1, s - 1, q, r - s).wait_recv()

            if s < R - 1:

                @pl.when((r - s >= 0) & (r < R - 1))
                def _():
                    self._copy(1, s, q, r - s).start()

            if s > 0:

                @pl.when(r + s < R)
                def _():
                    self._copy(0, s - 1, q, r + s).wait_recv()

            if s < R - 1:

                @pl.when((r + s < R) & (r > 0))
                def _():
                    self._copy(0, s, q, r + s).start()

    def finish(self):
        net = self.net
        r, R = net.r, net.R
        for s in range(R - 1):
            for q in range(self.parts):

                @pl.when((r - s >= 0) & (r < R - 1))
                def _():
                    self._copy(1, s, q, r - s).wait_send()

                @pl.when((r + s < R) & (r > 0))
                def _():
                    self._copy(0, s, q, r + s).wait_send()


class LineSum:
    def __init__(self, net, part, from_below, from_above, parts=PARTS):
        self.net, self.part, self.bu, self.bd, self.parts = net, part, from_below, from_above, parts
        self.base = net.n
        net.n += 2 * net.R * parts

    def _at(self, buf, j, q):
        return shard(buf, j, q, self.parts)

    def _copy(self, up, j, q):
        net = self.net
        j = jnp.clip(j, 0, net.R - 1)
        to = jnp.minimum(net.r + 1, net.R - 1) if up else jnp.maximum(net.r - 1, 0)
        return net.like(
            self.base + (2 * q + up) * net.R + j, self._at(self.part, j, q),
            self._at(self.bu if up else self.bd, j, q), net.at_row(to),
        )

    def _add(self, j, q, buf):
        mine, got = self._at(self.part, j, q), self._at(buf, j, q)
        mine[...] = (mine[...].astype(F32) + got[...].astype(F32)).astype(BF)

    def step(self, t, which=None):
        net = self.net
        r, R = net.r, net.R
        j = t - (R - 1 - r)
        k = R - 1 - (t - r)
        for q in range(self.parts) if which is None else which:

            @pl.when((j >= 0) & (r < R - 1))
            def _():
                self._copy(0, j, q).wait_recv()

            @pl.when((j >= 0) & (j < r))
            def _():
                @pl.when(r < R - 1)
                def _():
                    self._add(j, q, self.bd)

                self._copy(0, j, q).start()

            @pl.when((k <= R - 1) & (r > 0))
            def _():
                self._copy(1, k, q).wait_recv()

            @pl.when((k <= R - 1) & (k > r))
            def _():
                @pl.when(r > 0)
                def _():
                    self._add(k, q, self.bu)

                self._copy(1, k, q).start()

    def finish(self):
        net = self.net
        r, R = net.r, net.R
        for j in range(R):
            for q in range(self.parts):

                @pl.when(j < r)
                def _():
                    self._copy(0, j, q).wait_send()

                @pl.when(j > r)
                def _():
                    self._copy(1, j, q).wait_send()

    def total_into(self, out):
        net = self.net
        r, R = net.r, net.R
        n = out.shape[0] // self.parts
        for q in range(self.parts):
            mine = out.at[pl.ds(q * n, n)]
            mine[...] += self._at(self.part, r, q)[...].astype(F32)

            @pl.when(r < R - 1)
            def _():
                mine[...] += self._at(self.bd, r, q)[...].astype(F32)

            @pl.when(r > 0)
            def _():
                mine[...] += self._at(self.bu, r, q)[...].astype(F32)


class WeightGather:
    def __init__(self, net, src, full, by_rows, piece=0, pieces=1, keep=True, crossed=None):
        self.net, self.full, self.by_rows = net, full, by_rows
        if by_rows:
            self.n, self.w = full.shape[0] // net.C, full.shape[1]
        else:
            self.n, self.w = full.shape[0] // pieces, full.shape[1] // net.C
        self.first = piece * self.n
        if src is not None:
            src = src.at[pl.ds(self.first, self.n)]
        c, p, h, o = net.c, net.across_c, net.h, net.other_h
        half = self.n // 2
        self.here = None
        if src is not None:
            if keep:
                self.here = net.here(src, self.view(c, 0, 2))
            own_half = src.at[pl.ds(pl.multiple_of(h * half, 16), half)]
            own = src
        else:
            own_half, own = self.view(c, h, 1), self.view(c, 0, 2)
        self.x, self.kept = None, None
        got = self.view(p, h, 1)
        if crossed is None:
            self.x = net.copy(own_half, self.view(c, h, 1), net.across)
        else:
            self.kept = net.here(crossed, got)
            got = crossed
        self.sib = net.copy(own, self.view(c, 0, 2), net.sibling)
        self.y = net.copy(got, self.view(p, h, 1), net.mate)
        self.sib_h = net.copy(got, self.view(p, h, 1), net.sibling)
        self.sib_o = net.copy(self.view(p, o, 1), self.view(p, o, 1), net.sibling)

    def view(self, b, h, halves):
        half = self.n // 2
        if self.by_rows:
            return self.full.at[pl.ds(pl.multiple_of(b * self.n + h * half, 16), halves * half)]
        return self.full.at[
            pl.ds(pl.multiple_of(self.first + h * half, 16), halves * half),
            pl.ds(pl.multiple_of(b * self.w, 128), self.w),
        ]

    def start(self):
        if self.here is not None:
            self.here.start()
        if self.x is None:
            self.kept.start()
            self.y.start()
            self.sib_h.start()
        else:
            self.x.start()
        self.sib.start()

    def pass_x(self):
        self.x.wait_recv()
        self.y.start()
        self.sib_h.start()

    def pass_y(self):
        self.y.wait_recv()
        self.sib_o.start()

    def arrive(self):
        if self.here is not None:
            self.here.wait()
        if self.kept is not None:
            self.kept.wait()
        self.sib.wait_recv()
        self.sib_h.wait_recv()
        self.sib_o.wait_recv()

    def finish(self):
        for cp in (self.x, self.sib, self.y, self.sib_h, self.sib_o):
            if cp is not None:
                cp.wait_send()


class BlockSum:
    def __init__(self, net, source, piece, from_x, from_mate):
        self.net, self.piece = net, piece
        self.from_x, self.from_mate = from_x, from_mate
        o = net.other_h
        self.first = [net.copy(source(1, k, 0), from_x.at[k], net.across) for k in (0, 1)]
        self.first += [net.copy(source(i, o, 1), from_mate.at[i], net.mate) for i in (0, 1)]
        self.second = []

    def start(self):
        for cp in self.first:
            cp.start()

    def add(self):
        h = self.net.h
        for cp in self.first:
            cp.wait_recv()
        for ref, got in (
            (self.piece(0, 0, 0), self.from_x.at[0]), (self.piece(0, 1, 0), self.from_x.at[1]),
            (self.piece(0, h, 1), self.from_mate.at[0]), (self.piece(1, h, 1), self.from_mate.at[1]),
        ):
            ref[...] = (ref[...].astype(F32) + got[...].astype(F32)).astype(BF)

    def pass_on(self, got, which=(0, 1)):
        net = self.net
        cut, rest = self.from_x.shape[1], self.from_mate.shape[1]
        for k in which:
            if k == 0:
                cp = net.copy(self.piece(0, net.other_h, 0), got.at[pl.ds(0, cut)], net.mate)
            else:
                cp = net.copy(self.piece(1, net.h, 1), got.at[pl.ds(cut, rest)], net.across)
            cp.start()
            self.second.append(cp)

    def finish(self):
        for cp in self.first:
            cp.wait_send()
        for cp in self.second:
            cp.wait_send()
            cp.wait_recv()


def halves(ref, cut):
    def piece(i, h, ab):
        rows = pl.ds(cut, ref.shape[1] - cut) if ab else pl.ds(0, cut)
        return ref.at[2 * i + h, rows]

    return piece


def x_first(rows):
    return rows * 5 // 12 // 16 * 16


def turn(values, cos2, sin2):
    heads = []
    for i in range(values.shape[1] // HEAD):
        v = values[:, i * HEAD : (i + 1) * HEAD]
        heads.append(v * cos2 + pltpu.roll(v, HEAD // 2, 1) * sin2)
    return jnp.concatenate(heads, axis=1) if len(heads) > 1 else heads[0]


def attention_kernel(
    sizes,
    tok, cot, wq, wkv, wo, wg, wu, wd, gain_a, gain_f, qb, kvb, lengths, rates,
    out_x, out_mid, out_nmlp, out_gains, out_turns, o_normed, o_q, o_kv, o_att, o_cot, o_wj, o_wo, o_wg, o_wu, o_wdx,
    xin, cin, small, gains, kvb2, nall, call, wj, wov, kv, qs, att, part, rbu, rbd, o_x, o_mid, o_nmlp, o_gains, turns,
    send, recv, local,
):
    net = Net(sizes, send, recv, local)
    net.arrive()
    R, C, r, c = net.R, net.C, net.r, net.c
    sub, width = nall.shape[1], nall.shape[2]
    block = tok.shape[1]
    row_tok = sub * C
    n_tok = sub * R
    qw = wq.shape[1]
    slot = lax.rem(r, 2)
    partner = net.at_row(r + 1 - 2 * slot)
    line = lambda ref: ref[...].astype(F32).reshape(1, ref.shape[0])
    small[:, :block] = line(gain_a)
    small[:, block:] = line(gain_f)
    kvb2[slot] = line(kvb)
    net.barrier()
    cos2, sin2 = turns.at[:, pl.ds(0, HEAD)], turns.at[:, pl.ds(HEAD, HEAD)]
    ends = [lengths[0, 0]]
    for i in range(1, lengths.shape[1] - 1):
        ends.append(ends[-1] + lengths[0, i])

    def place_of(rr):
        here = rr * row_tok + c * sub + lax.broadcasted_iota(jnp.int32, (sub, 1), 0)
        first = jnp.zeros((sub, 1), jnp.int32)
        for end in ends:
            first = jnp.where(here >= end, end, first)
        return here, first

    def spread(src, dst):
        mine = pl.multiple_of(c * sub, sub)
        local_copy = net.here(src.at[pl.ds(mine, sub)], dst.at[c])
        copies = []
        for k in range(1, C):
            to = lax.rem(c + k, C)
            frm = lax.rem(c + C - k, C)
            i = net.n
            net.n += 1
            rows = pl.ds(pl.multiple_of(to * sub, sub), sub)
            copies.append(
                (net.like(i, src.at[rows], dst.at[c], net.at_col(to)),
                 net.like(i, src.at[rows], dst.at[frm], net.at_col(to)))
            )
        return local_copy, copies

    def begin(pair):
        pair[0].start()
        for out, _ in pair[1]:
            out.start()

    def arrived(pair):
        pair[0].wait()
        for _, inc in pair[1]:
            inc.wait_recv()

    tok_in, cot_in = spread(tok, xin), spread(cot, cin)
    gain_own = net.here(small, gains.at[c])
    gain_own.start()
    gain_copies = []
    for k in range(1, C):
        to, frm = lax.rem(c + k, C), lax.rem(c + C - k, C)
        i = net.n
        net.n += 1
        out = net.like(i, small, gains.at[c], net.at_col(to))
        gain_copies.append((out, net.like(i, small, gains.at[frm], net.at_col(to))))
        out.start()
    begin(tok_in)
    own_rows = pl.ds(pl.multiple_of(c * block, block), block)
    col_own = pl.ds(pl.multiple_of(qw + slot * HEAD, HEAD), HEAD)
    col_mate = pl.ds(pl.multiple_of(qw + (1 - slot) * HEAD, HEAD), HEAD)
    kv_x = net.copy(wkv, wj.at[own_rows, col_own], partner)
    kv_in = net.like(net.n - 1, wkv, wj.at[own_rows, col_mate], partner)
    kv_x.start()
    kvb_x = net.copy(kvb2.at[slot], kvb2.at[slot], partner)
    kvb_in = net.like(net.n - 1, kvb2.at[slot], kvb2.at[1 - slot], partner)
    kvb_x.start()
    wq_own = net.here(wq, wj.at[own_rows, pl.ds(0, qw)])
    wq_own.start()
    wkv_own = net.here(wkv, wj.at[own_rows, col_own])
    wkv_own.start()
    g_joint = WeightGather(net, None, wj, True)
    g_out = WeightGather(net, wo, wov, False)
    bulk = [WeightGather(net, w, o, False, i, 2, False) for w, o in ((wg, o_wg), (wu, o_wu)) for i in (0, 1)]

    wq_own.wait()
    wkv_own.wait()
    kv_in.wait_recv()
    g_joint.start()
    g_out.start()
    begin(cot_in)
    bulk[0].start()
    bulk[1].start()

    arrived(tok_in)
    gain_own.wait()
    for _, inc in gain_copies:
        inc.wait_recv()
    for k in range(C):
        o_gains[:, k * block : (k + 1) * block] = gains[k, :, :block]
        o_gains[:, width + k * block : width + (k + 1) * block] = gains[k, :, block:]
    x = jnp.concatenate([xin[k].astype(F32) for k in range(C)], axis=1)
    o_mid[...] = x
    o_x[...] = x.astype(BF)
    inv = lax.rsqrt(jnp.mean(x * x, axis=-1, keepdims=True) + epsilon)
    nall[r] = (x * inv * o_gains[0:1, :width]).astype(BF)
    g_n = LineGather(net, nall)
    g_n.step(0)
    g_joint.pass_x()
    g_out.pass_x()
    g_n.step(1)
    g_joint.pass_y()
    g_out.pass_y()
    arrived(cot_in)
    for k in range(C):
        call[r, :, k * block : (k + 1) * block] = cin[k]
    lane = lax.broadcasted_iota(jnp.int32, (1, HEAD), 1)
    for rr in range(R):
        here, first = place_of(rr)
        angle = (here - first).astype(F32) * rates[...]
        mine = slice(rr * sub, (rr + 1) * sub)
        cos2[mine, :] = jnp.cos(angle)
        sin2[mine, :] = jnp.where(lane < HEAD // 2, -1.0, 1.0) * jnp.sin(angle)
    g_n.step(2)
    bulk[0].pass_x()
    g_joint.arrive()
    kvb_in.wait_recv()
    bias = jnp.concatenate([line(qb), kvb2[0], kvb2[1]], axis=1)
    n = sub // PARTS
    kv_far, kv_sib, kv_pass = [], [], []
    for q in range(PARTS):
        g_n.step(3, (q,))
        spots = [slice(rr * sub + q * n, rr * sub + (q + 1) * n) for rr in range(R)]
        cos_q, sin_q = (jnp.concatenate([t[p, :] for p in spots], axis=0) for t in (cos2, sin2))
        some = slice(q * n, (q + 1) * n)
        joint = dot(nall[:, some, :].reshape(R * n, width), wj[...]) + bias
        kv[:, c, some, :HEAD] = turn(joint[:, qw : qw + HEAD], cos_q, sin_q).astype(BF).reshape(R, n, HEAD)
        kv[:, c, some, HEAD:] = joint[:, qw + HEAD :].astype(BF).reshape(R, n, HEAD)
        own, far = (kv.at[:, k, pl.ds(q * n, n)] for k in (c, net.across_c))
        kv_far.append(net.copy(own, own, net.across))
        kv_sib.append(net.copy(own, own, net.sibling))
        kv_pass.append(net.copy(far, far, net.sibling))
        kv_far[q].start()
        kv_sib[q].start()
        queries = turn(joint[:, :qw], cos_q, sin_q).astype(BF)
        for rr, p in enumerate(spots):
            qs[p, :] = queries[rr * n : (rr + 1) * n]
    g_cot = LineGather(net, call)
    g_cot.step(0)
    tail = [net.here(o_x, out_x), net.here(o_gains, out_gains), net.here(turns, out_turns)]
    for cp in tail:
        cp.start()
    out_normed = net.here(nall, o_normed)
    out_normed.start()
    out_wj = net.here(wj, o_wj)
    out_wj.start()
    bulk[0].pass_y()
    bulk[1].pass_x()
    bulk[2].start()
    bulk[3].start()
    rows_d = wd.shape[0] // PIECES
    half_d = rows_d // 2
    early = [
        net.copy(
            wd.at[pl.ds(pl.multiple_of(i * rows_d + net.h * half_d, 16), half_d)], o_wdx.at[i], net.across
        )
        for i in range(EARLY)
    ]
    for cp in early:
        cp.start()
    for q in range(PARTS):
        kv_far[q].wait_recv()
        kv_pass[q].start()
    for cp in kv_sib + kv_pass:
        cp.wait_recv()
    g_cot.step(1)
    out_kv = net.here(kv, o_kv)
    out_kv.start()
    scale = HEAD ** (-0.5)
    g_out.arrive()
    rs = LineSum(net, part, rbu, rbd)
    for rr in [R - 1, 0] + list(range(R - 2, 0, -1)):
        limit = (rr + 1) * row_tok
        keys = kv[: rr + 1, :, :, :HEAD].reshape(limit, HEAD)
        values = kv[: rr + 1, :, :, HEAD:].reshape(limit, HEAD)
        mine = slice(rr * sub, (rr + 1) * sub)
        place = lax.broadcasted_iota(jnp.int32, (sub, limit), 1)
        here, first = place_of(rr)
        allowed = (place >= first) & (place <= here)
        for h in range(qw // HEAD):
            cols = slice(h * HEAD, (h + 1) * HEAD)
            s = jnp.where(allowed, dot(qs[mine, cols], keys, 1, 1) * scale, masked_score)
            e = jnp.exp(s - jnp.max(s, axis=-1, keepdims=True))
            p = e * (1.0 / jnp.sum(e, axis=-1, keepdims=True))
            att[mine, cols] = dot(p.astype(BF), values).astype(BF)
        part[rr] = dot(att[mine, :], wov[...]).astype(BF)
        if rr == 0:
            rs.step(0)
    out_q = net.here(qs, o_q)
    out_q.start()
    out_att = net.here(att, o_att)
    out_att.start()
    out_wo = net.here(wov, o_wo)
    out_wo.start()
    bulk[2].pass_x()
    g_cot.step(2)
    bulk[1].pass_y()
    rs.step(1)
    bulk[3].pass_x()
    g_cot.step(3)
    out_cot = net.here(call, o_cot)
    out_cot.start()
    rs.step(2)
    bulk[2].pass_y()
    rs.step(3)
    rs.total_into(o_mid)
    mid = o_mid[...]
    inv = lax.rsqrt(jnp.mean(mid * mid, axis=-1, keepdims=True) + epsilon)
    o_nmlp[...] = (mid * inv * o_gains[0:1, width:]).astype(BF)
    for src, dst in ((o_mid, out_mid), (o_nmlp, out_nmlp)):
        cp = net.here(src, dst)
        cp.start()
        tail.append(cp)
    bulk[3].pass_y()
    for g in bulk:
        g.arrive()
    for cp in early:
        cp.wait()
    for g in [g_joint, g_out, g_n, g_cot, rs] + bulk:
        g.finish()
    for out, _ in tok_in[1] + cot_in[1] + gain_copies:
        out.wait_send()
    for cp in kv_far + kv_sib + kv_pass:
        cp.wait_send()
    kv_x.wait_send()
    kvb_x.wait_send()
    for cp in tail + [out_normed, out_wj, out_kv, out_q, out_att, out_wo, out_cot]:
        cp.wait()


def attention_forward(
    sizes, tok, cot, wq, wkv, wo, wg, wu, wd, gain_a, gain_f, qb, kvb, lengths, rates
):
    dp, R, C = sizes
    sub = tok.shape[0] // C
    block = tok.shape[1]
    width = block * C
    qw, jw = wq.shape[1], wq.shape[1] + 2 * HEAD
    n = sub * R
    ff = wg.shape[0]
    shape = jax.ShapeDtypeStruct
    outs = [
        (shape((sub, width), BF), ANY),
        (shape((sub, width), F32), ANY), (shape((sub, width), BF), ANY),
        (shape((1, 2 * width), F32), ANY), (shape((n, 2 * HEAD), F32), ANY),
        (shape((R, sub, width), BF), ANY),
        (shape((n, qw), BF), ANY), (shape((R, C, sub, 2 * HEAD), BF), ANY),
        (shape((n, qw), BF), ANY), (shape((R, sub, width), BF), ANY),
        (shape((width, jw), BF), ANY), (shape((qw, width), BF), ANY),
        (shape((ff, width), BF), ANY), (shape((ff, width), BF), ANY),
        (shape((EARLY, ff // PIECES // 2, block), BF), ANY),
    ]
    return pl.pallas_call(
        functools.partial(attention_kernel, sizes),
        out_shape=[o for o, _ in outs],
        in_specs=[ANY] * 8 + [VMEM] * 4 + [SMEM, VMEM],
        out_specs=[s for _, s in outs],
        scratch_shapes=[
            pltpu.VMEM((C, sub, block), BF), pltpu.VMEM((C, sub, block), BF),
            pltpu.VMEM((1, 2 * block), F32), pltpu.VMEM((C, 1, 2 * block), F32), pltpu.VMEM((2, 1, HEAD), F32),
            pltpu.VMEM((R, sub, width), BF), pltpu.VMEM((R, sub, width), BF),
            pltpu.VMEM((width, jw), BF), pltpu.VMEM((qw, width), BF),
            pltpu.VMEM((R, C, sub, 2 * HEAD), BF), pltpu.VMEM((n, qw), BF),
            pltpu.VMEM((n, qw), BF), pltpu.VMEM((R, sub, width), BF),
            pltpu.VMEM((R, sub, width), BF), pltpu.VMEM((R, sub, width), BF),
            pltpu.VMEM((sub, width), BF), pltpu.VMEM((sub, width), F32),
            pltpu.VMEM((sub, width), BF), pltpu.VMEM((1, 2 * width), F32),
            pltpu.VMEM((n, 2 * HEAD), F32),
            pltpu.SemaphoreType.DMA((128,)), pltpu.SemaphoreType.DMA((128,)),
            pltpu.SemaphoreType.DMA((32,)),
        ],
        compiler_params=pltpu.CompilerParams(
            collective_id=1, has_side_effects=True, vmem_limit_bytes=VMEM_LIMIT
        ),
        name="attention_forward",
    )(tok, cot, wq, wkv, wo, wg, wu, wd, gain_a, gain_f, qb, kvb, lengths, rates)


def feedforward_kernel(
    sizes,
    nmlp, in_mid, in_gains, cot, wg, wu, wd, wdx, own_g, own_u,
    out_gmid, out_gain, o_down, o_sd, o_sm, o_sx, o_sg, o_gu, o_xt,
    w_gate, w_up, w_down, xall, call, acc, hid, gg, gu, cc, xt, part, rbu, rbd, dpart, g, x_d, y_d, o_gmid, o_gain, mid, gains,
    send, recv, local,
):
    net = Net(sizes, send, recv, local)
    net.arrive()
    R, C, r, c = net.R, net.C, net.r, net.c
    sub, width = nmlp.shape
    block = width // C
    n_tok = sub * R
    n_part = n_tok // PARTS
    n = sub // PARTS
    ff = w_gate.shape[0]
    tile = acc.shape[2]
    wide = width // tile
    own_cols = [pl.ds(pl.multiple_of(b * block, HEAD), block) for b in (c, net.across_c)]
    g_down = [
        WeightGather(
            net, wd, w_down, False, i, PIECES, crossed=wdx.at[i] if i < EARLY else None
        )
        for i in range(PIECES)
    ]
    in_x = [net.here(nmlp.at[pl.ds(q * n, n)], xall.at[q, r]) for q in range(PARTS)]
    in_norm = [net.here(in_mid, mid), net.here(in_gains, gains)]
    for cp in in_x + in_norm:
        cp.start()
    in_cot = [net.here(cot.at[:, pl.ds(q * n, n)], call.at[q]) for q in range(PARTS)]
    for cp in in_cot:
        cp.start()
    in_w = []
    for full, own, w in ((wg, own_g, w_gate), (wu, own_u, w_up)):
        for k in range(C):
            cols = pl.ds(pl.multiple_of(lax.rem(c + k, C) * block, HEAD), block)
            cp = net.here(full.at[:, cols] if k else own, w.at[:, cols])
            cp.start()
            in_w.append(cp)
    if hid.shape[1] > ff:
        for ref in (hid, gg, gu):
            ref[:n_tok, ff:] = jnp.zeros((n_tok, hid.shape[1] - ff), BF)
    net.barrier()
    for cp in in_x:
        cp.wait()
    g_x = LineGather(net, xall)
    g_x.step(0, (0,))
    for g_piece in g_down:
        g_piece.start()
    for cp in in_cot:
        cp.wait()
    call_out = net.copy(call, part, net.sibling)
    call_out.start()
    for i in (0, 1):
        cc[0, :, :, :, i * block : (i + 1) * block] = call[:, :, :, own_cols[i]]

    acts_out = [
        [
            net.copy(
                ref.at[pl.ds(q * n_part, n_part)], ref.at[pl.ds(n_tok + q * n_part, n_part)],
                net.sibling,
            )
            for ref in (hid, gg, gu)
        ]
        for q in range(PARTS)
    ]
    x_out = net.copy(xall, dpart, net.sibling)
    to_sibling = [cp for pair in acts_out for cp in pair]
    rs = LineSum(net, part, rbu, rbd)
    full = ff // tile
    rest = pl.ds(full * tile, ff - full * tile)

    def act(q, rows, back):
        mine = pl.ds(pl.multiple_of(q * n_part, n_part), n_part)
        x = xall[q].reshape(n_part, width)
        gate = dot(x, w_gate[rows, :], 1, 1)
        up = dot(x, w_up[rows, :], 1, 1)
        s = jax.nn.sigmoid(gate)
        silu = gate * s
        hid[mine, rows] = (silu * up).astype(BF)
        gg[mine, rows] = (back * up * s * (1.0 + gate * (1.0 - s))).astype(BF)
        gu[mine, rows] = (back * silu).astype(BF)

    g_x.step(1, (0,))
    g_x.step(0, (1,))
    g_down[0].pass_y()
    g_down[3].pass_x()
    call_out.wait_recv()
    for i in (0, 1):
        cc[1, :, :, :, i * block : (i + 1) * block] = part[:, :, :, own_cols[i]]
    g_down[1].pass_y()
    g_down[4].pass_x()
    g_x.step(2, (0,))

    def hidden_back(t):
        rows = pl.ds(pl.multiple_of(t * tile, tile), tile)
        acc[t] = dot(call[...].reshape(n_tok, width), w_down[rows, :], 1, 1)

    @pl.loop(0, 3)
    def _(t):
        @pl.when(t == 0)
        def _():
            g_down[0].arrive()
            g_down[1].arrive()

        @pl.when(t == 1)
        def _():
            g_down[2].pass_y()
            g_x.step(1, (1,))
            g_down[2].arrive()

        @pl.when(t == 2)
        def _():
            g_down[3].pass_y()
            g_down[3].arrive()

        hidden_back(t)

    for cp in in_w:
        cp.wait()
    g_x.step(3, (0,))

    @pl.loop(0, PARTS)
    def _(q):
        @pl.loop(0, full)
        def _(t):
            rows = pl.ds(pl.multiple_of(t * tile, tile), tile)

            @pl.when((q == 1) & (t == 0))
            def _():
                g_x.step(3, (1,))

            @pl.when(q == 0)
            def _():
                @pl.when(t == 2)
                def _():
                    g_down[4].pass_y()

                @pl.when(t == 3)
                def _():
                    g_down[4].arrive()
                    hidden_back(t)

            act(q, rows, acc[t, pl.ds(pl.multiple_of(q * n_part, n_part), n_part)])

            @pl.when((q == 1) & (t == full - 1))
            def _():
                rs.step(1, (0,))

            @pl.when((q == 0) & (t == full - 1))
            def _():
                g_x.step(2, (1,))

        act(q, rest, dot(call[q].reshape(n_part, width), w_down[rest, :], 1, 1))

        for k in range(PARTS):

            @pl.when(q == k)
            def _():
                for cp in acts_out[k]:
                    cp.start()

        mine = pl.ds(pl.multiple_of(q * n_part, n_part), n_part)

        @pl.loop(0, wide)
        def _(i):
            cols = pl.ds(pl.multiple_of(i * tile, tile), tile)
            total = dot(gg[mine, :ff], w_gate[:, cols]) + dot(gu[mine, :ff], w_up[:, cols])
            part[q, :, :, cols] = total.astype(BF).reshape(R, n, tile)

        @pl.when(q == 0)
        def _():
            rs.step(0, (0,))

        @pl.when(q == 1)
        def _():
            rs.step(0, (1,))
            rs.step(2, (0,))
            x_out.start()

    for g_piece in g_down:
        g_piece.finish()
    for cp in to_sibling:
        cp.wait_recv()
    outs = [net.here(gu, o_gu)]
    outs[0].start()

    def all_tiles(body):
        @pl.loop(0, full)
        def _(t):
            body(pl.ds(pl.multiple_of(t * tile, tile), tile))

        body(rest)

    def down_grad(rows):
        total = dot(hid[:, rows], cc[...].reshape(2 * n_tok, 2 * block), 0, 0)
        w_gate[rows, : 2 * block] = total.astype(BF)

    all_tiles(down_grad)
    half_ff = ff // 2
    cut = x_d.shape[1]

    def down_piece(i, h, ab):
        first, count = (cut, half_ff - cut) if ab else (0, cut)
        return w_gate.at[
            pl.ds(pl.multiple_of(h * half_ff + first, 16), count), pl.ds(i * block, block)
        ]

    sum_d = BlockSum(net, down_piece, down_piece, x_d, y_d)
    sum_d.start()
    rs.step(1, (1,))
    rs.step(3, (0,))

    x_out.wait_recv()
    for i in (0, 1):
        rows = slice(i * block, (i + 1) * block)
        xt[rows, :n_tok] = xall[:, :, :, own_cols[i]].reshape(n_tok, block).T
        xt[rows, n_tok:] = dpart[:, :, :, own_cols[i]].reshape(n_tok, block).T

    @pl.loop(0, wide)
    def _(i):
        cols = pl.ds(pl.multiple_of(i * tile, tile), tile)
        total = dot(hid[:n_tok, :ff], w_down[:, cols])
        dpart[:, :, :, cols] = total.astype(BF).reshape(PARTS, R, n, tile)

    rs.step(2, (1,))
    out_down = [net.here(dpart.at[q], o_down.at[:, pl.ds(q * n, n)]) for q in range(PARTS)]
    for cp in out_down:
        cp.start()
    def gate_grad(cols):
        total = dot(xt[...], gg[:, cols])
        g[:, :, cols] = total.astype(BF).reshape(4, g.shape[1], cols.size)

    all_tiles(gate_grad)
    for src, dst in ((g, o_sg), (xt, o_xt)):
        cp = net.here(src, dst)
        cp.start()
        outs.append(cp)
    rs.step(3, (1,))
    o_gmid[...] = jnp.zeros_like(o_gmid)
    rs.total_into(o_gmid)
    for cp in in_norm:
        cp.wait()
    grad = o_gmid[...]
    m = mid[...]
    inv = lax.rsqrt(jnp.mean(m * m, axis=-1, keepdims=True) + epsilon)
    normal = m * inv
    e = grad * gains[0:1, width:]
    back = inv * (e - normal * jnp.mean(e * normal, axis=-1, keepdims=True))
    o_gain[...] = jnp.sum(grad * normal, axis=0, keepdims=True)
    for q in range(PARTS):
        rows = slice(q * n, (q + 1) * n)
        o_gmid[rows] = call[q, r].astype(F32) + back[rows]
    for src, dst in ((o_gmid, out_gmid), (o_gain, out_gain)):
        cp = net.here(src, dst)
        cp.start()
        outs.append(cp)
    rs.finish()
    sum_d.add()
    own_half = w_gate.at[
        pl.ds(pl.multiple_of(net.h * half_ff, 16), half_ff), pl.ds(0, block)
    ]
    for src, dst in (
        (own_half, o_sd), (down_piece(0, net.other_h, 0), o_sm), (down_piece(1, net.h, 1), o_sx)
    ):
        cp = net.here(src, dst)
        cp.start()
        outs.append(cp)
    sum_d.finish()
    g_x.finish()
    for cp in to_sibling + [call_out, x_out]:
        cp.wait_send()
    for cp in outs + out_down:
        cp.wait()


def feedforward(sizes, nmlp, mid, gains, cot, wg, wu, wd, wdx, own_g, own_u):
    dp, R, C = sizes
    sub, width = nmlp.shape
    block = width // C
    n_tok = R * sub
    ff = wd.shape[0]
    tile = 512
    cut = ff // 4
    shape = jax.ShapeDtypeStruct
    outs = [
        (shape((sub, width), F32), ANY), (shape((1, width), F32), ANY),
        (shape((R, sub, width), BF), ANY), (shape((ff // 2, block), BF), ANY),
        (shape((cut, block), BF), ANY), (shape((ff // 2 - cut, block), BF), ANY),
        (shape((4, block // 2, ff), BF), ANY),
        (shape((2 * n_tok, -(-ff // HEAD) * HEAD), BF), ANY),
        (shape((2 * block, 2 * n_tok), BF), ANY),
    ]
    v = pltpu.VMEM
    line = v((PARTS, R, sub // PARTS, width), BF)
    acts = v((2 * n_tok, -(-ff // HEAD) * HEAD), BF)
    weight = v((ff, width), BF)
    return pl.pallas_call(
        functools.partial(feedforward_kernel, sizes),
        out_shape=[o for o, _ in outs],
        in_specs=[ANY] * 10,
        out_specs=[s for _, s in outs],
        scratch_shapes=[
            weight, weight, weight, line, line, v((ff // tile, n_tok, tile), F32), acts, acts, acts,
            v((2, PARTS, R, sub // PARTS, 2 * block), BF),
            v((2 * block, 2 * n_tok), BF), line, line, line, line, v((4, block // 2, ff), BF),
            v((2, cut, block), BF), v((2, ff // 2 - cut, block), BF),
            v((sub, width), F32), v((1, width), F32), v((sub, width), F32), v((1, 2 * width), F32),
            pltpu.SemaphoreType.DMA((128,)), pltpu.SemaphoreType.DMA((128,)),
            pltpu.SemaphoreType.DMA((32,)),
        ],
        compiler_params=pltpu.CompilerParams(
            collective_id=2, has_side_effects=True, vmem_limit_bytes=VMEM_LIMIT
        ),
        name="feedforward",
    )(nmlp, mid, gains, cot, wg, wu, wd, wdx, own_g, own_u)


def backward_kernel(
    sizes,
    in_gmid, in_x, in_mid, in_gains, in_gain_mlp, lengths, in_turns,
    normed, q, kv, att, wj, wo, down, sm, sx, sg, up_grads, xt_in,
    o_layer, o_input, out_vec, out_j, o_db, o_ga, o_gb, o_ua, o_ub, o_oa, o_ob,
    mall, nall, qs, kvs, atts, wjs, wos, dpart, drbu, drbd, part, rbu, rbd, grads, dq, dkv, dkv16, dk_sib, dk_in,
    joint, lay,
    s_g, s_u, x_g, x_u, y_g, y_u,
    wjo, wjx, s_j, x_j, y_j, woo, wox, s_o, x_o, y_o, jb, jk, jk2, jgot, v1, v1in, v2, v2in, o_vec, o_j,
    gmid, x_in, mid, gains, gain_mlp, turns, gu, xt,
    send, recv, local,
):
    net = Net(sizes, send, recv, local)
    R, C, r, c = net.R, net.C, net.r, net.c
    sem = pltpu.get_barrier_semaphore()
    half = net.dp // 2
    others = [(net.d, r, lax.rem(c + k, C)) for k in range(1, C)]
    others += [(net.d, lax.rem(r + k, R), c) for k in range(1, R)]
    others += [(net.mate[0], lax.rem(r + k, R), c) for k in range(R)]
    for dev in others:
        pl.semaphore_signal(sem, inc=1, device_id=dev, device_id_type=MESH)
    R, C, r, c = net.R, net.C, net.r, net.c
    sub, width = in_gmid.shape
    block = width // C
    n_tok = sub * R
    row_tok = sub * C
    qw = qs.shape[1]
    slot = lax.rem(r, 2)
    cos2, sin2 = turns.at[:, pl.ds(0, HEAD)], turns.at[:, pl.ds(HEAD, HEAD)]
    partner_r = r + 1 - 2 * slot
    small_loads = [
        net.here(a, b) for a, b in
        ((in_gmid, gmid), (in_x, x_in), (in_mid, mid), (in_gains, gains), (in_gain_mlp, gain_mlp),
         (in_turns, turns))
    ]
    up_loads = [net.here(up_grads, gu), net.here(xt_in, xt)]
    for cp in small_loads + up_loads:
        cp.start()
    loads = [
        net.here(a, b) for a, b in
        ((wo, wos), (att, atts), (q, qs), (kv, kvs), (down, dpart), (sg, s_g),
         (normed, nall), (wj, wjs))
    ]
    for cp in loads:
        cp.start()
    pl.semaphore_wait(sem, len(others))

    small_loads[0].wait()
    mall[r] = gmid[...].astype(BF)
    g_m = LineGather(net, mall)
    g_m.step(0)
    sum_g = BlockSum(net, halves(sg, x_g.shape[1]), halves(s_g, x_g.shape[1]), x_g, y_g)
    sum_u = BlockSum(net, halves(s_u, x_u.shape[1]), halves(s_u, x_u.shape[1]), x_u, y_u)
    sum_g.start()
    for cp in up_loads:
        cp.wait()
    ff = s_u.shape[2]

    def up_tile(cols):
        total = dot(xt[...], gu[:, cols])
        s_u[:, :, cols] = total.astype(BF).reshape(4, s_u.shape[1], cols.size)

    @pl.loop(0, ff // 512)
    def _(t):
        up_tile(pl.ds(pl.multiple_of(t * 512, 512), 512))

    up_tile(pl.ds(ff // 512 * 512, ff % 512))
    sum_u.start()
    cut_d, rest_d = sm.shape[0], sx.shape[0]
    sum_d = [
        net.copy(sx, o_db.at[pl.ds(cut_d, rest_d)], net.across),
        net.copy(sm, o_db.at[pl.ds(0, cut_d)], net.mate),
    ]
    sum_d[0].start()
    g_m.step(1)
    for cp in loads[:6] + small_loads[1:]:
        cp.wait()
    g_m.step(2)
    sum_g.add()
    sum_g.pass_on(o_gb, (0,))
    g_m.step(3)
    rs_d = LineSum(net, dpart, drbu, drbd)
    rs_d.step(0)
    m_all = mall[...].reshape(n_tok, width)
    grads[...] = dot(m_all, wos[...], 1, 1).astype(BF)

    def to_columns(src, dst):
        rows = pl.ds(pl.multiple_of(c * sub, sub), sub)
        mine = net.here(src.at[:, pl.ds(pl.multiple_of(c * block, HEAD), block)], dst.at[rows])
        mine.start()
        pairs = []
        for k in range(1, C):
            to, frm = lax.rem(c + k, C), lax.rem(c + C - k, C)
            i = net.n
            net.n += 1
            cut = src.at[:, pl.ds(pl.multiple_of(to * block, HEAD), block)]
            out = net.like(i, cut, dst.at[rows], net.at_col(to))
            out.start()
            from_rows = pl.ds(pl.multiple_of(frm * sub, sub), sub)
            pairs.append((out, net.like(i, cut, dst.at[from_rows], net.at_col(to))))
        return mine, pairs

    def settle(exchange):
        exchange[0].wait()
        for out, inc in exchange[1]:
            inc.wait_recv()
            out.wait_send()

    sib_blocks = [b + 1 - 2 * lax.rem(b, 2) for b in (c, net.across_c)]
    total = dot(atts[...], m_all, 0, 0)
    for b in range(C):
        woo[2 * b : 2 * b + 2] = (
            total[:, b * block : (b + 1) * block].astype(BF).reshape(2, qw // 2, block)
        )
    out_x = [net.copy(woo.at[pl.ds(2 * b, 2)], wox.at[i], net.sibling) for i, b in enumerate(sib_blocks)]
    for cp in out_x:
        cp.start()
    scale = HEAD ** (-0.5)
    heads = qw // HEAD
    ends = [lengths[0, 0]]
    for i in range(1, lengths.shape[1] - 1):
        ends.append(ends[-1] + lengths[0, i])
    for rr in reversed(range(R)):
        limit = (rr + 1) * row_tok
        keys = kvs[: rr + 1, :, :, :HEAD].reshape(limit, HEAD)
        values = kvs[: rr + 1, :, :, HEAD:].reshape(limit, HEAD)
        mine = slice(rr * sub, (rr + 1) * sub)
        stack = lambda ref: jnp.concatenate(
            [ref[mine, h * HEAD : (h + 1) * HEAD] for h in range(heads)], axis=0
        )
        qh, gh = stack(qs), stack(grads)
        place = lax.broadcasted_iota(jnp.int32, (limit, heads * sub), 0)
        lane = lax.broadcasted_iota(jnp.int32, (1, heads * sub), 1)
        here = rr * row_tok + c * sub + lax.rem(lane, sub)
        first = jnp.zeros_like(here)
        for end in ends:
            first = jnp.where(here >= end, end, first)
        s = jnp.where(
            (place >= first) & (place <= here), dot(keys, qh, 1, 1) * scale, masked_score
        )
        e = jnp.exp(s - jnp.max(s, axis=0, keepdims=True))
        p = e * (1.0 / jnp.sum(e, axis=0, keepdims=True))
        g = dot(values, gh, 1, 1)
        ds = (p * (g - jnp.sum(p * g, axis=0, keepdims=True))).astype(BF)
        dv = dot(p.astype(BF), gh)
        dk = dot(ds, qh) * scale
        if rr == R - 1:
            dkv[:, :HEAD] = dk
            dkv[:, HEAD:] = dv
        else:
            dkv[:limit, :HEAD] += dk
            dkv[:limit, HEAD:] += dv
        dqs = dot(ds, keys, 0, 0) * scale
        for h in range(heads):
            dq[mine, h * HEAD : (h + 1) * HEAD] = dqs[h * sub : (h + 1) * sub]
        if rr == R - 2:
            rs_d.step(1)
            for i, b in enumerate((c, net.across_c)):
                out_x[i].wait_recv()
                s_o[2 * i : 2 * i + 2] = (
                    woo[pl.ds(2 * b, 2)].astype(F32) + wox[i].astype(F32)
                ).astype(BF)
    sib_c = c + 1 - 2 * lax.rem(c, 2)
    far_c = net.across_c
    far_sib_c = far_c + 1 - 2 * lax.rem(far_c, 2)
    dkv16[...] = dkv[...].astype(BF).reshape(dkv16.shape)
    dk_copies = [
        net.copy(dkv16.at[:, far_sib_c], dk_sib.at[1], net.sibling),
        net.copy(dkv16.at[:, sib_c], dk_sib.at[0], net.sibling),
    ]
    for cp in dk_copies:
        cp.start()
    dk_copies[0].wait_recv()
    dk_in[0] = (dkv16[:, far_c].astype(F32) + dk_sib[1].astype(F32)).astype(BF)
    dk_copies.append(net.copy(dk_in.at[0], dk_in.at[1], net.across))
    dk_copies[2].start()
    sum_g.pass_on(o_gb, (1,))
    sum_o = BlockSum(net, halves(s_o, x_o.shape[1]), halves(s_o, x_o.shape[1]), x_o, y_o)
    sum_o.start()
    rs_d.step(2)
    for cp in loads[6:]:
        cp.wait()
    slots = dkv16[:, c].astype(F32)
    dk_copies[1].wait_recv()
    slots = slots + dk_sib[0].astype(F32)
    dk_copies[2].wait_recv()
    slots = slots + dk_in[1].astype(F32)
    slots = slots.reshape(n_tok, 2 * HEAD)
    joint[:, :qw] = turn(dq[...], cos2[...], -sin2[...]).astype(BF)
    joint[:, qw : qw + HEAD] = turn(slots[:, :HEAD], cos2[...], -sin2[...]).astype(BF)
    joint[:, qw + HEAD :] = slots[:, HEAD:].astype(BF)
    part[...] = dot(joint[...], wjs[...], 1, 1).astype(BF).reshape(R, sub, width)
    rs = LineSum(net, part, rbu, rbd)
    rs.step(0)
    total = dot(nall[...].reshape(n_tok, width), joint[...], 0, 0)
    wjo[...] = total.astype(BF).reshape(wjo.shape)
    joint_x = [net.copy(wjo.at[pl.ds(2 * b, 2)], wjx.at[i], net.sibling) for i, b in enumerate(sib_blocks)]
    for cp in joint_x:
        cp.start()
    bias = jnp.sum(joint[...].astype(F32), axis=0, keepdims=True)
    for i, b in enumerate((c, net.across_c)):
        joint_x[i].wait_recv()
        s_j[2 * i : 2 * i + 2] = (
            wjo[pl.ds(2 * b, 2)].astype(F32) + wjx[i].astype(F32)
        ).astype(BF)
    sum_j = BlockSum(net, halves(s_j, x_j.shape[1]), halves(s_j, x_j.shape[1]), x_j, y_j)
    sum_j.start()
    sum_u.add()
    sum_u.pass_on(o_ub)
    rs_d.step(3)
    lay[0] = mid[...]
    rs_d.total_into(lay.at[0])
    jk[...] = lay[0].astype(BF)
    rs.step(1)
    sum_o.add()
    sum_o.pass_on(o_ob)
    rs.step(2)
    sum_j.add()
    sum_j.pass_on(jb)
    sum_d[1].start()
    keeps = [
        net.here(src.at[net.h], dst)
        for src, dst in ((s_g, o_ga), (s_u, o_ua), (s_o, o_oa))
    ]
    for cp in keeps:
        cp.start()
    rs.step(3)
    lay[1] = jnp.zeros_like(lay[1])
    rs.total_into(lay.at[1])
    grad = lay[1]
    x = x_in[...].astype(F32)
    inv = lax.rsqrt(jnp.mean(x * x, axis=-1, keepdims=True) + epsilon)
    normal = x * inv
    e = grad * gains[0:1, :width]
    back = inv * (e - normal * jnp.mean(e * normal, axis=-1, keepdims=True))
    gain_attn = jnp.sum(grad * normal, axis=0, keepdims=True)
    for k in range(C):
        cut = slice(k * block, (k + 1) * block)
        v1[k, :, :block] = gain_attn[:, cut]
        v1[k, :, block : 2 * block] = gain_mlp[:, cut]
        v1[k, :, 2 * block :] = bias
    v_copies = []
    for k in range(1, C):
        to, frm = lax.rem(c + k, C), lax.rem(c + C - k, C)
        i = net.n
        net.n += 1
        out = net.like(i, v1.at[to], v1in.at[c], net.at_col(to))
        out.start()
        v_copies.append((out, net.like(i, v1.at[to], v1in.at[frm], net.at_col(to)), frm))
    jk2[...] = (gmid[...] + back).astype(BF)
    input_x = to_columns(jk2, o_input)
    layer_x = to_columns(jk, o_layer)
    sum_j.finish()
    ja = s_j.at[net.h]
    own_cols = pl.ds(pl.multiple_of(qw + slot * HEAD, HEAD), HEAD)
    mate_cols = pl.ds(pl.multiple_of(qw + (1 - slot) * HEAD, HEAD), HEAD)
    jgot[0] = ja[:, mate_cols].astype(F32) + jb[:, mate_cols].astype(F32)
    slot_x = net.copy(jgot.at[0], jgot.at[1], net.at_row(partner_r))
    slot_x.start()
    o_j[:, :qw] = ja[:, :qw].astype(F32) + jb[:, :qw].astype(F32)
    total = v1[c]
    for _, inc, frm in v_copies:
        inc.wait_recv()
        total = total + v1in[frm]
    v2[...] = total
    far = []
    for same in (1, 0):
        for k in range(R):
            if same and k == 0:
                continue
            to, frm = lax.rem(r + k, R), lax.rem(r + R - k, R)
            i = net.n
            net.n += 1
            dst_d = net.d if same else net.mate[0]
            hs = net.h if same else net.other_h
            out = net.like(i, v2, v2in.at[net.h, r], (dst_d, to, c))
            out.start()
            far.append((out, net.like(i, v2, v2in.at[hs, frm], (dst_d, to, c))))
    v2in[net.h, r] = total
    slot_x.wait_recv()
    o_j[:, qw:] = ja[:, own_cols].astype(F32) + jb[:, own_cols].astype(F32) + jgot[1]
    tail = [net.here(o_j, out_j)]
    tail[0].start()
    for g in (sum_g, sum_u, sum_o):
        g.finish()
    for cp in sum_d:
        cp.wait()
    for cp in keeps:
        cp.wait()
    for _, inc in far:
        inc.wait_recv()
    gain_sum = v2in[0, 0, :, : 2 * block]
    for hh in (0, 1):
        for k in range(R):
            if hh or k:
                gain_sum = gain_sum + v2in[hh, k, :, : 2 * block]
    o_vec[:, : 2 * block] = gain_sum
    o_vec[:, 2 * block : 2 * block + qw] = (
        v2in[0, r, :, 2 * block : 2 * block + qw] + v2in[1, r, :, 2 * block : 2 * block + qw]
    )
    cols = pl.ds(pl.multiple_of(2 * block + qw + slot * HEAD, HEAD), HEAD)
    o_vec[:, 2 * block + qw :] = (
        v2in[0, r, :, cols] + v2in[1, r, :, cols]
        + v2in[0, partner_r, :, cols] + v2in[1, partner_r, :, cols]
    )
    tail.append(net.here(o_vec, out_vec))
    tail[1].start()
    settle(layer_x)
    settle(input_x)
    for g in (g_m, rs_d, rs):
        g.finish()
    for cp in out_x + joint_x + [slot_x]:
        cp.wait_send()
    for cp in dk_copies:
        cp.wait_send()
    for cps in v_copies + far:
        cps[0].wait_send()
    for cp in tail:
        cp.wait()


def backward(sizes, gmid, x_in, mid, gains, gain_mlp, lengths, turns, normed, q, kv, att, wj, wo,
             down, sm, sx, sg, up_grads, xt):
    dp, R, C = sizes
    sub, width = gmid.shape
    block = width // C
    n, qw = q.shape
    jw = wj.shape[1]
    ff = sg.shape[2]
    shape = jax.ShapeDtypeStruct
    d2, g2, w2, j2 = (ff // 2, block), (block // 2, ff), (qw // 2, block), (block // 2, jw)
    vec = 2 * block + jw
    outs = [
        (shape((C * sub, block), BF), ANY), (shape((C * sub, block), BF), ANY),
        (shape((1, vec - HEAD), F32), ANY), (shape((block // 2, jw - HEAD), F32), ANY),
        (shape(d2, BF), ANY), (shape(g2, BF), ANY), (shape(g2, BF), ANY),
        (shape(g2, BF), ANY), (shape(g2, BF), ANY), (shape(w2, BF), ANY), (shape(w2, BF), ANY),
    ]
    v = pltpu.VMEM
    four = lambda s: v((4,) + s, BF)

    def landing(s):
        cut = x_first(s[0])
        return [v((2, cut) + s[1:], BF), v((2, s[0] - cut) + s[1:], BF)]

    x_g, y_g = landing(g2)
    x_o, y_o = landing(w2)
    x_j, y_j = landing(j2)
    line = v((R, sub, width), BF)
    return pl.pallas_call(
        functools.partial(backward_kernel, sizes),
        out_shape=[o for o, _ in outs],
        in_specs=[ANY] * 5 + [SMEM] + [ANY] * 13,
        out_specs=[s for _, s in outs],
        scratch_shapes=[
            line, line, v((n, qw), BF), v(kv.shape, BF), v((n, qw), BF), v((width, jw), BF),
            v((qw, width), BF), line, line, line, line, line, line, v((n, qw), BF), v((n, qw), F32),
            v((n * C, 2 * HEAD), F32), v(kv.shape, BF), v((2, R, sub, 2 * HEAD), BF),
            v((2, R, sub, 2 * HEAD), BF),
            v((n, jw), BF), v((2, sub, width), F32),
            four(g2), four(g2), x_g, x_g, y_g, y_g,
            v((8,) + j2, BF), v((2, 2) + j2, BF), four(j2), x_j, y_j,
            v((8,) + w2, BF), v((2, 2) + w2, BF), four(w2), x_o, y_o,
            v(j2, BF), v((sub, width), BF), v((sub, width), BF), v((2, j2[0], HEAD), F32),
            v((C, 1, vec), F32), v((C, 1, vec), F32), v((1, vec), F32), v((2, R, 1, vec), F32),
            v((1, vec - HEAD), F32), v((block // 2, jw - HEAD), F32),
            v(gmid.shape, F32), v(x_in.shape, BF), v(mid.shape, F32), v(gains.shape, F32),
            v(gain_mlp.shape, F32), v(turns.shape, F32), v(up_grads.shape, BF), v(xt.shape, BF),
            pltpu.SemaphoreType.DMA((128,)), pltpu.SemaphoreType.DMA((128,)),
            pltpu.SemaphoreType.DMA((32,)),
        ],
        compiler_params=pltpu.CompilerParams(
            collective_id=3, has_side_effects=True, vmem_limit_bytes=VMEM_LIMIT
        ),
        name="backward",
    )(gmid, x_in, mid, gains, gain_mlp, lengths, turns, normed, q, kv, att, wj, wo, down, sm, sx, sg, up_grads, xt)

def finish_kernel(
    d, vec, joint, da, db, ga, gb, ua, ub, oa, ob, layer, inp,
    o_again, o_fgain, o_qb, o_kvb, o_q, o_kv, o_out, o_gate, o_up, o_down, o_layer, o_input,
    vec_v, joint_v, da_v, db_v, ga_v, gb_v, ua_v, ub_v, oa_v, ob_v,
    layer_v, inp_v, again_v, fgain_v, qb_v, kvb_v, q_v, kv_v, out_v, gate_v, up_v, down_v, sem_in, sem_out,
):
    pairs = (
        (vec, vec_v), (joint, joint_v), (oa, oa_v), (ob, ob_v), (da, da_v), (db, db_v),
        (ga, ga_v), (gb, gb_v), (ua, ua_v), (ub, ub_v), (layer, layer_v), (inp, inp_v),
    )
    loads = [pltpu.make_async_copy(s, t, sem_in.at[i]) for i, (s, t) in enumerate(pairs)]
    for cp in loads:
        cp.start()
    stores = []

    def store(src, dst):
        cp = pltpu.make_async_copy(src, dst, sem_out.at[len(stores)])
        cp.start()
        stores.append(cp)

    block, qw = o_again.shape[0], o_q.shape[1]
    loads[0].wait()
    second = d[0, 0] == 1
    again_v[...] = vec_v[0, :block]
    fgain_v[...] = vec_v[0, block : 2 * block]
    bias = vec_v[0:1, 2 * block :]
    pick = lambda v: jnp.where(second, v[:, v.shape[1] // 2 :], v[:, : v.shape[1] // 2])
    qb_v[...] = pick(bias[:, :qw])[0]
    kvb_v[...] = pick(bias[:, qw:])[0]
    for src, dst in ((again_v, o_again), (fgain_v, o_fgain), (qb_v, o_qb), (kvb_v, o_kvb)):
        store(src, dst)
    loads[1].wait()
    q_v[...] = joint_v[:, :qw]
    kv_v[...] = joint_v[:, qw:]
    store(q_v, o_q)
    store(kv_v, o_kv)
    for i, (a, b, f, o) in enumerate(
        ((oa_v, ob_v, out_v, o_out), (da_v, db_v, down_v, o_down), (ga_v, gb_v, gate_v, o_gate),
         (ua_v, ub_v, up_v, o_up))
    ):
        loads[2 + 2 * i].wait()
        loads[3 + 2 * i].wait()
        f[...] = a[...].astype(F32) + b[...].astype(F32)
        store(f, o)
    for i, (src, dst) in enumerate(((layer_v, o_layer), (inp_v, o_input))):
        loads[10 + i].wait()
        store(src, dst)
    for cp in stores:
        cp.wait()


def finish(d, layer, inp, vec, joint, da, db, ga, gb, ua, ub, oa, ob):
    block, qw, kvw = layer.shape[1], oa.shape[0] * 2, joint.shape[1] - oa.shape[0] * 2
    f32 = lambda *s: jax.ShapeDtypeStruct(s, F32)
    like = lambda v: jax.ShapeDtypeStruct(v.shape, F32)
    results = [
        f32(block), f32(block), f32(qw // 2), f32(kvw // 2), f32(joint.shape[0], qw),
        f32(joint.shape[0], kvw), like(oa), like(ga), like(ua), like(da),
    ]
    v = lambda a: pltpu.VMEM(a.shape, a.dtype)
    out = pl.pallas_call(
        finish_kernel,
        out_shape=results + [jax.ShapeDtypeStruct(a.shape, BF) for a in (layer, inp)],
        in_specs=[SMEM] + [ANY] * 12,
        out_specs=[ANY] * 12,
        scratch_shapes=[v(a) for a in (vec, joint, da, db, ga, gb, ua, ub, oa, ob, layer, inp)]
        + [v(a) for a in results]
        + [pltpu.SemaphoreType.DMA((12,)), pltpu.SemaphoreType.DMA((12,))],
        compiler_params=pltpu.CompilerParams(vmem_limit_bytes=VMEM_LIMIT),
        name="finish",
    )(d, vec, joint, da, db, ga, gb, ua, ub, oa, ob, layer, inp)
    again, fgain, q_bias, kv_bias, q, kv, o, gate, up, down, layer, inp = out
    return layer, inp, again, q, q_bias, kv, kv_bias, o, fgain, gate, up, down


def on_device(
    tokens_in, seq_lengths, attention_gain, query_weight, query_bias, keyvalue_weight,
    keyvalue_bias, output_weight, feedforward_gain, gate_weight, up_weight, down_weight,
    cotangent,
):
    sizes = dp, rows, cols = tuple(lax.axis_size(a) for a in ("dp", "row", "col"))
    d, col = lax.axis_index("dp"), lax.axis_index("col")
    sub = tokens_in.shape[0] // cols
    block = tokens_in.shape[1]
    wq_width = query_weight.shape[1]
    lane = np.arange(HEAD) % (HEAD // 2)
    rates = jnp.asarray((rope_base ** (-lane * (2.0 / HEAD))).astype(np.float32)[None])
    (x_own, middle, nmlp, gains, turns, normed, queries, kv, attended, cot_all, w_joint, w_out,
     w_gate, w_up, down_crossed) = attention_forward(
        sizes, tokens_in, cotangent, query_weight, keyvalue_weight, output_weight, gate_weight.T,
        up_weight.T, down_weight, attention_gain, feedforward_gain, query_bias, keyvalue_bias, seq_lengths, rates,
    )
    grad_middle, gain_mlp, down_part, da, sum_mate, sum_across, sum_gate, up_grads, up_tokens = feedforward(
        sizes, nmlp, middle, gains, cot_all, w_gate, w_up, down_weight, down_crossed,
        gate_weight.T, up_weight.T,
    )
    layer_out, input_grad, vec, joint, db, ga, gb, ua, ub, oa, ob = backward(
        sizes, grad_middle, x_own, middle, gains, gain_mlp, seq_lengths, turns, normed, queries, kv,
        attended, w_joint, w_out, down_part, sum_mate, sum_across, sum_gate,
        up_grads, up_tokens,
    )
    if dp == 2:
        return finish(
            d.reshape(1, 1), layer_out, input_grad, vec, joint, da, db, ga, gb, ua, ub, oa, ob
        )
    h = d // (dp // 2)

    def rest_of_dp(v):
        full = jnp.concatenate([jnp.where(h == 0, v, 0.0), jnp.where(h == 1, v, 0.0)], axis=0)
        return lax.psum_scatter(full, "dp", scatter_dimension=0, tiled=True)

    vec = lax.psum(jnp.where(h == 0, vec[0], 0.0), "dp")

    def own_share(v):
        n = v.shape[0] // dp
        return lax.dynamic_slice_in_dim(v, d * n, n)

    both = lambda a, b: rest_of_dp(a.astype(F32) + b.astype(F32))
    joint = rest_of_dp(joint)
    bias = vec[2 * block :]
    return (
        layer_out, input_grad, vec[:block], joint[:, :wq_width], own_share(bias[:wq_width]),
        joint[:, wq_width:], own_share(bias[wq_width:]), both(oa, ob), vec[block : 2 * block],
        both(ga, gb), both(ua, ub), both(da, db),
    )


def solution(mesh):
    return jax.shard_map(
        on_device,
        mesh=mesh,
        in_specs=(
            P(("dp", "row"), "col"), P("dp", None), P("col"), P("col", "row"), P("row"),
            P("col", "row"), P("row"), P("row", "col"), P("col"), P("col", "row"),
            P("col", "row"), P("row", "col"), P(("dp", "row"), "col"),
        ),
        out_specs=(
            P(("dp", "row"), "col"), P(("dp", "row"), "col"), P("col"),
            P(("col", "dp"), "row"), P(("row", "dp")), P(("col", "dp"), "row"),
            P(("row", "dp")), P(("row", "dp"), "col"), P("col"), P(("col", "dp"), "row"),
            P(("col", "dp"), "row"), P(("row", "dp"), "col"),
        ),
        check_vma=False,
    )
```

```python
import functools

import jax
import jax.numpy as jnp
import numpy as np
from jax import lax
from jax.experimental import pallas as pl
from jax.experimental.pallas import tpu as pltpu
from jax.sharding import PartitionSpec as P

HEAD = 128
epsilon = 1e-06
rope_base = 1000000.0
masked_score = -1e30
BF = jnp.bfloat16
F32 = jnp.float32
MESH = pl.DeviceIdType.MESH
ANY = pl.BlockSpec(memory_space=pl.ANY)
VMEM = pl.BlockSpec(memory_space=pltpu.VMEM)
SMEM = pl.BlockSpec(memory_space=pltpu.SMEM)
VMEM_LIMIT = 63 * 2**20


def dot(a, b, ca=1, cb=0):
    return lax.dot_general(a, b, (((ca,), (cb,)), ((), ())), preferred_element_type=F32)


class Net:
    def __init__(self, sizes, send, recv, local):
        self.dp, self.R, self.C = sizes
        self.d = lax.axis_index("dp")
        self.r = lax.axis_index("row")
        self.c = lax.axis_index("col")
        half = self.dp // 2
        self.h = self.d // half
        self.send, self.recv, self.local = send, recv, local
        self.n = 0
        self.n_local = 0
        self.other_h = 1 - self.h
        self.mate = (lax.rem(self.d + half, self.dp), self.r, self.c)
        self.sibling = self.at_col(self.c + 1 - 2 * lax.rem(self.c, 2))
        self.across_c = lax.rem(self.c + 2, 4)
        self.across = self.at_col(self.across_c)

    def at_col(self, c):
        return (self.d, self.r, c)

    def at_row(self, r):
        return (self.d, r, self.c)

    def copy(self, src, dst, dev):
        i = self.n
        self.n += 1
        return pltpu.make_async_remote_copy(
            src_ref=src, dst_ref=dst, send_sem=self.send.at[i], recv_sem=self.recv.at[i],
            device_id=dev, device_id_type=MESH,
        )

    def like(self, copy_index, src, dst, dev):
        return pltpu.make_async_remote_copy(
            src_ref=src, dst_ref=dst, send_sem=self.send.at[copy_index],
            recv_sem=self.recv.at[copy_index], device_id=dev, device_id_type=MESH,
        )

    def here(self, src, dst):
        i = self.n_local
        self.n_local += 1
        return pltpu.make_async_copy(src, dst, self.local.at[i])

    def arrive(self):
        sem = pltpu.get_barrier_semaphore()
        for k in range(1, self.C):
            pl.semaphore_signal(
                sem, inc=1, device_id=self.at_col(lax.rem(self.c + k, self.C)), device_id_type=MESH
            )
        pl.semaphore_signal(sem, inc=1, device_id=self.mate, device_id_type=MESH)

        @pl.when(self.r > 0)
        def _():
            pl.semaphore_signal(sem, inc=1, device_id=self.at_row(self.r - 1), device_id_type=MESH)

        @pl.when(self.r < self.R - 1)
        def _():
            pl.semaphore_signal(sem, inc=1, device_id=self.at_row(self.r + 1), device_id_type=MESH)

    def barrier(self):
        sem = pltpu.get_barrier_semaphore()
        count = self.C + (self.r > 0).astype(jnp.int32) + (self.r < self.R - 1).astype(jnp.int32)
        pl.semaphore_wait(sem, count)


PARTS = 2
PIECES = 5
EARLY = 4


def shard(buf, j, q, parts):
    if len(buf.shape) == 4:
        return buf.at[q, j]
    n = buf.shape[1] // parts
    return buf.at[j, pl.ds(q * n, n)]


class LineGather:
    def __init__(self, net, buf, parts=PARTS):
        self.net, self.buf, self.parts = net, buf, parts
        self.base = net.n
        net.n += 2 * (net.R - 1) * parts

    def _copy(self, up, s, q, j):
        net = self.net
        b = shard(self.buf, jnp.clip(j, 0, net.R - 1), q, self.parts)
        to = jnp.minimum(net.r + 1, net.R - 1) if up else jnp.maximum(net.r - 1, 0)
        return net.like(self.base + 2 * (s * self.parts + q) + up, b, b, net.at_row(to))

    def step(self, s, which=None):
        net = self.net
        r, R = net.r, net.R
        for q in range(self.parts) if which is None else which:
            if s > 0:

                @pl.when(r - s >= 0)
                def _():
                    self._copy(1, s - 1, q, r - s).wait_recv()

            if s < R - 1:

                @pl.when((r - s >= 0) & (r < R - 1))
                def _():
                    self._copy(1, s, q, r - s).start()

            if s > 0:

                @pl.when(r + s < R)
                def _():
                    self._copy(0, s - 1, q, r + s).wait_recv()

            if s < R - 1:

                @pl.when((r + s < R) & (r > 0))
                def _():
                    self._copy(0, s, q, r + s).start()

    def finish(self):
        net = self.net
        r, R = net.r, net.R
        for s in range(R - 1):
            for q in range(self.parts):

                @pl.when((r - s >= 0) & (r < R - 1))
                def _():
                    self._copy(1, s, q, r - s).wait_send()

                @pl.when((r + s < R) & (r > 0))
                def _():
                    self._copy(0, s, q, r + s).wait_send()


class LineSum:
    def __init__(self, net, part, from_below, from_above, parts=PARTS):
        self.net, self.part, self.bu, self.bd, self.parts = net, part, from_below, from_above, parts
        self.base = net.n
        net.n += 2 * net.R * parts

    def _at(self, buf, j, q):
        return shard(buf, j, q, self.parts)

    def _copy(self, up, j, q):
        net = self.net
        j = jnp.clip(j, 0, net.R - 1)
        to = jnp.minimum(net.r + 1, net.R - 1) if up else jnp.maximum(net.r - 1, 0)
        return net.like(
            self.base + (2 * q + up) * net.R + j, self._at(self.part, j, q),
            self._at(self.bu if up else self.bd, j, q), net.at_row(to),
        )

    def _add(self, j, q, buf):
        mine, got = self._at(self.part, j, q), self._at(buf, j, q)
        mine[...] = (mine[...].astype(F32) + got[...].astype(F32)).astype(BF)

    def step(self, t, which=None):
        net = self.net
        r, R = net.r, net.R
        j = t - (R - 1 - r)
        k = R - 1 - (t - r)
        for q in range(self.parts) if which is None else which:

            @pl.when((j >= 0) & (r < R - 1))
            def _():
                self._copy(0, j, q).wait_recv()

            @pl.when((j >= 0) & (j < r))
            def _():
                @pl.when(r < R - 1)
                def _():
                    self._add(j, q, self.bd)

                self._copy(0, j, q).start()

            @pl.when((k <= R - 1) & (r > 0))
            def _():
                self._copy(1, k, q).wait_recv()

            @pl.when((k <= R - 1) & (k > r))
            def _():
                @pl.when(r > 0)
                def _():
                    self._add(k, q, self.bu)

                self._copy(1, k, q).start()

    def finish(self):
        net = self.net
        r, R = net.r, net.R
        for j in range(R):
            for q in range(self.parts):

                @pl.when(j < r)
                def _():
                    self._copy(0, j, q).wait_send()

                @pl.when(j > r)
                def _():
                    self._copy(1, j, q).wait_send()

    def total_into(self, out):
        net = self.net
        r, R = net.r, net.R
        n = out.shape[0] // self.parts
        for q in range(self.parts):
            mine = out.at[pl.ds(q * n, n)]
            mine[...] += self._at(self.part, r, q)[...].astype(F32)

            @pl.when(r < R - 1)
            def _():
                mine[...] += self._at(self.bd, r, q)[...].astype(F32)

            @pl.when(r > 0)
            def _():
                mine[...] += self._at(self.bu, r, q)[...].astype(F32)


class WeightGather:
    def __init__(self, net, src, full, by_rows, piece=0, pieces=1, keep=True, crossed=None):
        self.net, self.full, self.by_rows = net, full, by_rows
        if by_rows:
            self.n, self.w = full.shape[0] // net.C, full.shape[1]
        else:
            self.n, self.w = full.shape[0] // pieces, full.shape[1] // net.C
        self.first = piece * self.n
        if src is not None:
            src = src.at[pl.ds(self.first, self.n)]
        c, p, h, o = net.c, net.across_c, net.h, net.other_h
        half = self.n // 2
        self.here = None
        if src is not None:
            if keep:
                self.here = net.here(src, self.view(c, 0, 2))
            own_half = src.at[pl.ds(pl.multiple_of(h * half, 16), half)]
            own = src
        else:
            own_half, own = self.view(c, h, 1), self.view(c, 0, 2)
        self.x, self.kept = None, None
        got = self.view(p, h, 1)
        if crossed is None:
            self.x = net.copy(own_half, self.view(c, h, 1), net.across)
        else:
            self.kept = net.here(crossed, got)
            got = crossed
        self.sib = net.copy(own, self.view(c, 0, 2), net.sibling)
        self.y = net.copy(got, self.view(p, h, 1), net.mate)
        self.sib_h = net.copy(got, self.view(p, h, 1), net.sibling)
        self.sib_o = net.copy(self.view(p, o, 1), self.view(p, o, 1), net.sibling)

    def view(self, b, h, halves):
        half = self.n // 2
        if self.by_rows:
            return self.full.at[pl.ds(pl.multiple_of(b * self.n + h * half, 16), halves * half)]
        return self.full.at[
            pl.ds(pl.multiple_of(self.first + h * half, 16), halves * half),
            pl.ds(pl.multiple_of(b * self.w, 128), self.w),
        ]

    def start(self):
        if self.here is not None:
            self.here.start()
        if self.x is None:
            self.kept.start()
            self.y.start()
            self.sib_h.start()
        else:
            self.x.start()
        self.sib.start()

    def pass_x(self):
        self.x.wait_recv()
        self.y.start()
        self.sib_h.start()

    def pass_y(self):
        self.y.wait_recv()
        self.sib_o.start()

    def arrive(self):
        if self.here is not None:
            self.here.wait()
        if self.kept is not None:
            self.kept.wait()
        self.sib.wait_recv()
        self.sib_h.wait_recv()
        self.sib_o.wait_recv()

    def finish(self):
        for cp in (self.x, self.sib, self.y, self.sib_h, self.sib_o):
            if cp is not None:
                cp.wait_send()


class BlockSum:
    def __init__(self, net, source, piece, from_x, from_mate):
        self.net, self.piece = net, piece
        self.from_x, self.from_mate = from_x, from_mate
        o = net.other_h
        self.first = [net.copy(source(1, k, 0), from_x.at[k], net.across) for k in (0, 1)]
        self.first += [net.copy(source(i, o, 1), from_mate.at[i], net.mate) for i in (0, 1)]
        self.second = []

    def start(self):
        for cp in self.first:
            cp.start()

    def add(self):
        h = self.net.h
        for cp in self.first:
            cp.wait_recv()
        for ref, got in (
            (self.piece(0, 0, 0), self.from_x.at[0]), (self.piece(0, 1, 0), self.from_x.at[1]),
            (self.piece(0, h, 1), self.from_mate.at[0]), (self.piece(1, h, 1), self.from_mate.at[1]),
        ):
            ref[...] = (ref[...].astype(F32) + got[...].astype(F32)).astype(BF)

    def pass_on(self, got, which=(0, 1)):
        net = self.net
        cut, rest = self.from_x.shape[1], self.from_mate.shape[1]
        for k in which:
            if k == 0:
                cp = net.copy(self.piece(0, net.other_h, 0), got.at[pl.ds(0, cut)], net.mate)
            else:
                cp = net.copy(self.piece(1, net.h, 1), got.at[pl.ds(cut, rest)], net.across)
            cp.start()
            self.second.append(cp)

    def finish(self):
        for cp in self.first:
            cp.wait_send()
        for cp in self.second:
            cp.wait_send()
            cp.wait_recv()


def halves(ref, cut):
    def piece(i, h, ab):
        rows = pl.ds(cut, ref.shape[1] - cut) if ab else pl.ds(0, cut)
        return ref.at[2 * i + h, rows]

    return piece


def x_first(rows):
    return rows * 5 // 12 // 16 * 16


def turn(values, cos2, sin2):
    heads = []
    for i in range(values.shape[1] // HEAD):
        v = values[:, i * HEAD : (i + 1) * HEAD]
        heads.append(v * cos2 + pltpu.roll(v, HEAD // 2, 1) * sin2)
    return jnp.concatenate(heads, axis=1) if len(heads) > 1 else heads[0]


def attention_kernel(
    sizes,
    tok, cot, wq, wkv, wo, wg, wu, wd, gain_a, gain_f, qb, kvb, lengths, rates,
    out_x, out_mid, out_nmlp, out_gains, out_turns, o_normed, o_q, o_kv, o_att, o_cot, o_wj, o_wo, o_wg, o_wu, o_wdx,
    xin, cin, small, gains, kvb2, nall, call, wj, wov, kv, qs, att, part, rbu, rbd, o_x, o_mid, o_nmlp, o_gains, turns,
    send, recv, local,
):
    net = Net(sizes, send, recv, local)
    net.arrive()
    R, C, r, c = net.R, net.C, net.r, net.c
    sub, width = nall.shape[1], nall.shape[2]
    block = tok.shape[1]
    row_tok = sub * C
    n_tok = sub * R
    qw = wq.shape[1]
    slot = lax.rem(r, 2)
    partner = net.at_row(r + 1 - 2 * slot)
    line = lambda ref: ref[...].astype(F32).reshape(1, ref.shape[0])
    small[:, :block] = line(gain_a)
    small[:, block:] = line(gain_f)
    kvb2[slot] = line(kvb)
    net.barrier()
    cos2, sin2 = turns.at[:, pl.ds(0, HEAD)], turns.at[:, pl.ds(HEAD, HEAD)]
    ends = [lengths[0, 0]]
    for i in range(1, lengths.shape[1] - 1):
        ends.append(ends[-1] + lengths[0, i])

    def place_of(rr):
        here = rr * row_tok + c * sub + lax.broadcasted_iota(jnp.int32, (sub, 1), 0)
        first = jnp.zeros((sub, 1), jnp.int32)
        for end in ends:
            first = jnp.where(here >= end, end, first)
        return here, first

    def spread(src, dst):
        mine = pl.multiple_of(c * sub, sub)
        local_copy = net.here(src.at[pl.ds(mine, sub)], dst.at[c])
        copies = []
        for k in range(1, C):
            to = lax.rem(c + k, C)
            frm = lax.rem(c + C - k, C)
            i = net.n
            net.n += 1
            rows = pl.ds(pl.multiple_of(to * sub, sub), sub)
            copies.append(
                (net.like(i, src.at[rows], dst.at[c], net.at_col(to)),
                 net.like(i, src.at[rows], dst.at[frm], net.at_col(to)))
            )
        return local_copy, copies

    def begin(pair):
        pair[0].start()
        for out, _ in pair[1]:
            out.start()

    def arrived(pair):
        pair[0].wait()
        for _, inc in pair[1]:
            inc.wait_recv()

    tok_in, cot_in = spread(tok, xin), spread(cot, cin)
    gain_own = net.here(small, gains.at[c])
    gain_own.start()
    gain_copies = []
    for k in range(1, C):
        to, frm = lax.rem(c + k, C), lax.rem(c + C - k, C)
        i = net.n
        net.n += 1
        out = net.like(i, small, gains.at[c], net.at_col(to))
        gain_copies.append((out, net.like(i, small, gains.at[frm], net.at_col(to))))
        out.start()
    begin(tok_in)
    own_rows = pl.ds(pl.multiple_of(c * block, block), block)
    col_own = pl.ds(pl.multiple_of(qw + slot * HEAD, HEAD), HEAD)
    col_mate = pl.ds(pl.multiple_of(qw + (1 - slot) * HEAD, HEAD), HEAD)
    kv_x = net.copy(wkv, wj.at[own_rows, col_own], partner)
    kv_in = net.like(net.n - 1, wkv, wj.at[own_rows, col_mate], partner)
    kv_x.start()
    kvb_x = net.copy(kvb2.at[slot], kvb2.at[slot], partner)
    kvb_in = net.like(net.n - 1, kvb2.at[slot], kvb2.at[1 - slot], partner)
    kvb_x.start()
    wq_own = net.here(wq, wj.at[own_rows, pl.ds(0, qw)])
    wq_own.start()
    wkv_own = net.here(wkv, wj.at[own_rows, col_own])
    wkv_own.start()
    g_joint = WeightGather(net, None, wj, True)
    g_out = WeightGather(net, wo, wov, False)
    bulk = [WeightGather(net, w, o, False, i, 2, False) for w, o in ((wg, o_wg), (wu, o_wu)) for i in (0, 1)]

    wq_own.wait()
    wkv_own.wait()
    kv_in.wait_recv()
    g_joint.start()
    g_out.start()
    begin(cot_in)
    bulk[0].start()
    bulk[1].start()

    arrived(tok_in)
    gain_own.wait()
    for _, inc in gain_copies:
        inc.wait_recv()
    for k in range(C):
        o_gains[:, k * block : (k + 1) * block] = gains[k, :, :block]
        o_gains[:, width + k * block : width + (k + 1) * block] = gains[k, :, block:]
    x = jnp.concatenate([xin[k].astype(F32) for k in range(C)], axis=1)
    o_mid[...] = x
    o_x[...] = x.astype(BF)
    inv = lax.rsqrt(jnp.mean(x * x, axis=-1, keepdims=True) + epsilon)
    nall[r] = (x * inv * o_gains[0:1, :width]).astype(BF)
    g_n = LineGather(net, nall)
    g_n.step(0)
    g_joint.pass_x()
    g_out.pass_x()
    g_n.step(1)
    g_joint.pass_y()
    g_out.pass_y()
    arrived(cot_in)
    for k in range(C):
        call[r, :, k * block : (k + 1) * block] = cin[k]
    lane = lax.broadcasted_iota(jnp.int32, (1, HEAD), 1)
    for rr in range(R):
        here, first = place_of(rr)
        angle = (here - first).astype(F32) * rates[...]
        mine = slice(rr * sub, (rr + 1) * sub)
        cos2[mine, :] = jnp.cos(angle)
        sin2[mine, :] = jnp.where(lane < HEAD // 2, -1.0, 1.0) * jnp.sin(angle)
    g_n.step(2)
    bulk[0].pass_x()
    g_joint.arrive()
    kvb_in.wait_recv()
    bias = jnp.concatenate([line(qb), kvb2[0], kvb2[1]], axis=1)
    n = sub // PARTS
    kv_far, kv_sib, kv_pass = [], [], []
    for q in range(PARTS):
        g_n.step(3, (q,))
        spots = [slice(rr * sub + q * n, rr * sub + (q + 1) * n) for rr in range(R)]
        cos_q, sin_q = (jnp.concatenate([t[p, :] for p in spots], axis=0) for t in (cos2, sin2))
        some = slice(q * n, (q + 1) * n)
        joint = dot(nall[:, some, :].reshape(R * n, width), wj[...]) + bias
        kv[:, c, some, :HEAD] = turn(joint[:, qw : qw + HEAD], cos_q, sin_q).astype(BF).reshape(R, n, HEAD)
        kv[:, c, some, HEAD:] = joint[:, qw + HEAD :].astype(BF).reshape(R, n, HEAD)
        own, far = (kv.at[:, k, pl.ds(q * n, n)] for k in (c, net.across_c))
        kv_far.append(net.copy(own, own, net.across))
        kv_sib.append(net.copy(own, own, net.sibling))
        kv_pass.append(net.copy(far, far, net.sibling))
        kv_far[q].start()
        kv_sib[q].start()
        queries = turn(joint[:, :qw], cos_q, sin_q).astype(BF)
        for rr, p in enumerate(spots):
            qs[p, :] = queries[rr * n : (rr + 1) * n]
    g_cot = LineGather(net, call)
    g_cot.step(0)
    tail = [net.here(o_x, out_x), net.here(o_gains, out_gains), net.here(turns, out_turns)]
    for cp in tail:
        cp.start()
    out_normed = net.here(nall, o_normed)
    out_normed.start()
    out_wj = net.here(wj, o_wj)
    out_wj.start()
    bulk[0].pass_y()
    bulk[1].pass_x()
    bulk[2].start()
    bulk[3].start()
    rows_d = wd.shape[0] // PIECES
    half_d = rows_d // 2
    early = [
        net.copy(
            wd.at[pl.ds(pl.multiple_of(i * rows_d + net.h * half_d, 16), half_d)], o_wdx.at[i], net.across
        )
        for i in range(EARLY)
    ]
    for cp in early:
        cp.start()
    for q in range(PARTS):
        kv_far[q].wait_recv()
        kv_pass[q].start()
    for cp in kv_sib + kv_pass:
        cp.wait_recv()
    g_cot.step(1)
    out_kv = net.here(kv, o_kv)
    out_kv.start()
    scale = HEAD ** (-0.5)
    g_out.arrive()
    rs = LineSum(net, part, rbu, rbd)
    for rr in [R - 1, 0] + list(range(R - 2, 0, -1)):
        limit = (rr + 1) * row_tok
        keys = kv[: rr + 1, :, :, :HEAD].reshape(limit, HEAD)
        values = kv[: rr + 1, :, :, HEAD:].reshape(limit, HEAD)
        mine = slice(rr * sub, (rr + 1) * sub)
        place = lax.broadcasted_iota(jnp.int32, (sub, limit), 1)
        here, first = place_of(rr)
        allowed = (place >= first) & (place <= here)
        for h in range(qw // HEAD):
            cols = slice(h * HEAD, (h + 1) * HEAD)
            s = jnp.where(allowed, dot(qs[mine, cols], keys, 1, 1) * scale, masked_score)
            e = jnp.exp(s - jnp.max(s, axis=-1, keepdims=True))
            p = e * (1.0 / jnp.sum(e, axis=-1, keepdims=True))
            att[mine, cols] = dot(p.astype(BF), values).astype(BF)
        part[rr] = dot(att[mine, :], wov[...]).astype(BF)
        if rr == 0:
            rs.step(0)
    out_q = net.here(qs, o_q)
    out_q.start()
    out_att = net.here(att, o_att)
    out_att.start()
    out_wo = net.here(wov, o_wo)
    out_wo.start()
    bulk[2].pass_x()
    g_cot.step(2)
    bulk[1].pass_y()
    rs.step(1)
    bulk[3].pass_x()
    g_cot.step(3)
    out_cot = net.here(call, o_cot)
    out_cot.start()
    rs.step(2)
    bulk[2].pass_y()
    rs.step(3)
    rs.total_into(o_mid)
    mid = o_mid[...]
    inv = lax.rsqrt(jnp.mean(mid * mid, axis=-1, keepdims=True) + epsilon)
    o_nmlp[...] = (mid * inv * o_gains[0:1, width:]).astype(BF)
    for src, dst in ((o_mid, out_mid), (o_nmlp, out_nmlp)):
        cp = net.here(src, dst)
        cp.start()
        tail.append(cp)
    bulk[3].pass_y()
    for g in bulk:
        g.arrive()
    for cp in early:
        cp.wait()
    for g in [g_joint, g_out, g_n, g_cot, rs] + bulk:
        g.finish()
    for out, _ in tok_in[1] + cot_in[1] + gain_copies:
        out.wait_send()
    for cp in kv_far + kv_sib + kv_pass:
        cp.wait_send()
    kv_x.wait_send()
    kvb_x.wait_send()
    for cp in tail + [out_normed, out_wj, out_kv, out_q, out_att, out_wo, out_cot]:
        cp.wait()


def attention_forward(
    sizes, tok, cot, wq, wkv, wo, wg, wu, wd, gain_a, gain_f, qb, kvb, lengths, rates
):
    dp, R, C = sizes
    sub = tok.shape[0] // C
    block = tok.shape[1]
    width = block * C
    qw, jw = wq.shape[1], wq.shape[1] + 2 * HEAD
    n = sub * R
    ff = wg.shape[0]
    shape = jax.ShapeDtypeStruct
    outs = [
        (shape((sub, width), BF), ANY),
        (shape((sub, width), F32), ANY), (shape((sub, width), BF), ANY),
        (shape((1, 2 * width), F32), ANY), (shape((n, 2 * HEAD), F32), ANY),
        (shape((R, sub, width), BF), ANY),
        (shape((n, qw), BF), ANY), (shape((R, C, sub, 2 * HEAD), BF), ANY),
        (shape((n, qw), BF), ANY), (shape((R, sub, width), BF), ANY),
        (shape((width, jw), BF), ANY), (shape((qw, width), BF), ANY),
        (shape((ff, width), BF), ANY), (shape((ff, width), BF), ANY),
        (shape((EARLY, ff // PIECES // 2, block), BF), ANY),
    ]
    return pl.pallas_call(
        functools.partial(attention_kernel, sizes),
        out_shape=[o for o, _ in outs],
        in_specs=[ANY] * 8 + [VMEM] * 4 + [SMEM, VMEM],
        out_specs=[s for _, s in outs],
        scratch_shapes=[
            pltpu.VMEM((C, sub, block), BF), pltpu.VMEM((C, sub, block), BF),
            pltpu.VMEM((1, 2 * block), F32), pltpu.VMEM((C, 1, 2 * block), F32), pltpu.VMEM((2, 1, HEAD), F32),
            pltpu.VMEM((R, sub, width), BF), pltpu.VMEM((R, sub, width), BF),
            pltpu.VMEM((width, jw), BF), pltpu.VMEM((qw, width), BF),
            pltpu.VMEM((R, C, sub, 2 * HEAD), BF), pltpu.VMEM((n, qw), BF),
            pltpu.VMEM((n, qw), BF), pltpu.VMEM((R, sub, width), BF),
            pltpu.VMEM((R, sub, width), BF), pltpu.VMEM((R, sub, width), BF),
            pltpu.VMEM((sub, width), BF), pltpu.VMEM((sub, width), F32),
            pltpu.VMEM((sub, width), BF), pltpu.VMEM((1, 2 * width), F32),
            pltpu.VMEM((n, 2 * HEAD), F32),
            pltpu.SemaphoreType.DMA((128,)), pltpu.SemaphoreType.DMA((128,)),
            pltpu.SemaphoreType.DMA((48,)),
        ],
        compiler_params=pltpu.CompilerParams(
            collective_id=1, has_side_effects=True, vmem_limit_bytes=VMEM_LIMIT
        ),
        name="attention_forward",
    )(tok, cot, wq, wkv, wo, wg, wu, wd, gain_a, gain_f, qb, kvb, lengths, rates)


def feedforward_kernel(
    sizes,
    nmlp, in_mid, in_gains, cot, wg, wu, wd, wdx, own_g, own_u,
    out_gmid, out_gain, o_down, o_sd, o_sm, o_sx, o_sg, o_gu, o_xt,
    w_gate, w_up, w_down, xall, call, acc, hid, gg, gu, cc, xt, part, rbu, rbd, dpart, g, x_d, y_d, o_gmid, o_gain, mid, gains,
    send, recv, local,
):
    net = Net(sizes, send, recv, local)
    net.arrive()
    R, C, r, c = net.R, net.C, net.r, net.c
    sub, width = nmlp.shape
    block = width // C
    n_tok = sub * R
    n_part = n_tok // PARTS
    n = sub // PARTS
    ff = w_gate.shape[0]
    tile = acc.shape[2]
    wide = width // tile
    own_cols = [pl.ds(pl.multiple_of(b * block, HEAD), block) for b in (c, net.across_c)]
    g_down = [
        WeightGather(
            net, wd, w_down, False, i, PIECES, crossed=wdx.at[i] if i < EARLY else None
        )
        for i in range(PIECES)
    ]
    in_x = [net.here(nmlp.at[pl.ds(q * n, n)], xall.at[q, r]) for q in range(PARTS)]
    in_norm = [net.here(in_mid, mid), net.here(in_gains, gains)]
    for cp in in_x + in_norm:
        cp.start()
    in_cot = [net.here(cot.at[:, pl.ds(q * n, n)], call.at[q]) for q in range(PARTS)]
    for cp in in_cot:
        cp.start()
    in_w = []
    for full, own, w in ((wg, own_g, w_gate), (wu, own_u, w_up)):
        for k in range(C):
            cols = pl.ds(pl.multiple_of(lax.rem(c + k, C) * block, HEAD), block)
            cp = net.here(full.at[:, cols] if k else own, w.at[:, cols])
            cp.start()
            in_w.append(cp)
    if hid.shape[1] > ff:
        for ref in (hid, gg, gu):
            ref[:n_tok, ff:] = jnp.zeros((n_tok, hid.shape[1] - ff), BF)
    net.barrier()
    for cp in in_x:
        cp.wait()
    g_x = LineGather(net, xall)
    g_x.step(0, (0,))
    for g_piece in g_down:
        g_piece.start()
    for cp in in_cot:
        cp.wait()
    call_out = net.copy(call, part, net.sibling)
    call_out.start()
    for i in (0, 1):
        cc[0, :, :, :, i * block : (i + 1) * block] = call[:, :, :, own_cols[i]]

    acts_out = [
        [
            net.copy(
                ref.at[pl.ds(q * n_part, n_part)], ref.at[pl.ds(n_tok + q * n_part, n_part)],
                net.sibling,
            )
            for ref in (hid, gg, gu)
        ]
        for q in range(PARTS)
    ]
    x_out = net.copy(xall, dpart, net.sibling)
    to_sibling = [cp for pair in acts_out for cp in pair]
    rs = LineSum(net, part, rbu, rbd)
    full = ff // tile
    rest = pl.ds(full * tile, ff - full * tile)

    def act(q, rows, back):
        mine = pl.ds(pl.multiple_of(q * n_part, n_part), n_part)
        x = xall[q].reshape(n_part, width)
        gate = dot(x, w_gate[rows, :], 1, 1)
        up = dot(x, w_up[rows, :], 1, 1)
        s = jax.nn.sigmoid(gate)
        silu = gate * s
        hid[mine, rows] = (silu * up).astype(BF)
        gg[mine, rows] = (back * up * s * (1.0 + gate * (1.0 - s))).astype(BF)
        gu[mine, rows] = (back * silu).astype(BF)

    g_x.step(1, (0,))
    g_x.step(0, (1,))
    g_down[0].pass_y()
    call_out.wait_recv()
    for i in (0, 1):
        cc[1, :, :, :, i * block : (i + 1) * block] = part[:, :, :, own_cols[i]]
    g_down[1].pass_y()
    g_down[4].pass_x()
    g_x.step(2, (0,))

    def hidden_back(t):
        rows = pl.ds(pl.multiple_of(t * tile, tile), tile)
        acc[t] = dot(call[...].reshape(n_tok, width), w_down[rows, :], 1, 1)

    @pl.loop(0, 3)
    def _(t):
        @pl.when(t == 0)
        def _():
            g_down[0].arrive()
            g_down[1].arrive()

        @pl.when(t == 1)
        def _():
            g_down[2].pass_y()
            g_x.step(1, (1,))
            g_down[2].arrive()

        @pl.when(t == 2)
        def _():
            g_down[3].pass_y()
            g_down[3].arrive()

        hidden_back(t)

    for cp in in_w:
        cp.wait()
    g_x.step(3, (0,))

    @pl.loop(0, PARTS)
    def _(q):
        @pl.loop(0, full)
        def _(t):
            rows = pl.ds(pl.multiple_of(t * tile, tile), tile)

            @pl.when((q == 1) & (t == 0))
            def _():
                g_x.step(3, (1,))

            @pl.when(q == 0)
            def _():
                @pl.when(t == 2)
                def _():
                    g_down[4].pass_y()

                @pl.when(t == 3)
                def _():
                    g_down[4].arrive()
                    hidden_back(t)

            act(q, rows, acc[t, pl.ds(pl.multiple_of(q * n_part, n_part), n_part)])

            @pl.when((q == 1) & (t == full - 1))
            def _():
                rs.step(1, (0,))

            @pl.when((q == 0) & (t == full - 1))
            def _():
                g_x.step(2, (1,))

        act(q, rest, dot(call[q].reshape(n_part, width), w_down[rest, :], 1, 1))

        for k in range(PARTS):

            @pl.when(q == k)
            def _():
                for cp in acts_out[k]:
                    cp.start()

        mine = pl.ds(pl.multiple_of(q * n_part, n_part), n_part)

        @pl.loop(0, wide)
        def _(i):
            cols = pl.ds(pl.multiple_of(i * tile, tile), tile)
            total = dot(gg[mine, :ff], w_gate[:, cols]) + dot(gu[mine, :ff], w_up[:, cols])
            part[q, :, :, cols] = total.astype(BF).reshape(R, n, tile)

        @pl.when(q == 0)
        def _():
            rs.step(0, (0,))

        @pl.when(q == 1)
        def _():
            rs.step(0, (1,))
            rs.step(2, (0,))
            x_out.start()

    for g_piece in g_down:
        g_piece.finish()
    for cp in to_sibling:
        cp.wait_recv()
    outs = [net.here(gu, o_gu)]
    outs[0].start()

    def all_tiles(body):
        @pl.loop(0, full)
        def _(t):
            body(pl.ds(pl.multiple_of(t * tile, tile), tile))

        body(rest)

    def down_grad(rows):
        total = dot(hid[:, rows], cc[...].reshape(2 * n_tok, 2 * block), 0, 0)
        w_gate[rows, : 2 * block] = total.astype(BF)

    all_tiles(down_grad)
    half_ff = ff // 2
    cut = x_d.shape[1]

    def down_piece(i, h, ab):
        first, count = (cut, half_ff - cut) if ab else (0, cut)
        return w_gate.at[
            pl.ds(pl.multiple_of(h * half_ff + first, 16), count), pl.ds(i * block, block)
        ]

    sum_d = BlockSum(net, down_piece, down_piece, x_d, y_d)
    sum_d.start()
    rs.step(1, (1,))
    rs.step(3, (0,))

    x_out.wait_recv()
    for i in (0, 1):
        rows = slice(i * block, (i + 1) * block)
        xt[rows, :n_tok] = xall[:, :, :, own_cols[i]].reshape(n_tok, block).T
        xt[rows, n_tok:] = dpart[:, :, :, own_cols[i]].reshape(n_tok, block).T

    @pl.loop(0, wide)
    def _(i):
        cols = pl.ds(pl.multiple_of(i * tile, tile), tile)
        total = dot(hid[:n_tok, :ff], w_down[:, cols])
        dpart[:, :, :, cols] = total.astype(BF).reshape(PARTS, R, n, tile)

    rs.step(2, (1,))
    out_down = [net.here(dpart.at[q], o_down.at[:, pl.ds(q * n, n)]) for q in range(PARTS)]
    for cp in out_down:
        cp.start()
    def gate_grad(cols):
        total = dot(xt[...], gg[:, cols])
        g[:, :, cols] = total.astype(BF).reshape(4, g.shape[1], cols.size)

    all_tiles(gate_grad)
    for src, dst in ((g, o_sg), (xt, o_xt)):
        cp = net.here(src, dst)
        cp.start()
        outs.append(cp)
    rs.step(3, (1,))
    o_gmid[...] = jnp.zeros_like(o_gmid)
    rs.total_into(o_gmid)
    for cp in in_norm:
        cp.wait()
    grad = o_gmid[...]
    m = mid[...]
    inv = lax.rsqrt(jnp.mean(m * m, axis=-1, keepdims=True) + epsilon)
    normal = m * inv
    e = grad * gains[0:1, width:]
    back = inv * (e - normal * jnp.mean(e * normal, axis=-1, keepdims=True))
    o_gain[...] = jnp.sum(grad * normal, axis=0, keepdims=True)
    for q in range(PARTS):
        rows = slice(q * n, (q + 1) * n)
        o_gmid[rows] = call[q, r].astype(F32) + back[rows]
    for src, dst in ((o_gmid, out_gmid), (o_gain, out_gain)):
        cp = net.here(src, dst)
        cp.start()
        outs.append(cp)
    rs.finish()
    sum_d.add()
    own_half = w_gate.at[
        pl.ds(pl.multiple_of(net.h * half_ff, 16), half_ff), pl.ds(0, block)
    ]
    for src, dst in (
        (own_half, o_sd), (down_piece(0, net.other_h, 0), o_sm), (down_piece(1, net.h, 1), o_sx)
    ):
        cp = net.here(src, dst)
        cp.start()
        outs.append(cp)
    sum_d.finish()
    g_x.finish()
    for cp in to_sibling + [call_out, x_out]:
        cp.wait_send()
    for cp in outs + out_down:
        cp.wait()


def feedforward(sizes, nmlp, mid, gains, cot, wg, wu, wd, wdx, own_g, own_u):
    dp, R, C = sizes
    sub, width = nmlp.shape
    block = width // C
    n_tok = R * sub
    ff = wd.shape[0]
    tile = 512
    cut = ff // 4
    shape = jax.ShapeDtypeStruct
    outs = [
        (shape((sub, width), F32), ANY), (shape((1, width), F32), ANY),
        (shape((R, sub, width), BF), ANY), (shape((ff // 2, block), BF), ANY),
        (shape((cut, block), BF), ANY), (shape((ff // 2 - cut, block), BF), ANY),
        (shape((4, block // 2, ff), BF), ANY),
        (shape((2 * n_tok, -(-ff // HEAD) * HEAD), BF), ANY),
        (shape((2 * block, 2 * n_tok), BF), ANY),
    ]
    v = pltpu.VMEM
    line = v((PARTS, R, sub // PARTS, width), BF)
    acts = v((2 * n_tok, -(-ff // HEAD) * HEAD), BF)
    weight = v((ff, width), BF)
    return pl.pallas_call(
        functools.partial(feedforward_kernel, sizes),
        out_shape=[o for o, _ in outs],
        in_specs=[ANY] * 10,
        out_specs=[s for _, s in outs],
        scratch_shapes=[
            weight, weight, weight, line, line, v((ff // tile, n_tok, tile), F32), acts, acts, acts,
            v((2, PARTS, R, sub // PARTS, 2 * block), BF),
            v((2 * block, 2 * n_tok), BF), line, line, line, line, v((4, block // 2, ff), BF),
            v((2, cut, block), BF), v((2, ff // 2 - cut, block), BF),
            v((sub, width), F32), v((1, width), F32), v((sub, width), F32), v((1, 2 * width), F32),
            pltpu.SemaphoreType.DMA((128,)), pltpu.SemaphoreType.DMA((128,)),
            pltpu.SemaphoreType.DMA((48,)),
        ],
        compiler_params=pltpu.CompilerParams(
            collective_id=2, has_side_effects=True, vmem_limit_bytes=VMEM_LIMIT
        ),
        name="feedforward",
    )(nmlp, mid, gains, cot, wg, wu, wd, wdx, own_g, own_u)


def backward_kernel(
    sizes,
    in_gmid, in_x, in_mid, in_gains, in_gain_mlp, lengths, in_turns,
    normed, q, kv, att, wj, wo, down, sm, sx, sg, up_grads, xt_in,
    o_layer, o_input, out_vec, out_j, o_db, o_ga, o_gb, o_ua, o_ub, o_oa, o_ob,
    mall, nall, qs, kvs, atts, wjs, wos, dpart, drbu, drbd, part, rbu, rbd, grads, dq, dkv, dkv16, dk_sib, dk_in,
    joint, lay,
    s_g, s_u, x_g, x_u, y_g, y_u,
    wjo, wjx, s_j, x_j, y_j, woo, wox, s_o, x_o, y_o, jb, jk, jk2, jgot, v1, v1in, v2, v2in, o_vec, o_j,
    gmid, x_in, mid, gains, gain_mlp, turns, gu, xt,
    send, recv, local,
):
    net = Net(sizes, send, recv, local)
    R, C, r, c = net.R, net.C, net.r, net.c
    sem = pltpu.get_barrier_semaphore()
    half = net.dp // 2
    others = [(net.d, r, lax.rem(c + k, C)) for k in range(1, C)]
    others += [(net.d, lax.rem(r + k, R), c) for k in range(1, R)]
    others += [(net.mate[0], lax.rem(r + k, R), c) for k in range(R)]
    for dev in others:
        pl.semaphore_signal(sem, inc=1, device_id=dev, device_id_type=MESH)
    R, C, r, c = net.R, net.C, net.r, net.c
    sub, width = in_gmid.shape
    block = width // C
    n_tok = sub * R
    row_tok = sub * C
    qw = qs.shape[1]
    slot = lax.rem(r, 2)
    cos2, sin2 = turns.at[:, pl.ds(0, HEAD)], turns.at[:, pl.ds(HEAD, HEAD)]
    partner_r = r + 1 - 2 * slot
    small_loads = [
        net.here(a, b) for a, b in
        ((in_gmid, gmid), (in_x, x_in), (in_mid, mid), (in_gains, gains), (in_gain_mlp, gain_mlp),
         (in_turns, turns))
    ]
    up_loads = [net.here(up_grads, gu), net.here(xt_in, xt)]
    for cp in small_loads + up_loads:
        cp.start()
    loads = [
        net.here(a, b) for a, b in
        ((wo, wos), (att, atts), (q, qs), (kv, kvs), (down, dpart), (sg, s_g),
         (normed, nall), (wj, wjs))
    ]
    for cp in loads:
        cp.start()
    pl.semaphore_wait(sem, len(others))

    small_loads[0].wait()
    mall[r] = gmid[...].astype(BF)
    g_m = LineGather(net, mall)
    g_m.step(0)
    sum_g = BlockSum(net, halves(sg, x_g.shape[1]), halves(s_g, x_g.shape[1]), x_g, y_g)
    sum_u = BlockSum(net, halves(s_u, x_u.shape[1]), halves(s_u, x_u.shape[1]), x_u, y_u)
    sum_g.start()
    for cp in up_loads:
        cp.wait()
    ff = s_u.shape[2]

    def up_tile(cols):
        total = dot(xt[...], gu[:, cols])
        s_u[:, :, cols] = total.astype(BF).reshape(4, s_u.shape[1], cols.size)

    @pl.loop(0, ff // 512)
    def _(t):
        up_tile(pl.ds(pl.multiple_of(t * 512, 512), 512))

    up_tile(pl.ds(ff // 512 * 512, ff % 512))
    sum_u.start()
    cut_d, rest_d = sm.shape[0], sx.shape[0]
    sum_d = [
        net.copy(sx, o_db.at[pl.ds(cut_d, rest_d)], net.across),
        net.copy(sm, o_db.at[pl.ds(0, cut_d)], net.mate),
    ]
    sum_d[0].start()
    g_m.step(1)
    for cp in loads[:6] + small_loads[1:]:
        cp.wait()
    g_m.step(2)
    sum_g.add()
    sum_g.pass_on(o_gb, (0,))
    g_m.step(3)
    rs_d = LineSum(net, dpart, drbu, drbd)
    rs_d.step(0)
    m_all = mall[...].reshape(n_tok, width)
    grads[...] = dot(m_all, wos[...], 1, 1).astype(BF)

    def to_columns(src, dst):
        rows = pl.ds(pl.multiple_of(c * sub, sub), sub)
        mine = net.here(src.at[:, pl.ds(pl.multiple_of(c * block, HEAD), block)], dst.at[rows])
        mine.start()
        pairs = []
        for k in range(1, C):
            to, frm = lax.rem(c + k, C), lax.rem(c + C - k, C)
            i = net.n
            net.n += 1
            cut = src.at[:, pl.ds(pl.multiple_of(to * block, HEAD), block)]
            out = net.like(i, cut, dst.at[rows], net.at_col(to))
            out.start()
            from_rows = pl.ds(pl.multiple_of(frm * sub, sub), sub)
            pairs.append((out, net.like(i, cut, dst.at[from_rows], net.at_col(to))))
        return mine, pairs

    def settle(exchange):
        exchange[0].wait()
        for out, inc in exchange[1]:
            inc.wait_recv()
            out.wait_send()

    sib_blocks = [b + 1 - 2 * lax.rem(b, 2) for b in (c, net.across_c)]
    total = dot(atts[...], m_all, 0, 0)
    for b in range(C):
        woo[2 * b : 2 * b + 2] = (
            total[:, b * block : (b + 1) * block].astype(BF).reshape(2, qw // 2, block)
        )
    out_x = [net.copy(woo.at[pl.ds(2 * b, 2)], wox.at[i], net.sibling) for i, b in enumerate(sib_blocks)]
    for cp in out_x:
        cp.start()
    scale = HEAD ** (-0.5)
    heads = qw // HEAD
    ends = [lengths[0, 0]]
    for i in range(1, lengths.shape[1] - 1):
        ends.append(ends[-1] + lengths[0, i])
    for rr in reversed(range(R)):
        limit = (rr + 1) * row_tok
        keys = kvs[: rr + 1, :, :, :HEAD].reshape(limit, HEAD)
        values = kvs[: rr + 1, :, :, HEAD:].reshape(limit, HEAD)
        mine = slice(rr * sub, (rr + 1) * sub)
        stack = lambda ref: jnp.concatenate(
            [ref[mine, h * HEAD : (h + 1) * HEAD] for h in range(heads)], axis=0
        )
        qh, gh = stack(qs), stack(grads)
        place = lax.broadcasted_iota(jnp.int32, (limit, heads * sub), 0)
        lane = lax.broadcasted_iota(jnp.int32, (1, heads * sub), 1)
        here = rr * row_tok + c * sub + lax.rem(lane, sub)
        first = jnp.zeros_like(here)
        for end in ends:
            first = jnp.where(here >= end, end, first)
        s = jnp.where(
            (place >= first) & (place <= here), dot(keys, qh, 1, 1) * scale, masked_score
        )
        e = jnp.exp(s - jnp.max(s, axis=0, keepdims=True))
        p = e * (1.0 / jnp.sum(e, axis=0, keepdims=True))
        g = dot(values, gh, 1, 1)
        ds = (p * (g - jnp.sum(p * g, axis=0, keepdims=True))).astype(BF)
        dv = dot(p.astype(BF), gh)
        dk = dot(ds, qh) * scale
        if rr == R - 1:
            dkv[:, :HEAD] = dk
            dkv[:, HEAD:] = dv
        else:
            dkv[:limit, :HEAD] += dk
            dkv[:limit, HEAD:] += dv
        dqs = dot(ds, keys, 0, 0) * scale
        for h in range(heads):
            dq[mine, h * HEAD : (h + 1) * HEAD] = dqs[h * sub : (h + 1) * sub]
        if rr == R - 2:
            rs_d.step(1)
            for i, b in enumerate((c, net.across_c)):
                out_x[i].wait_recv()
                s_o[2 * i : 2 * i + 2] = (
                    woo[pl.ds(2 * b, 2)].astype(F32) + wox[i].astype(F32)
                ).astype(BF)
    sib_c = c + 1 - 2 * lax.rem(c, 2)
    far_c = net.across_c
    far_sib_c = far_c + 1 - 2 * lax.rem(far_c, 2)
    dkv16[...] = dkv[...].astype(BF).reshape(dkv16.shape)
    dk_copies = [
        net.copy(dkv16.at[:, far_sib_c], dk_sib.at[1], net.sibling),
        net.copy(dkv16.at[:, sib_c], dk_sib.at[0], net.sibling),
    ]
    for cp in dk_copies:
        cp.start()
    dk_copies[0].wait_recv()
    dk_in[0] = (dkv16[:, far_c].astype(F32) + dk_sib[1].astype(F32)).astype(BF)
    dk_copies.append(net.copy(dk_in.at[0], dk_in.at[1], net.across))
    dk_copies[2].start()
    sum_g.pass_on(o_gb, (1,))
    sum_o = BlockSum(net, halves(s_o, x_o.shape[1]), halves(s_o, x_o.shape[1]), x_o, y_o)
    sum_o.start()
    rs_d.step(2)
    for cp in loads[6:]:
        cp.wait()
    slots = dkv16[:, c].astype(F32)
    dk_copies[1].wait_recv()
    slots = slots + dk_sib[0].astype(F32)
    dk_copies[2].wait_recv()
    slots = slots + dk_in[1].astype(F32)
    slots = slots.reshape(n_tok, 2 * HEAD)
    joint[:, :qw] = turn(dq[...], cos2[...], -sin2[...]).astype(BF)
    joint[:, qw : qw + HEAD] = turn(slots[:, :HEAD], cos2[...], -sin2[...]).astype(BF)
    joint[:, qw + HEAD :] = slots[:, HEAD:].astype(BF)
    part[...] = dot(joint[...], wjs[...], 1, 1).astype(BF).reshape(R, sub, width)
    rs = LineSum(net, part, rbu, rbd)
    rs.step(0)
    total = dot(nall[...].reshape(n_tok, width), joint[...], 0, 0)
    wjo[...] = total.astype(BF).reshape(wjo.shape)
    joint_x = [net.copy(wjo.at[pl.ds(2 * b, 2)], wjx.at[i], net.sibling) for i, b in enumerate(sib_blocks)]
    for cp in joint_x:
        cp.start()
    bias = jnp.sum(joint[...].astype(F32), axis=0, keepdims=True)
    for i, b in enumerate((c, net.across_c)):
        joint_x[i].wait_recv()
        s_j[2 * i : 2 * i + 2] = (
            wjo[pl.ds(2 * b, 2)].astype(F32) + wjx[i].astype(F32)
        ).astype(BF)
    sum_j = BlockSum(net, halves(s_j, x_j.shape[1]), halves(s_j, x_j.shape[1]), x_j, y_j)
    sum_j.start()
    sum_u.add()
    sum_u.pass_on(o_ub)
    rs_d.step(3)
    lay[0] = mid[...]
    rs_d.total_into(lay.at[0])
    jk[...] = lay[0].astype(BF)
    rs.step(1)
    sum_o.add()
    sum_o.pass_on(o_ob)
    rs.step(2)
    sum_j.add()
    sum_j.pass_on(jb)
    sum_d[1].start()
    keeps = [
        net.here(src.at[net.h], dst)
        for src, dst in ((s_g, o_ga), (s_u, o_ua), (s_o, o_oa))
    ]
    for cp in keeps:
        cp.start()
    rs.step(3)
    lay[1] = jnp.zeros_like(lay[1])
    rs.total_into(lay.at[1])
    grad = lay[1]
    x = x_in[...].astype(F32)
    inv = lax.rsqrt(jnp.mean(x * x, axis=-1, keepdims=True) + epsilon)
    normal = x * inv
    e = grad * gains[0:1, :width]
    back = inv * (e - normal * jnp.mean(e * normal, axis=-1, keepdims=True))
    gain_attn = jnp.sum(grad * normal, axis=0, keepdims=True)
    for k in range(C):
        cut = slice(k * block, (k + 1) * block)
        v1[k, :, :block] = gain_attn[:, cut]
        v1[k, :, block : 2 * block] = gain_mlp[:, cut]
        v1[k, :, 2 * block :] = bias
    v_copies = []
    for k in range(1, C):
        to, frm = lax.rem(c + k, C), lax.rem(c + C - k, C)
        i = net.n
        net.n += 1
        out = net.like(i, v1.at[to], v1in.at[c], net.at_col(to))
        out.start()
        v_copies.append((out, net.like(i, v1.at[to], v1in.at[frm], net.at_col(to)), frm))
    jk2[...] = (gmid[...] + back).astype(BF)
    input_x = to_columns(jk2, o_input)
    layer_x = to_columns(jk, o_layer)
    sum_j.finish()
    ja = s_j.at[net.h]
    own_cols = pl.ds(pl.multiple_of(qw + slot * HEAD, HEAD), HEAD)
    mate_cols = pl.ds(pl.multiple_of(qw + (1 - slot) * HEAD, HEAD), HEAD)
    jgot[0] = ja[:, mate_cols].astype(F32) + jb[:, mate_cols].astype(F32)
    slot_x = net.copy(jgot.at[0], jgot.at[1], net.at_row(partner_r))
    slot_x.start()
    o_j[:, :qw] = ja[:, :qw].astype(F32) + jb[:, :qw].astype(F32)
    total = v1[c]
    for _, inc, frm in v_copies:
        inc.wait_recv()
        total = total + v1in[frm]
    v2[...] = total
    far = []
    for same in (1, 0):
        for k in range(R):
            if same and k == 0:
                continue
            to, frm = lax.rem(r + k, R), lax.rem(r + R - k, R)
            i = net.n
            net.n += 1
            dst_d = net.d if same else net.mate[0]
            hs = net.h if same else net.other_h
            out = net.like(i, v2, v2in.at[net.h, r], (dst_d, to, c))
            out.start()
            far.append((out, net.like(i, v2, v2in.at[hs, frm], (dst_d, to, c))))
    v2in[net.h, r] = total
    slot_x.wait_recv()
    o_j[:, qw:] = ja[:, own_cols].astype(F32) + jb[:, own_cols].astype(F32) + jgot[1]
    tail = [net.here(o_j, out_j)]
    tail[0].start()
    for g in (sum_g, sum_u, sum_o):
        g.finish()
    for cp in sum_d:
        cp.wait()
    for cp in keeps:
        cp.wait()
    for _, inc in far:
        inc.wait_recv()
    gain_sum = v2in[0, 0, :, : 2 * block]
    for hh in (0, 1):
        for k in range(R):
            if hh or k:
                gain_sum = gain_sum + v2in[hh, k, :, : 2 * block]
    o_vec[:, : 2 * block] = gain_sum
    o_vec[:, 2 * block : 2 * block + qw] = (
        v2in[0, r, :, 2 * block : 2 * block + qw] + v2in[1, r, :, 2 * block : 2 * block + qw]
    )
    cols = pl.ds(pl.multiple_of(2 * block + qw + slot * HEAD, HEAD), HEAD)
    o_vec[:, 2 * block + qw :] = (
        v2in[0, r, :, cols] + v2in[1, r, :, cols]
        + v2in[0, partner_r, :, cols] + v2in[1, partner_r, :, cols]
    )
    tail.append(net.here(o_vec, out_vec))
    tail[1].start()
    settle(layer_x)
    settle(input_x)
    for g in (g_m, rs_d, rs):
        g.finish()
    for cp in out_x + joint_x + [slot_x]:
        cp.wait_send()
    for cp in dk_copies:
        cp.wait_send()
    for cps in v_copies + far:
        cps[0].wait_send()
    for cp in tail:
        cp.wait()


def backward(sizes, gmid, x_in, mid, gains, gain_mlp, lengths, turns, normed, q, kv, att, wj, wo,
             down, sm, sx, sg, up_grads, xt):
    dp, R, C = sizes
    sub, width = gmid.shape
    block = width // C
    n, qw = q.shape
    jw = wj.shape[1]
    ff = sg.shape[2]
    shape = jax.ShapeDtypeStruct
    d2, g2, w2, j2 = (ff // 2, block), (block // 2, ff), (qw // 2, block), (block // 2, jw)
    vec = 2 * block + jw
    outs = [
        (shape((C * sub, block), BF), ANY), (shape((C * sub, block), BF), ANY),
        (shape((1, vec - HEAD), F32), ANY), (shape((block // 2, jw - HEAD), F32), ANY),
        (shape(d2, BF), ANY), (shape(g2, BF), ANY), (shape(g2, BF), ANY),
        (shape(g2, BF), ANY), (shape(g2, BF), ANY), (shape(w2, BF), ANY), (shape(w2, BF), ANY),
    ]
    v = pltpu.VMEM
    four = lambda s: v((4,) + s, BF)

    def landing(s):
        cut = x_first(s[0])
        return [v((2, cut) + s[1:], BF), v((2, s[0] - cut) + s[1:], BF)]

    x_g, y_g = landing(g2)
    x_o, y_o = landing(w2)
    x_j, y_j = landing(j2)
    line = v((R, sub, width), BF)
    return pl.pallas_call(
        functools.partial(backward_kernel, sizes),
        out_shape=[o for o, _ in outs],
        in_specs=[ANY] * 5 + [SMEM] + [ANY] * 13,
        out_specs=[s for _, s in outs],
        scratch_shapes=[
            line, line, v((n, qw), BF), v(kv.shape, BF), v((n, qw), BF), v((width, jw), BF),
            v((qw, width), BF), line, line, line, line, line, line, v((n, qw), BF), v((n, qw), F32),
            v((n * C, 2 * HEAD), F32), v(kv.shape, BF), v((2, R, sub, 2 * HEAD), BF),
            v((2, R, sub, 2 * HEAD), BF),
            v((n, jw), BF), v((2, sub, width), F32),
            four(g2), four(g2), x_g, x_g, y_g, y_g,
            v((8,) + j2, BF), v((2, 2) + j2, BF), four(j2), x_j, y_j,
            v((8,) + w2, BF), v((2, 2) + w2, BF), four(w2), x_o, y_o,
            v(j2, BF), v((sub, width), BF), v((sub, width), BF), v((2, j2[0], HEAD), F32),
            v((C, 1, vec), F32), v((C, 1, vec), F32), v((1, vec), F32), v((2, R, 1, vec), F32),
            v((1, vec - HEAD), F32), v((block // 2, jw - HEAD), F32),
            v(gmid.shape, F32), v(x_in.shape, BF), v(mid.shape, F32), v(gains.shape, F32),
            v(gain_mlp.shape, F32), v(turns.shape, F32), v(up_grads.shape, BF), v(xt.shape, BF),
            pltpu.SemaphoreType.DMA((128,)), pltpu.SemaphoreType.DMA((128,)),
            pltpu.SemaphoreType.DMA((48,)),
        ],
        compiler_params=pltpu.CompilerParams(
            collective_id=3, has_side_effects=True, vmem_limit_bytes=VMEM_LIMIT
        ),
        name="backward",
    )(gmid, x_in, mid, gains, gain_mlp, lengths, turns, normed, q, kv, att, wj, wo, down, sm, sx, sg, up_grads, xt)

def finish_kernel(
    d, vec, joint, da, db, ga, gb, ua, ub, oa, ob, layer, inp,
    o_again, o_fgain, o_qb, o_kvb, o_q, o_kv, o_out, o_gate, o_up, o_down, o_layer, o_input,
    vec_v, joint_v, da_v, db_v, ga_v, gb_v, ua_v, ub_v, oa_v, ob_v,
    layer_v, inp_v, again_v, fgain_v, qb_v, kvb_v, q_v, kv_v, out_v, gate_v, up_v, down_v, sem_in, sem_out,
):
    pairs = (
        (vec, vec_v), (joint, joint_v), (oa, oa_v), (ob, ob_v), (da, da_v), (db, db_v),
        (ga, ga_v), (gb, gb_v), (ua, ua_v), (ub, ub_v), (layer, layer_v), (inp, inp_v),
    )
    loads = [pltpu.make_async_copy(s, t, sem_in.at[i]) for i, (s, t) in enumerate(pairs)]
    for cp in loads:
        cp.start()
    stores = []

    def store(src, dst):
        cp = pltpu.make_async_copy(src, dst, sem_out.at[len(stores)])
        cp.start()
        stores.append(cp)

    block, qw = o_again.shape[0], o_q.shape[1]
    loads[0].wait()
    second = d[0, 0] == 1
    again_v[...] = vec_v[0, :block]
    fgain_v[...] = vec_v[0, block : 2 * block]
    bias = vec_v[0:1, 2 * block :]
    pick = lambda v: jnp.where(second, v[:, v.shape[1] // 2 :], v[:, : v.shape[1] // 2])
    qb_v[...] = pick(bias[:, :qw])[0]
    kvb_v[...] = pick(bias[:, qw:])[0]
    for src, dst in ((again_v, o_again), (fgain_v, o_fgain), (qb_v, o_qb), (kvb_v, o_kvb)):
        store(src, dst)
    loads[1].wait()
    q_v[...] = joint_v[:, :qw]
    kv_v[...] = joint_v[:, qw:]
    store(q_v, o_q)
    store(kv_v, o_kv)
    for i, (a, b, f, o) in enumerate(
        ((oa_v, ob_v, out_v, o_out), (da_v, db_v, down_v, o_down), (ga_v, gb_v, gate_v, o_gate),
         (ua_v, ub_v, up_v, o_up))
    ):
        loads[2 + 2 * i].wait()
        loads[3 + 2 * i].wait()
        f[...] = a[...].astype(F32) + b[...].astype(F32)
        store(f, o)
    for i, (src, dst) in enumerate(((layer_v, o_layer), (inp_v, o_input))):
        loads[10 + i].wait()
        store(src, dst)
    for cp in stores:
        cp.wait()


def finish(d, layer, inp, vec, joint, da, db, ga, gb, ua, ub, oa, ob):
    block, qw, kvw = layer.shape[1], oa.shape[0] * 2, joint.shape[1] - oa.shape[0] * 2
    f32 = lambda *s: jax.ShapeDtypeStruct(s, F32)
    like = lambda v: jax.ShapeDtypeStruct(v.shape, F32)
    results = [
        f32(block), f32(block), f32(qw // 2), f32(kvw // 2), f32(joint.shape[0], qw),
        f32(joint.shape[0], kvw), like(oa), like(ga), like(ua), like(da),
    ]
    v = lambda a: pltpu.VMEM(a.shape, a.dtype)
    out = pl.pallas_call(
        finish_kernel,
        out_shape=results + [jax.ShapeDtypeStruct(a.shape, BF) for a in (layer, inp)],
        in_specs=[SMEM] + [ANY] * 12,
        out_specs=[ANY] * 12,
        scratch_shapes=[v(a) for a in (vec, joint, da, db, ga, gb, ua, ub, oa, ob, layer, inp)]
        + [v(a) for a in results]
        + [pltpu.SemaphoreType.DMA((12,)), pltpu.SemaphoreType.DMA((12,))],
        compiler_params=pltpu.CompilerParams(vmem_limit_bytes=VMEM_LIMIT),
        name="finish",
    )(d, vec, joint, da, db, ga, gb, ua, ub, oa, ob, layer, inp)
    again, fgain, q_bias, kv_bias, q, kv, o, gate, up, down, layer, inp = out
    return layer, inp, again, q, q_bias, kv, kv_bias, o, fgain, gate, up, down


def on_device(
    tokens_in, seq_lengths, attention_gain, query_weight, query_bias, keyvalue_weight,
    keyvalue_bias, output_weight, feedforward_gain, gate_weight, up_weight, down_weight,
    cotangent,
):
    sizes = dp, rows, cols = tuple(lax.axis_size(a) for a in ("dp", "row", "col"))
    d, col = lax.axis_index("dp"), lax.axis_index("col")
    sub = tokens_in.shape[0] // cols
    block = tokens_in.shape[1]
    wq_width = query_weight.shape[1]
    lane = np.arange(HEAD) % (HEAD // 2)
    rates = jnp.asarray((rope_base ** (-lane * (2.0 / HEAD))).astype(np.float32)[None])
    (x_own, middle, nmlp, gains, turns, normed, queries, kv, attended, cot_all, w_joint, w_out,
     w_gate, w_up, down_crossed) = attention_forward(
        sizes, tokens_in, cotangent, query_weight, keyvalue_weight, output_weight, gate_weight.T,
        up_weight.T, down_weight, attention_gain, feedforward_gain, query_bias, keyvalue_bias, seq_lengths, rates,
    )
    grad_middle, gain_mlp, down_part, da, sum_mate, sum_across, sum_gate, up_grads, up_tokens = feedforward(
        sizes, nmlp, middle, gains, cot_all, w_gate, w_up, down_weight, down_crossed,
        gate_weight.T, up_weight.T,
    )
    layer_out, input_grad, vec, joint, db, ga, gb, ua, ub, oa, ob = backward(
        sizes, grad_middle, x_own, middle, gains, gain_mlp, seq_lengths, turns, normed, queries, kv,
        attended, w_joint, w_out, down_part, sum_mate, sum_across, sum_gate,
        up_grads, up_tokens,
    )
    if dp == 2:
        return finish(
            d.reshape(1, 1), layer_out, input_grad, vec, joint, da, db, ga, gb, ua, ub, oa, ob
        )
    h = d // (dp // 2)

    def rest_of_dp(v):
        full = jnp.concatenate([jnp.where(h == 0, v, 0.0), jnp.where(h == 1, v, 0.0)], axis=0)
        return lax.psum_scatter(full, "dp", scatter_dimension=0, tiled=True)

    vec = lax.psum(jnp.where(h == 0, vec[0], 0.0), "dp")

    def own_share(v):
        n = v.shape[0] // dp
        return lax.dynamic_slice_in_dim(v, d * n, n)

    both = lambda a, b: rest_of_dp(a.astype(F32) + b.astype(F32))
    joint = rest_of_dp(joint)
    bias = vec[2 * block :]
    return (
        layer_out, input_grad, vec[:block], joint[:, :wq_width], own_share(bias[:wq_width]),
        joint[:, wq_width:], own_share(bias[wq_width:]), both(oa, ob), vec[block : 2 * block],
        both(ga, gb), both(ua, ub), both(da, db),
    )


def solution(mesh):
    return jax.shard_map(
        on_device,
        mesh=mesh,
        in_specs=(
            P(("dp", "row"), "col"), P("dp", None), P("col"), P("col", "row"), P("row"),
            P("col", "row"), P("row"), P("row", "col"), P("col"), P("col", "row"),
            P("col", "row"), P("row", "col"), P(("dp", "row"), "col"),
        ),
        out_specs=(
            P(("dp", "row"), "col"), P(("dp", "row"), "col"), P("col"),
            P(("col", "dp"), "row"), P(("row", "dp")), P(("col", "dp"), "row"),
            P(("row", "dp")), P(("row", "dp"), "col"), P("col"), P(("col", "dp"), "row"),
            P(("col", "dp"), "row"), P(("row", "dp"), "col"),
        ),
        check_vma=False,
    )
```
